32 devices in a mesh: dp: 4 (over y, core), seq: 8 (over z, x).
Axes of the slice: x: 2, y: 2, z: 4, core: 2. Of those that a mesh axis runs over, the one named last changes fastest.
Arguments:
- inputs: bfloat16 [4, 2048, 1024], P('dp', 'seq'), may hold values from -6 to 6
- segments: int32 [4, 2048], P('dp'), may hold values from 0 to 8, as said below
- cotangent: bfloat16 [4, 2048, 1024], P('dp', 'seq'), may hold values from -6 to 6
- input_gain: float32 [1024], replicated, may hold values from 0.5 to 1.5
- query_weight: bfloat16 [1024, 512], replicated, may hold values from -0.1875 to 0.1875
- key_weight: bfloat16 [1024, 128], replicated, may hold values from -0.1875 to 0.1875
- value_weight: bfloat16 [1024, 128], replicated, may hold values from -0.1875 to 0.1875
- attention_weight: bfloat16 [512, 1024], replicated, may hold values from -2 to 2
- gating_weight: bfloat16 [1024, 1536], replicated, may hold values from -0.1875 to 0.1875
- inner_weight: bfloat16 [1024, 1792], replicated, may hold values from -0.1875 to 0.1875
- step_weight: bfloat16 [1024, 24], replicated, may hold values from -0.1875 to 0.1875
- step_bias: float32 [24], replicated, may hold values from -1 to 0.5
- decay_log: float32 [24], replicated
- skip_scale: float32 [24], replicated, may hold values from 0.5 to 1.5
- conv_weight: float32 [4, 1792], replicated, may hold values from -3 to 3
- conv_bias: float32 [1792], replicated, may hold values from -3 to 3
- mixer_gain: float32 [1536], replicated, may hold values from 0.5 to 1.5
- mixer_weight: bfloat16 [1536, 1024], replicated, may hold values from -0.15625 to 0.15625
- feed_gain: float32 [1024], replicated, may hold values from 0.5 to 1.5
- gate_weight: bfloat16 [1024, 2048], replicated, may hold values from -0.1875 to 0.1875
- up_weight: bfloat16 [1024, 2048], replicated, may hold values from -0.1875 to 0.1875
- down_weight: bfloat16 [2048, 1024], replicated, may hold values from -0.125 to 0.125
Outputs:
- output: bfloat16 [4, 2048, 1024], P('dp', 'seq')
- input_gradient: float32 [4, 2048, 1024], P('dp', 'seq')
- input_gain_gradient: float32 [1024], replicated
- query_gradient: float32 [1024, 512], P(('dp', 'seq'))
- key_gradient: float32 [1024, 128], P(('dp', 'seq'))
- value_gradient: float32 [1024, 128], P(('dp', 'seq'))
- attention_gradient: float32 [512, 1024], P(None, ('dp', 'seq'))
- gating_gradient: float32 [1024, 1536], P(('dp', 'seq'))
- inner_gradient: float32 [1024, 1792], P(('dp', 'seq'))
- step_gradient: float32 [1024, 24], replicated
- step_bias_gradient: float32 [24], replicated
- decay_gradient: float32 [24], replicated
- skip_gradient: float32 [24], replicated
- conv_gradient: float32 [4, 1792], replicated
- conv_bias_gradient: float32 [1792], replicated
- mixer_gain_gradient: float32 [1536], replicated
- mixer_gradient: float32 [1536, 1024], P(None, ('dp', 'seq'))
- feed_gain_gradient: float32 [1024], replicated
- gate_gradient: float32 [1024, 2048], P(('dp', 'seq'))
- up_gradient: float32 [1024, 2048], P(('dp', 'seq'))
- down_gradient: float32 [2048, 1024], P(None, ('dp', 'seq'))
The draws below stay inside these ranges and needn't reach their ends.
Inputs may be any that keep to these rules, and one draw needn't show every extreme that they name: `segments`: within a row, segment numbers start at 0 and rise by at most one from a position to the next; every row holds nine documents; one document begins inside the row's first 256 positions and ends inside its last 256.
All inputs are finite; a program needn't handle non-finite values.
Results may differ from the reference program's by a relative error of at most 0.018.
Values may be sent and summed in bfloat16 or wider, within the bound.
No kernel may reach another device: no remote copies, remote signals or barrier semaphores. Data moves between devices by JAX's collectives and lax.ppermute only.
A program may use at most 384 MiB of HBM per device.

```python
import math
import jax
import jax.numpy as jnp
from jax import lax

D = 1024
HEADS = 8
KV_HEADS = 2
HEAD = 64
SSM_HEADS = 24
SSM_HEAD = 64
STATE = 128
KERNEL = 4
FF = 2048
STRETCH = 128
TOK_DEV = 256
ROWS = 4
SEQ_LEN = 2048
D_SSM = 1536
XBC = 1792


def draw_segments(key, part):
    key = jax.random.fold_in(key, 11)
    key_begin, key_finish = jax.random.split(key, 2)
    begin = jax.random.randint(key_begin, (ROWS, 1), 4, TOK_DEV)
    finish = jax.random.randint(key_finish, (ROWS, 1), SEQ_LEN - TOK_DEV + 1, SEQ_LEN - 3)
    places = jnp.arange(SEQ_LEN)[None, :]
    starts = (places == begin) | (places == finish)
    for index in range(1, 4):
        early = begin * index // 4
        later = finish + (SEQ_LEN - finish) * index // 4
        starts = starts | (places == early) | (places == later)
    return jnp.cumsum(starts.astype(jnp.int32), axis=1).astype(jnp.int32)


def draw_decay_log(key, part):
    key = jax.random.fold_in(key, 12)
    key_kind, key_slow, key_fast = jax.random.split(key, 3)
    slow = jax.random.randint(key_kind, (SSM_HEADS,), 0, 2) > 0
    slow_rate = jnp.exp(jax.random.uniform(key_slow, (SSM_HEADS,), jnp.float32, math.log(0.05), math.log(0.5))) / SEQ_LEN
    fast_rate = jnp.exp(jax.random.uniform(key_fast, (SSM_HEADS,), jnp.float32, math.log(0.02), math.log(0.06)))
    rate = jnp.where(slow, slow_rate, fast_rate)
    return jnp.log(rate / 0.7).astype(jnp.float32)


def block_scale(stream_key, shape, cuts, least, top_value):
    level = 1.0
    for axis_at, parts in cuts:
        draws = jax.random.uniform(jax.random.fold_in(jax.random.fold_in(stream_key, 6), axis_at), (parts,), jnp.float32, least / len(cuts), top_value / len(cuts))
        level = level * jnp.repeat(jnp.exp(draws), shape[axis_at] // parts).reshape((-1,) + (1,) * (len(shape) - 1 - axis_at))
    return level


def scatter_about(stream_key, shape, spread, limit, cuts=(), kind=jnp.bfloat16):
    drawn = spread * jax.random.normal(stream_key, shape, jnp.float32)
    if cuts:
        drawn = drawn * block_scale(stream_key, shape, cuts, -0.22, 0.18)
    return jnp.clip(drawn, -limit, limit).astype(kind)


def setup_inputs(seed: int = 0) -> dict:
    seeds = jax.random.split(jax.random.key(seed), 23)
    inputs = scatter_about(seeds[0], (ROWS, SEQ_LEN, D), 1.0, 6.0, ((0, 4), (1, 8)))
    segments = draw_segments(jax.random.fold_in(seeds[22], 71), 0)
    cotangent = scatter_about(seeds[2], (ROWS, SEQ_LEN, D), 1.0, 6.0, ((0, 4), (1, 8)))
    input_gain = jnp.clip(1.0 + 0.1 * jax.random.normal(seeds[3], (D,), jnp.float32), 0.5, 1.5)
    query_weight = scatter_about(seeds[4], (D, HEADS * HEAD), D ** -0.5, 0.1875)
    key_weight = scatter_about(seeds[5], (D, KV_HEADS * HEAD), D ** -0.5, 0.1875)
    value_weight = scatter_about(seeds[6], (D, KV_HEADS * HEAD), D ** -0.5, 0.1875)
    attention_weight = scatter_about(seeds[7], (HEADS * HEAD, D), 8 ** -0.5, 2.0)
    gating_weight = scatter_about(seeds[8], (D, D_SSM), D ** -0.5, 0.1875)
    inner_weight = scatter_about(seeds[9], (D, XBC), D ** -0.5, 0.1875)
    step_weight = scatter_about(seeds[10], (D, SSM_HEADS), D ** -0.5, 0.1875)
    step_bias = jnp.clip(jax.random.uniform(seeds[11], (SSM_HEADS,), jnp.float32, -1.0, 0.5), -1.0, 0.5)
    decay_log = draw_decay_log(jax.random.fold_in(seeds[22], 71), 0)
    skip_scale = jnp.clip(jax.random.uniform(seeds[13], (SSM_HEADS,), jnp.float32, 0.5, 1.5), 0.5, 1.5)
    conv_weight = scatter_about(seeds[14], (KERNEL, XBC), KERNEL ** -0.5, 3.0, (), jnp.float32)
    conv_bias = scatter_about(seeds[15], (XBC,), 0.3, 3.0, (), jnp.float32)
    mixer_gain = jnp.clip(1.0 + 0.1 * jax.random.normal(seeds[16], (D_SSM,), jnp.float32), 0.5, 1.5)
    mixer_weight = scatter_about(seeds[17], (D_SSM, D), D_SSM ** -0.5, 0.15625)
    feed_gain = jnp.clip(1.0 + 0.1 * jax.random.normal(seeds[18], (D,), jnp.float32), 0.5, 1.5)
    gate_weight = scatter_about(seeds[19], (D, FF), D ** -0.5, 0.1875)
    up_weight = scatter_about(seeds[20], (D, FF), D ** -0.5, 0.1875)
    down_weight = scatter_about(seeds[21], (FF, D), FF ** -0.5, 0.125)
    return {"inputs": inputs, "segments": segments, "cotangent": cotangent, "input_gain": input_gain, "query_weight": query_weight, "key_weight": key_weight, "value_weight": value_weight, "attention_weight": attention_weight, "gating_weight": gating_weight, "inner_weight": inner_weight, "step_weight": step_weight, "step_bias": step_bias, "decay_log": decay_log, "skip_scale": skip_scale, "conv_weight": conv_weight, "conv_bias": conv_bias, "mixer_gain": mixer_gain, "mixer_weight": mixer_weight, "feed_gain": feed_gain, "gate_weight": gate_weight, "up_weight": up_weight, "down_weight": down_weight}


EPS = 1e-05
ROPE_BASE = 100000000000.0
NEG = -1e+30
HIGH = lax.Precision.HIGHEST

@jax.custom_vjp
def low(v):
    return lax.optimization_barrier(v.astype(jnp.bfloat16)).astype(jnp.float32)

@jax.custom_vjp
def low_back(v):
    return v

def low_keep(v):
    return (low(v), None)

def low_pass(kept, grad):
    return (grad,)

def back_keep(v):
    return (v, None)

def back_low(kept, grad):
    return (low(grad),)
low.defvjp(low_keep, low_pass)
low_back.defvjp(back_keep, back_low)

def product(left, right):
    return jnp.dot(left, right, preferred_element_type=jnp.float32, precision=HIGH)

def norm_rows(values, gain):
    return values * lax.rsqrt(lax.optimization_barrier(jnp.mean(values * values, -1, keepdims=True)) + EPS) * gain

def rotate(tensor, places, sign):
    half = tensor.shape[-1] // 2
    freq = ROPE_BASE ** (-(jnp.arange(half).astype(jnp.float32) * 2.0 / tensor.shape[-1]))
    angle = places[:, None] * freq[None, :]
    shape = (tensor.shape[0],) + (1,) * (tensor.ndim - 2) + (half,)
    cosine = jnp.cos(angle).reshape(shape)
    sine = sign * jnp.sin(angle).reshape(shape)
    front = tensor[..., :half]
    behind = tensor[..., half:]
    return jnp.concatenate([front * cosine - behind * sine, behind * cosine + front * sine], -1)

def gated_unit(gate, upward):
    return jax.nn.silu(gate) * upward

def prepare(extended, seg_ext, seg_here, conv_weight, conv_bias, step_raw, step_bias):
    rows = seg_here.shape[0]
    total = jnp.zeros((rows, extended.shape[1]), jnp.float32) + conv_bias[None, :]
    for offset in range(conv_weight.shape[0]):
        same = (lax.slice_in_dim(seg_ext, offset, offset + rows) == seg_here)[:, None]
        total = total + conv_weight[offset][None, :] * jnp.where(same, lax.slice_in_dim(extended, offset, offset + rows), 0.0)
    convolved = jax.nn.silu(total)
    width = SSM_HEADS * SSM_HEAD
    channels = convolved[:, :width].reshape(rows, SSM_HEADS, SSM_HEAD)
    inflow = convolved[:, width:width + STATE]
    readout = convolved[:, width + STATE:]
    steps = jax.nn.softplus(step_raw + step_bias[None, :])
    return (channels, steps, inflow, readout)

def stretch_decay(steps, seg, seg_before, rates):
    size = seg.shape[0]
    logs = jnp.cumsum(steps * rates[None, :], axis=0).T
    last = seg[size - 1]
    tail = jnp.where((seg == last)[None, :], jnp.exp(logs[:, size - 1:] - logs), 0.0) * steps.T
    through = jnp.where(seg_before == last, jnp.exp(logs[:, size - 1]), 0.0)
    return (logs, last, tail, through)

def stretch_state(state, channels, inflow, tail, through):
    return jnp.einsum('hs,shp,sn->hpn', tail, channels, inflow, precision=HIGH) + through[:, None, None] * state

def stretch_output(state, channels, steps, inflow, readout, seg, seg_before, logs):
    size = seg.shape[0]
    order = jnp.arange(size)
    inside = (seg[:, None] == seg[None, :]) & (order[:, None] >= order[None, :])
    gap = jnp.where(inside[None], logs[:, :, None] - logs[:, None, :], 0.0)
    decay = jnp.where(inside[None], jnp.exp(gap), 0.0)
    intersection = jnp.dot(readout, inflow.T, precision=HIGH)
    mixing = decay * intersection[None] * steps.T[:, None, :]
    inner_part = jnp.einsum('hts,shp->thp', mixing, channels, precision=HIGH)
    enter = jnp.where((seg == seg_before)[None, :], jnp.exp(logs), 0.0)
    state_part = jnp.einsum('tn,hpn->thp', readout, state, precision=HIGH) * enter.T[:, :, None]
    return inner_part + state_part

def ssd_scan(channels, steps, inflow, readout, seg, seg_before, state, decay_log):
    rates = -jnp.exp(decay_log)
    blocks = seg.shape[0] // STRETCH
    stacked = (channels.reshape(blocks, STRETCH, channels.shape[1], channels.shape[2]), steps.reshape(blocks, STRETCH, steps.shape[1]), inflow.reshape(blocks, STRETCH, inflow.shape[1]), readout.reshape(blocks, STRETCH, readout.shape[1]), seg.reshape(blocks, STRETCH))

    def advance(carry, pieces):
        state_now, before = carry
        block_channels, block_steps, block_inflow, block_readout, block_seg = pieces
        logs, last, tail, through = stretch_decay(block_steps, block_seg, before, rates)
        result = stretch_output(state_now, block_channels, block_steps, block_inflow, block_readout, block_seg, before, logs)
        return ((stretch_state(state_now, block_channels, block_inflow, tail, through), last), result)
    (state, ending), outputs = lax.scan(jax.checkpoint(advance), (state, seg_before), stacked)
    return (outputs.reshape(channels.shape), state)

def gated_norm(scanned, channels, gating, skip_scale, gain):
    full = scanned + skip_scale[None, :, None] * channels
    gated = full.reshape(full.shape[0], -1) * jax.nn.silu(gating)
    return norm_rows(gated, gain)

def row_forward(params, row, seg):
    input_gain, query_weight, key_weight, value_weight, attention_weight, gating_weight, inner_weight, step_weight, step_bias, decay_log, skip_scale, conv_weight, conv_bias, mixer_gain, mixer_weight, feed_gain, gate_weight, up_weight, down_weight = params
    length = row.shape[0]
    group = HEADS // KV_HEADS
    places = jnp.arange(length).astype(jnp.float32)
    positions = jnp.arange(length)
    normed = low(norm_rows(row, input_gain))
    queries = low(rotate(low_back(product(normed, query_weight)).reshape(length, KV_HEADS, group, HEAD), places, 1.0))
    keys = low(rotate(low_back(product(normed, key_weight)).reshape(length, KV_HEADS, HEAD), places, 1.0))
    values = low(low_back(product(normed, value_weight)).reshape(length, KV_HEADS, HEAD))
    block = math.gcd(length, 512)

    def attend(index):
        start = index * block
        part = lax.dynamic_slice_in_dim(queries, start, block, 0)
        seg_part = lax.dynamic_slice_in_dim(seg, start, block, 0)
        place_part = start + jnp.arange(block)
        scores = low_back(jnp.einsum('qgrd,kgd->grqk', part, keys, precision=HIGH) * HEAD ** (-0.5))
        mask = (seg_part[:, None] == seg[None, :]) & (place_part[:, None] >= positions[None, :])
        masked = jnp.where(mask, scores, NEG)
        top = lax.optimization_barrier(jnp.max(masked, -1, keepdims=True))
        weights = jnp.where(mask, jnp.exp(masked - top), 0.0)
        weights = weights / lax.optimization_barrier(jnp.sum(weights, -1, keepdims=True))
        return jnp.einsum('grqk,kgd->qgrd', low(weights), values, precision=HIGH)
    attended = lax.map(jax.checkpoint(attend), jnp.arange(length // block))
    attended = low(low_back(attended.reshape(length, HEADS * HEAD)))
    gating = low_back(product(normed, gating_weight))
    inner = low(low_back(product(normed, inner_weight)))
    extended = jnp.concatenate([jnp.zeros((KERNEL - 1, inner.shape[1]), jnp.float32), inner], 0)
    seg_ext = jnp.concatenate([jnp.full((KERNEL - 1,), -1, jnp.int32), seg])
    channels, steps, inflow, readout = prepare(extended, seg_ext, seg, conv_weight, conv_bias, product(normed, step_weight), step_bias)
    start_state = jnp.zeros((SSM_HEADS, SSM_HEAD, STATE), jnp.float32)
    scanned, ending = ssd_scan(channels, steps, inflow, readout, seg, jnp.array(-1, jnp.int32), start_state, decay_log)
    tail = low(gated_norm(scanned, channels, gating, skip_scale, mixer_gain))
    mixed = row + low_back(product(attended, attention_weight)) + low_back(product(tail, mixer_weight))
    feed = low(norm_rows(mixed, feed_gain))
    hidden = low(gated_unit(low_back(product(feed, gate_weight)), low_back(product(feed, up_weight))))
    return mixed + low_back(product(hidden, down_weight))

def reference(inputs, segments, cotangent, input_gain, query_weight, key_weight, value_weight, attention_weight, gating_weight, inner_weight, step_weight, step_bias, decay_log, skip_scale, conv_weight, conv_bias, mixer_gain, mixer_weight, feed_gain, gate_weight, up_weight, down_weight):
    params = tuple((weight.astype(jnp.float32) for weight in (input_gain, query_weight, key_weight, value_weight, attention_weight, gating_weight, inner_weight, step_weight, step_bias, decay_log, skip_scale, conv_weight, conv_bias, mixer_gain, mixer_weight, feed_gain, gate_weight, up_weight, down_weight)))

    def forward(values, weights):

        def one_row(pieces):
            return row_forward(weights, pieces[0], pieces[1])
        return lax.map(one_row, (values, segments))
    result, pull = jax.vjp(forward, inputs.astype(jnp.float32), params)
    input_gradient, slopes = pull(cotangent.astype(jnp.float32))
    gain_a, query_g, key_g, value_g, attention_g, gating_g, inner_g, step_g, step_bias_g, decay_g, skip_g, conv_g, conv_bias_g, mixer_gain_g, mixer_g, feed_g, gate_g, up_g, down_g = slopes
    return (result.astype(jnp.bfloat16), input_gradient, gain_a, query_g, key_g, value_g, attention_g, gating_g, inner_g, step_g, step_bias_g, decay_g, skip_g, conv_g, conv_bias_g, mixer_gain_g, mixer_g, feed_g, gate_g, up_g, down_g)
```

```python
import jax
import jax.numpy as jnp
from jax import lax
from jax.experimental import pallas as pl
from jax.experimental.pallas import tpu as pltpu
from jax.sharding import PartitionSpec as P

HEADS = 8
KV_HEADS = 2
HEAD = 64
SSM_HEADS = 24
SSM_HEAD = 64
STATE = 128
KERNEL = 4
STRETCH = 128


EPS = 1e-05
ROPE_BASE = 100000000000.0
NEG = -1e30
HIGH = lax.Precision.HIGHEST


def passed_along(shard, axis, by):
    peers = lax.axis_size(axis)
    pairs = [(i, i + by) for i in range(peers) if 0 <= i + by < peers]
    return lax.ppermute(shard, axis, pairs)


def carried_in(shard, axis, combine, identity):
    peers, position = (lax.axis_size(axis), lax.axis_index(axis))
    everything = jax.tree.map(
        lambda part, kind: lax.all_gather(part.astype(kind), axis),
        shard,
        (jnp.bfloat16, jnp.bfloat16),
    )
    start = jax.tree.map(
        lambda part, zero: jnp.broadcast_to(jnp.asarray(zero, part.dtype), part.shape),
        shard,
        identity,
    )

    def step(k, before):
        reached = k < position
        new = combine(
            before, jax.tree.map(lambda part, own: part[k].astype(own.dtype), everything, shard)
        )
        return jax.tree.map(lambda a, b: jnp.where(reached, a, b), new, before)

    return lax.fori_loop(0, peers, step, start)


def entering_2(shard, axis, join, neutral):
    count = lax.axis_size(axis)
    place = lax.axis_index(axis)
    ahead = count - 1 - place
    gathered = jax.tree.map(
        lambda a, kind: lax.all_gather(a.astype(kind), axis),
        shard,
        jax.tree.map(lambda a: jnp.bfloat16 if a.dtype == jnp.float32 else a.dtype, shard),
    )
    state = jax.tree.map(lambda a, e: jnp.zeros_like(a) + jnp.asarray(e, a.dtype), shard, neutral)

    def one(step, state):
        source = count - 1 - step
        return join(
            state,
            jax.tree.map(
                lambda a, own: lax.dynamic_index_in_dim(a, source, 0, False).astype(own.dtype),
                gathered,
                shard,
            ),
        )

    return lax.fori_loop(0, ahead, one, state)


def product(left, right):
    return jnp.dot(left, right, preferred_element_type=jnp.float32)


def product_left(left, right):
    return lax.dot_general(
        left, right, (((0,), (0,)), ((), ())), preferred_element_type=jnp.float32
    )


def product_right(left, right):
    return lax.dot_general(
        left, right, (((1,), (1,)), ((), ())), preferred_element_type=jnp.float32
    )


def precise(left, right):
    return jnp.dot(left, right, preferred_element_type=jnp.float32, precision=HIGH)


def norm_rows(values, gain):
    return values * lax.rsqrt(jnp.mean(values * values, -1, keepdims=True) + EPS) * gain


def rotate(tensor, places, sign):
    half = tensor.shape[-1] // 2
    freq = ROPE_BASE ** (-(jnp.arange(half).astype(jnp.float32) * 2.0 / tensor.shape[-1]))
    angle = places[:, None] * freq[None, :]
    shape = (tensor.shape[0],) + (1,) * (tensor.ndim - 2) + (half,)
    cosine = jnp.cos(angle).reshape(shape)
    sine = sign * jnp.sin(angle).reshape(shape)
    front = tensor[..., :half]
    behind = tensor[..., half:]
    return jnp.concatenate([front * cosine - behind * sine, behind * cosine + front * sine], -1)


def gated_unit(gate, upward):
    return jax.nn.silu(gate) * upward


def prepare(extended, seg_ext, seg_here, conv_weight, conv_bias, step_raw, step_bias):
    rows = seg_here.shape[0]
    total = jnp.zeros((rows, extended.shape[1]), jnp.float32) + conv_bias[None, :]
    for offset in range(conv_weight.shape[0]):
        same = (lax.slice_in_dim(seg_ext, offset, offset + rows) == seg_here)[:, None]
        total = total + conv_weight[offset][None, :] * jnp.where(
            same, lax.slice_in_dim(extended, offset, offset + rows), 0.0
        )
    convolved = jax.nn.silu(total)
    width = SSM_HEADS * SSM_HEAD
    channels = convolved[:, :width].reshape(rows, SSM_HEADS, SSM_HEAD)
    inflow = convolved[:, width : width + STATE]
    readout = convolved[:, width + STATE :]
    steps = jax.nn.softplus(step_raw + step_bias[None, :])
    return (channels, steps, inflow, readout)


def stretch_decay(steps, seg, seg_before, rates):
    size = seg.shape[0]
    logs = jnp.cumsum(steps * rates[None, :], axis=0).T
    last = seg[size - 1]
    tail = jnp.where((seg == last)[None, :], jnp.exp(logs[:, size - 1 :] - logs), 0.0) * steps.T
    through = jnp.where(seg_before == last, jnp.exp(logs[:, size - 1]), 0.0)
    return (logs, last, tail, through)


def stretch_state(state, channels, inflow, tail, through):
    return (
        jnp.einsum("hs,shp,sn->hpn", tail, channels, inflow, precision=HIGH)
        + through[:, None, None] * state
    )


def stretch_output(state, channels, steps, inflow, readout, seg, seg_before, logs):
    size = seg.shape[0]
    order = jnp.arange(size)
    inside = (seg[:, None] == seg[None, :]) & (order[:, None] >= order[None, :])
    gap = jnp.where(inside[None], logs[:, :, None] - logs[:, None, :], 0.0)
    decay = jnp.where(inside[None], jnp.exp(gap), 0.0)
    intersection = jnp.dot(readout, inflow.T, precision=HIGH)
    mixing = decay * intersection[None] * steps.T[:, None, :]
    inner_part = jnp.einsum("hts,shp->thp", mixing, channels, precision=HIGH)
    enter = jnp.where((seg == seg_before)[None, :], jnp.exp(logs), 0.0)
    state_part = jnp.einsum("tn,hpn->thp", readout, state, precision=HIGH) * enter.T[:, :, None]
    return inner_part + state_part


def stack_blocks(channels, steps, inflow, readout, seg):
    blocks = seg.shape[0] // STRETCH
    return (
        channels.reshape(blocks, STRETCH, channels.shape[1], channels.shape[2]),
        steps.reshape(blocks, STRETCH, steps.shape[1]),
        inflow.reshape(blocks, STRETCH, inflow.shape[1]),
        readout.reshape(blocks, STRETCH, readout.shape[1]),
        seg.reshape(blocks, STRETCH),
    )


def ssd_scan(channels, steps, inflow, readout, seg, seg_before, state, decay_log):
    rates = -jnp.exp(decay_log)

    def advance(carry, pieces):
        state_now, before = carry
        block_channels, block_steps, block_inflow, block_readout, block_seg = pieces
        logs, last, tail, through = stretch_decay(block_steps, block_seg, before, rates)
        result = stretch_output(
            state_now,
            block_channels,
            block_steps,
            block_inflow,
            block_readout,
            block_seg,
            before,
            logs,
        )
        return (
            (stretch_state(state_now, block_channels, block_inflow, tail, through), last),
            result,
        )

    (state, ending), outputs = lax.scan(
        advance, (state, seg_before), stack_blocks(channels, steps, inflow, readout, seg)
    )
    return outputs.reshape(channels.shape)


def ssd_states(channels, steps, inflow, seg, seg_before, decay_log):
    rates = -jnp.exp(decay_log)

    def advance(carry, pieces):
        state_now, before, kept = carry
        block_channels, block_steps, block_inflow, block_readout, block_seg = pieces
        logs, last, tail, through = stretch_decay(block_steps, block_seg, before, rates)
        return (
            (
                stretch_state(state_now, block_channels, block_inflow, tail, through),
                last,
                kept * through,
            ),
            None,
        )

    start = (
        jnp.zeros((channels.shape[1], channels.shape[2], inflow.shape[1]), jnp.float32),
        seg_before,
        jnp.ones((channels.shape[1],), jnp.float32),
    )
    (state, ending, kept), unused = lax.scan(
        advance, start, stack_blocks(channels, steps, inflow, inflow, seg)
    )
    return (state, kept)


def gated_norm(scanned, channels, gating, skip_scale, gain):
    full = scanned + skip_scale[None, :, None] * channels
    gated = full.reshape(full.shape[0], -1) * jax.nn.silu(gating)
    return norm_rows(gated, gain)


def combine_states(earlier, later):
    return (earlier[0] * later[0], later[0][:, None, None] * earlier[1] + later[1])


CORES = 2
DEPTH = 4
LANES = 128


class Place:
    def __init__(self):
        self.dp = lax.axis_size("dp")
        self.seq = lax.axis_size("seq")
        self.sizes = {
            "y": self.dp // CORES,
            "core": CORES,
            "z": DEPTH,
            "x": self.seq // DEPTH,
        }
        dp, seq = lax.axis_index("dp"), lax.axis_index("seq")
        self.at = {
            "y": dp // CORES,
            "core": dp % CORES,
            "z": seq // self.sizes["x"],
            "x": seq % self.sizes["x"],
        }

    def split(self, index):
        dp, seq = index // self.seq, index % self.seq
        return {
            "y": dp // CORES,
            "core": dp % CORES,
            "z": seq // self.sizes["x"],
            "x": seq % self.sizes["x"],
        }

    def join(self, at):
        return (at["y"] * CORES + at["core"]) * self.seq + at["z"] * self.sizes["x"] + at["x"]

    def turn(self, shard, axis, by):
        pairs = []
        for index in range(self.dp * self.seq):
            at = self.split(index)
            at[axis] = (at[axis] + by) % self.sizes[axis]
            pairs.append((index, self.join(at)))
        return lax.ppermute(shard, ("dp", "seq"), pairs)

    def share_order(self, width):
        sizes, at = self.sizes, self.at
        rows = width // (self.dp * self.seq)
        k = lax.broadcasted_iota(jnp.int32, (width, 1), 0)
        within = k % rows
        rest = k // rows
        dz = rest % sizes["z"]
        rest = rest // sizes["z"]
        dy = rest % sizes["y"]
        rest = rest // sizes["y"]
        dx = rest % sizes["x"]
        dc = rest // sizes["x"]
        owner = self.join(
            {
                "y": (at["y"] + dy) % sizes["y"],
                "core": (at["core"] + dc) % sizes["core"],
                "z": (at["z"] + dz) % sizes["z"],
                "x": (at["x"] + dx) % sizes["x"],
            }
        )
        source = owner * rows + within
        columns = lax.broadcasted_iota(jnp.int32, (1, width), 1)
        return (source == columns).astype(jnp.bfloat16)


def joint_kernel(xs, ys, left_ref, left_sib_ref, a_ref, a_sib_ref, b_ref, b_sib_ref, *outs):
    a_outs, b_outs = outs[:xs], outs[xs:]
    part = left_ref.shape[0] // (xs * ys)
    for source, sibling, targets, first in (
        (a_ref, a_sib_ref, a_outs, True),
        (b_ref, b_sib_ref, b_outs, False),
    ):
        total = jnp.dot(left_ref[...], source[...], preferred_element_type=jnp.float32)
        total = total + jnp.dot(
            left_sib_ref[...], sibling[...], preferred_element_type=jnp.float32
        )
        total = total.astype(jnp.bfloat16)
        for x in range(xs):
            for y in range(ys):
                piece = total[(x * ys + y) * part : (x * ys + y + 1) * part]
                if first:
                    targets[x][y * part : (y + 1) * part] = piece
                else:
                    targets[y][x * part : (x + 1) * part] = piece


def joint_gradient(place, left, right, left_sib, right_sib):
    rows, tokens = left.shape
    width = right.shape[1]
    xs, ys = place.sizes["x"], place.sizes["y"]
    half = width // 2
    tile = next(t for t in (512, 384, 256, 128) if half % t == 0)
    steps = half // tile
    whole = pl.BlockSpec((rows, tokens), lambda j: (0, 0))
    early = pl.BlockSpec((tokens, tile), lambda j: (0, j))
    late = pl.BlockSpec((tokens, tile), lambda j: (0, j + steps))
    shapes = [rows // xs] * xs + [rows // ys] * ys
    outs = pl.pallas_call(
        lambda *refs: joint_kernel(xs, ys, *refs),
        grid=(steps,),
        in_specs=[whole, whole, early, early, late, late],
        out_specs=[pl.BlockSpec((r, tile), lambda j: (0, j)) for r in shapes],
        out_shape=[jax.ShapeDtypeStruct((r, half), jnp.bfloat16) for r in shapes],
        compiler_params=pltpu.CompilerParams(vmem_limit_bytes=40 * 1024 * 1024),
        cost_estimate=pl.CostEstimate(
            flops=4 * rows * tokens * width,
            bytes_accessed=2 * (rows * width + 2 * tokens * (rows + width)),
            transcendentals=0,
        ),
        name="joint_gradient",
    )(left, left_sib, right, right_sib, right, right_sib)
    return outs[:xs], outs[xs:]


def reduced(place, pieces, first, second):
    n_first, n_second = place.sizes[first], place.sizes[second]
    kept = pieces[0]
    arrived = [place.turn(pieces[k], first, k) for k in range(1, n_first)]
    share = kept.shape[0] // n_second

    def summed(k):
        window = slice(k * share, (k + 1) * share)
        total = kept[window].astype(jnp.float32)
        for piece in arrived:
            total = total + piece[window].astype(jnp.float32)
        return total

    total = summed(0)
    for k in range(1, n_second):
        total = total + place.turn(summed(k).astype(jnp.bfloat16), second, k).astype(jnp.float32)
    return total


def own_share(place, left, right, left_sib, right_sib):
    first, second = joint_gradient(place, left, right, left_sib, right_sib)
    total = jnp.concatenate(
        [reduced(place, first, "x", "y"), reduced(place, second, "y", "x")], 1
    )
    depth = place.sizes["z"]
    rows = total.shape[0] // depth
    share = total[:rows]
    for k in range(1, depth):
        share = share + place.turn(
            total[k * rows : (k + 1) * rows].astype(jnp.bfloat16), "z", k
        ).astype(jnp.float32)
    return share


def arranged(order, left):
    return lax.dot_general(
        order, left, (((1,), (1,)), ((), ())), preferred_element_type=jnp.float32
    ).astype(jnp.bfloat16)


def weight_shares(place, order, left, rights):
    half = left.shape[1] // CORES
    ordered = arranged(order, left)
    width = sum(r.shape[1] for r in rights)
    right = jnp.concatenate(rights, 1)
    left_sib = place.turn(ordered[half:], "core", 1)
    right_sib = place.turn(right, "core", 1)
    share = own_share(place, ordered[:half], right, left_sib, right_sib)
    shares = []
    offset = 0
    for piece in rights:
        shares.append(share[:, offset : offset + piece.shape[1]])
        offset += piece.shape[1]
    return shares


def body(
    inputs,
    segments,
    cotangent,
    input_gain,
    query_weight,
    key_weight,
    value_weight,
    attention_weight,
    gating_weight,
    inner_weight,
    step_weight,
    step_bias,
    decay_log,
    skip_scale,
    conv_weight,
    conv_bias,
    mixer_gain,
    mixer_weight,
    feed_gain,
    gate_weight,
    up_weight,
    down_weight,
):
    count = inputs.shape[1]
    group = HEADS // KV_HEADS
    pair_width = KV_HEADS * HEAD
    scale = HEAD ** (-0.5)
    hidden = inputs[0].astype(jnp.float32)
    seg_row = segments[0]
    length = seg_row.shape[0]
    first = lax.axis_index("seq") * count
    seg_here = lax.dynamic_slice_in_dim(seg_row, first, count)
    query_places = first + jnp.arange(count)
    places = query_places.astype(jnp.float32)
    normed, norm_back = jax.vjp(norm_rows, hidden, input_gain)
    normed_low = normed.astype(jnp.bfloat16)
    query_raw = product(normed_low, query_weight)
    key_raw = product(normed_low, key_weight)
    value_raw = product(normed_low, value_weight)
    queries = rotate(query_raw.reshape(count, KV_HEADS, group, HEAD), places, 1.0).astype(
        jnp.bfloat16
    )
    keys_here = rotate(key_raw.reshape(count, KV_HEADS, HEAD), places, 1.0)
    pairs = jnp.concatenate([keys_here.reshape(count, pair_width), value_raw], 1).astype(
        jnp.bfloat16
    )

    def block_mask(rows):
        key_places = jnp.arange(rows)
        return (seg_here[:, None] == seg_row[None, :]) & (
            query_places[:, None] >= key_places[None, :]
        )

    def block_live(start, rows):
        return (start <= first + count - 1) & (seg_row[start + rows - 1] >= seg_here[0])

    def unchanged(carry):
        return carry

    start_carry = (
        jnp.full((KV_HEADS, group, count), NEG, jnp.float32),
        jnp.zeros((KV_HEADS, group, count), jnp.float32),
        jnp.zeros((count, KV_HEADS, group, HEAD), jnp.float32),
    )
    carry = start_carry
    piece = lax.all_gather(pairs, "seq", axis=0, tiled=True)
    rows = piece.shape[0]

    def compute(carry):
        top, total, gathered = carry
        piece_keys = piece[:, :pair_width].reshape(rows, KV_HEADS, HEAD)
        piece_values = piece[:, pair_width:].reshape(rows, KV_HEADS, HEAD)
        mask = block_mask(rows)
        scores = (
            jnp.einsum("qgrd,kgd->grqk", queries, piece_keys, preferred_element_type=jnp.float32)
            * scale
        )
        masked = jnp.where(mask, scores, NEG)
        new_top = jnp.maximum(top, jnp.max(masked, -1))
        weights = jnp.where(mask, jnp.exp(masked - new_top[..., None]), 0.0)
        total = jnp.sum(weights, -1)
        gathered = jnp.einsum(
            "grqk,kgd->qgrd",
            weights.astype(jnp.bfloat16),
            piece_values,
            preferred_element_type=jnp.float32,
        )
        return (new_top, total, gathered)

    top, total, gathered = lax.cond(block_live(jnp.int32(0), rows), compute, unchanged, carry)
    attention = gathered / total.transpose(2, 0, 1)[..., None]
    spread = top + jnp.log(total)
    attention_low = attention.reshape(count, HEADS * HEAD).astype(jnp.bfloat16)
    attention_branch = product(attention_low, attention_weight)
    gating = product(normed_low, gating_weight)
    inner = product(normed_low, inner_weight).astype(jnp.bfloat16)
    step_raw = product(normed_low, step_weight)
    borrowed = passed_along(inner[count - KERNEL + 1 :], "seq", 1)
    extended = jnp.concatenate([borrowed, inner], 0).astype(jnp.float32)
    lead = first - (KERNEL - 1) + jnp.arange(KERNEL - 1)
    seg_lead = jnp.where(lead >= 0, seg_row[jnp.maximum(lead, 0)], -1)
    seg_ext = jnp.concatenate([seg_lead, seg_here])
    seg_before = seg_ext[KERNEL - 2]

    def prepare_local(extended, conv_weight, conv_bias, step_raw, step_bias):
        return prepare(extended, seg_ext, seg_here, conv_weight, conv_bias, step_raw, step_bias)

    (channels, steps, inflow, readout), prepare_back = jax.vjp(
        prepare_local, extended, conv_weight, conv_bias, step_raw, step_bias
    )

    def shard_state(channels, steps, inflow, decay_log):
        return ssd_states(channels, steps, inflow, seg_here, seg_before, decay_log)

    (local_state, through), state_back = jax.vjp(shard_state, channels, steps, inflow, decay_log)
    identity = (
        jnp.ones((SSM_HEADS,), jnp.float32),
        jnp.zeros((SSM_HEADS, SSM_HEAD, STATE), jnp.float32),
    )
    passed, entering = carried_in((through, local_state), "seq", combine_states, identity)

    def shard_output(channels, steps, inflow, readout, decay_log, entering):
        return ssd_scan(channels, steps, inflow, readout, seg_here, seg_before, entering, decay_log)

    scanned, output_back = jax.vjp(
        shard_output, channels, steps, inflow, readout, decay_log, entering
    )
    tail, tail_back = jax.vjp(gated_norm, scanned, channels, gating, skip_scale, mixer_gain)
    tail_low = tail.astype(jnp.bfloat16)
    mixed_sum = hidden + attention_branch + product(tail_low, mixer_weight)
    feed, feed_back = jax.vjp(norm_rows, mixed_sum, feed_gain)
    feed_low = feed.astype(jnp.bfloat16)
    activated, unit_back = jax.vjp(
        gated_unit, product(feed_low, gate_weight), product(feed_low, up_weight)
    )
    activated_low = activated.astype(jnp.bfloat16)
    output = mixed_sum + product(activated_low, down_weight)
    slope = cotangent[0]
    place = Place()
    order = place.share_order(slope.shape[1])
    (share_down,) = weight_shares(place, order, slope, (activated_low,))
    gate_slope, up_slope = unit_back(product_right(slope, down_weight))
    gate_low = gate_slope.astype(jnp.bfloat16)
    up_low = up_slope.astype(jnp.bfloat16)
    share_gate, share_up = weight_shares(place, order, feed_low, (gate_low, up_low))
    mixed_part, grad_feed_gain = feed_back(
        product_right(gate_low, gate_weight) + product_right(up_low, up_weight)
    )
    mixed_slope = slope.astype(jnp.float32) + mixed_part
    branch_low = mixed_slope.astype(jnp.bfloat16)
    attention_slope = (
        product_right(branch_low, attention_weight)
        .astype(jnp.bfloat16)
        .reshape(count, KV_HEADS, group, HEAD)
    )
    share_attention, share_mixer = weight_shares(
        place, order, branch_low, (attention_low, tail_low)
    )
    scanned_slope, channels_tail, gating_slope, grad_skip, grad_mixer_gain = tail_back(
        product_right(branch_low, mixer_weight)
    )
    channels_out, steps_out, inflow_out, readout_out, decay_out, entering_slope = output_back(
        scanned_slope
    )
    passed_back, leaving = entering_2((through, entering_slope), "seq", combine_states, identity)
    through_slope = jnp.sum(leaving * entering, axis=(1, 2))
    channels_state, steps_state, inflow_state, decay_state = state_back((leaving, through_slope))
    extended_slope, grad_conv_weight, grad_conv_bias, step_raw_slope, grad_step_bias = prepare_back(
        (
            channels_tail + channels_out + channels_state,
            steps_out + steps_state,
            inflow_out + inflow_state,
            readout_out,
        )
    )
    grad_decay = decay_out + decay_state
    returned = passed_along(extended_slope[: KERNEL - 1], "seq", -1)
    inner_slope = extended_slope[KERNEL - 1 :].at[count - KERNEL + 1 :].add(returned)
    inner_low = inner_slope.astype(jnp.bfloat16)
    gating_low = gating_slope.astype(jnp.bfloat16)
    normed_float = normed_low.astype(jnp.float32)
    delta = jnp.einsum("qgrd,qgrd->grq", attention_slope.astype(jnp.float32), attention)
    back_carry = (
        jnp.zeros((count, KV_HEADS, group, HEAD), jnp.float32),
        jnp.zeros((length, 2 * pair_width), jnp.float32),
    )
    carry = back_carry
    attend_piece = lax.all_gather(pairs, "seq", axis=0, tiled=True)
    attend_rows = attend_piece.shape[0]

    def compute(carry):
        piece_keys = attend_piece[:, :pair_width].reshape(attend_rows, KV_HEADS, HEAD)
        piece_values = attend_piece[:, pair_width:].reshape(attend_rows, KV_HEADS, HEAD)
        mask = block_mask(attend_rows)
        scores = (
            jnp.einsum("qgrd,kgd->grqk", queries, piece_keys, preferred_element_type=jnp.float32)
            * scale
        )
        weights = jnp.where(mask, jnp.exp(jnp.where(mask, scores - spread[..., None], NEG)), 0.0)
        dots = jnp.einsum(
            "qgrd,kgd->grqk", attention_slope, piece_values, preferred_element_type=jnp.float32
        )
        score_slope = (weights * (dots - delta[..., None])).astype(jnp.bfloat16)
        query_slope = (
            jnp.einsum(
                "grqk,kgd->qgrd", score_slope, piece_keys, preferred_element_type=jnp.float32
            )
            * scale
        )
        key_part = (
            jnp.einsum("grqk,qgrd->kgd", score_slope, queries, preferred_element_type=jnp.float32)
            * scale
        )
        value_part = jnp.einsum(
            "grqk,qgrd->kgd",
            weights.astype(jnp.bfloat16),
            attention_slope,
            preferred_element_type=jnp.float32,
        )
        part = jnp.concatenate(
            [
                key_part.reshape(attend_rows, pair_width),
                value_part.reshape(attend_rows, pair_width),
            ],
            1,
        )
        return (query_slope, part)

    query_slope, pair_slope = lax.cond(
        block_live(jnp.int32(0), attend_rows), compute, unchanged, carry
    )
    owned = lax.psum_scatter(
        pair_slope.astype(jnp.bfloat16), "seq", scatter_dimension=0, tiled=True
    ).astype(jnp.float32)
    key_low = (
        rotate(owned[:, :pair_width].reshape(count, KV_HEADS, HEAD), places, -1.0)
        .reshape(count, pair_width)
        .astype(jnp.bfloat16)
    )
    value_low = owned[:, pair_width:].astype(jnp.bfloat16)
    query_low = rotate(query_slope, places, -1.0).reshape(count, HEADS * HEAD).astype(jnp.bfloat16)
    share_gating, share_inner, share_query, share_key, share_value = weight_shares(
        place, order, normed_low, (gating_low, inner_low, query_low, key_low, value_low)
    )
    grad_step = precise(normed_float.T, step_raw_slope)
    normed_slope = (
        product_right(query_low, query_weight)
        + product_right(key_low, key_weight)
        + product_right(value_low, value_weight)
    )
    normed_slope = (
        normed_slope
        + product_right(gating_low, gating_weight)
        + product_right(inner_low, inner_weight)
    )
    normed_slope = normed_slope + precise(step_raw_slope, step_weight.astype(jnp.float32).T)
    input_part, grad_input_gain = norm_back(normed_slope)
    input_gradient = mixed_slope + input_part
    head_parts = lax.psum(
        (
            grad_step_bias,
            grad_decay,
            grad_skip,
            grad_mixer_gain,
            grad_conv_weight,
            grad_conv_bias,
            grad_input_gain,
            grad_feed_gain,
            grad_step,
        ),
        ("dp", "seq"),
    )
    (
        step_bias_sum,
        decay_sum,
        skip_sum,
        mixer_gain_sum,
        conv_sum,
        conv_bias_sum,
        gain_sum,
        feed_gain_sum,
        step_sum,
    ) = head_parts
    return (
        output.astype(jnp.bfloat16)[None],
        input_gradient[None],
        gain_sum,
        share_query,
        share_key,
        share_value,
        share_attention.T,
        share_gating,
        share_inner,
        step_sum,
        step_bias_sum,
        decay_sum,
        skip_sum,
        conv_sum,
        conv_bias_sum,
        mixer_gain_sum,
        share_mixer.T,
        feed_gain_sum,
        share_gate,
        share_up,
        share_down.T,
    )


def solution(mesh):
    in_specs = (
        P("dp", "seq", None),
        P("dp", None),
        P("dp", "seq", None),
        P(),
        P(),
        P(),
        P(),
        P(),
        P(),
        P(),
        P(),
        P(),
        P(),
        P(),
        P(),
        P(),
        P(),
        P(),
        P(),
        P(),
        P(),
        P(),
    )
    out_specs = (
        P("dp", "seq", None),
        P("dp", "seq", None),
        P(),
        P(("dp", "seq"), None),
        P(("dp", "seq"), None),
        P(("dp", "seq"), None),
        P(None, ("dp", "seq")),
        P(("dp", "seq"), None),
        P(("dp", "seq"), None),
        P(),
        P(),
        P(),
        P(),
        P(),
        P(),
        P(),
        P(None, ("dp", "seq")),
        P(),
        P(("dp", "seq"), None),
        P(("dp", "seq"), None),
        P(None, ("dp", "seq")),
    )
    return jax.shard_map(body, mesh=mesh, in_specs=in_specs, out_specs=out_specs, check_vma=False)
```

```python
import jax
import jax.numpy as jnp
from jax import lax
from jax.experimental import pallas as pl
from jax.experimental.pallas import tpu as pltpu
from jax.sharding import PartitionSpec as P

HEADS = 8
KV_HEADS = 2
HEAD = 64
SSM_HEADS = 24
SSM_HEAD = 64
STATE = 128
KERNEL = 4


EPS = 1e-05
ROPE_BASE = 100000000000.0
NEG = -1e30
HIGH = lax.Precision.HIGHEST


def passed_along(shard, axis, by):
    peers = lax.axis_size(axis)
    pairs = [(i, i + by) for i in range(peers) if 0 <= i + by < peers]
    return lax.ppermute(shard, axis, pairs)


def product(left, right):
    return jnp.dot(left, right, preferred_element_type=jnp.float32)


def product_left(left, right):
    return lax.dot_general(
        left, right, (((0,), (0,)), ((), ())), preferred_element_type=jnp.float32
    )


def product_right(left, right):
    return lax.dot_general(
        left, right, (((1,), (1,)), ((), ())), preferred_element_type=jnp.float32
    )


def precise(left, right):
    return jnp.dot(left, right, preferred_element_type=jnp.float32, precision=HIGH)


def norm_rows(values, gain):
    return values * lax.rsqrt(jnp.mean(values * values, -1, keepdims=True) + EPS) * gain


def gated_unit(gate, upward):
    return jax.nn.silu(gate) * upward


CORES = 2
DEPTH = 4
LANES = 128


class Place:
    def __init__(self):
        self.dp = lax.axis_size("dp")
        self.seq = lax.axis_size("seq")
        self.sizes = {
            "y": self.dp // CORES,
            "core": CORES,
            "z": DEPTH,
            "x": self.seq // DEPTH,
        }
        dp, seq = lax.axis_index("dp"), lax.axis_index("seq")
        self.at = {
            "y": dp // CORES,
            "core": dp % CORES,
            "z": seq // self.sizes["x"],
            "x": seq % self.sizes["x"],
        }

    def split(self, index):
        dp, seq = index // self.seq, index % self.seq
        return {
            "y": dp // CORES,
            "core": dp % CORES,
            "z": seq // self.sizes["x"],
            "x": seq % self.sizes["x"],
        }

    def join(self, at):
        return (at["y"] * CORES + at["core"]) * self.seq + at["z"] * self.sizes["x"] + at["x"]

    def turn(self, shard, axis, by):
        pairs = []
        for index in range(self.dp * self.seq):
            at = self.split(index)
            at[axis] = (at[axis] + by) % self.sizes[axis]
            pairs.append((index, self.join(at)))
        return lax.ppermute(shard, ("dp", "seq"), pairs)

    def share_order(self, width):
        sizes, at = self.sizes, self.at
        rows = width // (self.dp * self.seq)
        k = lax.broadcasted_iota(jnp.int32, (width, 1), 0)
        within = k % rows
        rest = k // rows
        dz = rest % sizes["z"]
        rest = rest // sizes["z"]
        dy = rest % sizes["y"]
        rest = rest // sizes["y"]
        dx = rest % sizes["x"]
        dc = rest // sizes["x"]
        owner = self.join(
            {
                "y": (at["y"] + dy) % sizes["y"],
                "core": (at["core"] + dc) % sizes["core"],
                "z": (at["z"] + dz) % sizes["z"],
                "x": (at["x"] + dx) % sizes["x"],
            }
        )
        source = owner * rows + within
        columns = lax.broadcasted_iota(jnp.int32, (1, width), 1)
        return (source == columns).astype(jnp.bfloat16)


F32 = jnp.float32
BF16 = jnp.bfloat16
PAIR = 2 * SSM_HEAD
WIDTH = SSM_HEADS * SSM_HEAD
PAIRS = WIDTH // PAIR
HALO = 8
EXTRA = 16
VMEM = pl.BlockSpec(memory_space=pltpu.VMEM)
SMEM = pl.BlockSpec(memory_space=pltpu.SMEM)


def local_call(kernel, outs, args, name, scratch=(), smem=(), flops=0):
    shapes = [jax.ShapeDtypeStruct(shape, kind) for shape, kind in outs]
    moved = sum(a.size * a.dtype.itemsize for a in args)
    moved += sum(s.size * s.dtype.itemsize for s in shapes)
    return pl.pallas_call(
        kernel,
        in_specs=[SMEM if i in smem else VMEM for i in range(len(args))],
        out_specs=[VMEM] * len(shapes),
        out_shape=shapes,
        scratch_shapes=list(scratch),
        compiler_params=pltpu.CompilerParams(vmem_limit_bytes=56 * 1024 * 1024),
        cost_estimate=pl.CostEstimate(flops=flops, bytes_accessed=moved, transcendentals=0),
        name=name,
    )(*args)


def dot(left, right):
    return jnp.dot(left, right, preferred_element_type=F32)


def dot_rows(left, right):
    return lax.dot_general(left, right, (((0,), (0,)), ((), ())), preferred_element_type=F32)


def dot_lanes(left, right):
    return lax.dot_general(left, right, (((1,), (1,)), ((), ())), preferred_element_type=F32)


def turned(values, cosine, sine):
    lane = lax.broadcasted_iota(jnp.int32, values.shape, 1)
    half = HEAD // 2
    swapped = jnp.where(
        lane % HEAD < half,
        pltpu.roll(values, LANES - half, 1),
        pltpu.roll(values, half, 1),
    )
    return values * cosine + swapped * sine


def turn_tables(first, count):
    lane = jnp.arange(LANES)
    place = (first + jnp.arange(count)).astype(F32)
    half = HEAD // 2
    freq = ROPE_BASE ** (-((lane % half).astype(F32) * 2.0 / HEAD))
    angle = place[:, None] * freq[None, :]
    sign = jnp.where(lane % HEAD < half, -1.0, 1.0)[None, :]
    return jnp.cos(angle), jnp.sin(angle) * sign


def lanes_of(index):
    return slice(index * LANES, (index + 1) * LANES)


def spread_pair(values, pair):
    rows = values.shape[0]
    lane = lax.broadcasted_iota(jnp.int32, (rows, LANES), 1)
    return jnp.where(
        lane < SSM_HEAD, values[:, 2 * pair : 2 * pair + 1], values[:, 2 * pair + 1 : 2 * pair + 2]
    )


def head_sum(values, pair):
    lane = lax.broadcasted_iota(jnp.int32, (LANES, LANES), 0)
    head = lax.broadcasted_iota(jnp.int32, (LANES, LANES), 1)
    chosen = (lane // SSM_HEAD + 2 * pair == head).astype(F32).astype(BF16)
    upper = values.astype(BF16)
    lower = (values - upper.astype(F32)).astype(BF16)
    return dot(upper, chosen) + dot(lower, chosen)


def silu_slope(values):
    gate = jax.nn.sigmoid(values)
    return gate * (1.0 + values * (1.0 - gate))


def front_kernel(x, gain, key_w, value_w, query_w, cosine, sine, normed, pairs, queries):
    values = x[...].astype(F32)
    scale = lax.rsqrt(jnp.mean(values * values, -1, keepdims=True) + EPS)
    normed[...] = (values * scale * gain[...]).astype(BF16)
    low = normed[...]
    cos, sin = cosine[...], sine[...]
    pairs[:, :LANES] = turned(dot(low, key_w[...]), cos, sin).astype(BF16)
    pairs[:, LANES:] = dot(low, value_w[...]).astype(BF16)
    raw = dot(low, query_w[...])
    for chunk in range(HEADS * HEAD // LANES):
        part = turned(raw[:, lanes_of(chunk)], cos, sin) * HEAD**-0.5
        queries[:, lanes_of(chunk)] = part.astype(BF16)


def block_mask(first, start, seg_keys, seg_queries):
    keys, queries = seg_keys.shape[0], seg_queries.shape[1]
    place = lax.broadcasted_iota(jnp.int32, (keys, queries), 0) + start
    reach = lax.broadcasted_iota(jnp.int32, (keys, queries), 1) + first
    return (seg_keys == seg_queries) & (place <= reach)


def attend_kernel(
    first_ref, queries, pairs, seg_keys, seg_queries, low, exact, spread, top, total, gathered
):
    count = queries.shape[0]
    first = first_ref[0]
    group = HEADS // KV_HEADS
    top[...] = jnp.full(top.shape, NEG, F32)
    total[...] = jnp.zeros(total.shape, F32)
    gathered[...] = jnp.zeros(gathered.shape, F32)

    def chunk(index, carry):
        start = pl.multiple_of(index * count, count)
        rows = pl.ds(start, count)
        mask = block_mask(first, start, seg_keys[rows, :], seg_queries[...])
        for head in range(HEADS):
            kv = head // group
            keys = pairs[rows, kv * HEAD : (kv + 1) * HEAD]
            values = pairs[rows, LANES + kv * HEAD : LANES + (kv + 1) * HEAD]
            scores = dot_lanes(keys, queries[:, head * HEAD : (head + 1) * HEAD])
            scores = jnp.where(mask, scores, NEG)
            before = top[head : head + 1]
            now = jnp.maximum(before, jnp.max(scores, 0, keepdims=True))
            weights = jnp.exp(scores - now)
            fade = jnp.exp(before - now)
            top[head : head + 1] = now
            total[head : head + 1] = total[head : head + 1] * fade + jnp.sum(
                weights, 0, keepdims=True
            )
            span = slice(head * HEAD, (head + 1) * HEAD)
            gathered[span] = gathered[span] * fade + dot_rows(values, weights.astype(BF16))
        return carry

    lax.fori_loop(0, first // count + 1, chunk, 0)
    spread[...] = top[...] + jnp.log(total[...])
    for head in range(HEADS):
        span = slice(head * HEAD, (head + 1) * HEAD)
        exact[span] = gathered[span] / total[head : head + 1]
    for chunk_at in range(HEADS * HEAD // LANES):
        low[:, lanes_of(chunk_at)] = exact[lanes_of(chunk_at)].T.astype(BF16)


def attend_back_kernel(
    first_ref,
    queries,
    pairs,
    slope,
    exact,
    spread,
    seg_keys,
    seg_queries,
    cosine,
    sine,
    query_low,
    pair_slope,
    turned_slope,
    delta,
    query_slope,
):
    count = queries.shape[0]
    length = pairs.shape[0]
    first = first_ref[0]
    group = HEADS // KV_HEADS
    for chunk_at in range(HEADS * HEAD // LANES):
        turned_slope[lanes_of(chunk_at)] = slope[:, lanes_of(chunk_at)].astype(F32).T
    for head in range(HEADS):
        span = slice(head * HEAD, (head + 1) * HEAD)
        delta[head : head + 1] = jnp.sum(turned_slope[span] * exact[span], 0, keepdims=True)
    query_slope[...] = jnp.zeros(query_slope.shape, F32)

    def chunk(index, carry):
        start = pl.multiple_of(index * count, count)
        rows = pl.ds(start, count)
        mask = block_mask(first, start, seg_keys[rows, :], seg_queries[...])
        for kv in range(KV_HEADS):
            keys = pairs[rows, kv * HEAD : (kv + 1) * HEAD]
            values = pairs[rows, LANES + kv * HEAD : LANES + (kv + 1) * HEAD]
            key_part = jnp.zeros((count, HEAD), F32)
            value_part = jnp.zeros((count, HEAD), F32)
            for head in range(kv * group, (kv + 1) * group):
                span = slice(head * HEAD, (head + 1) * HEAD)
                asked = queries[:, span]
                sloped = slope[:, span]
                scores = dot_lanes(keys, asked)
                weights = jnp.exp(jnp.where(mask, scores - spread[head : head + 1], NEG))
                dots = dot_lanes(values, sloped)
                score_slope = (weights * (dots - delta[head : head + 1])).astype(BF16)
                value_part = value_part + dot(weights.astype(BF16), sloped)
                key_part = key_part + dot(score_slope, asked)
                query_slope[span] = query_slope[span] + dot_rows(keys, score_slope)
            pair_slope[rows, kv * HEAD : (kv + 1) * HEAD] = key_part.astype(BF16)
            pair_slope[rows, LANES + kv * HEAD : LANES + (kv + 1) * HEAD] = value_part.astype(BF16)
        return carry

    def blank(index, carry):
        start = pl.multiple_of(index * count, count)
        pair_slope[pl.ds(start, count), :] = jnp.zeros((count, 2 * LANES), BF16)
        return carry

    live = first // count + 1
    lax.fori_loop(0, live, chunk, 0)
    lax.fori_loop(live, length // count, blank, 0)
    for chunk_at in range(HEADS * HEAD // LANES):
        part = query_slope[lanes_of(chunk_at)].T * HEAD**-0.5
        query_low[:, lanes_of(chunk_at)] = turned(part, cosine[...], -sine[...]).astype(BF16)


def pairs_back_kernel(owned, cosine, sine, low):
    keys = owned[:, :LANES].astype(F32)
    low[:, :LANES] = turned(keys, cosine[...], -sine[...]).astype(BF16)
    low[:, LANES:] = owned[:, LANES:]


def conv_total(inner, taps, bias, marks, chunk):
    span = lanes_of(chunk)
    extended = inner[:, span].astype(F32)
    total = bias[:, span] + taps[KERNEL - 1 : KERNEL, span] * extended[HALO:]
    shifted = []
    for tap in range(KERNEL - 1):
        moved = pltpu.roll(extended, KERNEL - 1 - tap, 0)[HALO:] * marks[:, tap : tap + 1]
        total = total + taps[tap : tap + 1, span] * moved
        shifted.append(moved)
    return total, shifted + [extended[HALO:]]


def triangle(count, strict=False, upper=False):
    row = lax.broadcasted_iota(jnp.int32, (count, count), 0)
    column = lax.broadcasted_iota(jnp.int32, (count, count), 1)
    if upper:
        row, column = column, row
    return (row > column if strict else row >= column).astype(F32)


def soft(values):
    return jnp.maximum(values, 0.0) + jnp.log1p(jnp.exp(-jnp.abs(values)))


def prep_kernel(
    inner,
    raw,
    step_bias,
    rates,
    taps,
    conv_bias,
    marks,
    channels,
    scaled,
    inflow,
    readout,
    steps,
    logs,
    logs_turned,
    state,
):
    count = raw.shape[0]
    steps[...] = soft(raw[...] + step_bias[...])
    logs[...] = precise(triangle(count), steps[...] * rates[...])
    logs_turned[...] = logs[...].T
    for chunk, target in ((PAIRS, inflow), (PAIRS + 1, readout)):
        total, _ = conv_total(inner, taps, conv_bias, marks, chunk)
        target[...] = (total * jax.nn.sigmoid(total)).astype(BF16)
    ending = logs[count - 1 : count]
    tail = jnp.exp(ending - logs[...]) * marks[:, 4:5]
    stepped = steps[...]
    row = lax.broadcasted_iota(jnp.int32, (EXTRA, LANES), 0)
    for pair in range(PAIRS):
        span = lanes_of(pair)
        total, _ = conv_total(inner, taps, conv_bias, marks, pair)
        value = total * jax.nn.sigmoid(total)
        channels[:, span] = value
        value = value * spread_pair(stepped, pair)
        scaled[:, span] = value.astype(BF16)
        weighted = (value * spread_pair(tail, pair)).astype(BF16)
        state[:STATE, span] = dot_rows(inflow[...], weighted).astype(BF16)
        whole = spread_pair(ending, pair)
        high = whole.astype(BF16).astype(F32)
        middle = (whole - high).astype(BF16).astype(F32)
        low = whole - high - middle
        state[STATE:, span] = jnp.where(
            row == 0, high, jnp.where(row == 1, middle, jnp.where(row == 2, low, 0.0))
        ).astype(BF16)


def decay_kernel_parts(logs, logs_turned, seg_column, seg_row, bias):
    count = logs.shape[0]
    row = lax.broadcasted_iota(jnp.int32, (count, count), 0)
    column = lax.broadcasted_iota(jnp.int32, (count, count), 1)
    inside = (seg_column[...] == seg_row[...]) & (row >= column)
    bias[...] = jnp.where(inside, 0.0, NEG)


IN_STEP = 4


def inner_kernel(logs, logs_turned, seg_column, seg_row, inflow, readout, scaled, result, bias, meet):
    count = logs.shape[0]
    step = pl.program_id(0)

    @pl.when(step == 0)
    def _():
        decay_kernel_parts(logs, logs_turned, seg_column, seg_row, bias)
        meet[...] = dot_lanes(readout[...], inflow[...])

    columns = pltpu.roll(logs[...], (LANES - IN_STEP * step) % LANES, 1)
    half = count // 2
    for k in range(IN_STEP):
        across = logs_turned[pl.ds(IN_STEP * step + k, 1), :]
        span = slice(k * SSM_HEAD, (k + 1) * SSM_HEAD)
        for top, width in ((0, half), (half, count)):
            rows = slice(top, top + half)
            gap = columns[rows, k : k + 1] - across[:, :width] + bias[rows, :width]
            mixing = (jnp.exp(gap) * meet[rows, :width]).astype(BF16)
            result[rows, span] = dot(mixing, scaled[:width, span])


def inner_back_kernel(
    logs,
    logs_turned,
    seg_column,
    seg_row,
    inflow,
    readout,
    scaled,
    slope,
    scaled_slope,
    inflow_slope,
    readout_slope,
    bias,
    meet,
    meet_slope,
):
    count = logs.shape[0]
    step = pl.program_id(0)

    @pl.when(step == 0)
    def _():
        decay_kernel_parts(logs, logs_turned, seg_column, seg_row, bias)
        meet[...] = dot_lanes(readout[...], inflow[...])
        meet_slope[...] = jnp.zeros(meet_slope.shape, F32)

    columns = pltpu.roll(logs[...], (LANES - IN_STEP * step) % LANES, 1)
    half = count // 2
    for top, width in ((0, half), (half, count)):
        rows = slice(top, top + half)
        gathered = jnp.zeros((half, width), F32)
        for k in range(IN_STEP):
            across = logs_turned[pl.ds(IN_STEP * step + k, 1), :]
            span = slice(k * SSM_HEAD, (k + 1) * SSM_HEAD)
            gap = columns[rows, k : k + 1] - across[:, :width] + bias[rows, :width]
            decay = jnp.exp(gap)
            mixing = (decay * meet[rows, :width]).astype(BF16)
            gathered = gathered + decay * dot_lanes(slope[rows, span], scaled[:width, span])
            part = dot_rows(mixing, slope[rows, span])
            if top:
                scaled_slope[:half, span] = scaled_slope[:half, span] + part[:half]
                scaled_slope[half:, span] = part[half:]
            else:
                scaled_slope[:half, span] = part
        meet_slope[rows, :width] = meet_slope[rows, :width] + gathered

    @pl.when(step == SSM_HEADS // IN_STEP - 1)
    def _():
        low = meet_slope[...].astype(BF16)
        inflow_slope[...] = dot_rows(low, readout[...])
        readout_slope[...] = dot(low, inflow[...])


def inner_call(kernel, fixed, moving, outs, fixed_outs, name, scratch):
    count = fixed[0].shape[0]
    steps = SSM_HEADS // IN_STEP
    width = IN_STEP * SSM_HEAD
    held = [pl.BlockSpec(a.shape, lambda j: (0, 0)) for a in fixed]
    passing = pl.BlockSpec((count, width), lambda j: (0, j))
    return pl.pallas_call(
        kernel,
        grid=(steps,),
        in_specs=held + [passing] * len(moving),
        out_specs=[passing] * len(outs)
        + [pl.BlockSpec(shape, lambda j: (0, 0)) for shape, _ in fixed_outs],
        out_shape=[jax.ShapeDtypeStruct((count, WIDTH), kind) for kind in outs]
        + [jax.ShapeDtypeStruct(shape, kind) for shape, kind in fixed_outs],
        scratch_shapes=[pltpu.VMEM((count, count), F32)] * scratch,
        compiler_params=pltpu.CompilerParams(vmem_limit_bytes=40 * 1024 * 1024),
        cost_estimate=pl.CostEstimate(
            flops=2 * scratch * count * count * WIDTH,
            bytes_accessed=8 * count * WIDTH,
            transcendentals=0,
        ),
        name=name,
    )(*fixed, *moving)


def entering_kernel(
    alive, gathered, inner_part, readout, logs, marks, channels, gating, skip, gain,
    tail, scanned, entering, walls, gated,
):
    count = logs.shape[0]
    peers = alive.shape[1]
    block = STATE + EXTRA
    enter = jnp.exp(logs[...]) * marks[:, 3:4]
    square = jnp.zeros((count, 1), F32)
    for pair in range(PAIRS):
        span = lanes_of(pair)
        total = jnp.zeros((STATE, LANES), F32)
        passed = jnp.zeros((1, LANES), F32)
        for peer in reversed(range(peers)):
            base = peer * block
            wall = gathered[base + STATE : base + block, span].astype(F32)
            wall = jnp.sum(wall, 0, keepdims=True)
            walls[peer : peer + 1, span] = wall
            total = total + gathered[base : base + STATE, span].astype(F32) * (
                jnp.exp(passed) * alive[0, peer]
            )
            passed = passed + wall * alive[1, peer]
        low = total.astype(BF16)
        entering[:, span] = low
        full = inner_part[:, span] + dot(readout[...], low) * spread_pair(enter, pair)
        scanned[:, span] = full
        gate = gating[:, span]
        full = (full + skip[:, span] * channels[:, span]) * (gate * jax.nn.sigmoid(gate))
        gated[:, span] = full
        square = square + jnp.sum(full * full, -1, keepdims=True)
    scale = lax.rsqrt(square / WIDTH + EPS)
    for pair in range(PAIRS):
        span = lanes_of(pair)
        tail[:, span] = (gated[:, span] * scale * gain[:, span]).astype(BF16)


def tail_back_kernel(
    slope, scanned, channels, gating, skip, gain, logs, marks, readout,
    scanned_slope, gating_slope, sums, state_slope, gated,
):
    count = logs.shape[0]
    enter = jnp.exp(logs[...]) * marks[:, 3:4]
    square = jnp.zeros((count, 1), F32)
    cross = jnp.zeros((count, 1), F32)
    for pair in range(PAIRS):
        span = lanes_of(pair)
        gate = gating[:, span]
        full = scanned[:, span] + skip[:, span] * channels[:, span]
        full = full * (gate * jax.nn.sigmoid(gate))
        gated[:, span] = full
        square = square + jnp.sum(full * full, -1, keepdims=True)
        cross = cross + jnp.sum(full * slope[:, span] * gain[:, span], -1, keepdims=True)
    scale = lax.rsqrt(square / WIDTH + EPS)
    cross = cross / WIDTH * scale * scale * scale
    for pair in range(PAIRS):
        span = lanes_of(pair)
        gate = gating[:, span]
        sigmoid = jax.nn.sigmoid(gate)
        back = slope[:, span]
        value = gated[:, span]
        sums[0:1, span] = jnp.sum(back * value * scale, 0, keepdims=True)
        back = back * gain[:, span] * scale - value * cross
        held = channels[:, span]
        full = scanned[:, span] + skip[:, span] * held
        gating_slope[:, span] = (
            back * full * sigmoid * (1.0 + gate * (1.0 - sigmoid))
        ).astype(BF16)
        back = back * (gate * sigmoid)
        sums[1:2, span] = jnp.sum(back * held, 0, keepdims=True)
        scanned_slope[:, span] = back.astype(BF16)
        weighted = (back * spread_pair(enter, pair)).astype(BF16)
        state_slope[:, span] = dot_rows(readout[...], weighted).astype(BF16)
    sums[2:8] = jnp.zeros((6, WIDTH), F32)


def leaving_kernel(
    alive, gathered, walls, entering, scanned, scanned_slope, scaled, channels, scaled_slope,
    inflow, readout, inflow_part, readout_part, steps, raw, step_bias, logs, rates, marks, skip,
    inner, taps, conv_bias,
    inner_low, edges, conv_sums, raw_slope, small,
    conv_slope,
):
    count = logs.shape[0]
    peers = alive.shape[1]
    ending = logs[count - 1 : count]
    tail = jnp.exp(ending - logs[...]) * marks[:, 4:5]
    enter = jnp.exp(logs[...]) * marks[:, 3:4]
    stepped = steps[...]
    inflow_slope = inflow_part[...]
    readout_slope = readout_part[...]
    inside = jnp.zeros((count, LANES), F32)
    outward = jnp.zeros((count, LANES), F32)
    direct = jnp.zeros((count, LANES), F32)
    through = jnp.zeros((8, LANES), F32)
    for pair in range(PAIRS):
        span = lanes_of(pair)
        total = jnp.zeros((STATE, LANES), F32)
        passed = jnp.zeros((1, LANES), F32)
        for peer in range(peers):
            total = total + gathered[peer * STATE : (peer + 1) * STATE, span].astype(F32) * (
                jnp.exp(passed) * alive[0, peer]
            )
            passed = passed + walls[peer : peer + 1, span] * alive[1, peer]
        low = total.astype(BF16)
        entered = entering[:, span]
        back = scanned_slope[:, span]
        lengths = spread_pair(stepped, pair)
        held = channels[:, span]
        short = scaled[:, span].astype(F32)
        tails = spread_pair(tail, pair)
        outer = dot(inflow[...], low) * tails
        within = scaled_slope[:, span]
        both = within + outer
        wide = back.astype(F32)
        inside = inside + head_sum(wide * scanned[:, span] - short * within, pair)
        outward = outward + head_sum(short * outer, pair)
        direct = direct + head_sum(held * both, pair)
        kept = jnp.sum(total * entered.astype(F32), 0, keepdims=True) * jnp.exp(
            spread_pair(ending, pair)
        )
        through = through + head_sum(jnp.broadcast_to(kept, (8, LANES)), pair)
        conv_slope[:, span] = both * lengths + skip[:, span] * wide
        inflow_slope = inflow_slope + dot_lanes((short * tails).astype(BF16), low)
        readout_slope = readout_slope + dot_lanes(
            (wide * spread_pair(enter, pair)).astype(BF16), entered
        )
    conv_slope[:, lanes_of(PAIRS)] = inflow_slope
    conv_slope[:, lanes_of(PAIRS + 1)] = readout_slope
    along = (
        precise(triangle(count, upper=True), inside)
        + precise(triangle(count, strict=True), outward)
        + through[:1] * alive[2, 0]
    )
    step_slope = direct + rates[...] * along
    step_slope = step_slope * jax.nn.sigmoid(raw[...] + step_bias[...])
    raw_slope[...] = step_slope.astype(BF16)
    small[0:1] = jnp.sum(step_slope, 0, keepdims=True)
    small[1:2] = rates[...] * jnp.sum(stepped * along, 0, keepdims=True)
    small[2:8] = jnp.zeros((6, LANES), F32)
    blank = jnp.zeros((HALO, LANES), F32)
    for chunk in range(PAIRS + 2):
        span = lanes_of(chunk)
        total, shifted = conv_total(inner, taps, conv_bias, marks, chunk)
        slope = conv_slope[:, span] * silu_slope(total)
        spread = jnp.concatenate([blank, slope * taps[KERNEL - 1 : KERNEL, span]], 0)
        for tap in range(KERNEL - 1):
            part = slope * taps[tap : tap + 1, span] * marks[:, tap : tap + 1]
            part = jnp.concatenate([blank, part], 0)
            spread = spread + pltpu.roll(part, HALO + count - (KERNEL - 1 - tap), 0)
        for tap in range(KERNEL):
            conv_sums[tap : tap + 1, span] = jnp.sum(slope * shifted[tap], 0, keepdims=True)
        conv_sums[KERNEL : KERNEL + 1, span] = jnp.sum(slope, 0, keepdims=True)
        conv_sums[KERNEL + 1 :, span] = jnp.zeros((8 - KERNEL - 1, LANES), F32)
        inner_low[:, span] = spread[HALO:].astype(BF16)
        edges[:HALO, span] = spread[:HALO]
        edges[HALO:, span] = spread[count:]


def joint_kernel(xs, ys, left_ref, left_sib_ref, a_ref, a_sib_ref, b_ref, b_sib_ref, *outs):
    a_outs, b_outs = outs[:xs], outs[xs:]
    part = left_ref.shape[0] // (xs * ys)
    for source, sibling, targets, first in (
        (a_ref, a_sib_ref, a_outs, True),
        (b_ref, b_sib_ref, b_outs, False),
    ):
        total = jnp.dot(left_ref[...], source[...], preferred_element_type=jnp.float32)
        total = total + jnp.dot(
            left_sib_ref[...], sibling[...], preferred_element_type=jnp.float32
        )
        total = total.astype(jnp.bfloat16)
        for x in range(xs):
            for y in range(ys):
                piece = total[(x * ys + y) * part : (x * ys + y + 1) * part]
                if first:
                    targets[x][y * part : (y + 1) * part] = piece
                else:
                    targets[y][x * part : (x + 1) * part] = piece


def joint_gradient(place, left, right, left_sib, right_sib):
    rows, tokens = left.shape
    width = right.shape[1]
    xs, ys = place.sizes["x"], place.sizes["y"]
    half = width // 2
    tile = next(t for t in (512, 384, 256, half) if half % t == 0)
    steps = half // tile
    whole = pl.BlockSpec((rows, tokens), lambda j: (0, 0))
    early = pl.BlockSpec((tokens, tile), lambda j: (0, j))
    late = pl.BlockSpec((tokens, tile), lambda j: (0, j + steps))
    shapes = [rows // xs] * xs + [rows // ys] * ys
    outs = pl.pallas_call(
        lambda *refs: joint_kernel(xs, ys, *refs),
        grid=(steps,),
        in_specs=[whole, whole, early, early, late, late],
        out_specs=[pl.BlockSpec((r, tile), lambda j: (0, j)) for r in shapes],
        out_shape=[jax.ShapeDtypeStruct((r, half), jnp.bfloat16) for r in shapes],
        compiler_params=pltpu.CompilerParams(vmem_limit_bytes=40 * 1024 * 1024),
        cost_estimate=pl.CostEstimate(
            flops=4 * rows * tokens * width,
            bytes_accessed=2 * (rows * width + 2 * tokens * (rows + width)),
            transcendentals=0,
        ),
        name="joint_gradient",
    )(left, left_sib, right, right_sib, right, right_sib)
    return outs[:xs], outs[xs:]


def reduced(place, pieces, first, second):
    n_first, n_second = place.sizes[first], place.sizes[second]
    kept = pieces[0]
    arrived = [place.turn(pieces[k], first, k) for k in range(1, n_first)]
    share = kept.shape[0] // n_second

    def summed(k):
        window = slice(k * share, (k + 1) * share)
        total = kept[window].astype(jnp.float32)
        for piece in arrived:
            total = total + piece[window].astype(jnp.float32)
        return total

    total = summed(0)
    for k in range(1, n_second):
        total = total + place.turn(summed(k).astype(jnp.bfloat16), second, k).astype(jnp.float32)
    return total


def own_share(place, left, right, left_sib, right_sib):
    first, second = joint_gradient(place, left, right, left_sib, right_sib)
    total = jnp.concatenate(
        [reduced(place, first, "x", "y"), reduced(place, second, "y", "x")], 1
    )
    depth = place.sizes["z"]
    rows = total.shape[0] // depth
    share = total[:rows]
    for k in range(1, depth):
        share = share + place.turn(
            total[k * rows : (k + 1) * rows].astype(jnp.bfloat16), "z", k
        ).astype(jnp.float32)
    return share


def arranged(order, left):
    return lax.dot_general(
        order, left, (((1,), (1,)), ((), ())), preferred_element_type=jnp.float32
    ).astype(jnp.bfloat16)


def own_half(ordered):
    return ordered[: ordered.shape[0] // CORES]


def other_half(ordered):
    return ordered[ordered.shape[0] // CORES :]


def weight_shares(place, ordered, rights):
    right = jnp.concatenate(rights, 1) if len(rights) > 1 else rights[0]
    left_sib = place.turn(other_half(ordered), "core", 1)
    right_sib = place.turn(right, "core", 1)
    share = own_share(place, own_half(ordered), right, left_sib, right_sib)
    shares = []
    offset = 0
    for piece in rights:
        shares.append(share[:, offset : offset + piece.shape[1]])
        offset += piece.shape[1]
    return shares


def body(
    inputs,
    segments,
    cotangent,
    input_gain,
    query_weight,
    key_weight,
    value_weight,
    attention_weight,
    gating_weight,
    inner_weight,
    step_weight,
    step_bias,
    decay_log,
    skip_scale,
    conv_weight,
    conv_bias,
    mixer_gain,
    mixer_weight,
    feed_gain,
    gate_weight,
    up_weight,
    down_weight,
):
    place = Place()
    order = place.share_order(inputs.shape[2])
    count = inputs.shape[1]
    low_input = inputs[0]
    hidden = low_input.astype(F32)
    slope = cotangent[0]
    seg_row = segments[0]
    length = seg_row.shape[0]
    peers = length // count
    position = lax.axis_index("seq")
    first = position * count
    seg_here = lax.dynamic_slice_in_dim(seg_row, first, count)
    first_ref = first.reshape(1).astype(jnp.int32)

    lead = first - (KERNEL - 1) + jnp.arange(KERNEL - 1)
    seg_lead = jnp.where(lead >= 0, seg_row[jnp.maximum(lead, 0)], -1)
    seg_ext = jnp.concatenate([seg_lead, seg_here])
    seg_before, seg_last = seg_lead[KERNEL - 2], seg_here[count - 1]
    marks = jnp.stack(
        [seg_ext[tap : tap + count] == seg_here for tap in range(KERNEL - 1)]
        + [seg_here == seg_before, seg_here == seg_last]
        + [seg_here < 0] * 3,
        1,
    ).astype(F32)
    endings = seg_row[count - 1 :: count]
    ranks = jnp.arange(peers)
    earlier, later = ranks < position, ranks > position
    alive = jnp.stack([earlier & (endings == seg_before), earlier]).astype(F32)
    starts = jnp.concatenate([jnp.full((1,), -1, seg_row.dtype), endings[:-1]])
    alive_back = jnp.stack(
        [later & (starts == seg_last), later, jnp.broadcast_to(seg_before == seg_last, (peers,))]
    ).astype(F32)
    seg_column, seg_across = seg_here[:, None], seg_here[None, :]

    halo = passed_along(low_input[count - HALO :], "seq", 1)
    cosine, sine = turn_tables(first, count)
    normed_low, pairs, queries = local_call(
        front_kernel,
        [((count, inputs.shape[2]), BF16), ((count, 2 * LANES), BF16), ((count, HEADS * HEAD), BF16)],
        (low_input, input_gain[None], key_weight, value_weight, query_weight, cosine, sine),
        "front",
        flops=2 * count * inputs.shape[2] * 768,
    )
    everything = lax.all_gather(pairs, "seq", axis=0, tiled=True)
    normed_halo = norm_rows(halo.astype(F32), input_gain).astype(BF16)
    inner = product(jnp.concatenate([normed_halo, normed_low], 0), inner_weight).astype(BF16)
    wide_step = jnp.pad(step_weight, ((0, 0), (0, LANES - SSM_HEADS)))
    raw = product(normed_low, wide_step)
    wide_bias = jnp.pad(step_bias, (0, LANES - SSM_HEADS))[None]
    rates = jnp.pad(-jnp.exp(decay_log), (0, LANES - SSM_HEADS))[None]
    channels, scaled, inflow, readout, steps, logs, logs_turned, state = local_call(
        prep_kernel,
        [
            ((count, WIDTH), F32),
            ((count, WIDTH), BF16),
            ((count, STATE), BF16),
            ((count, STATE), BF16),
            ((count, LANES), F32),
            ((count, LANES), F32),
            ((LANES, count), F32),
            ((STATE + EXTRA, WIDTH), BF16),
        ],
        (inner, raw, wide_bias, rates, conv_weight, conv_bias[None], marks),
        "prepare",
        flops=2 * count * WIDTH * STATE,
    )
    states = lax.all_gather(state, "seq", axis=0, tiled=True)
    gating = product(normed_low, gating_weight)
    fixed = (logs, logs_turned, seg_column, seg_across, inflow, readout)
    (inner_part,) = inner_call(inner_kernel, fixed, (scaled,), (F32,), (), "inner", 2)
    attention_low, exact, spread = local_call(
        attend_kernel,
        [((count, HEADS * HEAD), BF16), ((HEADS * HEAD, count), F32), ((HEADS, count), F32)],
        (first_ref, queries, everything, seg_row[:, None], seg_across),
        "attend",
        scratch=[
            pltpu.VMEM((HEADS, count), F32),
            pltpu.VMEM((HEADS, count), F32),
            pltpu.VMEM((HEADS * HEAD, count), F32),
        ],
        smem=(0,),
        flops=4 * count * length * HEADS * HEAD,
    )
    attention_branch = product(attention_low, attention_weight)
    skip_wide = jnp.repeat(skip_scale, SSM_HEAD)[None]
    tail_low, scanned, entering, walls = local_call(
        entering_kernel,
        [
            ((count, WIDTH), BF16),
            ((count, WIDTH), F32),
            ((STATE, WIDTH), BF16),
            ((peers, WIDTH), F32),
        ],
        (
            alive,
            states,
            inner_part,
            readout,
            logs,
            marks,
            channels,
            gating,
            skip_wide,
            mixer_gain[None],
        ),
        "entering",
        scratch=[pltpu.VMEM((count, WIDTH), F32)],
        smem=(0,),
        flops=2 * count * WIDTH * STATE,
    )
    mixed_sum = hidden + attention_branch + product(tail_low, mixer_weight)
    feed, feed_back = jax.vjp(norm_rows, mixed_sum, feed_gain)
    feed_low = feed.astype(BF16)
    activated, unit_back = jax.vjp(
        gated_unit, product(feed_low, gate_weight), product(feed_low, up_weight)
    )
    activated_low = activated.astype(BF16)
    output = mixed_sum + product(activated_low, down_weight)

    (share_down,) = weight_shares(place, arranged(order, slope), (activated_low,))
    gate_slope, up_slope = unit_back(product_right(slope, down_weight))
    gate_low = gate_slope.astype(BF16)
    up_low = up_slope.astype(BF16)
    share_gate, share_up = weight_shares(place, arranged(order, feed_low), (gate_low, up_low))
    mixed_part, grad_feed_gain = feed_back(
        product_right(gate_low, gate_weight) + product_right(up_low, up_weight)
    )
    mixed_slope = slope.astype(F32) + mixed_part
    branch_low = mixed_slope.astype(BF16)
    scanned_slope, gating_low, tail_sums, state_slope = local_call(
        tail_back_kernel,
        [
            ((count, WIDTH), BF16),
            ((count, WIDTH), BF16),
            ((8, WIDTH), F32),
            ((STATE, WIDTH), BF16),
        ],
        (
            product_right(branch_low, mixer_weight),
            scanned,
            channels,
            gating,
            skip_wide,
            mixer_gain[None],
            logs,
            marks,
            readout,
        ),
        "tail_back",
        scratch=[pltpu.VMEM((count, WIDTH), F32)],
        flops=2 * count * WIDTH * STATE,
    )
    state_slopes = lax.all_gather(state_slope, "seq", axis=0, tiled=True)
    attention_slope = product_right(branch_low, attention_weight).astype(BF16)
    query_low, pair_slope = local_call(
        attend_back_kernel,
        [((count, HEADS * HEAD), BF16), ((length, 2 * LANES), BF16)],
        (
            first_ref,
            queries,
            everything,
            attention_slope,
            exact,
            spread,
            seg_row[:, None],
            seg_across,
            cosine,
            sine,
        ),
        "attend_back",
        scratch=[
            pltpu.VMEM((HEADS * HEAD, count), F32),
            pltpu.VMEM((HEADS, count), F32),
            pltpu.VMEM((HEADS * HEAD, count), F32),
        ],
        smem=(0,),
        flops=10 * count * length * HEADS * HEAD,
    )
    owned = lax.psum_scatter(pair_slope, "seq", scatter_dimension=0, tiled=True)
    share_attention, share_mixer = weight_shares(
        place, arranged(order, branch_low), (attention_low, tail_low)
    )
    ordered = arranged(order, normed_low)
    (share_gating,) = weight_shares(place, ordered, (gating_low,))
    scaled_slope, inflow_part, readout_part = inner_call(
        inner_back_kernel,
        fixed,
        (scaled, scanned_slope),
        (F32,),
        (((count, STATE), F32), ((count, STATE), F32)),
        "inner_back",
        3,
    )
    inner_low, edges, conv_sums, raw_slope, small = local_call(
        leaving_kernel,
        [
            ((count, inner.shape[1]), BF16),
            ((2 * HALO, inner.shape[1]), F32),
            ((8, inner.shape[1]), F32),
            ((count, LANES), BF16),
            ((8, LANES), F32),
        ],
        (
            alive_back,
            state_slopes,
            walls,
            entering,
            scanned,
            scanned_slope,
            scaled,
            channels,
            scaled_slope,
            inflow,
            readout,
            inflow_part,
            readout_part,
            steps,
            raw,
            wide_bias,
            logs,
            rates,
            marks,
            skip_wide,
            inner,
            conv_weight,
            conv_bias[None],
        ),
        "leaving",
        scratch=[
            pltpu.VMEM((count, inner.shape[1]), F32),
        ],
        smem=(0,),
        flops=8 * count * WIDTH * STATE,
    )
    returned = passed_along(edges[:HALO], "seq", -1)
    inner_low = lax.dynamic_update_slice(
        inner_low, (edges[HALO:] + returned).astype(BF16), (count - HALO, 0)
    )
    (pair_low,) = local_call(
        pairs_back_kernel, [((count, 2 * LANES), BF16)], (owned, cosine, sine), "pairs_back"
    )
    wide_slope = jnp.pad(raw_slope, ((0, 0), (0, LANES)))
    share_inner, share_query, share_pair, share_step = weight_shares(
        place, ordered, (inner_low, query_low, pair_low, wide_slope)
    )
    normed_slope = (
        product_right(gating_low, gating_weight)
        + product_right(inner_low, inner_weight)
        + product_right(query_low, query_weight)
        + product_right(pair_low, jnp.concatenate([key_weight, value_weight], 1))
        + product_right(raw_slope, wide_step)
    )
    input_part, grad_input_gain = jax.vjp(norm_rows, hidden, input_gain)[1](normed_slope)
    input_gradient = mixed_slope + input_part
    step_sum = lax.all_gather(share_step[:, :SSM_HEADS], ("dp", "seq"), axis=0, tiled=True)
    (
        step_bias_sum,
        decay_sum,
        skip_sum,
        mixer_gain_sum,
        conv_sum,
        conv_bias_sum,
        gain_sum,
        feed_gain_sum,
    ) = lax.psum(
        (
            small[0, :SSM_HEADS],
            small[1, :SSM_HEADS],
            jnp.sum(tail_sums[1].reshape(SSM_HEADS, SSM_HEAD), 1),
            tail_sums[0],
            conv_sums[:KERNEL],
            conv_sums[KERNEL],
            grad_input_gain,
            grad_feed_gain,
        ),
        ("dp", "seq"),
    )
    return (
        output.astype(BF16)[None],
        input_gradient[None],
        gain_sum,
        share_query,
        share_pair[:, :LANES],
        share_pair[:, LANES:],
        share_attention.T,
        share_gating,
        share_inner,
        step_sum,
        step_bias_sum,
        decay_sum,
        skip_sum,
        conv_sum,
        conv_bias_sum,
        mixer_gain_sum,
        share_mixer.T,
        feed_gain_sum,
        share_gate,
        share_up,
        share_down.T,
    )


def solution(mesh):
    in_specs = (
        P("dp", "seq", None),
        P("dp", None),
        P("dp", "seq", None),
        P(),
        P(),
        P(),
        P(),
        P(),
        P(),
        P(),
        P(),
        P(),
        P(),
        P(),
        P(),
        P(),
        P(),
        P(),
        P(),
        P(),
        P(),
        P(),
    )
    out_specs = (
        P("dp", "seq", None),
        P("dp", "seq", None),
        P(),
        P(("dp", "seq"), None),
        P(("dp", "seq"), None),
        P(("dp", "seq"), None),
        P(None, ("dp", "seq")),
        P(("dp", "seq"), None),
        P(("dp", "seq"), None),
        P(),
        P(),
        P(),
        P(),
        P(),
        P(),
        P(),
        P(None, ("dp", "seq")),
        P(),
        P(("dp", "seq"), None),
        P(("dp", "seq"), None),
        P(None, ("dp", "seq")),
    )
    return jax.shard_map(body, mesh=mesh, in_specs=in_specs, out_specs=out_specs, check_vma=False)
```

```python
import functools

import jax
import jax.numpy as jnp
from jax import lax
from jax.experimental import pallas as pl
from jax.experimental.pallas import tpu as pltpu
from jax.sharding import PartitionSpec as P

HEADS = 8
KV_HEADS = 2
HEAD = 64
SSM_HEADS = 24
SSM_HEAD = 64
STATE = 128
KERNEL = 4


EPS = 1e-05
ROPE_BASE = 100000000000.0
NEG = -1e30
HIGH = lax.Precision.HIGHEST


def passed_along(shard, axis, by):
    peers = lax.axis_size(axis)
    pairs = [(i, i + by) for i in range(peers) if 0 <= i + by < peers]
    return lax.ppermute(shard, axis, pairs)


def product(left, right):
    return jnp.dot(left, right, preferred_element_type=jnp.float32)


def product_left(left, right):
    return lax.dot_general(
        left, right, (((0,), (0,)), ((), ())), preferred_element_type=jnp.float32
    )


def product_right(left, right):
    return lax.dot_general(
        left, right, (((1,), (1,)), ((), ())), preferred_element_type=jnp.float32
    )


def precise(left, right):
    return jnp.dot(left, right, preferred_element_type=jnp.float32, precision=HIGH)


def norm_rows(values, gain):
    return values * lax.rsqrt(jnp.mean(values * values, -1, keepdims=True) + EPS) * gain


def gated_unit(gate, upward):
    return jax.nn.silu(gate) * upward


CORES = 2
DEPTH = 4
LANES = 128


class Place:
    def __init__(self):
        self.dp = lax.axis_size("dp")
        self.seq = lax.axis_size("seq")
        self.sizes = {
            "y": self.dp // CORES,
            "core": CORES,
            "z": DEPTH,
            "x": self.seq // DEPTH,
        }

    def split(self, index):
        dp, seq = index // self.seq, index % self.seq
        return {
            "y": dp // CORES,
            "core": dp % CORES,
            "z": seq // self.sizes["x"],
            "x": seq % self.sizes["x"],
        }

    def join(self, at):
        return (at["y"] * CORES + at["core"]) * self.seq + at["z"] * self.sizes["x"] + at["x"]

    def turn(self, shard, axis, by):
        pairs = []
        for index in range(self.dp * self.seq):
            at = self.split(index)
            at[axis] = (at[axis] + by) % self.sizes[axis]
            pairs.append((index, self.join(at)))
        return lax.ppermute(shard, ("dp", "seq"), pairs)

    def swap(self, shard, axis, bit):
        pairs = []
        for index in range(self.dp * self.seq):
            at = self.split(index)
            at[axis] ^= bit
            pairs.append((index, self.join(at)))
        return lax.ppermute(shard, ("dp", "seq"), pairs)

    def share_order(self, width, group, along):
        sizes, at = self.sizes, self.split(group * self.seq + along)
        rows = width // (self.dp * self.seq)
        k = lax.broadcasted_iota(jnp.int32, (width, 1), 0)
        within = k % rows
        rest = k // rows
        dz = rest % sizes["z"]
        rest = rest // sizes["z"]
        dy = rest % sizes["y"]
        rest = rest // sizes["y"]
        dx = rest % sizes["x"]
        dc = rest // sizes["x"]
        owner = self.join(
            {
                "y": (at["y"] + dy) % sizes["y"],
                "core": (at["core"] + dc) % sizes["core"],
                "z": at["z"] ^ (dz // 2 + 2 * (dz % 2)),
                "x": (at["x"] + dx) % sizes["x"],
            }
        )
        source = owner * rows + within
        columns = lax.broadcasted_iota(jnp.int32, (1, width), 1)
        return (source == columns).astype(jnp.bfloat16)


F32 = jnp.float32
BF16 = jnp.bfloat16
PAIR = 2 * SSM_HEAD
WIDTH = SSM_HEADS * SSM_HEAD
PAIRS = WIDTH // PAIR
HALO = 16
EXTRA = 16
WALLS = 16
VMEM = pl.BlockSpec(memory_space=pltpu.VMEM)
SMEM = pl.BlockSpec(memory_space=pltpu.SMEM)


def local_call(kernel, outs, args, name, scratch=(), smem=(), flops=0):
    shapes = [jax.ShapeDtypeStruct(shape, kind) for shape, kind in outs]
    moved = sum(a.size * a.dtype.itemsize for a in args)
    moved += sum(s.size * s.dtype.itemsize for s in shapes)
    return pl.pallas_call(
        kernel,
        in_specs=[SMEM if i in smem else VMEM for i in range(len(args))],
        out_specs=[VMEM] * len(shapes),
        out_shape=shapes,
        scratch_shapes=list(scratch),
        compiler_params=pltpu.CompilerParams(vmem_limit_bytes=56 * 1024 * 1024),
        cost_estimate=pl.CostEstimate(flops=0, bytes_accessed=0, transcendentals=0),
        name=name,
    )(*args)


def dot(left, right):
    return jnp.dot(left, right, preferred_element_type=F32)


def dot_rows(left, right):
    return lax.dot_general(left, right, (((0,), (0,)), ((), ())), preferred_element_type=F32)


def dot_lanes(left, right):
    return lax.dot_general(left, right, (((1,), (1,)), ((), ())), preferred_element_type=F32)


def turned(values, cosine, sine):
    lane = lax.broadcasted_iota(jnp.int32, values.shape, 1)
    half = HEAD // 2
    swapped = jnp.where(
        lane % HEAD < half,
        pltpu.roll(values, LANES - half, 1),
        pltpu.roll(values, half, 1),
    )
    return values * cosine + swapped * sine


def turn_tables(first, count):
    lane = jnp.arange(LANES)
    place = (first + jnp.arange(count)).astype(F32)
    half = HEAD // 2
    freq = ROPE_BASE ** (-((lane % half).astype(F32) * 2.0 / HEAD))
    angle = place[:, None] * freq[None, :]
    sign = jnp.where(lane % HEAD < half, -1.0, 1.0)[None, :]
    return jnp.cos(angle), jnp.sin(angle) * sign


def lanes_of(index):
    return slice(index * LANES, (index + 1) * LANES)


def spread_pair(values, pair):
    rows = values.shape[0]
    lane = lax.broadcasted_iota(jnp.int32, (rows, LANES), 1)
    return jnp.where(
        lane < SSM_HEAD, values[:, 2 * pair : 2 * pair + 1], values[:, 2 * pair + 1 : 2 * pair + 2]
    )


def head_sum(values, pair):
    lane = lax.broadcasted_iota(jnp.int32, (LANES, LANES), 0)
    head = lax.broadcasted_iota(jnp.int32, (LANES, LANES), 1)
    chosen = (lane // SSM_HEAD + 2 * pair == head).astype(F32).astype(BF16)
    upper = values.astype(BF16)
    lower = (values - upper.astype(F32)).astype(BF16)
    return dot(upper, chosen) + dot(lower, chosen)


def silu_slope(values):
    gate = jax.nn.sigmoid(values)
    return gate * (1.0 + values * (1.0 - gate))


def front_kernel(
    x, key_w, value_w, cosine, sine, conv_bias, input_gain, mixer_gain, skip, step_bias, decay_log,
    normed, pairs, table,
):
    table[...] = jnp.zeros(table.shape, F32)
    for row, source in (
        (ROW_CONV, conv_bias),
        (ROW_GAIN, input_gain),
        (ROW_MIXER, mixer_gain),
        (ROW_STEP, step_bias),
    ):
        table[row : row + 1, : source.shape[0]] = source[...].reshape(1, source.shape[0])
    rates = -jnp.exp(decay_log[...].reshape(1, SSM_HEADS))
    table[ROW_RATE : ROW_RATE + 1, :SSM_HEADS] = rates
    skips = skip[...].reshape(1, SSM_HEADS)
    for pair in range(PAIRS):
        table[ROW_SKIP : ROW_SKIP + 1, lanes_of(pair)] = spread_pair(skips, pair)
    values = x[...].astype(F32)
    scale = lax.rsqrt(jnp.mean(values * values, -1, keepdims=True) + EPS)
    gain = table[ROW_GAIN : ROW_GAIN + 1, : values.shape[1]]
    normed[...] = (values * scale * gain).astype(BF16)
    low = normed[...]
    pairs[:, :LANES] = turned(dot(low, key_w[...]), cosine[...], sine[...]).astype(BF16)
    pairs[:, LANES:] = dot(low, value_w[...]).astype(BF16)


def block_mask(first, start, segments, count):
    def row(at):
        return segments[:, pl.ds(pl.multiple_of(at, LANES), count)].astype(F32)

    place = lax.broadcasted_iota(jnp.int32, (count, count), 0) + start
    reach = lax.broadcasted_iota(jnp.int32, (count, count), 1) + first
    keys = jnp.broadcast_to(row(start), (8, count)).T[:, :1]
    return (keys == row(first)) & (place <= reach)


def head_columns(pairs, rows):
    keys = [pairs[rows, kv * HEAD : (kv + 1) * HEAD] for kv in range(KV_HEADS)]
    values = [
        pairs[rows, LANES + kv * HEAD : LANES + (kv + 1) * HEAD] for kv in range(KV_HEADS)
    ]
    return keys, values


def attend_kernel(
    position, normed, query_w, cosine, sine, pairs, segments,
    queries, low, exact, spread, top, total, gathered,
):
    count = queries.shape[0]
    raw = dot(normed[...], query_w[...])
    for chunk_at in range(HEADS * HEAD // LANES):
        part = turned(raw[:, lanes_of(chunk_at)], cosine[...], sine[...]) * HEAD**-0.5
        queries[:, lanes_of(chunk_at)] = part.astype(BF16)
    first = position[0] * count
    group = HEADS // KV_HEADS
    top[...] = jnp.full(top.shape, NEG, F32)
    total[...] = jnp.zeros(total.shape, F32)
    gathered[...] = jnp.zeros(gathered.shape, F32)

    def chunk(index, carry):
        start = pl.multiple_of(index * count, count)
        rows = pl.ds(start, count)
        mask = block_mask(first, start, segments, count)
        keys, values = head_columns(pairs, rows)
        values = [value.T for value in values]
        before = top[...]
        scores = []
        for head in range(HEADS):
            score = dot_lanes(keys[head // group], queries[:, head * HEAD : (head + 1) * HEAD])
            scores.append(jnp.where(mask, score, NEG))
        now = jnp.maximum(
            before, jnp.concatenate([jnp.max(score, 0, keepdims=True) for score in scores], 0)
        )
        fade = jnp.exp(before - now)
        weights = [jnp.exp(score - now[head : head + 1]) for head, score in enumerate(scores)]
        sums = jnp.concatenate([jnp.sum(weight, 0, keepdims=True) for weight in weights], 0)
        top[...] = now
        total[...] = total[...] * fade + sums
        for head in range(HEADS):
            span = slice(head * HEAD, (head + 1) * HEAD)
            gathered[span] = gathered[span] * fade[head : head + 1] + dot(
                values[head // group], weights[head].astype(BF16)
            )
        return carry

    lax.fori_loop(0, first // count + 1, chunk, 0)
    spread[...] = top[...] + jnp.log(total[...])
    for head in range(HEADS):
        span = slice(head * HEAD, (head + 1) * HEAD)
        exact[span] = gathered[span] / total[head : head + 1]
    for chunk_at in range(HEADS * HEAD // LANES):
        low[:, lanes_of(chunk_at)] = exact[lanes_of(chunk_at)].T.astype(BF16)


def attend_back_kernel(
    xs, position, queries, pairs, slope, exact, spread, segments, cosine, sine,
    query_low, pair_slope, turned_slope, delta, query_slope,
):
    count = queries.shape[0]
    length = pairs.shape[0]
    first = position[0] * count
    group = HEADS // KV_HEADS
    for chunk_at in range(HEADS * HEAD // LANES):
        turned_slope[lanes_of(chunk_at)] = slope[:, lanes_of(chunk_at)].astype(F32).T
    for head in range(HEADS):
        span = slice(head * HEAD, (head + 1) * HEAD)
        delta[head : head + 1] = jnp.sum(turned_slope[span] * exact[span], 0, keepdims=True)
    query_slope[...] = jnp.zeros(query_slope.shape, F32)

    def target(index):
        if xs != 2:
            return pl.ds(pl.multiple_of(index * count, count), count)
        far = (index // xs) ^ (position[0] // xs)
        side = lax.rem(index, xs) ^ lax.rem(position[0], xs)
        turn = (far & 1) * 4 + (far >> 1) * 2 + side
        return pl.ds(pl.multiple_of(turn * count, count), count)

    def chunk(index, carry):
        start = pl.multiple_of(index * count, count)
        rows = pl.ds(start, count)
        mask = block_mask(first, start, segments, count)
        into = target(index)
        keys, values = head_columns(pairs, rows)
        asked = [queries[:, head * HEAD : (head + 1) * HEAD] for head in range(HEADS)]
        sloped = [slope[:, head * HEAD : (head + 1) * HEAD] for head in range(HEADS)]
        scores = [dot_lanes(keys[head // group], asked[head]) for head in range(HEADS)]
        dots = [dot_lanes(values[head // group], sloped[head]) for head in range(HEADS)]
        weights, score_slopes = [], []
        for head in range(HEADS):
            row = slice(head, head + 1)
            weight = jnp.exp(jnp.where(mask, scores[head] - spread[row], NEG))
            score_slopes.append((weight * (dots[head] - delta[row])).astype(BF16))
            weights.append(weight.astype(BF16))
        for kv in range(KV_HEADS):
            heads = range(kv * group, (kv + 1) * group)
            value_part = sum(dot(weights[head], sloped[head]) for head in heads)
            key_part = sum(dot(score_slopes[head], asked[head]) for head in heads)
            pair_slope[into, kv * HEAD : (kv + 1) * HEAD] = key_part.astype(BF16)
            pair_slope[into, LANES + kv * HEAD : LANES + (kv + 1) * HEAD] = value_part.astype(BF16)
        keys = [key.T for key in keys]
        for head in range(HEADS):
            span = slice(head * HEAD, (head + 1) * HEAD)
            query_slope[span] = query_slope[span] + dot(keys[head // group], score_slopes[head])
        return carry

    def blank(index, carry):
        pair_slope[target(index), :] = jnp.zeros((count, 2 * LANES), BF16)
        return carry

    live = first // count + 1
    lax.fori_loop(0, live, chunk, 0)
    lax.fori_loop(live, length // count, blank, 0)
    for chunk_at in range(HEADS * HEAD // LANES):
        part = query_slope[lanes_of(chunk_at)].T * HEAD**-0.5
        query_low[:, lanes_of(chunk_at)] = turned(part, cosine[...], -sine[...]).astype(BF16)


def pairs_back_kernel(*refs):
    *summands, cosine, sine, low = refs
    owned = sum(ref[...].astype(F32) for ref in summands)
    low[:, :LANES] = turned(owned[:, :LANES], cosine[...], -sine[...]).astype(BF16)
    low[:, LANES:] = owned[:, LANES:].astype(BF16)


def conv_total(inner, taps, table, marks, chunk):
    span = lanes_of(chunk)
    extended = inner[:, span].astype(F32)
    total = table[ROW_CONV : ROW_CONV + 1, span] + taps[KERNEL - 1 : KERNEL, span] * extended[HALO:]
    shifted = []
    for tap in range(KERNEL - 1):
        moved = pltpu.roll(extended, KERNEL - 1 - tap, 0)[HALO:] * marks[:, tap : tap + 1]
        total = total + taps[tap : tap + 1, span] * moved
        shifted.append(moved)
    return total, shifted + [extended[HALO:]]


def triangle(count, strict=False, upper=False):
    row = lax.broadcasted_iota(jnp.int32, (count, count), 0)
    column = lax.broadcasted_iota(jnp.int32, (count, count), 1)
    if upper:
        row, column = column, row
    return (row > column if strict else row >= column).astype(F32)


def soft(values):
    return jnp.maximum(values, 0.0) + jnp.log1p(jnp.exp(-jnp.abs(values)))


def part_pieces(parts, pair):
    width = WIDTH // parts
    if width % LANES == 0:
        start = pair * LANES % width
        return [(pair * LANES // width, slice(start, start + LANES), slice(0, LANES))]
    pieces = []
    for half in range(2):
        column = pair * LANES + half * SSM_HEAD
        start = column % width
        pieces.append(
            (
                column // width,
                slice(start, start + SSM_HEAD),
                slice(half * SSM_HEAD, (half + 1) * SSM_HEAD),
            )
        )
    return pieces


ROW_CONV, ROW_GAIN, ROW_MIXER, ROW_SKIP, ROW_STEP, ROW_RATE, ROW_FEED = range(7)
MARK_ENTER, MARK_TAIL, MARK_SEGMENT = KERNEL - 1, KERNEL, KERNEL + 1


def mark_rows(position, segments, count):
    first = pl.multiple_of(position * count, LANES)
    here = segments[:, pl.ds(first, count)].astype(F32)
    before = segments[:, pl.ds(pl.multiple_of(jnp.maximum(first - count, 0), LANES), count)]
    before = jnp.where(position > 0, before.astype(F32), -1.0)
    both = jnp.concatenate([before, here], 1)
    rows = []
    for tap in range(KERNEL - 1):
        moved = pltpu.roll(jnp.broadcast_to(both, (8, 2 * count)), KERNEL - 1 - tap, 1)
        rows.append(flag(moved[:1, count:] == here))
    rows.append(flag(here == before[:, count - 1 :]))
    rows.append(flag(here == here[:, count - 1 :]))
    rows.append(here)
    rows += [jnp.zeros((1, count), F32)] * (8 - len(rows))
    return jnp.concatenate(rows, 0)


def hold_part(hold, pair, rows, value):
    for part, lanes, within in part_pieces(hold.shape[0], pair):
        hold[part, rows, lanes] = value[:, within]


def hand_out(hold, at_x, targets):
    for k, target in enumerate(targets):
        target[...] = hold[lax.rem(at_x + k, len(targets))]


def picked(pieces, at_x, pair):
    xs = len(pieces)
    values = []
    for part, lanes, _ in part_pieces(xs, pair):
        value = pieces[0][:, lanes]
        for k in range(1, xs):
            value = jnp.where(lax.rem(at_x - k + xs, xs) == part, pieces[k][:, lanes], value)
        values.append(value)
    return values[0] if len(values) == 1 else jnp.concatenate(values, 1)


def flag(condition):
    return jnp.where(condition, 1.0, 0.0)


def wall_rows(high, middle, low):
    row = lax.broadcasted_iota(jnp.int32, (EXTRA, high.shape[1]), 0)
    return jnp.where(
        row == 0, high, jnp.where(row == 1, middle, jnp.where(row == 2, low, 0.0))
    ).astype(BF16)


def ahead(forward, one, other):
    return one < other if forward else one > other


def mixed(flags, rows, width):
    total = jnp.zeros((1, width), F32)
    for chosen, row in zip(flags, rows):
        total = total + row * chosen
    return jnp.exp(total)


class Endings:
    def __init__(self, segments, count):
        self.segments, self.count = segments, count

    def __getitem__(self, index):
        return self.segments[index * self.count + self.count - 1]


def level_kernel(forward, xs, count, position, segments, *refs):
    pieces = refs[:xs]
    if forward:
        total_out, walls = refs[xs:]
    else:
        walls, total_out = refs[xs:]
    at_z, at_x = position[0] // xs, lax.rem(position[0], xs)
    endings = Endings(segments, count)
    width = pieces[0].shape[1]
    places = [lax.rem(at_x - k + xs, xs) for k in range(xs)]
    if forward:
        rows = []
        for k in range(xs):
            rows.append(jnp.sum(pieces[k][STATE:].astype(F32), 0, keepdims=True))
            walls[k : k + 1] = rows[k]
        walls[xs:] = jnp.zeros((WALLS - xs, width), F32)
        border = endings[at_z * xs + xs - 1]
    else:
        rows = [walls[k : k + 1] for k in range(xs)]
        border = endings[jnp.maximum(at_z * xs - 1, 0)]
    total = jnp.zeros((STATE, width), F32)
    for k in range(xs):
        index = at_z * xs + places[k]
        reached = endings[index if forward else jnp.maximum(index - 1, 0)] == border
        flags = [flag(ahead(forward, places[k], places[m])) for m in range(xs)]
        total = total + pieces[k][:STATE].astype(F32) * (
            mixed(flags, rows, width) * flag(reached)
        )
    total_out[:STATE] = total.astype(BF16)
    if forward:
        whole = sum(rows)
        high = whole.astype(BF16).astype(F32)
        middle = (whole - high).astype(BF16).astype(F32)
        total_out[STATE:] = wall_rows(high, middle, whole - high - middle)


def arrival_kernel(forward, xs, zs, count, position, segments, *refs):
    pieces = refs[:xs]
    totals = refs[xs : xs + zs - 1]
    walls = refs[xs + zs - 1]
    if forward:
        own, *results, level_walls = refs[xs + zs :]
    else:
        level_walls, *results = refs[xs + zs :]
    at_z, at_x = position[0] // xs, lax.rem(position[0], xs)
    endings = Endings(segments, count)
    width = pieces[0].shape[1]
    x_at = [lax.rem(at_x - k + xs, xs) for k in range(xs)]
    z_at = [lax.rem(at_z - k + zs, zs) for k in range(zs)]
    rows = [walls[k : k + 1] for k in range(xs)]
    if forward:
        levels = [jnp.sum(own[STATE:].astype(F32), 0, keepdims=True)]
        for total in totals:
            levels.append(jnp.sum(total[STATE:].astype(F32), 0, keepdims=True))
        for k in range(zs):
            level_walls[k : k + 1] = levels[k]
        level_walls[zs:] = jnp.zeros((WALLS - zs, width), F32)
        border = endings[jnp.maximum(at_z * xs - 1, 0)]
    else:
        levels = [level_walls[k : k + 1] for k in range(zs)]
        border = endings[at_z * xs + xs - 1]
    outside = jnp.zeros((STATE, width), F32)
    for k in range(1, zs):
        far = endings[z_at[k] * xs + xs - 1 if forward else jnp.maximum(z_at[k] * xs - 1, 0)]
        reached = ahead(forward, z_at[k], at_z) & (far == border)
        flags = [
            flag(ahead(forward, z_at[k], z_at[m]) & ahead(forward, z_at[m], at_z))
            for m in range(zs)
        ]
        outside = outside + totals[k - 1][:STATE].astype(F32) * (
            mixed(flags, levels, width) * flag(reached)
        )
    for r in range(xs):
        target = lax.rem(at_x + r, xs)
        index = at_z * xs + target
        edge = endings[jnp.maximum(index - 1, 0) if forward else index]
        flags = [flag(ahead(forward, x_at[m], target)) for m in range(xs)]
        total = outside * (mixed(flags, rows, width) * flag(edge == border))
        for k in range(xs):
            source = at_z * xs + x_at[k]
            far = endings[source if forward else jnp.maximum(source - 1, 0)]
            reached = ahead(forward, x_at[k], target) & (far == edge)
            flags = [
                flag(ahead(forward, x_at[k], x_at[m]) & ahead(forward, x_at[m], target))
                for m in range(xs)
            ]
            total = total + pieces[k][:STATE].astype(F32) * (
                mixed(flags, rows, width) * flag(reached)
            )
        results[r][...] = total.astype(BF16)


def dealt(place, parts):
    return (parts[0],) + tuple(
        place.turn(part, "x", k) for k, part in enumerate(parts[1:], start=1)
    )


def levels_met(place, total):
    return tuple(place.turn(total, "z", k) for k in range(1, place.sizes["z"]))


def level(place, pieces, position, segments, count):
    xs, width = place.sizes["x"], pieces[0].shape[1]
    return local_call(
        functools.partial(level_kernel, True, xs, count),
        [((STATE + EXTRA, width), BF16), ((WALLS, width), F32)],
        (position, segments, *pieces),
        "level",
        smem=(0, 1),
    )


def level_back(place, pieces, walls, position, segments, count):
    xs, width = place.sizes["x"], pieces[0].shape[1]
    return local_call(
        functools.partial(level_kernel, False, xs, count),
        [((STATE, width), BF16)],
        (position, segments, *pieces, walls),
        "level_back",
        smem=(0, 1),
    )[0]


def arrival(place, pieces, totals, walls, total, position, segments, count):
    xs, zs, width = place.sizes["x"], place.sizes["z"], pieces[0].shape[1]
    *results, level_walls = local_call(
        functools.partial(arrival_kernel, True, xs, zs, count),
        [((STATE, width), BF16)] * xs + [((WALLS, width), F32)],
        (position, segments, *pieces, *totals, walls, total),
        "arrival",
        smem=(0, 1),
    )
    return tuple(results), level_walls


def arrival_back(place, pieces, totals, walls, level_walls, position, segments, count):
    xs, zs, width = place.sizes["x"], place.sizes["z"], pieces[0].shape[1]
    return tuple(
        local_call(
            functools.partial(arrival_kernel, False, xs, zs, count),
            [((STATE, width), BF16)] * xs,
            (position, segments, *pieces, *totals, walls, level_walls),
            "arrival_back",
            smem=(0, 1),
        )
    )


def prep_kernel(
    xs, position, halo, normed, table, inner_w, step_w, taps, segments,
    inner, raw, channels, scaled, inflow, readout, steps, logs, logs_turned, marks, marks_turned,
    *refs,
):
    states, (extended, hold) = refs[:xs], refs[xs:]
    count, width = normed.shape
    at_x = lax.rem(position[0], xs)
    marks_turned[...] = mark_rows(position[0], segments, count)
    marks[...] = marks_turned[...].T
    values = halo[...].astype(F32)
    scale = lax.rsqrt(jnp.mean(values * values, -1, keepdims=True) + EPS)
    extended[:HALO] = (values * scale * table[ROW_GAIN : ROW_GAIN + 1, :width]).astype(BF16)
    extended[HALO:] = normed[...]
    raw[...] = jnp.zeros(raw.shape, F32)
    raw[:, :SSM_HEADS] = dot(normed[...], step_w[...])
    for chunk in range(PAIRS + 2):
        span = lanes_of(chunk)
        inner[:, span] = dot(extended[...], inner_w[:, span]).astype(BF16)
    steps[...] = soft(raw[...] + table[ROW_STEP : ROW_STEP + 1, :LANES])
    logs[...] = precise(triangle(count), steps[...] * table[ROW_RATE : ROW_RATE + 1, :LANES])
    logs_turned[...] = logs[...].T
    for chunk, target in ((PAIRS, inflow), (PAIRS + 1, readout)):
        total, _ = conv_total(inner, taps, table, marks, chunk)
        target[...] = (total * jax.nn.sigmoid(total)).astype(BF16)
    ending = logs[count - 1 : count]
    tail = jnp.exp(ending - logs[...]) * marks[:, MARK_TAIL : MARK_TAIL + 1]
    stepped = steps[...]
    for pair in range(PAIRS):
        span = lanes_of(pair)
        total, _ = conv_total(inner, taps, table, marks, pair)
        value = total * jax.nn.sigmoid(total)
        channels[:, span] = value
        value = value * spread_pair(stepped, pair)
        scaled[:, span] = value.astype(BF16)
        weighted = (value * spread_pair(tail, pair)).astype(BF16)
        own = dot_rows(inflow[...], weighted).astype(BF16)
        whole = spread_pair(ending, pair)
        high = whole.astype(BF16).astype(F32)
        middle = (whole - high).astype(BF16).astype(F32)
        wall = wall_rows(high, middle, whole - high - middle)
        hold_part(hold, pair, slice(0, STATE), own)
        hold_part(hold, pair, slice(STATE, STATE + EXTRA), wall)
    hand_out(hold, at_x, states)


def decay_kernel_parts(marks, marks_turned, bias):
    count = marks.shape[0]
    row = lax.broadcasted_iota(jnp.int32, (count, count), 0)
    column = lax.broadcasted_iota(jnp.int32, (count, count), 1)
    span = slice(MARK_SEGMENT, MARK_SEGMENT + 1)
    inside = (marks[:, span] == marks_turned[span]) & (row >= column)
    bias[...] = jnp.where(inside, 0.0, NEG)


IN_STEP = 4


def inner_kernel(logs, logs_turned, marks, marks_turned, inflow, readout, scaled, result, bias, meet):
    count = logs.shape[0]
    step = pl.program_id(0)

    @pl.when(step == 0)
    def _():
        decay_kernel_parts(marks, marks_turned, bias)
        meet[...] = dot_lanes(readout[...], inflow[...])

    columns = pltpu.roll(logs[...], (LANES - IN_STEP * step) % LANES, 1)
    half = count // 2
    for k in range(IN_STEP):
        across = logs_turned[pl.ds(IN_STEP * step + k, 1), :]
        span = slice(k * SSM_HEAD, (k + 1) * SSM_HEAD)
        for top, width in ((0, half), (half, count)):
            rows = slice(top, top + half)
            gap = columns[rows, k : k + 1] - across[:, :width] + bias[rows, :width]
            mixing = (jnp.exp(gap) * meet[rows, :width]).astype(BF16)
            result[rows, span] = dot(mixing, scaled[:width, span])


def inner_back_kernel(
    logs,
    logs_turned,
    marks,
    marks_turned,
    inflow,
    readout,
    scaled,
    slope,
    scaled_slope,
    inflow_slope,
    readout_slope,
    bias,
    meet,
    meet_slope,
):
    count = logs.shape[0]
    step = pl.program_id(0)

    @pl.when(step == 0)
    def _():
        decay_kernel_parts(marks, marks_turned, bias)
        meet[...] = dot_lanes(readout[...], inflow[...])
        meet_slope[...] = jnp.zeros(meet_slope.shape, F32)

    columns = pltpu.roll(logs[...], (LANES - IN_STEP * step) % LANES, 1)
    half = count // 2
    for top, width in ((0, half), (half, count)):
        rows = slice(top, top + half)
        gathered = jnp.zeros((half, width), F32)
        for k in range(IN_STEP):
            across = logs_turned[pl.ds(IN_STEP * step + k, 1), :]
            span = slice(k * SSM_HEAD, (k + 1) * SSM_HEAD)
            gap = columns[rows, k : k + 1] - across[:, :width] + bias[rows, :width]
            decay = jnp.exp(gap)
            mixing = (decay * meet[rows, :width]).astype(BF16)
            gathered = gathered + decay * dot_lanes(slope[rows, span], scaled[:width, span])
            part = dot_rows(mixing, slope[rows, span])
            if top:
                scaled_slope[:half, span] = scaled_slope[:half, span] + part[:half]
                scaled_slope[half:, span] = part[half:]
            else:
                scaled_slope[:half, span] = part
        meet_slope[rows, :width] = meet_slope[rows, :width] + gathered

    @pl.when(step == SSM_HEADS // IN_STEP - 1)
    def _():
        low = meet_slope[...].astype(BF16)
        inflow_slope[...] = dot_rows(low, readout[...])
        readout_slope[...] = dot(low, inflow[...])


def inner_call(kernel, fixed, moving, outs, fixed_outs, name, scratch):
    count = fixed[0].shape[0]
    steps = SSM_HEADS // IN_STEP
    width = IN_STEP * SSM_HEAD
    held = [pl.BlockSpec(a.shape, lambda j: (0, 0)) for a in fixed]
    passing = pl.BlockSpec((count, width), lambda j: (0, j))
    return pl.pallas_call(
        kernel,
        grid=(steps,),
        in_specs=held + [passing] * len(moving),
        out_specs=[passing] * len(outs)
        + [pl.BlockSpec(shape, lambda j: (0, 0)) for shape, _ in fixed_outs],
        out_shape=[jax.ShapeDtypeStruct((count, WIDTH), kind) for kind in outs]
        + [jax.ShapeDtypeStruct(shape, kind) for shape, kind in fixed_outs],
        scratch_shapes=[pltpu.VMEM((count, count), F32)] * scratch,
        compiler_params=pltpu.CompilerParams(vmem_limit_bytes=40 * 1024 * 1024),
        cost_estimate=pl.CostEstimate(flops=0, bytes_accessed=0, transcendentals=0),
        name=name,
    )(*fixed, *moving)


def entering_kernel(
    xs, position, inner_part, readout, logs, marks, channels, gating, table, *refs
):
    pieces, (tail, scanned, entering, gated) = refs[:xs], refs[xs:]
    at_x = lax.rem(position[0], xs)
    count = logs.shape[0]
    enter = jnp.exp(logs[...]) * marks[:, MARK_ENTER : MARK_ENTER + 1]
    square = jnp.zeros((count, 1), F32)
    for pair in range(PAIRS):
        span = lanes_of(pair)
        entered = picked(pieces, at_x, pair)
        entering[:, span] = entered
        full = inner_part[:, span] + dot(readout[...], entered) * spread_pair(enter, pair)
        scanned[:, span] = full
        gate = gating[:, span]
        skip = table[ROW_SKIP : ROW_SKIP + 1, span]
        full = (full + skip * channels[:, span]) * (gate * jax.nn.sigmoid(gate))
        gated[:, span] = full
        square = square + jnp.sum(full * full, -1, keepdims=True)
    scale = lax.rsqrt(square / WIDTH + EPS)
    for pair in range(PAIRS):
        span = lanes_of(pair)
        gain = table[ROW_MIXER : ROW_MIXER + 1, span]
        tail[:, span] = (gated[:, span] * scale * gain).astype(BF16)


def tail_back_kernel(
    xs, position, slope, scanned, channels, gating, table, logs, marks, readout,
    scanned_slope, gating_slope, sums, *refs,
):
    states, (gated, hold) = refs[:xs], refs[xs:]
    at_x = lax.rem(position[0], xs)
    count = logs.shape[0]
    enter = jnp.exp(logs[...]) * marks[:, MARK_ENTER : MARK_ENTER + 1]
    square = jnp.zeros((count, 1), F32)
    cross = jnp.zeros((count, 1), F32)
    for pair in range(PAIRS):
        span = lanes_of(pair)
        gate = gating[:, span]
        full = scanned[:, span] + table[ROW_SKIP : ROW_SKIP + 1, span] * channels[:, span]
        full = full * (gate * jax.nn.sigmoid(gate))
        gated[:, span] = full
        gain = table[ROW_MIXER : ROW_MIXER + 1, span]
        square = square + jnp.sum(full * full, -1, keepdims=True)
        cross = cross + jnp.sum(full * slope[:, span] * gain, -1, keepdims=True)
    scale = lax.rsqrt(square / WIDTH + EPS)
    cross = cross / WIDTH * scale * scale * scale
    for pair in range(PAIRS):
        span = lanes_of(pair)
        gate = gating[:, span]
        sigmoid = jax.nn.sigmoid(gate)
        back = slope[:, span]
        value = gated[:, span]
        sums[0:1, span] = jnp.sum(back * value * scale, 0, keepdims=True)
        back = back * table[ROW_MIXER : ROW_MIXER + 1, span] * scale - value * cross
        held = channels[:, span]
        full = scanned[:, span] + table[ROW_SKIP : ROW_SKIP + 1, span] * held
        gating_slope[:, span] = (
            back * full * sigmoid * (1.0 + gate * (1.0 - sigmoid))
        ).astype(BF16)
        back = back * (gate * sigmoid)
        sums[1:2, span] = jnp.sum(back * held, 0, keepdims=True)
        scanned_slope[:, span] = back.astype(BF16)
        weighted = (back * spread_pair(enter, pair)).astype(BF16)
        own = dot_rows(readout[...], weighted).astype(BF16)
        hold_part(hold, pair, slice(0, STATE), own)
    hand_out(hold, at_x, states)
    sums[2:8] = jnp.zeros((6, WIDTH), F32)


def leaving_kernel(
    xs, position, entering, scanned, scanned_slope, scaled, channels, scaled_slope,
    inflow, readout, inflow_part, readout_part, steps, raw, logs, marks, inner, taps, table, *refs,
):
    pieces, (inner_low, edges, conv_sums, raw_slope, small, conv_slope) = refs[:xs], refs[xs:]
    at_x = lax.rem(position[0], xs)
    rates = table[ROW_RATE : ROW_RATE + 1, :LANES]
    count = logs.shape[0]
    ending = logs[count - 1 : count]
    tail = jnp.exp(ending - logs[...]) * marks[:, MARK_TAIL : MARK_TAIL + 1]
    enter = jnp.exp(logs[...]) * marks[:, MARK_ENTER : MARK_ENTER + 1]
    stepped = steps[...]
    inflow_slope = inflow_part[...]
    readout_slope = readout_part[...]
    inside = jnp.zeros((count, LANES), F32)
    outward = jnp.zeros((count, LANES), F32)
    direct = jnp.zeros((count, LANES), F32)
    through = jnp.zeros((8, LANES), F32)
    for pair in range(PAIRS):
        span = lanes_of(pair)
        low = picked(pieces, at_x, pair)
        entered = entering[:, span]
        back = scanned_slope[:, span]
        lengths = spread_pair(stepped, pair)
        held = channels[:, span]
        short = scaled[:, span].astype(F32)
        tails = spread_pair(tail, pair)
        outer = dot(inflow[...], low) * tails
        within = scaled_slope[:, span]
        both = within + outer
        wide = back.astype(F32)
        inside = inside + head_sum(wide * scanned[:, span] - short * within, pair)
        outward = outward + head_sum(short * outer, pair)
        direct = direct + head_sum(held * both, pair)
        kept = jnp.sum(low.astype(F32) * entered.astype(F32), 0, keepdims=True) * jnp.exp(
            spread_pair(ending, pair)
        )
        through = through + head_sum(jnp.broadcast_to(kept, (8, LANES)), pair)
        skip = table[ROW_SKIP : ROW_SKIP + 1, span]
        conv_slope[:, span] = both * lengths + skip * wide
        inflow_slope = inflow_slope + dot_lanes((short * tails).astype(BF16), low)
        readout_slope = readout_slope + dot_lanes(
            (wide * spread_pair(enter, pair)).astype(BF16), entered
        )
    conv_slope[:, lanes_of(PAIRS)] = inflow_slope
    conv_slope[:, lanes_of(PAIRS + 1)] = readout_slope
    enter_last = marks[count - 1 :, MARK_ENTER : MARK_ENTER + 1]
    along = (
        precise(triangle(count, upper=True), inside)
        + precise(triangle(count, strict=True), outward)
        + through[:1] * enter_last
    )
    step_slope = direct + rates * along
    step_slope = step_slope * jax.nn.sigmoid(raw[...] + table[ROW_STEP : ROW_STEP + 1, :LANES])
    raw_slope[...] = step_slope.astype(BF16)
    small[0:1] = jnp.sum(step_slope, 0, keepdims=True)
    small[1:2] = rates * jnp.sum(stepped * along, 0, keepdims=True)
    small[2:8] = jnp.zeros((6, LANES), F32)
    blank = jnp.zeros((HALO, LANES), F32)
    for chunk in range(PAIRS + 2):
        span = lanes_of(chunk)
        total, shifted = conv_total(inner, taps, table, marks, chunk)
        slope = conv_slope[:, span] * silu_slope(total)
        spread = jnp.concatenate([blank, slope * taps[KERNEL - 1 : KERNEL, span]], 0)
        for tap in range(KERNEL - 1):
            part = slope * taps[tap : tap + 1, span] * marks[:, tap : tap + 1]
            part = jnp.concatenate([blank, part], 0)
            spread = spread + pltpu.roll(part, HALO + count - (KERNEL - 1 - tap), 0)
        for tap in range(KERNEL):
            conv_sums[tap : tap + 1, span] = jnp.sum(slope * shifted[tap], 0, keepdims=True)
        conv_sums[KERNEL : KERNEL + 1, span] = jnp.sum(slope, 0, keepdims=True)
        conv_sums[KERNEL + 1 :, span] = jnp.zeros((8 - KERNEL - 1, LANES), F32)
        inner_low[:, span] = spread[HALO:].astype(BF16)
        edges[:HALO, span] = spread[:HALO]
        edges[HALO:, span] = spread[count:]


PACK_ROWS = 48


def finish_kernel(
    normed_slope, low_input, table, mixed_slope, raw_slope, normed, tail_sums, conv_sums, small, feed,
    input_gradient, packed,
):
    values = low_input[...].astype(F32)
    width = values.shape[1]
    scale = lax.rsqrt(jnp.mean(values * values, -1, keepdims=True) + EPS)
    slope = normed_slope[...]
    packed[SSM_HEADS : SSM_HEADS + 1] = jnp.sum(slope * values * scale, 0, keepdims=True)
    slope = slope * table[ROW_GAIN : ROW_GAIN + 1, :width]
    cross = jnp.mean(slope * values, -1, keepdims=True) * scale * scale * scale
    input_gradient[...] = mixed_slope[...] + slope * scale - values * cross
    packed[:SSM_HEADS] = dot_rows(raw_slope[...], normed[...])[:SSM_HEADS]
    packed[SSM_HEADS + 1 : SSM_HEADS + 2] = feed[...]
    packed[SSM_HEADS + 2 :] = jnp.zeros((PACK_ROWS - SSM_HEADS - 2, width), F32)
    row = SSM_HEADS + 2
    for source, rows in ((tail_sums, 2), (small, 2), (conv_sums, KERNEL + 1)):
        for index in range(rows):
            for start in range(0, source.shape[1], width):
                stop = min(start + width, source.shape[1])
                packed[row : row + 1, : stop - start] = source[index : index + 1, start:stop]
                row += 1


def unpacked(packed, widths):
    row = SSM_HEADS + 2
    size = packed.shape[1]
    vectors = []
    for width in widths:
        rows = -(-width // size)
        vectors.append(packed[row : row + rows].reshape(-1)[:width])
        row += rows
    return vectors


def all_sum(place, shard, axes):
    for axis in axes:
        bit = 1
        while bit < place.sizes[axis]:
            low = shard.astype(BF16)
            shard = low.astype(F32) + place.swap(low, axis, bit).astype(F32)
            bit *= 2
    return shard


def joint_kernel(xs, ys, widths, left, left_sib, right, right_sib, *outs):
    rows = left.shape[0] // len(widths)
    part = rows // (xs * ys)
    start = offset = 0
    for section, width in enumerate(widths):
        span = slice(section * rows, (section + 1) * rows)
        half = width // 2
        tile = next(t for t in (512, 384, 256, 128) if half % t == 0)
        for first in range(2):
            targets = outs[xs:] if first else outs[:xs]
            for column in range(0, half, tile):
                source = slice(start + first * half + column, start + first * half + column + tile)
                total = dot(left[span], right[:, source]) + dot(left_sib[span], right_sib[:, source])
                total = total.astype(BF16)
                into = slice(offset + column, offset + column + tile)
                for x in range(xs):
                    for y in range(ys):
                        piece = total[(x * ys + y) * part : (x * ys + y + 1) * part]
                        if first:
                            targets[y][x * part : (x + 1) * part, into] = piece
                        else:
                            targets[x][y * part : (y + 1) * part, into] = piece
        start += width
        offset += half


def joint_gradient(place, left, right, left_sib, right_sib, widths):
    sections = len(widths)
    rows, tokens = left.shape[0] // sections, left.shape[1]
    width = sum(widths)
    xs, ys = place.sizes["x"], place.sizes["y"]
    half = width // 2
    shapes = [(rows // xs, half)] * xs + [(rows // ys, half)] * ys
    outs = local_call(
        functools.partial(joint_kernel, xs, ys, widths),
        [(shape, BF16) for shape in shapes],
        (left, left_sib, right, right_sib),
        "joint_gradient",
    )
    return outs[:xs], outs[xs:]


def arranged(order, left):
    return lax.dot_general(
        order, left, (((1,), (1,)), ((), ())), preferred_element_type=jnp.float32
    ).astype(jnp.bfloat16)


def own_half(ordered):
    return ordered[: ordered.shape[0] // CORES]


def other_half(ordered):
    return ordered[ordered.shape[0] // CORES :]


def together(*values):
    return lax.optimization_barrier(values)


def fold_kernel(counts, splits, merged, *refs):
    at = 0
    outs = refs[sum(counts) :]
    for block, count in enumerate(counts):
        total = refs[at][...].astype(F32)
        for ref in refs[at + 1 : at + count]:
            total = total + ref[...].astype(F32)
        at += count
        low = total.astype(BF16)
        rows = low.shape[-2] // splits[block]
        for k in range(splits[block]):
            piece = low[..., k * rows : (k + 1) * rows, :]
            if merged:
                outs[k][block] = piece
            else:
                outs[sum(splits[:block]) + k][...] = piece


def fold(blocks, splits, merged):
    flat = [a for block in blocks for a in block]
    shape = flat[0].shape
    columns = shape[-1]
    tile = max(t for t in range(LANES, 1025, LANES) if columns % t == 0 and t <= columns // 2)

    def spec(full):
        lead = (0,) * (len(full) - 1)
        return pl.BlockSpec(full[:-1] + (tile,), lambda j: lead + (j,))

    if merged:
        outs = [(len(blocks), shape[0] // splits[0], columns)] * splits[0]
    else:
        outs = []
        for block, cuts in zip(blocks, splits):
            full = block[0].shape
            outs += [full[:-2] + (full[-2] // cuts, columns)] * cuts
    return pl.pallas_call(
        functools.partial(fold_kernel, [len(b) for b in blocks], splits, merged),
        grid=(columns // tile,),
        in_specs=[spec(a.shape) for a in flat],
        out_specs=[spec(full) for full in outs],
        out_shape=[jax.ShapeDtypeStruct(full, BF16) for full in outs],
        compiler_params=pltpu.CompilerParams(vmem_limit_bytes=40 * 1024 * 1024),
        cost_estimate=pl.CostEstimate(flops=0, bytes_accessed=0, transcendentals=0),
        name="fold",
    )(*flat)


class Shares:
    ORDERS = (("x", "y"), ("y", "x"))

    def __init__(self, place, lefts, rights):
        self.place = place
        self.widths = [sum(r.shape[1] for r in section) for section in rights]
        self.columns = [[r.shape[1] for r in section] for section in rights]
        flat = [r for section in rights for r in section]
        self.right = jnp.concatenate(flat, 1) if len(flat) > 1 else flat[0]
        self.lefts = lefts

    def to_core(self):
        return self.right

    def go_core(self, sent):
        return self.place.turn(sent, "core", 1)

    def join(self, left_siblings, right_sibling):
        left, sibling = (
            (pieces[0] if len(pieces) == 1 else jnp.concatenate(pieces, 0))
            for pieces in ([own_half(left) for left in self.lefts], left_siblings)
        )
        self.pieces = joint_gradient(
            self.place, left, self.right, sibling, right_sibling, self.widths
        )
        return tuple(tuple(pieces[1:]) for pieces in self.pieces)

    def go(self, sent, stage):
        return tuple(
            tuple(self.place.turn(piece, order[stage], k + 1) for k, piece in enumerate(pieces))
            for pieces, order in zip(sent, self.ORDERS)
        )

    def to_second(self, arrived):
        splits = [self.place.sizes[order[1]] for order in self.ORDERS]
        blocks = [(self.pieces[half][0],) + arrived[half] for half in range(2)]
        outs = fold(blocks, splits, False)
        self.kept = (outs[0], outs[splits[0]])
        return tuple(outs[1 : splits[0]]), tuple(outs[splits[0] + 1 :])

    def to_third(self, arrived):
        blocks = [(self.kept[half],) + arrived[half] for half in range(2)]
        self.kept, sent = fold(blocks, (2, 2), True)
        return sent

    def go_third(self, sent):
        return self.place.swap(sent, "z", 1)

    def to_fourth(self, arrived):
        self.kept, sent = fold([(self.kept, arrived)], (2,), False)
        return sent

    def go_fourth(self, sent):
        return self.place.swap(sent, "z", 2)

    def to_owners(self, arrived):
        cuts = self.place.sizes["z"]
        blocks = [(self.kept[half],) + arrived[half] for half in range(2)]
        self.kept, *sent = fold(blocks, (cuts, cuts), True)
        return tuple(sent)

    def go_owners(self, sent):
        return tuple(
            self.place.swap(piece, "z", k // 2 + 2 * (k % 2))
            for k, piece in enumerate(sent, start=1)
        )

    def shares(self, *arrived):
        total = self.kept.astype(F32)
        for piece in arrived:
            total = total + piece.astype(F32)
        shares = []
        offset = 0
        for width, columns in zip(self.widths, self.columns):
            section = jnp.concatenate(
                [total[half, :, offset : offset + width // 2] for half in range(2)], 1
            )
            offset += width // 2
            start = 0
            for w in columns:
                shares.append(section[:, start : start + w])
                start += w
        return shares


class KeyOwners:
    def __init__(self, place, slopes):
        self.place = place
        self.paired = place.sizes["x"] == 2
        self.kept = slopes

    def to_first(self):
        if not self.paired:
            return self.kept
        half = self.kept.shape[0] // 2
        sent = self.kept[half:]
        self.kept = self.kept[:half]
        return sent

    def go(self, sent, stage):
        if not self.paired:
            if stage:
                return sent
            return lax.psum_scatter(sent, "seq", scatter_dimension=0, tiled=True)
        axis, bit = (("z", 1), ("z", 2), ("x", 1))[stage]
        return self.place.swap(sent, axis, bit)

    def to_next(self, arrived):
        if not self.paired:
            return arrived
        total = (self.kept.astype(F32) + arrived.astype(F32)).astype(BF16)
        half = total.shape[0] // 2
        self.kept = total[:half]
        return total[half:]

    def summands(self, arrived):
        return (self.kept, arrived) if self.paired else (arrived,)


def body(
    inputs,
    segments,
    cotangent,
    input_gain,
    query_weight,
    key_weight,
    value_weight,
    attention_weight,
    gating_weight,
    inner_weight,
    step_weight,
    step_bias,
    decay_log,
    skip_scale,
    conv_weight,
    conv_bias,
    mixer_gain,
    mixer_weight,
    feed_gain,
    gate_weight,
    up_weight,
    down_weight,
):
    place = Place()
    xs = place.sizes["x"]
    count, width = inputs.shape[1], inputs.shape[2]
    low_input = inputs[0]
    hidden = low_input.astype(F32)
    slope = cotangent[0]
    seg_row = segments[0]
    length = seg_row.shape[0]
    group, along = lax.axis_index("dp"), lax.axis_index("seq")
    position = along.reshape(1).astype(jnp.int32)
    inner_width = inner_weight.shape[1]
    part_width = WIDTH // xs

    halo = passed_along(low_input[count - HALO :], "seq", 1)
    cosine, sine = turn_tables(along * count, count)
    normed_low, pairs, table = local_call(
        front_kernel,
        [((count, width), BF16), ((count, 2 * LANES), BF16), ((8, inner_width), F32)],
        (
            low_input,
            key_weight,
            value_weight,
            cosine,
            sine,
            conv_bias,
            input_gain,
            mixer_gain,
            skip_scale,
            step_bias,
            decay_log,
        ),
        "front",
    )
    everything = lax.all_gather(pairs, "seq", axis=0, tiled=True)
    (
        inner,
        raw,
        channels,
        scaled,
        inflow,
        readout,
        steps,
        logs,
        logs_turned,
        marks,
        marks_turned,
        *states,
    ) = local_call(
        functools.partial(prep_kernel, xs),
        [
            ((HALO + count, inner_width), BF16),
            ((count, LANES), F32),
            ((count, WIDTH), F32),
            ((count, WIDTH), BF16),
            ((count, STATE), BF16),
            ((count, STATE), BF16),
            ((count, LANES), F32),
            ((count, LANES), F32),
            ((LANES, count), F32),
            ((count, 8), F32),
            ((8, count), F32),
        ]
        + [((STATE + EXTRA, part_width), BF16)] * xs,
        (position, halo, normed_low, table, inner_weight, step_weight, conv_weight, segments),
        "prepare",
        scratch=[
            pltpu.VMEM((HALO + count, width), BF16),
            pltpu.VMEM((xs, STATE + EXTRA, part_width), BF16),
        ],
        smem=(0,),
    )

    states, normed_low, group, along = together(tuple(states), normed_low, group, along)
    pieces = dealt(place, states)
    gating = product(normed_low, gating_weight)
    order = place.share_order(width, group, along)
    ordered = arranged(order, normed_low)
    pieces, gating, normed_low, order, ordered = together(
        pieces, gating, normed_low, order, ordered
    )
    total, walls = level(place, pieces, position, seg_row, count)

    total, normed_low, ordered = together(total, normed_low, ordered)
    totals = levels_met(place, total)
    ordered_sibling = place.turn(other_half(ordered), "core", 1)
    queries, attention_low, exact, spread = local_call(
        attend_kernel,
        [
            ((count, HEADS * HEAD), BF16),
            ((count, HEADS * HEAD), BF16),
            ((HEADS * HEAD, count), F32),
            ((HEADS, count), F32),
        ],
        (position, normed_low, query_weight, cosine, sine, everything, segments),
        "attend",
        scratch=[
            pltpu.VMEM((HEADS, count), F32),
            pltpu.VMEM((HEADS, count), F32),
            pltpu.VMEM((HEADS * HEAD, count), F32),
        ],
        smem=(0,),
    )
    totals, attention_low, ordered_sibling, scaled, slope, order = together(
        totals, attention_low, ordered_sibling, scaled, slope, order
    )
    results, level_walls = arrival(
        place, pieces, totals, walls, total, position, seg_row, count
    )

    results, scaled, attention_low, slope, order = together(
        results, scaled, attention_low, slope, order
    )
    pieces = dealt(place, results)
    fixed = (logs, logs_turned, marks, marks_turned, inflow, readout)
    (inner_part,) = inner_call(inner_kernel, fixed, (scaled,), (F32,), (), "inner", 2)
    attention_branch = product(attention_low, attention_weight)
    ordered_slope = arranged(order, slope)
    pieces, inner_part, attention_branch, ordered_slope = together(
        pieces, inner_part, attention_branch, ordered_slope
    )
    tail_low, scanned, entering = local_call(
        functools.partial(entering_kernel, xs),
        [((count, WIDTH), BF16), ((count, WIDTH), F32), ((STATE, WIDTH), BF16)],
        (position, inner_part, readout, logs, marks, channels, gating, table, *pieces),
        "entering",
        scratch=[pltpu.VMEM((count, WIDTH), F32)],
        smem=(0,),
    )
    mixed_sum = hidden + attention_branch + product(tail_low, mixer_weight)
    feed, feed_back = jax.vjp(norm_rows, mixed_sum, feed_gain)
    feed_low = feed.astype(BF16)
    gate_raw, up_raw = product(feed_low, gate_weight), product(feed_low, up_weight)
    activated_low = gated_unit(gate_raw, up_raw).astype(BF16)

    down = Shares(place, (ordered_slope,), ((activated_low,),))
    sent, slope_half, gate_raw, up_raw, slope, feed_low, order = together(
        down.to_core(), other_half(ordered_slope), gate_raw, up_raw, slope, feed_low, order
    )
    arrived = down.go_core(sent)
    slope_sibling = place.turn(slope_half, "core", 1)
    _, unit_back = jax.vjp(gated_unit, gate_raw, up_raw)
    gate_slope, up_slope = unit_back(product_right(slope, down_weight))
    gate_low, up_low = gate_slope.astype(BF16), up_slope.astype(BF16)
    ordered_feed = arranged(order, feed_low)
    arrived, slope_sibling, gate_low, up_low, ordered_feed = together(
        arrived, slope_sibling, gate_low, up_low, ordered_feed
    )
    sent = down.join([slope_sibling], arrived)

    gate = Shares(place, (ordered_feed,), ((gate_low,),))
    up = Shares(place, (ordered_feed,), ((up_low,),))
    sent, feed_half, gate_low, up_low = together(
        sent, other_half(ordered_feed), gate_low, up_low
    )
    arrived = down.go(sent, 0)
    gate_arrived, up_arrived = gate.go_core(gate_low), up.go_core(up_low)
    feed_sibling = place.turn(feed_half, "core", 1)
    mixed_part, grad_feed_gain = feed_back(
        product_right(gate_low, gate_weight) + product_right(up_low, up_weight)
    )
    mixed_slope = slope.astype(F32) + mixed_part
    branch_low = mixed_slope.astype(BF16)
    scanned_slope, gating_low, tail_sums, *state_slopes = local_call(
        functools.partial(tail_back_kernel, xs),
        [((count, WIDTH), BF16), ((count, WIDTH), BF16), ((8, WIDTH), F32)]
        + [((STATE, part_width), BF16)] * xs,
        (
            position,
            product_right(branch_low, mixer_weight),
            scanned,
            channels,
            gating,
            table,
            logs,
            marks,
            readout,
        ),
        "tail_back",
        scratch=[
            pltpu.VMEM((count, WIDTH), F32),
            pltpu.VMEM((xs, STATE, part_width), BF16),
        ],
        smem=(0,),
    )
    (
        arrived,
        gate_arrived,
        up_arrived,
        feed_sibling,
        state_slopes,
        branch_low,
        scanned_slope,
        gating_low,
        order,
    ) = together(
        arrived,
        gate_arrived,
        up_arrived,
        feed_sibling,
        tuple(state_slopes),
        branch_low,
        scanned_slope,
        gating_low,
        order,
    )

    gate_sent = gate.join([feed_sibling], gate_arrived)
    ordered_branch = arranged(order, branch_low)
    mixers = Shares(place, (ordered_branch, ordered), ((attention_low, tail_low), (gating_low,)))
    state_slopes, gate_sent, mixers_sent, branch_half, arrived, branch_low = together(
        state_slopes,
        gate_sent,
        mixers.to_core(),
        other_half(ordered_branch),
        arrived,
        branch_low,
    )
    state_pieces = dealt(place, state_slopes)
    gate_arrived = gate.go(gate_sent, 0)
    mixers_arrived = mixers.go_core(mixers_sent)
    branch_sibling = place.turn(branch_half, "core", 1)
    attention_slope = product_right(branch_low, attention_weight).astype(BF16)
    down_sent = down.to_second(arrived)
    mixers_sent = mixers.join([branch_sibling, ordered_sibling], mixers_arrived)
    state_pieces, gate_arrived, mixers_sent, down_sent, attention_slope = together(
        state_pieces, gate_arrived, mixers_sent, down_sent, attention_slope
    )
    total = level_back(place, state_pieces, walls, position, seg_row, count)

    total, mixers_sent, attention_slope, up_arrived, feed_sibling, gate_arrived = together(
        total, mixers_sent, attention_slope, up_arrived, feed_sibling, gate_arrived
    )
    totals = levels_met(place, total)
    mixers_arrived = mixers.go(mixers_sent, 0)
    query_low, pair_slope = local_call(
        functools.partial(attend_back_kernel, xs),
        [((count, HEADS * HEAD), BF16), ((length, 2 * LANES), BF16)],
        (
            position,
            queries,
            everything,
            attention_slope,
            exact,
            spread,
            segments,
            cosine,
            sine,
        ),
        "attend_back",
        scratch=[
            pltpu.VMEM((HEADS * HEAD, count), F32),
            pltpu.VMEM((HEADS, count), F32),
            pltpu.VMEM((HEADS * HEAD, count), F32),
        ],
        smem=(0,),
    )
    owners = KeyOwners(place, pair_slope)
    pair_sent = owners.to_first()
    up_sent = up.join([feed_sibling], up_arrived)
    totals, mixers_arrived, pair_sent, up_sent = together(
        totals, mixers_arrived, pair_sent, up_sent
    )
    results = arrival_back(
        place, state_pieces, totals, walls, level_walls, position, seg_row, count
    )

    results, pair_sent, up_sent, mixers_arrived, gate_arrived, scanned_slope = together(
        results, pair_sent, up_sent, mixers_arrived, gate_arrived, scanned_slope
    )
    pieces = dealt(place, results)
    pair_arrived = owners.go(pair_sent, 0)
    up_arrived = up.go(up_sent, 0)
    scaled_slope, inflow_part, readout_part = inner_call(
        inner_back_kernel,
        fixed,
        (scaled, scanned_slope),
        (F32,),
        (((count, STATE), F32), ((count, STATE), F32)),
        "inner_back",
        3,
    )
    mixers_sent = mixers.to_second(mixers_arrived)
    gate_sent = gate.to_second(gate_arrived)
    pieces, pair_arrived, up_arrived, mixers_sent, gate_sent, scaled_slope = together(
        pieces, pair_arrived, up_arrived, mixers_sent, gate_sent, scaled_slope
    )

    pieces, pair_sent, mixers_sent, gate_sent, up_arrived = together(
        pieces, owners.to_next(pair_arrived), mixers_sent, gate_sent, up_arrived
    )
    mixers_arrived = mixers.go(mixers_sent, 1)
    gate_arrived = gate.go(gate_sent, 1)
    pair_arrived = owners.go(pair_sent, 1)
    inner_low, edges, conv_sums, raw_slope, small = local_call(
        functools.partial(leaving_kernel, xs),
        [
            ((count, inner_width), BF16),
            ((2 * HALO, inner_width), F32),
            ((8, inner_width), F32),
            ((count, LANES), BF16),
            ((8, LANES), F32),
        ],
        (
            position,
            entering,
            scanned,
            scanned_slope,
            scaled,
            channels,
            scaled_slope,
            inflow,
            readout,
            inflow_part,
            readout_part,
            steps,
            raw,
            logs,
            marks,
            inner,
            conv_weight,
            table,
            *pieces,
        ),
        "leaving",
        scratch=[pltpu.VMEM((count, inner_width), F32)],
        smem=(0,),
    )
    mixers_arrived, gate_arrived, pair_arrived, inner_low, edges = together(
        mixers_arrived, gate_arrived, pair_arrived, inner_low, edges
    )

    mixers_sent, pair_sent, down_sent, inner_low, edges, up_arrived, gate_arrived = together(
        mixers.to_third(mixers_arrived),
        owners.to_next(pair_arrived),
        down_sent,
        inner_low,
        edges,
        up_arrived,
        gate_arrived,
    )
    returned = passed_along(edges[:HALO], "seq", -1)
    pair_arrived = owners.go(pair_sent, 2)
    down_arrived = down.go(down_sent, 1)
    mixers_arrived = mixers.go_third(mixers_sent)
    up_sent = up.to_second(up_arrived)
    gate_sent = gate.to_third(gate_arrived)
    returned, pair_arrived, down_arrived, mixers_arrived, up_sent, gate_sent = together(
        returned, pair_arrived, down_arrived, mixers_arrived, up_sent, gate_sent
    )
    inner_low = lax.dynamic_update_slice(
        inner_low, (edges[HALO:] + returned).astype(BF16), (count - HALO, 0)
    )
    (pair_low,) = local_call(
        pairs_back_kernel,
        [((count, 2 * LANES), BF16)],
        (*owners.summands(pair_arrived), cosine, sine),
        "pairs_back",
    )

    rest = Shares(place, (ordered,), ((inner_low, query_low, pair_low),))
    (
        rest_sent,
        up_sent,
        mixers_sent,
        gate_sent,
        down_arrived,
        activated_low,
        gating_low,
        query_low,
    ) = together(
        rest.to_core(),
        up_sent,
        mixers.to_fourth(mixers_arrived),
        gate_sent,
        down_arrived,
        activated_low,
        gating_low,
        query_low,
    )
    rest_arrived = rest.go_core(rest_sent)
    up_arrived = up.go(up_sent, 1)
    mixers_arrived = mixers.go_fourth(mixers_sent)
    gate_arrived = gate.go_third(gate_sent)
    down_sent = down.to_third(down_arrived)
    output = (mixed_sum + product(activated_low, down_weight)).astype(BF16)
    normed_slope = product_right(gating_low, gating_weight) + product_right(
        query_low, query_weight
    )
    rest_sent = rest.join([ordered_sibling], rest_arrived)
    rest_sent, up_arrived, mixers_arrived, gate_arrived, down_sent, output, normed_slope = together(
        rest_sent, up_arrived, mixers_arrived, gate_arrived, down_sent, output, normed_slope
    )

    rest_sent, gate_sent, up_sent, down_sent, pair_low, inner_low, normed_slope = together(
        rest_sent,
        gate.to_fourth(gate_arrived),
        up.to_third(up_arrived),
        down_sent,
        pair_low,
        inner_low,
        normed_slope,
    )
    rest_arrived = rest.go(rest_sent, 0)
    gate_arrived = gate.go_fourth(gate_sent)
    up_arrived = up.go_third(up_sent)
    down_arrived = down.go_third(down_sent)
    normed_slope = (
        normed_slope
        + product_right(inner_low, inner_weight)
        + product_right(pair_low, jnp.concatenate([key_weight, value_weight], 1))
        + product_right(raw_slope[:, :SSM_HEADS], step_weight)
    )
    input_gradient, packed = local_call(
        finish_kernel,
        [((count, width), F32), ((PACK_ROWS, width), F32)],
        (
            normed_slope,
            low_input,
            table,
            mixed_slope,
            raw_slope,
            normed_low,
            tail_sums,
            conv_sums,
            small,
            grad_feed_gain[None],
        ),
        "finish",
    )
    share_attention, share_mixer, share_gating = mixers.shares(mixers_arrived)
    share_attention, share_mixer = share_attention.T, share_mixer.T
    rest_arrived, gate_arrived, up_arrived, down_arrived, packed, share_attention, share_mixer = (
        together(
            rest_arrived,
            gate_arrived,
            up_arrived,
            down_arrived,
            packed,
            share_attention,
            share_mixer,
        )
    )

    rest_sent, up_sent, down_sent, gate_arrived, packed = together(
        rest.to_second(rest_arrived),
        up.to_fourth(up_arrived),
        down.to_fourth(down_arrived),
        gate_arrived,
        packed,
    )
    rest_arrived = rest.go(rest_sent, 1)
    up_arrived = up.go_fourth(up_sent)
    down_arrived = down.go_fourth(down_sent)
    packed = all_sum(place, packed, ("core", "x"))
    (share_gate,) = gate.shares(gate_arrived)
    rest_arrived, up_arrived, down_arrived, packed, share_gate = together(
        rest_arrived, up_arrived, down_arrived, packed, share_gate
    )

    rest_sent, up_arrived, down_arrived, packed = together(
        rest.to_owners(rest_arrived), up_arrived, down_arrived, packed
    )
    rest_arrived = rest.go_owners(rest_sent)
    packed = all_sum(place, packed, ("y", "z"))
    (share_up,), (share_down,) = up.shares(up_arrived), down.shares(down_arrived)
    share_down = share_down.T
    share_inner, share_query, share_pair = rest.shares(*rest_arrived)
    step_sum = packed[:SSM_HEADS].T
    gain_sum, feed_gain_sum = packed[SSM_HEADS], packed[SSM_HEADS + 1]
    taps = conv_weight.shape[1]
    mixer_gain_sum, skip_sum, step_bias_sum, decay_sum, *conv_sum = unpacked(
        packed, [WIDTH] * 2 + [LANES] * 2 + [taps] * (KERNEL + 1)
    )
    skip_sum = jnp.sum(skip_sum.reshape(SSM_HEADS, SSM_HEAD), 1)
    return (
        output[None],
        input_gradient[None],
        gain_sum,
        share_query,
        share_pair[:, :LANES],
        share_pair[:, LANES:],
        share_attention,
        share_gating,
        share_inner,
        step_sum,
        step_bias_sum[:SSM_HEADS],
        decay_sum[:SSM_HEADS],
        skip_sum,
        jnp.stack(conv_sum[:KERNEL]),
        conv_sum[KERNEL],
        mixer_gain_sum,
        share_mixer,
        feed_gain_sum,
        share_gate,
        share_up,
        share_down,
    )


def solution(mesh):
    in_specs = (
        P("dp", "seq", None),
        P("dp", None),
        P("dp", "seq", None),
        P(),
        P(),
        P(),
        P(),
        P(),
        P(),
        P(),
        P(),
        P(),
        P(),
        P(),
        P(),
        P(),
        P(),
        P(),
        P(),
        P(),
        P(),
        P(),
    )
    out_specs = (
        P("dp", "seq", None),
        P("dp", "seq", None),
        P(),
        P(("dp", "seq"), None),
        P(("dp", "seq"), None),
        P(("dp", "seq"), None),
        P(None, ("dp", "seq")),
        P(("dp", "seq"), None),
        P(("dp", "seq"), None),
        P(),
        P(),
        P(),
        P(),
        P(),
        P(),
        P(),
        P(None, ("dp", "seq")),
        P(),
        P(("dp", "seq"), None),
        P(("dp", "seq"), None),
        P(None, ("dp", "seq")),
    )
    return jax.shard_map(body, mesh=mesh, in_specs=in_specs, out_specs=out_specs, check_vma=False)
```

```python
import functools
import math

import jax
import jax.numpy as jnp
from jax import lax
from jax.experimental import pallas as pl
from jax.experimental.pallas import tpu as pltpu
from jax.sharding import PartitionSpec as P

HEADS = 8
KV_HEADS = 2
HEAD = 64
SSM_HEADS = 24
SSM_HEAD = 64
STATE = 128
KERNEL = 4


EPS = 1e-05
ROPE_BASE = 100000000000.0
NEG = -1e30
HIGH = lax.Precision.HIGHEST


def passed_along(shard, axis, by):
    peers = lax.axis_size(axis)
    pairs = [(i, i + by) for i in range(peers) if 0 <= i + by < peers]
    return lax.ppermute(shard, axis, pairs)


def product(left, right):
    return jnp.dot(left, right, preferred_element_type=jnp.float32)


def product_left(left, right):
    return lax.dot_general(
        left, right, (((0,), (0,)), ((), ())), preferred_element_type=jnp.float32
    )


def product_right(left, right):
    return lax.dot_general(
        left, right, (((1,), (1,)), ((), ())), preferred_element_type=jnp.float32
    )


def precise(left, right):
    return jnp.dot(left, right, preferred_element_type=jnp.float32, precision=HIGH)


def norm_rows(values, gain):
    return values * lax.rsqrt(jnp.mean(values * values, -1, keepdims=True) + EPS) * gain


def gated_unit(gate, upward):
    return jax.nn.silu(gate) * upward


CORES = 2
DEPTH = 4
LANES = 128


class Place:
    def __init__(self):
        self.dp = lax.axis_size("dp")
        self.seq = lax.axis_size("seq")
        self.sizes = {
            "y": self.dp // CORES,
            "core": CORES,
            "z": DEPTH,
            "x": self.seq // DEPTH,
        }

    def split(self, index):
        dp, seq = index // self.seq, index % self.seq
        return {
            "y": dp // CORES,
            "core": dp % CORES,
            "z": seq // self.sizes["x"],
            "x": seq % self.sizes["x"],
        }

    def join(self, at):
        return (at["y"] * CORES + at["core"]) * self.seq + at["z"] * self.sizes["x"] + at["x"]

    def turn(self, shard, axis, by):
        pairs = []
        for index in range(self.dp * self.seq):
            at = self.split(index)
            at[axis] = (at[axis] + by) % self.sizes[axis]
            pairs.append((index, self.join(at)))
        return lax.ppermute(shard, ("dp", "seq"), pairs)

    def swap(self, shard, axis, bit):
        pairs = []
        for index in range(self.dp * self.seq):
            at = self.split(index)
            at[axis] ^= bit
            pairs.append((index, self.join(at)))
        return lax.ppermute(shard, ("dp", "seq"), pairs)

    def share_order(self, width, group, along):
        sizes, at = self.sizes, self.split(group * self.seq + along)
        rows = width // (self.dp * self.seq)
        k = lax.broadcasted_iota(jnp.int32, (width, 1), 0)
        within = k % rows
        rest = k // rows
        dz = rest % sizes["z"]
        rest = rest // sizes["z"]
        dy = rest % sizes["y"]
        rest = rest // sizes["y"]
        dx = rest % sizes["x"]
        dc = rest // sizes["x"]
        owner = self.join(
            {
                "y": (at["y"] + dy) % sizes["y"],
                "core": (at["core"] + dc) % sizes["core"],
                "z": at["z"] ^ (dz // 2 + 2 * (dz % 2)),
                "x": (at["x"] + dx) % sizes["x"],
            }
        )
        source = owner * rows + within
        columns = lax.broadcasted_iota(jnp.int32, (1, width), 1)
        return (source == columns).astype(jnp.bfloat16)


F32 = jnp.float32
BF16 = jnp.bfloat16
PAIR = 2 * SSM_HEAD
WIDTH = SSM_HEADS * SSM_HEAD
PAIRS = WIDTH // PAIR
HALO = 16
EXTRA = 16
WALLS = 16
VMEM = pl.BlockSpec(memory_space=pltpu.VMEM)
SMEM = pl.BlockSpec(memory_space=pltpu.SMEM)


def room(arrays):
    total = 0
    for a in arrays:
        *lead, last = a.shape if len(a.shape) > 1 else (8, *a.shape)
        total += math.prod(lead) * (-(-last // LANES) * LANES) * jnp.dtype(a.dtype).itemsize
    return total


def local_call(kernel, outs, args, name, scratch=(), smem=(), slack=10, alone=False):
    shapes = [jax.ShapeDtypeStruct(shape, kind) for shape, kind in outs]
    held = [a for i, a in enumerate(args) if i not in smem]
    needed = (56 if alone else slack) * 1024 * 1024
    if not alone:
        needed += room(held) + room(shapes) + room(scratch)
    return pl.pallas_call(
        kernel,
        in_specs=[SMEM if i in smem else VMEM for i in range(len(args))],
        out_specs=[VMEM] * len(shapes),
        out_shape=shapes,
        scratch_shapes=list(scratch),
        compiler_params=pltpu.CompilerParams(vmem_limit_bytes=needed),
        cost_estimate=pl.CostEstimate(flops=0, bytes_accessed=0, transcendentals=0),
        name=name,
    )(*args)


def dot(left, right):
    return jnp.dot(left, right, preferred_element_type=F32)


def dot_rows(left, right):
    return lax.dot_general(left, right, (((0,), (0,)), ((), ())), preferred_element_type=F32)


def dot_lanes(left, right):
    return lax.dot_general(left, right, (((1,), (1,)), ((), ())), preferred_element_type=F32)


def turned(values, cosine, sine):
    lane = lax.broadcasted_iota(jnp.int32, values.shape, 1)
    half = HEAD // 2
    swapped = jnp.where(
        lane % HEAD < half,
        pltpu.roll(values, LANES - half, 1),
        pltpu.roll(values, half, 1),
    )
    return values * cosine + swapped * sine


def turn_tables(first, count):
    lane = jnp.arange(LANES)
    place = (first + jnp.arange(count)).astype(F32)
    half = HEAD // 2
    freq = ROPE_BASE ** (-((lane % half).astype(F32) * 2.0 / HEAD))
    angle = place[:, None] * freq[None, :]
    sign = jnp.where(lane % HEAD < half, -1.0, 1.0)[None, :]
    return jnp.cos(angle), jnp.sin(angle) * sign


def lanes_of(index):
    return slice(index * LANES, (index + 1) * LANES)


def spread_pair(values, pair):
    rows = values.shape[0]
    lane = lax.broadcasted_iota(jnp.int32, (rows, LANES), 1)
    return jnp.where(
        lane < SSM_HEAD, values[:, 2 * pair : 2 * pair + 1], values[:, 2 * pair + 1 : 2 * pair + 2]
    )


def head_lanes(selector):
    head = lax.broadcasted_iota(jnp.int32, (LANES, LANES), 0)
    lane = lax.broadcasted_iota(jnp.int32, (LANES, LANES), 1)
    for pair in range(PAIRS):
        chosen = (lane // SSM_HEAD + 2 * pair == head).astype(F32).astype(BF16)
        selector[:LANES, lanes_of(pair)] = chosen
        selector[LANES:, lanes_of(pair)] = chosen


def halves(values):
    upper = values.astype(BF16)
    return jnp.concatenate([upper, (values - upper.astype(F32)).astype(BF16)], 1)


def split_into(target, span, values):
    upper = values.astype(BF16)
    target[0, :, span] = upper
    target[1, :, span] = (values - upper.astype(F32)).astype(BF16)


def head_sums(parts, selector):
    chosen = selector[:LANES]
    return dot_lanes(parts[0], chosen) + dot_lanes(parts[1], chosen)


def silu_slope(values):
    gate = jax.nn.sigmoid(values)
    return gate * (1.0 + values * (1.0 - gate))


def front_kernel(
    x, key_w, value_w, cosine, sine, conv_bias, input_gain, mixer_gain, skip, step_bias, decay_log,
    normed, pairs, table,
):
    table[...] = jnp.zeros(table.shape, F32)
    for row, source in (
        (ROW_CONV, conv_bias),
        (ROW_GAIN, input_gain),
        (ROW_MIXER, mixer_gain),
        (ROW_STEP, step_bias),
    ):
        table[row : row + 1, : source.shape[0]] = source[...].reshape(1, source.shape[0])
    rates = -jnp.exp(decay_log[...].reshape(1, SSM_HEADS))
    table[ROW_RATE : ROW_RATE + 1, :SSM_HEADS] = rates
    skips = skip[...].reshape(1, SSM_HEADS)
    for pair in range(PAIRS):
        table[ROW_SKIP : ROW_SKIP + 1, lanes_of(pair)] = spread_pair(skips, pair)
    values = x[...].astype(F32)
    scale = lax.rsqrt(jnp.mean(values * values, -1, keepdims=True) + EPS)
    gain = table[ROW_GAIN : ROW_GAIN + 1, : values.shape[1]]
    normed[...] = (values * scale * gain).astype(BF16)
    low = normed[...]
    pairs[:, :LANES] = turned(dot(low, key_w[...]), cosine[...], sine[...]).astype(BF16)
    pairs[:, LANES:] = dot(low, value_w[...]).astype(BF16)


def block_mask(first, start, segments, count):
    def row(at):
        return segments[:, pl.ds(pl.multiple_of(at, LANES), count)].astype(F32)

    place = lax.broadcasted_iota(jnp.int32, (count, count), 0) + start
    reach = lax.broadcasted_iota(jnp.int32, (count, count), 1) + first
    keys = jnp.broadcast_to(row(start), (8, count)).T[:, :1]
    return (keys == row(first)) & (place <= reach)


def key_rows(xs, zs, position, index, count):
    far = position // xs - index // xs
    side = lax.rem(lax.rem(position, xs) - lax.rem(index, xs) + xs, xs)
    return pl.ds(pl.multiple_of((side * zs + far) * count, count), count)


def head_columns(pairs, rows):
    keys = [pairs[rows, kv * HEAD : (kv + 1) * HEAD] for kv in range(KV_HEADS)]
    values = [
        pairs[rows, LANES + kv * HEAD : LANES + (kv + 1) * HEAD] for kv in range(KV_HEADS)
    ]
    return keys, values


def attend_kernel(
    xs, zs, position, normed, query_w, cosine, sine, pairs, segments,
    queries, low, exact, spread, top, total, gathered,
):
    count = queries.shape[0]
    raw = dot(normed[...], query_w[...])
    for chunk_at in range(HEADS * HEAD // LANES):
        part = turned(raw[:, lanes_of(chunk_at)], cosine[...], sine[...]) * HEAD**-0.5
        queries[:, lanes_of(chunk_at)] = part.astype(BF16)
    first = position[0] * count
    group = HEADS // KV_HEADS
    top[...] = jnp.full(top.shape, NEG, F32)
    total[...] = jnp.zeros(total.shape, F32)
    gathered[...] = jnp.zeros(gathered.shape, F32)

    def chunk(index, carry):
        start = pl.multiple_of(index * count, count)
        rows = key_rows(xs, zs, position[0], index, count)
        mask = block_mask(first, start, segments, count)
        keys, values = head_columns(pairs, rows)
        values = [value.T for value in values]
        before = top[...]
        scores = []
        for head in range(HEADS):
            score = dot_lanes(keys[head // group], queries[:, head * HEAD : (head + 1) * HEAD])
            scores.append(jnp.where(mask, score, NEG))
        now = jnp.maximum(
            before, jnp.concatenate([jnp.max(score, 0, keepdims=True) for score in scores], 0)
        )
        fade = jnp.exp(before - now)
        weights = [jnp.exp(score - now[head : head + 1]) for head, score in enumerate(scores)]
        sums = jnp.concatenate([jnp.sum(weight, 0, keepdims=True) for weight in weights], 0)
        top[...] = now
        total[...] = total[...] * fade + sums
        for head in range(HEADS):
            span = slice(head * HEAD, (head + 1) * HEAD)
            gathered[span] = gathered[span] * fade[head : head + 1] + dot(
                values[head // group], weights[head].astype(BF16)
            )
        return carry

    lax.fori_loop(0, first // count + 1, chunk, 0)
    spread[...] = top[...] + jnp.log(total[...])
    for head in range(HEADS):
        span = slice(head * HEAD, (head + 1) * HEAD)
        exact[span] = gathered[span] / total[head : head + 1]
    for chunk_at in range(HEADS * HEAD // LANES):
        low[:, lanes_of(chunk_at)] = exact[lanes_of(chunk_at)].T.astype(BF16)


def attend_back_kernel(
    xs, zs, position, queries, pairs, slope, exact, spread, segments, cosine, sine,
    query_low, pair_slope, turned_slope, delta, query_slope,
):
    count = queries.shape[0]
    length = pairs.shape[0]
    first = position[0] * count
    group = HEADS // KV_HEADS
    for chunk_at in range(HEADS * HEAD // LANES):
        turned_slope[lanes_of(chunk_at)] = slope[:, lanes_of(chunk_at)].astype(F32).T
    for head in range(HEADS):
        span = slice(head * HEAD, (head + 1) * HEAD)
        delta[head : head + 1] = jnp.sum(turned_slope[span] * exact[span], 0, keepdims=True)
    query_slope[...] = jnp.zeros(query_slope.shape, F32)

    def target(index):
        if xs != 2:
            return pl.ds(pl.multiple_of(index * count, count), count)
        far = (index // xs) ^ (position[0] // xs)
        side = lax.rem(index, xs) ^ lax.rem(position[0], xs)
        turn = (far & 1) * 4 + (far >> 1) * 2 + side
        return pl.ds(pl.multiple_of(turn * count, count), count)

    def chunk(index, carry):
        start = pl.multiple_of(index * count, count)
        rows = key_rows(xs, zs, position[0], index, count)
        mask = block_mask(first, start, segments, count)
        into = target(index)
        keys, values = head_columns(pairs, rows)
        asked = [queries[:, head * HEAD : (head + 1) * HEAD] for head in range(HEADS)]
        sloped = [slope[:, head * HEAD : (head + 1) * HEAD] for head in range(HEADS)]
        scores = [dot_lanes(keys[head // group], asked[head]) for head in range(HEADS)]
        dots = [dot_lanes(values[head // group], sloped[head]) for head in range(HEADS)]
        weights, score_slopes = [], []
        for head in range(HEADS):
            row = slice(head, head + 1)
            weight = jnp.exp(jnp.where(mask, scores[head] - spread[row], NEG))
            score_slopes.append((weight * (dots[head] - delta[row])).astype(BF16))
            weights.append(weight.astype(BF16))
        for kv in range(KV_HEADS):
            heads = range(kv * group, (kv + 1) * group)
            value_part = sum(dot(weights[head], sloped[head]) for head in heads)
            key_part = sum(dot(score_slopes[head], asked[head]) for head in heads)
            pair_slope[into, kv * HEAD : (kv + 1) * HEAD] = key_part.astype(BF16)
            pair_slope[into, LANES + kv * HEAD : LANES + (kv + 1) * HEAD] = value_part.astype(BF16)
        keys = [key.T for key in keys]
        for head in range(HEADS):
            span = slice(head * HEAD, (head + 1) * HEAD)
            query_slope[span] = query_slope[span] + dot(keys[head // group], score_slopes[head])
        return carry

    def blank(index, carry):
        pair_slope[target(index), :] = jnp.zeros((count, 2 * LANES), BF16)
        return carry

    live = first // count + 1
    lax.fori_loop(0, live, chunk, 0)
    lax.fori_loop(live, length // count, blank, 0)
    for chunk_at in range(HEADS * HEAD // LANES):
        part = query_slope[lanes_of(chunk_at)].T * HEAD**-0.5
        query_low[:, lanes_of(chunk_at)] = turned(part, cosine[...], -sine[...]).astype(BF16)


def pairs_back_kernel(*refs):
    *summands, cosine, sine, low = refs
    owned = sum(ref[...].astype(F32) for ref in summands)
    low[:, :LANES] = turned(owned[:, :LANES], cosine[...], -sine[...]).astype(BF16)
    low[:, LANES:] = owned[:, LANES:].astype(BF16)


def wide_marks(marks):
    return [
        jnp.broadcast_to(marks[:, tap : tap + 1], (marks.shape[0], LANES))
        for tap in range(KERNEL - 1)
    ]


def conv_total(inner, taps, table, wide, chunk):
    span = lanes_of(chunk)
    extended = inner[:, span].astype(F32)
    total = table[ROW_CONV : ROW_CONV + 1, span] + taps[KERNEL - 1 : KERNEL, span] * extended[HALO:]
    for tap in range(KERNEL - 1):
        moved = pltpu.roll(extended, KERNEL - 1 - tap, 0)[HALO:] * wide[tap]
        total = total + taps[tap : tap + 1, span] * moved
    return total


def triangle(count, strict=False, upper=False):
    row = lax.broadcasted_iota(jnp.int32, (count, count), 0)
    column = lax.broadcasted_iota(jnp.int32, (count, count), 1)
    if upper:
        row, column = column, row
    return (row > column if strict else row >= column).astype(F32)


def soft(values):
    return jnp.maximum(values, 0.0) + jnp.log1p(jnp.exp(-jnp.abs(values)))


def part_pieces(parts, pair):
    width = WIDTH // parts
    if width % LANES == 0:
        start = pair * LANES % width
        return [(pair * LANES // width, slice(start, start + LANES), slice(0, LANES))]
    pieces = []
    for half in range(2):
        column = pair * LANES + half * SSM_HEAD
        start = column % width
        pieces.append(
            (
                column // width,
                slice(start, start + SSM_HEAD),
                slice(half * SSM_HEAD, (half + 1) * SSM_HEAD),
            )
        )
    return pieces


ROW_CONV, ROW_GAIN, ROW_MIXER, ROW_SKIP, ROW_STEP, ROW_RATE, ROW_FEED = range(7)
MARK_ENTER, MARK_TAIL, MARK_SEGMENT = KERNEL - 1, KERNEL, KERNEL + 1


def mark_rows(position, segments, count):
    first = pl.multiple_of(position * count, LANES)
    here = segments[:, pl.ds(first, count)].astype(F32)
    before = segments[:, pl.ds(pl.multiple_of(jnp.maximum(first - count, 0), LANES), count)]
    before = jnp.where(position > 0, before.astype(F32), -1.0)
    both = jnp.concatenate([before, here], 1)
    rows = []
    for tap in range(KERNEL - 1):
        moved = pltpu.roll(jnp.broadcast_to(both, (8, 2 * count)), KERNEL - 1 - tap, 1)
        rows.append(flag(moved[:1, count:] == here))
    rows.append(flag(here == before[:, count - 1 :]))
    rows.append(flag(here == here[:, count - 1 :]))
    rows.append(here)
    rows += [jnp.zeros((1, count), F32)] * (8 - len(rows))
    return jnp.concatenate(rows, 0)


def hold_part(hold, pair, rows, value):
    for part, lanes, within in part_pieces(hold.shape[0], pair):
        hold[part, rows, lanes] = value[:, within]


def hold_all(hold, rows, values):
    width = hold.shape[2]
    for part in range(hold.shape[0]):
        hold[part, rows] = values[:, part * width : (part + 1) * width]


def hand_out(hold, at_x, targets):
    for k, target in enumerate(targets):
        target[...] = hold[lax.rem(at_x + k, len(targets))]


def picked(pieces, at_x, pair):
    xs = len(pieces)
    values = []
    for part, lanes, _ in part_pieces(xs, pair):
        value = pieces[0][:, lanes]
        for k in range(1, xs):
            value = jnp.where(lax.rem(at_x - k + xs, xs) == part, pieces[k][:, lanes], value)
        values.append(value)
    return values[0] if len(values) == 1 else jnp.concatenate(values, 1)


def flag(condition):
    return jnp.where(condition, 1.0, 0.0)


def wall_rows(high, middle, low):
    row = lax.broadcasted_iota(jnp.int32, (EXTRA, high.shape[1]), 0)
    return jnp.where(
        row == 0, high, jnp.where(row == 1, middle, jnp.where(row == 2, low, 0.0))
    ).astype(BF16)


def ahead(forward, one, other):
    return one < other if forward else one > other


def mixed(flags, rows, width):
    total = jnp.zeros((1, width), F32)
    for chosen, row in zip(flags, rows):
        total = total + row * chosen
    return jnp.exp(total)


class Endings:
    def __init__(self, segments, count):
        self.segments, self.count = segments, count

    def __getitem__(self, index):
        return self.segments[index * self.count + self.count - 1]


def level_kernel(forward, xs, count, position, segments, *refs):
    pieces = refs[:xs]
    if forward:
        total_out, walls = refs[xs:]
    else:
        walls, total_out = refs[xs:]
    at_z, at_x = position[0] // xs, lax.rem(position[0], xs)
    endings = Endings(segments, count)
    width = pieces[0].shape[1]
    places = [lax.rem(at_x - k + xs, xs) for k in range(xs)]
    if forward:
        rows = []
        for k in range(xs):
            rows.append(jnp.sum(pieces[k][STATE:].astype(F32), 0, keepdims=True))
            walls[k : k + 1] = rows[k]
        walls[xs:] = jnp.zeros((WALLS - xs, width), F32)
        border = endings[at_z * xs + xs - 1]
    else:
        rows = [walls[k : k + 1] for k in range(xs)]
        border = endings[jnp.maximum(at_z * xs - 1, 0)]
    total = jnp.zeros((STATE, width), F32)
    for k in range(xs):
        index = at_z * xs + places[k]
        reached = endings[index if forward else jnp.maximum(index - 1, 0)] == border
        flags = [flag(ahead(forward, places[k], places[m])) for m in range(xs)]
        total = total + pieces[k][:STATE].astype(F32) * (
            mixed(flags, rows, width) * flag(reached)
        )
    total_out[:STATE] = total.astype(BF16)
    if forward:
        whole = sum(rows)
        high = whole.astype(BF16).astype(F32)
        middle = (whole - high).astype(BF16).astype(F32)
        total_out[STATE:] = wall_rows(high, middle, whole - high - middle)


def arrival_kernel(forward, xs, zs, count, position, segments, *refs):
    pieces = refs[:xs]
    totals = refs[xs : xs + zs - 1]
    walls = refs[xs + zs - 1]
    if forward:
        own, *results, level_walls = refs[xs + zs :]
    else:
        level_walls, *results = refs[xs + zs :]
    at_z, at_x = position[0] // xs, lax.rem(position[0], xs)
    endings = Endings(segments, count)
    width = pieces[0].shape[1]
    x_at = [lax.rem(at_x - k + xs, xs) for k in range(xs)]
    z_at = [lax.rem(at_z - k + zs, zs) for k in range(zs)]
    rows = [walls[k : k + 1] for k in range(xs)]
    if forward:
        levels = [jnp.sum(own[STATE:].astype(F32), 0, keepdims=True)]
        for total in totals:
            levels.append(jnp.sum(total[STATE:].astype(F32), 0, keepdims=True))
        for k in range(zs):
            level_walls[k : k + 1] = levels[k]
        level_walls[zs:] = jnp.zeros((WALLS - zs, width), F32)
        border = endings[jnp.maximum(at_z * xs - 1, 0)]
    else:
        levels = [level_walls[k : k + 1] for k in range(zs)]
        border = endings[at_z * xs + xs - 1]
    outside = jnp.zeros((STATE, width), F32)
    for k in range(1, zs):
        far = endings[z_at[k] * xs + xs - 1 if forward else jnp.maximum(z_at[k] * xs - 1, 0)]
        reached = ahead(forward, z_at[k], at_z) & (far == border)
        flags = [
            flag(ahead(forward, z_at[k], z_at[m]) & ahead(forward, z_at[m], at_z))
            for m in range(zs)
        ]
        outside = outside + totals[k - 1][:STATE].astype(F32) * (
            mixed(flags, levels, width) * flag(reached)
        )
    for r in range(xs):
        target = lax.rem(at_x + r, xs)
        index = at_z * xs + target
        edge = endings[jnp.maximum(index - 1, 0) if forward else index]
        flags = [flag(ahead(forward, x_at[m], target)) for m in range(xs)]
        total = outside * (mixed(flags, rows, width) * flag(edge == border))
        for k in range(xs):
            source = at_z * xs + x_at[k]
            far = endings[source if forward else jnp.maximum(source - 1, 0)]
            reached = ahead(forward, x_at[k], target) & (far == edge)
            flags = [
                flag(ahead(forward, x_at[k], x_at[m]) & ahead(forward, x_at[m], target))
                for m in range(xs)
            ]
            total = total + pieces[k][:STATE].astype(F32) * (
                mixed(flags, rows, width) * flag(reached)
            )
        results[r][...] = total.astype(BF16)


def dealt(place, parts):
    return (parts[0],) + tuple(
        place.turn(part, "x", k) for k, part in enumerate(parts[1:], start=1)
    )


def levels_met(place, total):
    return tuple(place.turn(total, "z", k) for k in range(1, place.sizes["z"]))


def level(place, pieces, position, segments, count):
    xs, width = place.sizes["x"], pieces[0].shape[1]
    return local_call(
        functools.partial(level_kernel, True, xs, count),
        [((STATE + EXTRA, width), BF16), ((WALLS, width), F32)],
        (position, segments, *pieces),
        "level",
        smem=(0, 1),
    )


def level_back(place, pieces, walls, position, segments, count):
    xs, width = place.sizes["x"], pieces[0].shape[1]
    return local_call(
        functools.partial(level_kernel, False, xs, count),
        [((STATE, width), BF16)],
        (position, segments, *pieces, walls),
        "level_back",
        smem=(0, 1),
    )[0]


def arrival(place, pieces, totals, walls, total, position, segments, count):
    xs, zs, width = place.sizes["x"], place.sizes["z"], pieces[0].shape[1]
    *results, level_walls = local_call(
        functools.partial(arrival_kernel, True, xs, zs, count),
        [((STATE, width), BF16)] * xs + [((WALLS, width), F32)],
        (position, segments, *pieces, *totals, walls, total),
        "arrival",
        smem=(0, 1),
    )
    return tuple(results), level_walls


def arrival_back(place, pieces, totals, walls, level_walls, position, segments, count):
    xs, zs, width = place.sizes["x"], place.sizes["z"], pieces[0].shape[1]
    return tuple(
        local_call(
            functools.partial(arrival_kernel, False, xs, zs, count),
            [((STATE, width), BF16)] * xs,
            (position, segments, *pieces, *totals, walls, level_walls),
            "arrival_back",
            smem=(0, 1),
        )
    )


def prep_kernel(
    xs, position, halo, normed, table, inner_w, step_w, taps, segments,
    inner, raw, channels, scaled, inflow, readout, steps, logs, logs_turned, marks, marks_turned,
    factor, *refs,
):
    states, (extended, hold, selector, lengths, tails, weighted) = refs[:xs], refs[xs:]
    count, width = normed.shape
    at_x = lax.rem(position[0], xs)
    marks_turned[...] = mark_rows(position[0], segments, count)
    marks[...] = marks_turned[...].T
    values = halo[...].astype(F32)
    scale = lax.rsqrt(jnp.mean(values * values, -1, keepdims=True) + EPS)
    extended[:HALO] = (values * scale * table[ROW_GAIN : ROW_GAIN + 1, :width]).astype(BF16)
    extended[HALO:] = normed[...]
    raw[...] = jnp.zeros(raw.shape, F32)
    raw[:, :SSM_HEADS] = dot(normed[...], step_w[...])
    head_lanes(selector)
    chunks = range(PAIRS + 2)
    for chunk in reversed(chunks):
        span = lanes_of(chunk)
        inner[:, span] = dot(extended[...], inner_w[:, span]).astype(BF16)
    steps[...] = soft(raw[...] + table[ROW_STEP : ROW_STEP + 1, :LANES])
    logs[...] = precise(triangle(count), steps[...] * table[ROW_RATE : ROW_RATE + 1, :LANES])
    logs_turned[...] = logs[...].T
    ending = logs[count - 1 : count]
    tail = jnp.exp(ending - logs[...]) * marks[:, MARK_TAIL : MARK_TAIL + 1]
    lengths[...] = dot(halves(steps[...]), selector[...])
    tails[...] = dot(halves(tail), selector[...])
    wide = wide_marks(marks)
    for chunk in reversed(chunks):
        span = lanes_of(chunk)
        total = conv_total(inner, taps, table, wide, chunk)
        gate = jax.nn.sigmoid(total)
        factor[:, span] = (gate * (1.0 + total * (1.0 - gate))).astype(BF16)
        value = total * gate
        if chunk == PAIRS + 1:
            readout[...] = value.astype(BF16)
        elif chunk == PAIRS:
            inflow[...] = value.astype(BF16)
        else:
            channels[:, span] = value
            value = value * lengths[:, span]
            scaled[:, span] = value.astype(BF16)
            weighted[:, span] = (value * tails[:, span]).astype(BF16)
    hold_all(hold, slice(0, STATE), dot(inflow[...].T, weighted[...]).astype(BF16))
    for pair in range(PAIRS):
        whole = spread_pair(ending, pair)
        high = whole.astype(BF16).astype(F32)
        middle = (whole - high).astype(BF16).astype(F32)
        wall = wall_rows(high, middle, whole - high - middle)
        hold_part(hold, pair, slice(STATE, STATE + EXTRA), wall)
    hand_out(hold, at_x, states)


def decay_kernel_parts(marks, marks_turned, bias):
    count = marks.shape[0]
    row = lax.broadcasted_iota(jnp.int32, (count, count), 0)
    column = lax.broadcasted_iota(jnp.int32, (count, count), 1)
    span = slice(MARK_SEGMENT, MARK_SEGMENT + 1)
    inside = (marks[:, span] == marks_turned[span]) & (row >= column)
    bias[...] = jnp.where(inside, 0.0, NEG)


IN_STEP = 4


def inner_kernel(logs, logs_turned, marks, marks_turned, inflow, readout, scaled, result, bias, meet):
    count = logs.shape[0]
    step = pl.program_id(0)

    @pl.when(step == 0)
    def _():
        decay_kernel_parts(marks, marks_turned, bias)
        meet[...] = dot_lanes(readout[...], inflow[...])

    columns = pltpu.roll(logs[...], (LANES - IN_STEP * step) % LANES, 1)
    half = count // 2
    for k in range(IN_STEP):
        across = logs_turned[pl.ds(IN_STEP * step + k, 1), :]
        span = slice(k * SSM_HEAD, (k + 1) * SSM_HEAD)
        for top, width in ((0, half), (half, count)):
            rows = slice(top, top + half)
            gap = columns[rows, k : k + 1] - across[:, :width] + bias[rows, :width]
            mixing = (jnp.exp(gap) * meet[rows, :width]).astype(BF16)
            result[rows, span] = dot(mixing, scaled[:width, span])


def inner_back_kernel(
    logs,
    logs_turned,
    marks,
    marks_turned,
    inflow,
    readout,
    scaled,
    slope,
    scaled_slope,
    inflow_slope,
    readout_slope,
    bias,
    meet,
    meet_slope,
):
    count = logs.shape[0]
    step = pl.program_id(0)

    @pl.when(step == 0)
    def _():
        decay_kernel_parts(marks, marks_turned, bias)
        meet[...] = dot_lanes(readout[...], inflow[...])
        meet_slope[...] = jnp.zeros(meet_slope.shape, F32)

    columns = pltpu.roll(logs[...], (LANES - IN_STEP * step) % LANES, 1)
    half = count // 2
    for top, width in ((0, half), (half, count)):
        rows = slice(top, top + half)
        gathered = jnp.zeros((half, width), F32)
        for k in range(IN_STEP):
            across = logs_turned[pl.ds(IN_STEP * step + k, 1), :]
            span = slice(k * SSM_HEAD, (k + 1) * SSM_HEAD)
            gap = columns[rows, k : k + 1] - across[:, :width] + bias[rows, :width]
            decay = jnp.exp(gap)
            mixing = (decay * meet[rows, :width]).astype(BF16)
            gathered = gathered + decay * dot_lanes(slope[rows, span], scaled[:width, span])
            part = dot_rows(mixing, slope[rows, span])
            if top:
                scaled_slope[:half, span] = scaled_slope[:half, span] + part[:half]
                scaled_slope[half:, span] = part[half:]
            else:
                scaled_slope[:half, span] = part
        meet_slope[rows, :width] = meet_slope[rows, :width] + gathered

    @pl.when(step == SSM_HEADS // IN_STEP - 1)
    def _():
        low = meet_slope[...].astype(BF16)
        inflow_slope[...] = dot_rows(low, readout[...])
        readout_slope[...] = dot(low, inflow[...])


def inner_call(kernel, fixed, moving, outs, fixed_outs, name, scratch):
    count = fixed[0].shape[0]
    steps = SSM_HEADS // IN_STEP
    width = IN_STEP * SSM_HEAD
    held = [pl.BlockSpec(a.shape, lambda j: (0, 0)) for a in fixed]
    passing = pl.BlockSpec((count, width), lambda j: (0, j))
    return pl.pallas_call(
        kernel,
        grid=(steps,),
        in_specs=held + [passing] * len(moving),
        out_specs=[passing] * len(outs)
        + [pl.BlockSpec(shape, lambda j: (0, 0)) for shape, _ in fixed_outs],
        out_shape=[jax.ShapeDtypeStruct((count, WIDTH), kind) for kind in outs]
        + [jax.ShapeDtypeStruct(shape, kind) for shape, kind in fixed_outs],
        scratch_shapes=[pltpu.VMEM((count, count), F32)] * scratch,
        compiler_params=pltpu.CompilerParams(vmem_limit_bytes=16 * 1024 * 1024),
        cost_estimate=pl.CostEstimate(flops=0, bytes_accessed=0, transcendentals=0),
        name=name,
    )(*fixed, *moving)


def entering_kernel(
    xs, position, inner_part, readout, logs, marks, channels, gating, table, *refs
):
    pieces, (tail, scanned, entering, gated, selector, wide) = refs[:xs], refs[xs:]
    at_x = lax.rem(position[0], xs)
    count = logs.shape[0]
    enter = halves(jnp.exp(logs[...]) * marks[:, MARK_ENTER : MARK_ENTER + 1])
    head_lanes(selector)
    for pair in range(PAIRS):
        entering[:, lanes_of(pair)] = picked(pieces, at_x, pair)
    wide[...] = dot(enter, selector[...])
    gated[...] = dot(readout[...], entering[...])
    square = jnp.zeros((count, LANES), F32)
    for pair in range(PAIRS):
        span = lanes_of(pair)
        full = inner_part[:, span] + gated[:, span] * wide[:, span]
        scanned[:, span] = full
        gate = gating[:, span]
        skip = table[ROW_SKIP : ROW_SKIP + 1, span]
        full = (full + skip * channels[:, span]) * (gate * jax.nn.sigmoid(gate))
        gated[:, span] = full
        square = square + full * full
    scale = lax.rsqrt(jnp.sum(square, -1, keepdims=True) / WIDTH + EPS)
    scale = jnp.broadcast_to(scale, (count, LANES))
    for pair in range(PAIRS):
        span = lanes_of(pair)
        gain = table[ROW_MIXER : ROW_MIXER + 1, span]
        tail[:, span] = (gated[:, span] * scale * gain).astype(BF16)


def tail_back_kernel(
    xs, position, branch, mixer_w, scanned, channels, gating, table, logs, marks, readout,
    scanned_slope, gating_slope, sums, *refs,
):
    states, (gated, hold, selector, wide, weighted, slope) = refs[:xs], refs[xs:]
    for start in range(0, WIDTH, 512):
        span = slice(start, start + 512)
        slope[:, span] = dot_lanes(branch[...], mixer_w[span])
    at_x = lax.rem(position[0], xs)
    count = logs.shape[0]
    enter = halves(jnp.exp(logs[...]) * marks[:, MARK_ENTER : MARK_ENTER + 1])
    head_lanes(selector)
    wide[...] = dot(enter, selector[...])
    square = jnp.zeros((count, LANES), F32)
    cross = jnp.zeros((count, LANES), F32)
    for pair in range(PAIRS):
        span = lanes_of(pair)
        gate = gating[:, span]
        full = scanned[:, span] + table[ROW_SKIP : ROW_SKIP + 1, span] * channels[:, span]
        full = full * (gate * jax.nn.sigmoid(gate))
        gated[:, span] = full
        gain = table[ROW_MIXER : ROW_MIXER + 1, span]
        square = square + full * full
        cross = cross + full * slope[:, span] * gain
    scale = lax.rsqrt(jnp.sum(square, -1, keepdims=True) / WIDTH + EPS)
    cross = jnp.sum(cross, -1, keepdims=True) / WIDTH * scale * scale * scale
    scale = jnp.broadcast_to(scale, (count, LANES))
    cross = jnp.broadcast_to(cross, (count, LANES))
    for pair in range(PAIRS):
        span = lanes_of(pair)
        gate = gating[:, span]
        sigmoid = jax.nn.sigmoid(gate)
        back = slope[:, span]
        value = gated[:, span]
        sums[0:1, span] = jnp.sum(back * value * scale, 0, keepdims=True)
        back = back * table[ROW_MIXER : ROW_MIXER + 1, span] * scale - value * cross
        held = channels[:, span]
        full = scanned[:, span] + table[ROW_SKIP : ROW_SKIP + 1, span] * held
        gating_slope[:, span] = (
            back * full * sigmoid * (1.0 + gate * (1.0 - sigmoid))
        ).astype(BF16)
        back = back * (gate * sigmoid)
        sums[1:2, span] = jnp.sum(back * held, 0, keepdims=True)
        scanned_slope[:, span] = back.astype(BF16)
        weighted[:, span] = (back * wide[:, span]).astype(BF16)
    hold_all(hold, slice(0, STATE), dot(readout[...].T, weighted[...]).astype(BF16))
    hand_out(hold, at_x, states)
    sums[2:8] = jnp.zeros((6, WIDTH), F32)


def leaving_kernel(
    xs, position, entering, scanned, scanned_slope, scaled, channels, scaled_slope,
    inflow, readout, inflow_part, readout_part, steps, raw, logs, marks, inner, factor, taps, table,
    *refs,
):
    pieces, outs = refs[:xs], refs[xs:]
    inner_low, edges, conv_sums, raw_slope, small, conv_slope, selector, *outs = outs
    low, outer, lengths, tails, enters, first, second, third, fourth, fifth = outs
    at_x = lax.rem(position[0], xs)
    rates = table[ROW_RATE : ROW_RATE + 1, :LANES]
    count = logs.shape[0]
    ending = logs[count - 1 : count]
    head_lanes(selector)
    stepped = steps[...]
    for pair in range(PAIRS):
        low[:, lanes_of(pair)] = picked(pieces, at_x, pair)
    outer[...] = dot(inflow[...], low[...])
    lengths[...] = dot(halves(stepped), selector[...])
    tail = jnp.exp(ending - logs[...]) * marks[:, MARK_TAIL : MARK_TAIL + 1]
    tails[...] = dot(halves(tail), selector[...])
    enter = jnp.exp(logs[...]) * marks[:, MARK_ENTER : MARK_ENTER + 1]
    enters[...] = dot(halves(enter), selector[...])
    through = jnp.zeros((8, LANES), F32)
    for pair in range(PAIRS):
        span = lanes_of(pair)
        wide = scanned_slope[:, span].astype(F32)
        held = channels[:, span]
        short = scaled[:, span].astype(F32)
        tail = tails[:, span]
        part = outer[:, span] * tail
        within = scaled_slope[:, span]
        both = within + part
        split_into(first, span, wide * scanned[:, span] - short * within)
        split_into(second, span, short * part)
        split_into(third, span, held * both)
        fourth[:, span] = (short * tail).astype(BF16)
        fifth[:, span] = (wide * enters[:, span]).astype(BF16)
        skip = table[ROW_SKIP : ROW_SKIP + 1, span]
        conv_slope[:, span] = both * lengths[:, span] + skip * wide
        kept = low[:, span].astype(F32) * entering[:, span].astype(F32)
        kept = jnp.sum(kept, 0, keepdims=True) * jnp.exp(spread_pair(ending, pair))
        kept = halves(jnp.broadcast_to(kept, (8, LANES)))
        chosen = selector[:LANES, span]
        through = through + dot_lanes(kept, jnp.concatenate([chosen, chosen], 1))
    inside, outward = head_sums(first, selector), head_sums(second, selector)
    direct = head_sums(third, selector)
    inflow_slope = inflow_part[...] + dot_lanes(fourth[...], low[...])
    readout_slope = readout_part[...] + dot_lanes(fifth[...], entering[...])
    conv_slope[:, lanes_of(PAIRS)] = inflow_slope
    conv_slope[:, lanes_of(PAIRS + 1)] = readout_slope
    enter_last = marks[count - 1 :, MARK_ENTER : MARK_ENTER + 1]
    along = (
        precise(triangle(count, upper=True), inside)
        + precise(triangle(count, strict=True), outward)
        + through[:1] * enter_last
    )
    step_slope = direct + rates * along
    step_slope = step_slope * jax.nn.sigmoid(raw[...] + table[ROW_STEP : ROW_STEP + 1, :LANES])
    raw_slope[...] = step_slope.astype(BF16)
    small[0:1] = jnp.sum(step_slope, 0, keepdims=True)
    small[1:2] = rates * jnp.sum(stepped * along, 0, keepdims=True)
    small[2:8] = jnp.zeros((6, LANES), F32)
    blank = jnp.zeros((HALO, LANES), F32)
    marked = wide_marks(marks)
    for chunk in range(PAIRS + 2):
        span = lanes_of(chunk)
        extended = inner[:, span].astype(F32)
        slope = conv_slope[:, span] * factor[:, span].astype(F32)
        spread = jnp.zeros((HALO + count, LANES), F32)
        for tap in range(KERNEL):
            part = slope * marked[tap] if tap < KERNEL - 1 else slope
            part = jnp.concatenate([blank, part], 0)
            if tap < KERNEL - 1:
                part = pltpu.roll(part, HALO + count - (KERNEL - 1 - tap), 0)
            conv_sums[tap : tap + 1, span] = jnp.sum(part * extended, 0, keepdims=True)
            spread = spread + part * taps[tap : tap + 1, span]
        conv_sums[KERNEL : KERNEL + 1, span] = jnp.sum(slope, 0, keepdims=True)
        conv_sums[KERNEL + 1 :, span] = jnp.zeros((8 - KERNEL - 1, LANES), F32)
        inner_low[:, span] = spread[HALO:].astype(BF16)
        edges[:HALO, span] = spread[:HALO]
        edges[HALO:, span] = spread[count:]


PACK_ROWS = 48


def unit_back_kernel(slope, down_w, gate_raw, up_raw, gate_low, up_low):
    for start in range(0, gate_raw.shape[1], 512):
        span = slice(start, start + 512)
        back = dot_lanes(slope[...], down_w[span])
        gate = gate_raw[:, span]
        sigmoid = jax.nn.sigmoid(gate)
        up_low[:, span] = (back * (gate * sigmoid)).astype(BF16)
        back = back * up_raw[:, span]
        gate_low[:, span] = (back * (sigmoid * (1.0 + gate * (1.0 - sigmoid)))).astype(BF16)


def feed_back_kernel(
    gate_low, up_low, gate_w, up_w, mixed_sum, slope, gain, mixed_slope, branch_low, sums
):
    values = mixed_sum[...]
    count, width = values.shape
    scale = lax.rsqrt(jnp.mean(values * values, -1, keepdims=True) + EPS)
    back = dot_lanes(gate_low[...], gate_w[...]) + dot_lanes(up_low[...], up_w[...])
    sums[...] = jnp.broadcast_to(jnp.sum(back * values * scale, 0, keepdims=True), sums.shape)
    back = back * gain[...].reshape(1, width)
    cross = jnp.mean(back * values, -1, keepdims=True) * scale * scale * scale
    whole = slope[...].astype(F32) + back * scale - values * cross
    mixed_slope[...] = whole
    branch_low[...] = whole.astype(BF16)


def finish_kernel(
    gating_low, query_low, inner_low, pair_low, gating_w, query_w, inner_w, key_w, value_w, step_w,
    low_input, table, mixed_slope, raw_slope, normed, tail_sums, conv_sums, small, feed,
    input_gradient, packed,
):
    normed_slope = (
        dot_lanes(gating_low[...], gating_w[...])
        + dot_lanes(query_low[...], query_w[...])
        + dot_lanes(inner_low[...], inner_w[...])
        + dot_lanes(pair_low[:, :LANES], key_w[...])
        + dot_lanes(pair_low[:, LANES:], value_w[...])
        + dot_lanes(raw_slope[:, :SSM_HEADS], step_w[...])
    )
    values = low_input[...].astype(F32)
    width = values.shape[1]
    scale = lax.rsqrt(jnp.mean(values * values, -1, keepdims=True) + EPS)
    slope = normed_slope
    packed[SSM_HEADS : SSM_HEADS + 1] = jnp.sum(slope * values * scale, 0, keepdims=True)
    slope = slope * table[ROW_GAIN : ROW_GAIN + 1, :width]
    cross = jnp.mean(slope * values, -1, keepdims=True) * scale * scale * scale
    input_gradient[...] = mixed_slope[...] + slope * scale - values * cross
    packed[:SSM_HEADS] = dot_rows(raw_slope[...], normed[...])[:SSM_HEADS]
    packed[SSM_HEADS + 1 : SSM_HEADS + 2] = feed[:1]
    packed[SSM_HEADS + 2 :] = jnp.zeros((PACK_ROWS - SSM_HEADS - 2, width), F32)
    row = SSM_HEADS + 2
    for source, rows in ((tail_sums, 2), (small, 2), (conv_sums, KERNEL + 1)):
        for index in range(rows):
            for start in range(0, source.shape[1], width):
                stop = min(start + width, source.shape[1])
                packed[row : row + 1, : stop - start] = source[index : index + 1, start:stop]
                row += 1


def unpacked(packed, widths):
    row = SSM_HEADS + 2
    size = packed.shape[1]
    vectors = []
    for width in widths:
        rows = -(-width // size)
        vectors.append(packed[row : row + rows].reshape(-1)[:width])
        row += rows
    return vectors


def all_sum(place, shard, axes):
    for name in axes:
        axis = name[0] if name[0] == "z" else name
        bit = 2 if name == "zh" else 1
        while bit < (2 if name == "zl" else place.sizes[axis]):
            low = shard.astype(BF16)
            shard = low.astype(F32) + place.swap(low, axis, bit).astype(F32)
            bit *= 2
    return shard


def joint_kernel(xs, ys, widths, left, left_sib, right, right_sib, *outs):
    rows = left.shape[0] // len(widths)
    part = rows // (xs * ys)
    start = offset = 0
    for section, width in enumerate(widths):
        span = slice(section * rows, (section + 1) * rows)
        half = width // 2
        tile = next(t for t in (512, 384, 256, 128) if half % t == 0)
        for first in range(2):
            targets = outs[xs:] if first else outs[:xs]
            for column in range(0, half, tile):
                source = slice(start + first * half + column, start + first * half + column + tile)
                total = dot(left[span], right[:, source]) + dot(left_sib[span], right_sib[:, source])
                total = total.astype(BF16)
                into = slice(offset + column, offset + column + tile)
                for x in range(xs):
                    for y in range(ys):
                        piece = total[(x * ys + y) * part : (x * ys + y + 1) * part]
                        if first:
                            targets[y][x * part : (x + 1) * part, into] = piece
                        else:
                            targets[x][y * part : (y + 1) * part, into] = piece
        start += width
        offset += half


def joint_gradient(place, left, right, left_sib, right_sib, widths):
    sections = len(widths)
    rows, tokens = left.shape[0] // sections, left.shape[1]
    width = sum(widths)
    xs, ys = place.sizes["x"], place.sizes["y"]
    half = width // 2
    shapes = [(rows // xs, half)] * xs + [(rows // ys, half)] * ys
    outs = local_call(
        functools.partial(joint_kernel, xs, ys, widths),
        [(shape, BF16) for shape in shapes],
        (left, left_sib, right, right_sib),
        "joint_gradient",
    )
    return outs[:xs], outs[xs:]


def arranged(order, left):
    return lax.dot_general(
        order, left, (((1,), (1,)), ((), ())), preferred_element_type=jnp.float32
    ).astype(jnp.bfloat16)


def own_half(ordered):
    return ordered[: ordered.shape[0] // CORES]


def other_half(ordered):
    return ordered[ordered.shape[0] // CORES :]


def together(*values):
    return lax.optimization_barrier(values)


def fold_kernel(counts, splits, merged, *refs):
    at = 0
    outs = refs[sum(counts) :]
    for block, count in enumerate(counts):
        total = refs[at][...].astype(F32)
        for ref in refs[at + 1 : at + count]:
            total = total + ref[...].astype(F32)
        at += count
        low = total.astype(BF16)
        rows = low.shape[-2] // splits[block]
        for k in range(splits[block]):
            piece = low[..., k * rows : (k + 1) * rows, :]
            if merged:
                outs[k][block] = piece
            else:
                outs[sum(splits[:block]) + k][...] = piece


def fold(blocks, splits, merged):
    flat = [a for block in blocks for a in block]
    shape = flat[0].shape
    columns = shape[-1]
    tile = max(t for t in range(LANES, 1025, LANES) if columns % t == 0 and t <= columns // 2)

    def spec(full):
        lead = (0,) * (len(full) - 1)
        return pl.BlockSpec(full[:-1] + (tile,), lambda j: lead + (j,))

    if merged:
        outs = [(len(blocks), shape[0] // splits[0], columns)] * splits[0]
    else:
        outs = []
        for block, cuts in zip(blocks, splits):
            full = block[0].shape
            outs += [full[:-2] + (full[-2] // cuts, columns)] * cuts
    return pl.pallas_call(
        functools.partial(fold_kernel, [len(b) for b in blocks], splits, merged),
        grid=(columns // tile,),
        in_specs=[spec(a.shape) for a in flat],
        out_specs=[spec(full) for full in outs],
        out_shape=[jax.ShapeDtypeStruct(full, BF16) for full in outs],
        compiler_params=pltpu.CompilerParams(vmem_limit_bytes=16 * 1024 * 1024),
        cost_estimate=pl.CostEstimate(flops=0, bytes_accessed=0, transcendentals=0),
        name="fold",
    )(*flat)


class Shares:
    ORDERS = (("x", "y"), ("y", "x"))

    def __init__(self, place, lefts, rights):
        self.place = place
        self.widths = [sum(r.shape[1] for r in section) for section in rights]
        self.columns = [[r.shape[1] for r in section] for section in rights]
        flat = [r for section in rights for r in section]
        self.right = jnp.concatenate(flat, 1) if len(flat) > 1 else flat[0]
        self.lefts = lefts

    def to_core(self):
        return self.right

    def go_core(self, sent):
        return self.place.turn(sent, "core", 1)

    def join(self, left_siblings, right_sibling):
        left, sibling = (
            (pieces[0] if len(pieces) == 1 else jnp.concatenate(pieces, 0))
            for pieces in ([own_half(left) for left in self.lefts], left_siblings)
        )
        self.pieces = joint_gradient(
            self.place, left, self.right, sibling, right_sibling, self.widths
        )
        return tuple(tuple(pieces[1:]) for pieces in self.pieces)

    def go(self, sent, stage):
        return tuple(
            tuple(self.place.turn(piece, order[stage], k + 1) for k, piece in enumerate(pieces))
            for pieces, order in zip(sent, self.ORDERS)
        )

    def to_second(self, arrived):
        splits = [self.place.sizes[order[1]] for order in self.ORDERS]
        blocks = [(self.pieces[half][0],) + arrived[half] for half in range(2)]
        outs = fold(blocks, splits, False)
        self.kept = (outs[0], outs[splits[0]])
        return tuple(outs[1 : splits[0]]), tuple(outs[splits[0] + 1 :])

    def to_third(self, arrived):
        blocks = [(self.kept[half],) + arrived[half] for half in range(2)]
        self.kept, sent = fold(blocks, (2, 2), True)
        return sent

    def go_third(self, sent):
        return self.place.swap(sent, "z", 1)

    def to_fourth(self, arrived):
        self.kept, sent = fold([(self.kept, arrived)], (2,), False)
        return sent

    def go_fourth(self, sent):
        return self.place.swap(sent, "z", 2)

    def to_owners(self, arrived):
        cuts = self.place.sizes["z"]
        blocks = [(self.kept[half],) + arrived[half] for half in range(2)]
        self.kept, *sent = fold(blocks, (cuts, cuts), True)
        return tuple(sent)

    def go_owners(self, sent):
        return tuple(
            self.place.swap(piece, "z", k // 2 + 2 * (k % 2))
            for k, piece in enumerate(sent, start=1)
        )

    def shares(self, *arrived):
        total = self.kept.astype(F32)
        for piece in arrived:
            total = total + piece.astype(F32)
        shares = []
        offset = 0
        for width, columns in zip(self.widths, self.columns):
            section = jnp.concatenate(
                [total[half, :, offset : offset + width // 2] for half in range(2)], 1
            )
            offset += width // 2
            start = 0
            for w in columns:
                shares.append(section[:, start : start + w])
                start += w
        return shares


class KeyOwners:
    def __init__(self, place, slopes):
        self.place = place
        self.paired = place.sizes["x"] == 2
        self.kept = slopes

    def to_first(self):
        if not self.paired:
            return self.kept
        half = self.kept.shape[0] // 2
        sent = self.kept[half:]
        self.kept = self.kept[:half]
        return sent

    def go(self, sent, stage):
        if not self.paired:
            if stage:
                return sent
            return lax.psum_scatter(sent, "seq", scatter_dimension=0, tiled=True)
        axis, bit = (("z", 1), ("z", 2), ("x", 1))[stage]
        return self.place.swap(sent, axis, bit)

    def to_next(self, arrived):
        if not self.paired:
            return arrived
        total = (self.kept.astype(F32) + arrived.astype(F32)).astype(BF16)
        half = total.shape[0] // 2
        self.kept = total[:half]
        return total[half:]

    def summands(self, arrived):
        return (self.kept, arrived) if self.paired else (arrived,)


def body(
    inputs,
    segments,
    cotangent,
    input_gain,
    query_weight,
    key_weight,
    value_weight,
    attention_weight,
    gating_weight,
    inner_weight,
    step_weight,
    step_bias,
    decay_log,
    skip_scale,
    conv_weight,
    conv_bias,
    mixer_gain,
    mixer_weight,
    feed_gain,
    gate_weight,
    up_weight,
    down_weight,
):
    place = Place()
    xs = place.sizes["x"]
    count, width = inputs.shape[1], inputs.shape[2]
    low_input = inputs[0]
    hidden = low_input.astype(F32)
    slope = cotangent[0]
    seg_row = segments[0]
    length = seg_row.shape[0]
    group, along = lax.axis_index("dp"), lax.axis_index("seq")
    position = along.reshape(1).astype(jnp.int32)
    inner_width = inner_weight.shape[1]
    part_width = WIDTH // xs

    halo = passed_along(low_input[count - HALO :], "seq", 1)
    cosine, sine = turn_tables(along * count, count)
    normed_low, pairs, table = local_call(
        front_kernel,
        [((count, width), BF16), ((count, 2 * LANES), BF16), ((8, inner_width), F32)],
        (
            low_input,
            key_weight,
            value_weight,
            cosine,
            sine,
            conv_bias,
            input_gain,
            mixer_gain,
            skip_scale,
            step_bias,
            decay_log,
        ),
        "front",
        alone=True,
    )
    mine = jnp.concatenate(
        [pairs] + [place.turn(pairs, "z", k) for k in range(1, place.sizes["z"])], 0
    )
    (
        inner,
        raw,
        channels,
        scaled,
        inflow,
        readout,
        steps,
        logs,
        logs_turned,
        marks,
        marks_turned,
        factor,
        *states,
    ) = local_call(
        functools.partial(prep_kernel, xs),
        [
            ((HALO + count, inner_width), BF16),
            ((count, LANES), F32),
            ((count, WIDTH), F32),
            ((count, WIDTH), BF16),
            ((count, STATE), BF16),
            ((count, STATE), BF16),
            ((count, LANES), F32),
            ((count, LANES), F32),
            ((LANES, count), F32),
            ((count, 8), F32),
            ((8, count), F32),
            ((count, inner_width), BF16),
        ]
        + [((STATE + EXTRA, part_width), BF16)] * xs,
        (position, halo, normed_low, table, inner_weight, step_weight, conv_weight, segments),
        "prepare",
        alone=True,
        scratch=[
            pltpu.VMEM((HALO + count, width), BF16),
            pltpu.VMEM((xs, STATE + EXTRA, part_width), BF16),
            pltpu.VMEM((2 * LANES, WIDTH), BF16),
            pltpu.VMEM((count, WIDTH), F32),
            pltpu.VMEM((count, WIDTH), F32),
            pltpu.VMEM((count, WIDTH), BF16),
        ],
        smem=(0,),
    )

    states, mine, normed_low, group, along = together(
        tuple(states), mine, normed_low, group, along
    )
    everything = jnp.concatenate([mine] + [place.turn(mine, "x", k) for k in range(1, xs)], 0)
    pieces = dealt(place, states)
    gating = product(normed_low, gating_weight)
    order = place.share_order(width, group, along)
    ordered = arranged(order, normed_low)
    pieces, gating, normed_low, order, ordered = together(
        pieces, gating, normed_low, order, ordered
    )
    total, walls = level(place, pieces, position, seg_row, count)

    total, normed_low, ordered = together(total, normed_low, ordered)
    totals = levels_met(place, total)
    ordered_sibling = place.turn(other_half(ordered), "core", 1)
    queries, attention_low, exact, spread = local_call(
        functools.partial(attend_kernel, xs, place.sizes["z"]),
        [
            ((count, HEADS * HEAD), BF16),
            ((count, HEADS * HEAD), BF16),
            ((HEADS * HEAD, count), F32),
            ((HEADS, count), F32),
        ],
        (position, normed_low, query_weight, cosine, sine, everything, segments),
        "attend",
        alone=True,
        scratch=[
            pltpu.VMEM((HEADS, count), F32),
            pltpu.VMEM((HEADS, count), F32),
            pltpu.VMEM((HEADS * HEAD, count), F32),
        ],
        smem=(0,),
    )
    totals, attention_low, ordered_sibling, scaled, slope, order = together(
        totals, attention_low, ordered_sibling, scaled, slope, order
    )
    results, level_walls = arrival(
        place, pieces, totals, walls, total, position, seg_row, count
    )

    results, scaled, attention_low, slope, order = together(
        results, scaled, attention_low, slope, order
    )
    pieces = dealt(place, results)
    fixed = (logs, logs_turned, marks, marks_turned, inflow, readout)
    (inner_part,) = inner_call(inner_kernel, fixed, (scaled,), (F32,), (), "inner", 2)
    attention_branch = product(attention_low, attention_weight)
    ordered_slope = arranged(order, slope)
    pieces, inner_part, attention_branch, ordered_slope = together(
        pieces, inner_part, attention_branch, ordered_slope
    )
    tail_low, scanned, entering = local_call(
        functools.partial(entering_kernel, xs),
        [((count, WIDTH), BF16), ((count, WIDTH), F32), ((STATE, WIDTH), BF16)],
        (position, inner_part, readout, logs, marks, channels, gating, table, *pieces),
        "entering",
        scratch=[
            pltpu.VMEM((count, WIDTH), F32),
            pltpu.VMEM((2 * LANES, WIDTH), BF16),
            pltpu.VMEM((count, WIDTH), F32),
        ],
        smem=(0,),
    )
    mixed_sum = hidden + attention_branch + product(tail_low, mixer_weight)
    feed_low = norm_rows(mixed_sum, feed_gain).astype(BF16)
    gate_raw, up_raw = product(feed_low, gate_weight), product(feed_low, up_weight)
    activated_low = gated_unit(gate_raw, up_raw).astype(BF16)

    down = Shares(place, (ordered_slope,), ((activated_low,),))
    sent, slope_half, gate_raw, up_raw, slope, feed_low, order = together(
        down.to_core(), other_half(ordered_slope), gate_raw, up_raw, slope, feed_low, order
    )
    arrived = down.go_core(sent)
    slope_sibling = place.turn(slope_half, "core", 1)
    gate_low, up_low = local_call(
        unit_back_kernel,
        [(gate_raw.shape, BF16), (up_raw.shape, BF16)],
        (slope, down_weight, gate_raw, up_raw),
        "unit_back",
    )
    ordered_feed = arranged(order, feed_low)
    arrived, slope_sibling, gate_low, up_low, ordered_feed = together(
        arrived, slope_sibling, gate_low, up_low, ordered_feed
    )
    sent = down.join([slope_sibling], arrived)

    gate = Shares(place, (ordered_feed,), ((gate_low,),))
    up = Shares(place, (ordered_feed,), ((up_low,),))
    sent, feed_half, gate_low, up_low = together(
        sent, other_half(ordered_feed), gate_low, up_low
    )
    arrived = down.go(sent, 0)
    gate_arrived, up_arrived = gate.go_core(gate_low), up.go_core(up_low)
    feed_sibling = place.turn(feed_half, "core", 1)
    mixed_slope, branch_low, feed_sums = local_call(
        feed_back_kernel,
        [((count, width), F32), ((count, width), BF16), ((8, width), F32)],
        (gate_low, up_low, gate_weight, up_weight, mixed_sum, slope, feed_gain),
        "feed_back",
    )
    scanned_slope, gating_low, tail_sums, *state_slopes = local_call(
        functools.partial(tail_back_kernel, xs),
        [((count, WIDTH), BF16), ((count, WIDTH), BF16), ((8, WIDTH), F32)]
        + [((STATE, part_width), BF16)] * xs,
        (
            position,
            branch_low,
            mixer_weight,
            scanned,
            channels,
            gating,
            table,
            logs,
            marks,
            readout,
        ),
        "tail_back",
        scratch=[
            pltpu.VMEM((count, WIDTH), F32),
            pltpu.VMEM((xs, STATE, part_width), BF16),
            pltpu.VMEM((2 * LANES, WIDTH), BF16),
            pltpu.VMEM((count, WIDTH), F32),
            pltpu.VMEM((count, WIDTH), BF16),
            pltpu.VMEM((count, WIDTH), F32),
        ],
        smem=(0,),
    )
    (
        arrived,
        gate_arrived,
        up_arrived,
        feed_sibling,
        state_slopes,
        branch_low,
        scanned_slope,
        gating_low,
        order,
    ) = together(
        arrived,
        gate_arrived,
        up_arrived,
        feed_sibling,
        tuple(state_slopes),
        branch_low,
        scanned_slope,
        gating_low,
        order,
    )

    gate_sent = gate.join([feed_sibling], gate_arrived)
    ordered_branch = arranged(order, branch_low)
    mixers = Shares(place, (ordered_branch, ordered), ((attention_low, tail_low), (gating_low,)))
    state_slopes, gate_sent, mixers_sent, branch_half, arrived, branch_low = together(
        state_slopes,
        gate_sent,
        mixers.to_core(),
        other_half(ordered_branch),
        arrived,
        branch_low,
    )
    state_pieces = dealt(place, state_slopes)
    gate_arrived = gate.go(gate_sent, 0)
    mixers_arrived = mixers.go_core(mixers_sent)
    branch_sibling = place.turn(branch_half, "core", 1)
    attention_slope = product_right(branch_low, attention_weight).astype(BF16)
    down_sent = down.to_second(arrived)
    mixers_sent = mixers.join([branch_sibling, ordered_sibling], mixers_arrived)
    state_pieces, gate_arrived, mixers_sent, down_sent, attention_slope = together(
        state_pieces, gate_arrived, mixers_sent, down_sent, attention_slope
    )
    total = level_back(place, state_pieces, walls, position, seg_row, count)

    total, mixers_sent, attention_slope, up_arrived, feed_sibling, gate_arrived = together(
        total, mixers_sent, attention_slope, up_arrived, feed_sibling, gate_arrived
    )
    totals = levels_met(place, total)
    mixers_arrived = mixers.go(mixers_sent, 0)
    query_low, pair_slope = local_call(
        functools.partial(attend_back_kernel, xs, place.sizes["z"]),
        [((count, HEADS * HEAD), BF16), ((length, 2 * LANES), BF16)],
        (
            position,
            queries,
            everything,
            attention_slope,
            exact,
            spread,
            segments,
            cosine,
            sine,
        ),
        "attend_back",
        scratch=[
            pltpu.VMEM((HEADS * HEAD, count), F32),
            pltpu.VMEM((HEADS, count), F32),
            pltpu.VMEM((HEADS * HEAD, count), F32),
        ],
        smem=(0,),
    )
    owners = KeyOwners(place, pair_slope)
    pair_sent = owners.to_first()
    up_sent = up.join([feed_sibling], up_arrived)
    totals, mixers_arrived, pair_sent, up_sent = together(
        totals, mixers_arrived, pair_sent, up_sent
    )
    results = arrival_back(
        place, state_pieces, totals, walls, level_walls, position, seg_row, count
    )

    (
        results,
        pair_sent,
        up_sent,
        mixers_arrived,
        gate_arrived,
        scanned_slope,
        activated_low,
    ) = together(
        results, pair_sent, up_sent, mixers_arrived, gate_arrived, scanned_slope, activated_low
    )
    pieces = dealt(place, results)
    pair_arrived = owners.go(pair_sent, 0)
    up_arrived = up.go(up_sent, 0)
    scaled_slope, inflow_part, readout_part = inner_call(
        inner_back_kernel,
        fixed,
        (scaled, scanned_slope),
        (F32,),
        (((count, STATE), F32), ((count, STATE), F32)),
        "inner_back",
        3,
    )
    mixers_sent = mixers.to_second(mixers_arrived)
    gate_sent = gate.to_second(gate_arrived)
    output = (mixed_sum + product(activated_low, down_weight)).astype(BF16)
    pieces, pair_arrived, up_arrived, mixers_sent, gate_sent, scaled_slope, output = together(
        pieces, pair_arrived, up_arrived, mixers_sent, gate_sent, scaled_slope, output
    )

    pieces, pair_sent, mixers_sent, gate_sent, up_arrived = together(
        pieces, owners.to_next(pair_arrived), mixers_sent, gate_sent, up_arrived
    )
    mixers_arrived = mixers.go(mixers_sent, 1)
    gate_arrived = gate.go(gate_sent, 1)
    pair_arrived = owners.go(pair_sent, 1)
    inner_low, edges, conv_sums, raw_slope, small = local_call(
        functools.partial(leaving_kernel, xs),
        [
            ((count, inner_width), BF16),
            ((2 * HALO, inner_width), F32),
            ((8, inner_width), F32),
            ((count, LANES), BF16),
            ((8, LANES), F32),
        ],
        (
            position,
            entering,
            scanned,
            scanned_slope,
            scaled,
            channels,
            scaled_slope,
            inflow,
            readout,
            inflow_part,
            readout_part,
            steps,
            raw,
            logs,
            marks,
            inner,
            factor,
            conv_weight,
            table,
            *pieces,
        ),
        "leaving",
        scratch=[
            pltpu.VMEM((count, inner_width), F32),
            pltpu.VMEM((2 * LANES, WIDTH), BF16),
            pltpu.VMEM((STATE, WIDTH), BF16),
        ]
        + [pltpu.VMEM((count, WIDTH), F32)] * 4
        + [pltpu.VMEM((2, count, WIDTH), BF16)] * 3
        + [pltpu.VMEM((count, WIDTH), BF16)] * 2,
        smem=(0,),
    )
    mixers_arrived, gate_arrived, pair_arrived, inner_low, edges = together(
        mixers_arrived, gate_arrived, pair_arrived, inner_low, edges
    )

    mixers_sent, pair_sent, down_sent, inner_low, edges, up_arrived, gate_arrived = together(
        mixers.to_third(mixers_arrived),
        owners.to_next(pair_arrived),
        down_sent,
        inner_low,
        edges,
        up_arrived,
        gate_arrived,
    )
    returned = passed_along(edges[:HALO], "seq", -1)
    pair_arrived = owners.go(pair_sent, 2)
    down_arrived = down.go(down_sent, 1)
    mixers_arrived = mixers.go_third(mixers_sent)
    up_sent = up.to_second(up_arrived)
    gate_sent = gate.to_third(gate_arrived)
    returned, pair_arrived, down_arrived, mixers_arrived, up_sent, gate_sent = together(
        returned, pair_arrived, down_arrived, mixers_arrived, up_sent, gate_sent
    )
    inner_low = lax.dynamic_update_slice(
        inner_low, (edges[HALO:] + returned).astype(BF16), (count - HALO, 0)
    )
    (pair_low,) = local_call(
        pairs_back_kernel,
        [((count, 2 * LANES), BF16)],
        (*owners.summands(pair_arrived), cosine, sine),
        "pairs_back",
    )

    rest = Shares(place, (ordered,), ((inner_low, query_low, pair_low),))
    (
        rest_sent,
        up_sent,
        mixers_arrived,
        gate_sent,
        down_arrived,
        gating_low,
        query_low,
        pair_low,
        inner_low,
    ) = together(
        rest.to_core(),
        up_sent,
        mixers_arrived,
        gate_sent,
        down_arrived,
        gating_low,
        query_low,
        pair_low,
        inner_low,
    )
    rest_arrived = rest.go_core(rest_sent)
    up_arrived = up.go(up_sent, 1)
    mixers_arrived = mixers.go_fourth(mixers.to_fourth(mixers_arrived))
    gate_arrived = gate.go_third(gate_sent)
    input_gradient, packed = local_call(
        finish_kernel,
        [((count, width), F32), ((PACK_ROWS, width), F32)],
        (
            gating_low,
            query_low,
            inner_low,
            pair_low,
            gating_weight,
            query_weight,
            inner_weight,
            key_weight,
            value_weight,
            step_weight,
            low_input,
            table,
            mixed_slope,
            raw_slope,
            normed_low,
            tail_sums,
            conv_sums,
            small,
            feed_sums,
        ),
        "finish",
    )
    rest_sent = rest.join([ordered_sibling], rest_arrived)
    rest_sent, up_arrived, mixers_arrived, gate_arrived, down_arrived, packed, input_gradient = (
        together(
            rest_sent, up_arrived, mixers_arrived, gate_arrived, down_arrived, packed, input_gradient
        )
    )

    rest_sent, gate_arrived, up_arrived, down_arrived, packed = together(
        rest_sent, gate_arrived, up_arrived, down_arrived, packed
    )
    rest_arrived = rest.go(rest_sent, 0)
    gate_arrived = gate.go_fourth(gate.to_fourth(gate_arrived))
    up_arrived = up.go_third(up.to_third(up_arrived))
    down_arrived = down.go_third(down.to_third(down_arrived))
    share_attention, share_mixer, share_gating = mixers.shares(mixers_arrived)
    share_attention, share_mixer = share_attention.T, share_mixer.T
    rest_arrived, gate_arrived, up_arrived, down_arrived, packed, share_attention, share_mixer = (
        together(
            rest_arrived,
            gate_arrived,
            up_arrived,
            down_arrived,
            packed,
            share_attention,
            share_mixer,
        )
    )

    rest_sent, up_sent, down_sent, gate_arrived, packed = together(
        rest.to_second(rest_arrived),
        up.to_fourth(up_arrived),
        down.to_fourth(down_arrived),
        gate_arrived,
        packed,
    )
    rest_arrived = rest.go(rest_sent, 1)
    up_arrived = up.go_fourth(up_sent)
    down_arrived = down.go_fourth(down_sent)
    packed = all_sum(place, packed, ("core", "x", "y"))
    (share_gate,) = gate.shares(gate_arrived)
    rest_arrived, up_arrived, down_arrived, packed, share_gate = together(
        rest_arrived, up_arrived, down_arrived, packed, share_gate
    )

    rest_sent, up_arrived, down_arrived, packed = together(
        rest.to_owners(rest_arrived), up_arrived, down_arrived, packed
    )
    rest_arrived = rest.go_owners(rest_sent)
    packed = all_sum(place, packed, ("z",))
    (share_up,), (share_down,) = up.shares(up_arrived), down.shares(down_arrived)
    share_down = share_down.T
    share_inner, share_query, share_pair = rest.shares(*rest_arrived)
    step_sum = packed[:SSM_HEADS].T
    gain_sum, feed_gain_sum = packed[SSM_HEADS], packed[SSM_HEADS + 1]
    taps = conv_weight.shape[1]
    mixer_gain_sum, skip_sum, step_bias_sum, decay_sum, *conv_sum = unpacked(
        packed, [WIDTH] * 2 + [LANES] * 2 + [taps] * (KERNEL + 1)
    )
    skip_sum = jnp.sum(skip_sum.reshape(SSM_HEADS, SSM_HEAD), 1)
    return (
        output[None],
        input_gradient[None],
        gain_sum,
        share_query,
        share_pair[:, :LANES],
        share_pair[:, LANES:],
        share_attention,
        share_gating,
        share_inner,
        step_sum,
        step_bias_sum[:SSM_HEADS],
        decay_sum[:SSM_HEADS],
        skip_sum,
        jnp.stack(conv_sum[:KERNEL]),
        conv_sum[KERNEL],
        mixer_gain_sum,
        share_mixer,
        feed_gain_sum,
        share_gate,
        share_up,
        share_down,
    )


def solution(mesh):
    in_specs = (
        P("dp", "seq", None),
        P("dp", None),
        P("dp", "seq", None),
        P(),
        P(),
        P(),
        P(),
        P(),
        P(),
        P(),
        P(),
        P(),
        P(),
        P(),
        P(),
        P(),
        P(),
        P(),
        P(),
        P(),
        P(),
        P(),
    )
    out_specs = (
        P("dp", "seq", None),
        P("dp", "seq", None),
        P(),
        P(("dp", "seq"), None),
        P(("dp", "seq"), None),
        P(("dp", "seq"), None),
        P(None, ("dp", "seq")),
        P(("dp", "seq"), None),
        P(("dp", "seq"), None),
        P(),
        P(),
        P(),
        P(),
        P(),
        P(),
        P(),
        P(None, ("dp", "seq")),
        P(),
        P(("dp", "seq"), None),
        P(("dp", "seq"), None),
        P(None, ("dp", "seq")),
    )
    return jax.shard_map(body, mesh=mesh, in_specs=in_specs, out_specs=out_specs, check_vma=False)
```

```python
import functools
import math

import jax
import jax.numpy as jnp
from jax import lax
from jax.experimental import pallas as pl
from jax.experimental.pallas import tpu as pltpu
from jax.sharding import PartitionSpec as P

HEADS = 8
KV_HEADS = 2
HEAD = 64
SSM_HEADS = 24
SSM_HEAD = 64
STATE = 128
KERNEL = 4


EPS = 1e-05
ROPE_BASE = 100000000000.0
NEG = -1e30
HIGH = lax.Precision.HIGHEST


def passed_along(shard, axis, by):
    peers = lax.axis_size(axis)
    pairs = [(i, i + by) for i in range(peers) if 0 <= i + by < peers]
    return lax.ppermute(shard, axis, pairs)


def product(left, right):
    return jnp.dot(left, right, preferred_element_type=jnp.float32)


def product_left(left, right):
    return lax.dot_general(
        left, right, (((0,), (0,)), ((), ())), preferred_element_type=jnp.float32
    )


def product_right(left, right):
    return lax.dot_general(
        left, right, (((1,), (1,)), ((), ())), preferred_element_type=jnp.float32
    )


def precise(left, right):
    return jnp.dot(left, right, preferred_element_type=jnp.float32, precision=HIGH)


def norm_rows(values, gain):
    return values * lax.rsqrt(jnp.mean(values * values, -1, keepdims=True) + EPS) * gain


def gated_unit(gate, upward):
    return jax.nn.silu(gate) * upward


CORES = 2
DEPTH = 4
LANES = 128


class Place:
    def __init__(self):
        self.dp = lax.axis_size("dp")
        self.seq = lax.axis_size("seq")
        self.sizes = {
            "y": self.dp // CORES,
            "core": CORES,
            "z": DEPTH,
            "x": self.seq // DEPTH,
        }

    def split(self, index):
        dp, seq = index // self.seq, index % self.seq
        return {
            "y": dp // CORES,
            "core": dp % CORES,
            "z": seq // self.sizes["x"],
            "x": seq % self.sizes["x"],
        }

    def join(self, at):
        return (at["y"] * CORES + at["core"]) * self.seq + at["z"] * self.sizes["x"] + at["x"]

    def turn(self, shard, axis, by):
        pairs = []
        for index in range(self.dp * self.seq):
            at = self.split(index)
            at[axis] = (at[axis] + by) % self.sizes[axis]
            pairs.append((index, self.join(at)))
        return lax.ppermute(shard, ("dp", "seq"), pairs)

    def swap(self, shard, axis, bit):
        pairs = []
        for index in range(self.dp * self.seq):
            at = self.split(index)
            at[axis] ^= bit
            pairs.append((index, self.join(at)))
        return lax.ppermute(shard, ("dp", "seq"), pairs)

    def share_order(self, width, group, along):
        sizes, at = self.sizes, self.split(group * self.seq + along)
        rows = width // (self.dp * self.seq)
        k = lax.broadcasted_iota(jnp.int32, (width, 1), 0)
        within = k % rows
        rest = k // rows
        dz = rest % sizes["z"]
        rest = rest // sizes["z"]
        dy = rest % sizes["y"]
        rest = rest // sizes["y"]
        dx = rest % sizes["x"]
        dc = rest // sizes["x"]
        owner = self.join(
            {
                "y": (at["y"] + dy) % sizes["y"],
                "core": (at["core"] + dc) % sizes["core"],
                "z": at["z"] ^ (dz // 2 + 2 * (dz % 2)),
                "x": (at["x"] + dx) % sizes["x"],
            }
        )
        source = owner * rows + within
        columns = lax.broadcasted_iota(jnp.int32, (1, width), 1)
        return (source == columns).astype(jnp.bfloat16)


F32 = jnp.float32
BF16 = jnp.bfloat16
PAIR = 2 * SSM_HEAD
WIDTH = SSM_HEADS * SSM_HEAD
PAIRS = WIDTH // PAIR
HALO = 16
EXTRA = 16
WALLS = 16
VMEM = pl.BlockSpec(memory_space=pltpu.VMEM)
SMEM = pl.BlockSpec(memory_space=pltpu.SMEM)
FAR = pl.BlockSpec(memory_space=pl.ANY)


def room(arrays):
    total = 0
    for a in arrays:
        *lead, last = a.shape if len(a.shape) > 1 else (8, *a.shape)
        total += math.prod(lead) * (-(-last // LANES) * LANES) * jnp.dtype(a.dtype).itemsize
    return total


def local_call(kernel, outs, args, name, scratch=(), smem=(), slack=3, alone=False, far=(), sems=()):
    shapes = [jax.ShapeDtypeStruct(shape, kind) for shape, kind in outs]
    held = [a for i, a in enumerate(args) if i not in smem and i not in far]
    needed = (56 if alone else slack) * 1024 * 1024
    if not alone:
        needed += room(held) + room(shapes) + room(scratch)
    return pl.pallas_call(
        kernel,
        in_specs=[
            SMEM if i in smem else (FAR if i in far else VMEM) for i in range(len(args))
        ],
        out_specs=[VMEM] * len(shapes),
        out_shape=shapes,
        scratch_shapes=list(scratch) + [pltpu.SemaphoreType.DMA((n,)) for n in sems],
        compiler_params=pltpu.CompilerParams(vmem_limit_bytes=needed),
        cost_estimate=pl.CostEstimate(flops=0, bytes_accessed=0, transcendentals=0),
        name=name,
    )(*args)


def dot(left, right):
    return jnp.dot(left, right, preferred_element_type=F32)


def dot_rows(left, right):
    return lax.dot_general(left, right, (((0,), (0,)), ((), ())), preferred_element_type=F32)


def dot_lanes(left, right):
    return lax.dot_general(left, right, (((1,), (1,)), ((), ())), preferred_element_type=F32)


def turned(values, cosine, sine):
    lane = lax.broadcasted_iota(jnp.int32, values.shape, 1)
    half = HEAD // 2
    swapped = jnp.where(
        lane % HEAD < half,
        pltpu.roll(values, LANES - half, 1),
        pltpu.roll(values, half, 1),
    )
    return values * cosine + swapped * sine


def turn_tables(first, count):
    lane = jnp.arange(LANES)
    place = (first + jnp.arange(count)).astype(F32)
    half = HEAD // 2
    freq = ROPE_BASE ** (-((lane % half).astype(F32) * 2.0 / HEAD))
    angle = place[:, None] * freq[None, :]
    sign = jnp.where(lane % HEAD < half, -1.0, 1.0)[None, :]
    return jnp.cos(angle), jnp.sin(angle) * sign


def lanes_of(index):
    return slice(index * LANES, (index + 1) * LANES)


def spread_pair(values, pair):
    rows = values.shape[0]
    lane = lax.broadcasted_iota(jnp.int32, (rows, LANES), 1)
    return jnp.where(
        lane < SSM_HEAD, values[:, 2 * pair : 2 * pair + 1], values[:, 2 * pair + 1 : 2 * pair + 2]
    )


def head_lanes(selector):
    head = lax.broadcasted_iota(jnp.int32, (LANES, LANES), 0)
    lane = lax.broadcasted_iota(jnp.int32, (LANES, LANES), 1)
    for pair in range(PAIRS):
        chosen = (lane // SSM_HEAD + 2 * pair == head).astype(F32).astype(BF16)
        selector[:LANES, lanes_of(pair)] = chosen
        selector[LANES:, lanes_of(pair)] = chosen


def halves(values):
    upper = values.astype(BF16)
    return jnp.concatenate([upper, (values - upper.astype(F32)).astype(BF16)], 1)


def split_into(target, span, values):
    upper = values.astype(BF16)
    target[0, :, span] = upper
    target[1, :, span] = (values - upper.astype(F32)).astype(BF16)


def head_sums(parts, selector):
    chosen = selector[:LANES]
    return dot_lanes(parts[0], chosen) + dot_lanes(parts[1], chosen)


def silu_slope(values):
    gate = jax.nn.sigmoid(values)
    return gate * (1.0 + values * (1.0 - gate))


def front_kernel(
    x, key_w, value_w, cosine, sine, conv_bias, input_gain, mixer_gain, skip, step_bias, decay_log,
    normed, pairs, table,
):
    table[...] = jnp.zeros(table.shape, F32)
    for row, source in (
        (ROW_CONV, conv_bias),
        (ROW_GAIN, input_gain),
        (ROW_MIXER, mixer_gain),
        (ROW_STEP, step_bias),
    ):
        table[row : row + 1, : source.shape[0]] = source[...].reshape(1, source.shape[0])
    rates = -jnp.exp(decay_log[...].reshape(1, SSM_HEADS))
    table[ROW_RATE : ROW_RATE + 1, :SSM_HEADS] = rates
    skips = skip[...].reshape(1, SSM_HEADS)
    for pair in range(PAIRS):
        table[ROW_SKIP : ROW_SKIP + 1, lanes_of(pair)] = spread_pair(skips, pair)
    values = x[...].astype(F32)
    scale = lax.rsqrt(jnp.mean(values * values, -1, keepdims=True) + EPS)
    gain = table[ROW_GAIN : ROW_GAIN + 1, : values.shape[1]]
    normed[...] = (values * scale * gain).astype(BF16)
    low = normed[...]
    pairs[:, :LANES] = turned(dot(low, key_w[...]), cosine[...], sine[...]).astype(BF16)
    pairs[:, LANES:] = dot(low, value_w[...]).astype(BF16)


def block_mask(first, start, segments, count):
    def row(at):
        return segments[:, pl.ds(pl.multiple_of(at, LANES), count)].astype(F32)

    place = lax.broadcasted_iota(jnp.int32, (count, count), 0) + start
    reach = lax.broadcasted_iota(jnp.int32, (count, count), 1) + first
    keys = jnp.broadcast_to(row(start), (8, count)).T[:, :1]
    return (keys == row(first)) & (place <= reach)


def key_rows(xs, position, index, count):
    far = position // xs - index // xs
    side = lax.rem(lax.rem(position, xs) - lax.rem(index, xs) + xs, xs)
    return pl.ds(pl.multiple_of((far * xs + side) * count, count), count)


def head_columns(pairs, rows):
    keys = [pairs[rows, kv * HEAD : (kv + 1) * HEAD] for kv in range(KV_HEADS)]
    values = [
        pairs[rows, LANES + kv * HEAD : LANES + (kv + 1) * HEAD] for kv in range(KV_HEADS)
    ]
    return keys, values


def attend_kernel(
    xs, position, normed, query_w, cosine, sine, segments, *refs
):
    *pieces, queries, low, exact, spread, pairs, top, total, gathered, arrived = refs
    count = queries.shape[0]
    block = pieces[0].shape[0]
    copies = [
        pltpu.make_async_copy(piece, pairs.at[k * block : (k + 1) * block], arrived.at[k])
        for k, piece in enumerate(pieces)
    ]
    for copy in copies:
        copy.start()
    raw = dot(normed[...], query_w[...])
    for chunk_at in range(HEADS * HEAD // LANES):
        part = turned(raw[:, lanes_of(chunk_at)], cosine[...], sine[...]) * HEAD**-0.5
        queries[:, lanes_of(chunk_at)] = part.astype(BF16)
    first = position[0] * count
    group = HEADS // KV_HEADS
    top[...] = jnp.full(top.shape, NEG, F32)
    total[...] = jnp.zeros(total.shape, F32)
    gathered[...] = jnp.zeros(gathered.shape, F32)

    def chunk(index, carry):
        start = pl.multiple_of(index * count, count)
        rows = key_rows(xs, position[0], index, count)
        mask = block_mask(first, start, segments, count)
        keys, values = head_columns(pairs, rows)
        values = [value.T for value in values]
        before = top[...]
        scores = []
        for head in range(HEADS):
            score = dot_lanes(keys[head // group], queries[:, head * HEAD : (head + 1) * HEAD])
            scores.append(jnp.where(mask, score, NEG))
        now = jnp.maximum(
            before, jnp.concatenate([jnp.max(score, 0, keepdims=True) for score in scores], 0)
        )
        fade = jnp.exp(before - now)
        weights = [jnp.exp(score - now[head : head + 1]) for head, score in enumerate(scores)]
        sums = jnp.concatenate([jnp.sum(weight, 0, keepdims=True) for weight in weights], 0)
        top[...] = now
        total[...] = total[...] * fade + sums
        for head in range(HEADS):
            span = slice(head * HEAD, (head + 1) * HEAD)
            gathered[span] = gathered[span] * fade[head : head + 1] + dot(
                values[head // group], weights[head].astype(BF16)
            )
        return carry

    for copy in copies:
        copy.wait()
    lax.fori_loop(0, first // count + 1, chunk, 0)
    spread[...] = top[...] + jnp.log(total[...])
    for head in range(HEADS):
        span = slice(head * HEAD, (head + 1) * HEAD)
        exact[span] = gathered[span] / total[head : head + 1]
    for chunk_at in range(HEADS * HEAD // LANES):
        low[:, lanes_of(chunk_at)] = exact[lanes_of(chunk_at)].T.astype(BF16)


def attend_back_kernel(
    xs, position, queries, pairs, slope, exact, spread, segments, cosine, sine,
    query_low, pair_slope, turned_slope, delta, query_slope,
):
    count = queries.shape[0]
    length = pairs.shape[0]
    first = position[0] * count
    group = HEADS // KV_HEADS
    for chunk_at in range(HEADS * HEAD // LANES):
        turned_slope[lanes_of(chunk_at)] = slope[:, lanes_of(chunk_at)].astype(F32).T
    for head in range(HEADS):
        span = slice(head * HEAD, (head + 1) * HEAD)
        delta[head : head + 1] = jnp.sum(turned_slope[span] * exact[span], 0, keepdims=True)
    query_slope[...] = jnp.zeros(query_slope.shape, F32)

    def target(index):
        if xs != 2:
            return pl.ds(pl.multiple_of(index * count, count), count)
        far = (index // xs) ^ (position[0] // xs)
        side = lax.rem(index, xs) ^ lax.rem(position[0], xs)
        turn = (far & 1) * 4 + (far >> 1) * 2 + side
        return pl.ds(pl.multiple_of(turn * count, count), count)

    def chunk(index, carry):
        start = pl.multiple_of(index * count, count)
        rows = key_rows(xs, position[0], index, count)
        mask = block_mask(first, start, segments, count)
        into = target(index)
        keys, values = head_columns(pairs, rows)
        asked = [queries[:, head * HEAD : (head + 1) * HEAD] for head in range(HEADS)]
        sloped = [slope[:, head * HEAD : (head + 1) * HEAD] for head in range(HEADS)]
        scores = [dot_lanes(keys[head // group], asked[head]) for head in range(HEADS)]
        dots = [dot_lanes(values[head // group], sloped[head]) for head in range(HEADS)]
        weights, score_slopes = [], []
        for head in range(HEADS):
            row = slice(head, head + 1)
            weight = jnp.exp(jnp.where(mask, scores[head] - spread[row], NEG))
            score_slopes.append((weight * (dots[head] - delta[row])).astype(BF16))
            weights.append(weight.astype(BF16))
        for kv in range(KV_HEADS):
            heads = range(kv * group, (kv + 1) * group)
            value_part = sum(dot(weights[head], sloped[head]) for head in heads)
            key_part = sum(dot(score_slopes[head], asked[head]) for head in heads)
            pair_slope[into, kv * HEAD : (kv + 1) * HEAD] = key_part.astype(BF16)
            pair_slope[into, LANES + kv * HEAD : LANES + (kv + 1) * HEAD] = value_part.astype(BF16)
        keys = [key.T for key in keys]
        for head in range(HEADS):
            span = slice(head * HEAD, (head + 1) * HEAD)
            query_slope[span] = query_slope[span] + dot(keys[head // group], score_slopes[head])
        return carry

    def blank(index, carry):
        pair_slope[target(index), :] = jnp.zeros((count, 2 * LANES), BF16)
        return carry

    live = first // count + 1
    lax.fori_loop(0, live, chunk, 0)
    lax.fori_loop(live, length // count, blank, 0)
    for chunk_at in range(HEADS * HEAD // LANES):
        part = query_slope[lanes_of(chunk_at)].T * HEAD**-0.5
        query_low[:, lanes_of(chunk_at)] = turned(part, cosine[...], -sine[...]).astype(BF16)


def pairs_back_kernel(*refs):
    *summands, cosine, sine, low = refs
    owned = sum(ref[...].astype(F32) for ref in summands)
    low[:, :LANES] = turned(owned[:, :LANES], cosine[...], -sine[...]).astype(BF16)
    low[:, LANES:] = owned[:, LANES:].astype(BF16)


def wide_marks(marks):
    return [
        jnp.broadcast_to(marks[:, tap : tap + 1], (marks.shape[0], LANES))
        for tap in range(KERNEL - 1)
    ]


def conv_total(inner, taps, table, wide, chunk):
    span = lanes_of(chunk)
    extended = inner[:, span].astype(F32)
    total = table[ROW_CONV : ROW_CONV + 1, span] + taps[KERNEL - 1 : KERNEL, span] * extended[HALO:]
    for tap in range(KERNEL - 1):
        moved = pltpu.roll(extended, KERNEL - 1 - tap, 0)[HALO:] * wide[tap]
        total = total + taps[tap : tap + 1, span] * moved
    return total


def triangle(count, strict=False, upper=False):
    row = lax.broadcasted_iota(jnp.int32, (count, count), 0)
    column = lax.broadcasted_iota(jnp.int32, (count, count), 1)
    if upper:
        row, column = column, row
    return (row > column if strict else row >= column).astype(F32)


def soft(values):
    return jnp.maximum(values, 0.0) + jnp.log1p(jnp.exp(-jnp.abs(values)))


def part_pieces(parts, pair):
    width = WIDTH // parts
    if width % LANES == 0:
        start = pair * LANES % width
        return [(pair * LANES // width, slice(start, start + LANES), slice(0, LANES))]
    pieces = []
    for half in range(2):
        column = pair * LANES + half * SSM_HEAD
        start = column % width
        pieces.append(
            (
                column // width,
                slice(start, start + SSM_HEAD),
                slice(half * SSM_HEAD, (half + 1) * SSM_HEAD),
            )
        )
    return pieces


ROW_CONV, ROW_GAIN, ROW_MIXER, ROW_SKIP, ROW_STEP, ROW_RATE, ROW_FEED = range(7)
MARK_ENTER, MARK_TAIL, MARK_SEGMENT = KERNEL - 1, KERNEL, KERNEL + 1


def mark_rows(position, segments, count):
    first = pl.multiple_of(position * count, LANES)
    here = segments[:, pl.ds(first, count)].astype(F32)
    before = segments[:, pl.ds(pl.multiple_of(jnp.maximum(first - count, 0), LANES), count)]
    before = jnp.where(position > 0, before.astype(F32), -1.0)
    both = jnp.concatenate([before, here], 1)
    rows = []
    for tap in range(KERNEL - 1):
        moved = pltpu.roll(jnp.broadcast_to(both, (8, 2 * count)), KERNEL - 1 - tap, 1)
        rows.append(flag(moved[:1, count:] == here))
    rows.append(flag(here == before[:, count - 1 :]))
    rows.append(flag(here == here[:, count - 1 :]))
    rows.append(here)
    rows += [jnp.zeros((1, count), F32)] * (8 - len(rows))
    return jnp.concatenate(rows, 0)


def hold_part(hold, pair, rows, value):
    for part, lanes, within in part_pieces(hold.shape[0], pair):
        hold[part, rows, lanes] = value[:, within]


def hold_all(hold, rows, values):
    width = hold.shape[2]
    for part in range(hold.shape[0]):
        hold[part, rows] = values[:, part * width : (part + 1) * width]


def hand_out(hold, at_x, targets):
    for k, target in enumerate(targets):
        target[...] = hold[lax.rem(at_x + k, len(targets))]


def picked(pieces, at_x, pair):
    xs = len(pieces)
    values = []
    for part, lanes, _ in part_pieces(xs, pair):
        value = pieces[0][:, lanes]
        for k in range(1, xs):
            value = jnp.where(lax.rem(at_x - k + xs, xs) == part, pieces[k][:, lanes], value)
        values.append(value)
    return values[0] if len(values) == 1 else jnp.concatenate(values, 1)


def flag(condition):
    return jnp.where(condition, 1.0, 0.0)


def wall_rows(high, middle, low):
    row = lax.broadcasted_iota(jnp.int32, (EXTRA, high.shape[1]), 0)
    return jnp.where(
        row == 0, high, jnp.where(row == 1, middle, jnp.where(row == 2, low, 0.0))
    ).astype(BF16)


def ahead(forward, one, other):
    return one < other if forward else one > other


def mixed(flags, rows, width):
    total = jnp.zeros((1, width), F32)
    for chosen, row in zip(flags, rows):
        total = total + row * chosen
    return jnp.exp(total)


class Endings:
    def __init__(self, segments, count):
        self.segments, self.count = segments, count

    def __getitem__(self, index):
        return self.segments[index * self.count + self.count - 1]


def level_kernel(forward, xs, count, position, segments, *refs):
    pieces = refs[:xs]
    if forward:
        total_out, walls = refs[xs:]
    else:
        walls, total_out = refs[xs:]
    at_z, at_x = position[0] // xs, lax.rem(position[0], xs)
    endings = Endings(segments, count)
    width = pieces[0].shape[1]
    places = [lax.rem(at_x - k + xs, xs) for k in range(xs)]
    if forward:
        rows = []
        for k in range(xs):
            rows.append(jnp.sum(pieces[k][STATE:].astype(F32), 0, keepdims=True))
            walls[k : k + 1] = rows[k]
        walls[xs:] = jnp.zeros((WALLS - xs, width), F32)
        border = endings[at_z * xs + xs - 1]
    else:
        rows = [walls[k : k + 1] for k in range(xs)]
        border = endings[jnp.maximum(at_z * xs - 1, 0)]
    total = jnp.zeros((STATE, width), F32)
    for k in range(xs):
        index = at_z * xs + places[k]
        reached = endings[index if forward else jnp.maximum(index - 1, 0)] == border
        flags = [flag(ahead(forward, places[k], places[m])) for m in range(xs)]
        total = total + pieces[k][:STATE].astype(F32) * (
            mixed(flags, rows, width) * flag(reached)
        )
    total_out[:STATE] = total.astype(BF16)
    if forward:
        whole = sum(rows)
        high = whole.astype(BF16).astype(F32)
        middle = (whole - high).astype(BF16).astype(F32)
        total_out[STATE:] = wall_rows(high, middle, whole - high - middle)


def arrival_kernel(forward, xs, zs, count, position, segments, *refs):
    pieces = refs[:xs]
    totals = refs[xs : xs + zs - 1]
    walls = refs[xs + zs - 1]
    if forward:
        own, *results, level_walls = refs[xs + zs :]
    else:
        level_walls, *results = refs[xs + zs :]
    at_z, at_x = position[0] // xs, lax.rem(position[0], xs)
    endings = Endings(segments, count)
    width = pieces[0].shape[1]
    x_at = [lax.rem(at_x - k + xs, xs) for k in range(xs)]
    z_at = [lax.rem(at_z - k + zs, zs) for k in range(zs)]
    rows = [walls[k : k + 1] for k in range(xs)]
    if forward:
        levels = [jnp.sum(own[STATE:].astype(F32), 0, keepdims=True)]
        for total in totals:
            levels.append(jnp.sum(total[STATE:].astype(F32), 0, keepdims=True))
        for k in range(zs):
            level_walls[k : k + 1] = levels[k]
        level_walls[zs:] = jnp.zeros((WALLS - zs, width), F32)
        border = endings[jnp.maximum(at_z * xs - 1, 0)]
    else:
        levels = [level_walls[k : k + 1] for k in range(zs)]
        border = endings[at_z * xs + xs - 1]
    outside = jnp.zeros((STATE, width), F32)
    for k in range(1, zs):
        far = endings[z_at[k] * xs + xs - 1 if forward else jnp.maximum(z_at[k] * xs - 1, 0)]
        reached = ahead(forward, z_at[k], at_z) & (far == border)
        flags = [
            flag(ahead(forward, z_at[k], z_at[m]) & ahead(forward, z_at[m], at_z))
            for m in range(zs)
        ]
        outside = outside + totals[k - 1][:STATE].astype(F32) * (
            mixed(flags, levels, width) * flag(reached)
        )
    for r in range(xs):
        target = lax.rem(at_x + r, xs)
        index = at_z * xs + target
        edge = endings[jnp.maximum(index - 1, 0) if forward else index]
        flags = [flag(ahead(forward, x_at[m], target)) for m in range(xs)]
        total = outside * (mixed(flags, rows, width) * flag(edge == border))
        for k in range(xs):
            source = at_z * xs + x_at[k]
            far = endings[source if forward else jnp.maximum(source - 1, 0)]
            reached = ahead(forward, x_at[k], target) & (far == edge)
            flags = [
                flag(ahead(forward, x_at[k], x_at[m]) & ahead(forward, x_at[m], target))
                for m in range(xs)
            ]
            total = total + pieces[k][:STATE].astype(F32) * (
                mixed(flags, rows, width) * flag(reached)
            )
        results[r][...] = total.astype(BF16)


def dealt(place, parts):
    return (parts[0],) + tuple(
        place.turn(part, "x", k) for k, part in enumerate(parts[1:], start=1)
    )


def levels_met(place, total):
    return tuple(place.turn(total, "z", k) for k in range(1, place.sizes["z"]))


def level(place, pieces, position, segments, count):
    xs, width = place.sizes["x"], pieces[0].shape[1]
    return local_call(
        functools.partial(level_kernel, True, xs, count),
        [((STATE + EXTRA, width), BF16), ((WALLS, width), F32)],
        (position, segments, *pieces),
        "level",
        smem=(0, 1),
    )


def level_back(place, pieces, walls, position, segments, count):
    xs, width = place.sizes["x"], pieces[0].shape[1]
    return local_call(
        functools.partial(level_kernel, False, xs, count),
        [((STATE, width), BF16)],
        (position, segments, *pieces, walls),
        "level_back",
        smem=(0, 1),
    )[0]


def arrival(place, pieces, totals, walls, total, position, segments, count):
    xs, zs, width = place.sizes["x"], place.sizes["z"], pieces[0].shape[1]
    *results, level_walls = local_call(
        functools.partial(arrival_kernel, True, xs, zs, count),
        [((STATE, width), BF16)] * xs + [((WALLS, width), F32)],
        (position, segments, *pieces, *totals, walls, total),
        "arrival",
        smem=(0, 1),
    )
    return tuple(results), level_walls


def arrival_back(place, pieces, totals, walls, level_walls, position, segments, count):
    xs, zs, width = place.sizes["x"], place.sizes["z"], pieces[0].shape[1]
    return tuple(
        local_call(
            functools.partial(arrival_kernel, False, xs, zs, count),
            [((STATE, width), BF16)] * xs,
            (position, segments, *pieces, *totals, walls, level_walls),
            "arrival_back",
            smem=(0, 1),
        )
    )


def prep_kernel(
    xs, position, halo, normed, table, inner_w, step_w, taps, segments,
    inner, raw, channels, scaled, inflow, readout, steps, logs, logs_turned, marks, marks_turned,
    factor, *refs,
):
    states, (extended, hold, selector, lengths, tails, weighted) = refs[:xs], refs[xs:]
    count, width = normed.shape
    at_x = lax.rem(position[0], xs)
    marks_turned[...] = mark_rows(position[0], segments, count)
    marks[...] = marks_turned[...].T
    values = halo[...].astype(F32)
    scale = lax.rsqrt(jnp.mean(values * values, -1, keepdims=True) + EPS)
    extended[:HALO] = (values * scale * table[ROW_GAIN : ROW_GAIN + 1, :width]).astype(BF16)
    extended[HALO:] = normed[...]
    raw[...] = jnp.zeros(raw.shape, F32)
    raw[:, :SSM_HEADS] = dot_lanes(normed[...], step_w[...])
    head_lanes(selector)
    chunks = range(PAIRS + 2)
    for chunk in reversed(chunks):
        span = lanes_of(chunk)
        inner[:, span] = dot(extended[...], inner_w[:, span]).astype(BF16)
    steps[...] = soft(raw[...] + table[ROW_STEP : ROW_STEP + 1, :LANES])
    logs[...] = precise(triangle(count), steps[...] * table[ROW_RATE : ROW_RATE + 1, :LANES])
    logs_turned[...] = logs[...].T
    ending = logs[count - 1 : count]
    tail = jnp.exp(ending - logs[...]) * marks[:, MARK_TAIL : MARK_TAIL + 1]
    lengths[...] = dot(halves(steps[...]), selector[...])
    tails[...] = dot(halves(tail), selector[...])
    wide = wide_marks(marks)
    for chunk in reversed(chunks):
        span = lanes_of(chunk)
        total = conv_total(inner, taps, table, wide, chunk)
        gate = jax.nn.sigmoid(total)
        factor[:, span] = (gate * (1.0 + total * (1.0 - gate))).astype(BF16)
        value = total * gate
        if chunk == PAIRS + 1:
            readout[...] = value.astype(BF16)
        elif chunk == PAIRS:
            inflow[...] = value.astype(BF16)
        else:
            channels[:, span] = value
            value = value * lengths[:, span]
            scaled[:, span] = value.astype(BF16)
            weighted[:, span] = (value * tails[:, span]).astype(BF16)
    hold_all(hold, slice(0, STATE), dot(inflow[...].T, weighted[...]).astype(BF16))
    for pair in range(PAIRS):
        whole = spread_pair(ending, pair)
        high = whole.astype(BF16).astype(F32)
        middle = (whole - high).astype(BF16).astype(F32)
        wall = wall_rows(high, middle, whole - high - middle)
        hold_part(hold, pair, slice(STATE, STATE + EXTRA), wall)
    hand_out(hold, at_x, states)


def decay_kernel_parts(marks, marks_turned, bias):
    count = marks.shape[0]
    row = lax.broadcasted_iota(jnp.int32, (count, count), 0)
    column = lax.broadcasted_iota(jnp.int32, (count, count), 1)
    span = slice(MARK_SEGMENT, MARK_SEGMENT + 1)
    inside = (marks[:, span] == marks_turned[span]) & (row >= column)
    bias[...] = jnp.where(inside, 0.0, NEG)


IN_STEP = 4


def inner_kernel(logs, logs_turned, marks, marks_turned, inflow, readout, scaled, result, bias, meet):
    count = logs.shape[0]
    step = pl.program_id(0)

    @pl.when(step == 0)
    def _():
        decay_kernel_parts(marks, marks_turned, bias)
        meet[...] = dot_lanes(readout[...], inflow[...])

    columns = pltpu.roll(logs[...], (LANES - IN_STEP * step) % LANES, 1)
    half = count // 2
    for k in range(IN_STEP):
        across = logs_turned[pl.ds(IN_STEP * step + k, 1), :]
        span = slice(k * SSM_HEAD, (k + 1) * SSM_HEAD)
        for top, width in ((0, half), (half, count)):
            rows = slice(top, top + half)
            gap = columns[rows, k : k + 1] - across[:, :width] + bias[rows, :width]
            mixing = (jnp.exp(gap) * meet[rows, :width]).astype(BF16)
            result[rows, span] = dot(mixing, scaled[:width, span])


def inner_back_kernel(
    logs,
    logs_turned,
    marks,
    marks_turned,
    inflow,
    readout,
    scaled,
    slope,
    scaled_slope,
    inflow_slope,
    readout_slope,
    bias,
    meet,
    meet_slope,
):
    count = logs.shape[0]
    step = pl.program_id(0)

    @pl.when(step == 0)
    def _():
        decay_kernel_parts(marks, marks_turned, bias)
        meet[...] = dot_lanes(readout[...], inflow[...])
        meet_slope[...] = jnp.zeros(meet_slope.shape, F32)

    columns = pltpu.roll(logs[...], (LANES - IN_STEP * step) % LANES, 1)
    half = count // 2
    for top, width in ((0, half), (half, count)):
        rows = slice(top, top + half)
        gathered = jnp.zeros((half, width), F32)
        for k in range(IN_STEP):
            across = logs_turned[pl.ds(IN_STEP * step + k, 1), :]
            span = slice(k * SSM_HEAD, (k + 1) * SSM_HEAD)
            gap = columns[rows, k : k + 1] - across[:, :width] + bias[rows, :width]
            decay = jnp.exp(gap)
            mixing = (decay * meet[rows, :width]).astype(BF16)
            gathered = gathered + decay * dot_lanes(slope[rows, span], scaled[:width, span])
            part = dot_rows(mixing, slope[rows, span])
            if top:
                scaled_slope[:half, span] = scaled_slope[:half, span] + part[:half]
                scaled_slope[half:, span] = part[half:]
            else:
                scaled_slope[:half, span] = part
        meet_slope[rows, :width] = meet_slope[rows, :width] + gathered

    @pl.when(step == SSM_HEADS // IN_STEP - 1)
    def _():
        low = meet_slope[...].astype(BF16)
        inflow_slope[...] = dot_rows(low, readout[...])
        readout_slope[...] = dot(low, inflow[...])


def inner_call(kernel, fixed, moving, outs, fixed_outs, name, scratch):
    count = fixed[0].shape[0]
    steps = SSM_HEADS // IN_STEP
    width = IN_STEP * SSM_HEAD
    held = [pl.BlockSpec(a.shape, lambda j: (0, 0)) for a in fixed]
    passing = pl.BlockSpec((count, width), lambda j: (0, j))
    return pl.pallas_call(
        kernel,
        grid=(steps,),
        in_specs=held + [passing] * len(moving),
        out_specs=[passing] * len(outs)
        + [pl.BlockSpec(shape, lambda j: (0, 0)) for shape, _ in fixed_outs],
        out_shape=[jax.ShapeDtypeStruct((count, WIDTH), kind) for kind in outs]
        + [jax.ShapeDtypeStruct(shape, kind) for shape, kind in fixed_outs],
        scratch_shapes=[pltpu.VMEM((count, count), F32)] * scratch,
        compiler_params=pltpu.CompilerParams(vmem_limit_bytes=8 * 1024 * 1024),
        cost_estimate=pl.CostEstimate(flops=0, bytes_accessed=0, transcendentals=0),
        name=name,
    )(*fixed, *moving)


def entering_kernel(
    xs, position, inner_part, readout, logs, marks, channels, gating, table, low_input, branch,
    feed_gain, mixer_w, gate_w, up_w, *refs,
):
    pieces, outs = refs[:xs], refs[xs:]
    tail, scanned, entering, mixed_sum, feed_low, gate_raw, up_raw, activated, *outs = outs
    gated, selector, wide, mixer_here, gate_here, up_here, arrived = outs
    copies = [
        pltpu.make_async_copy(source, target, arrived.at[k])
        for k, (source, target) in enumerate(
            ((mixer_w, mixer_here), (gate_w, gate_here), (up_w, up_here))
        )
    ]
    for copy in copies:
        copy.start()
    at_x = lax.rem(position[0], xs)
    count = logs.shape[0]
    enter = halves(jnp.exp(logs[...]) * marks[:, MARK_ENTER : MARK_ENTER + 1])
    head_lanes(selector)
    for pair in range(PAIRS):
        entering[:, lanes_of(pair)] = picked(pieces, at_x, pair)
    wide[...] = dot(enter, selector[...])
    gated[...] = dot(readout[...], entering[...])
    square = jnp.zeros((count, LANES), F32)
    for pair in range(PAIRS):
        span = lanes_of(pair)
        full = inner_part[:, span] + gated[:, span] * wide[:, span]
        scanned[:, span] = full
        gate = gating[:, span]
        skip = table[ROW_SKIP : ROW_SKIP + 1, span]
        full = (full + skip * channels[:, span]) * (gate * jax.nn.sigmoid(gate))
        gated[:, span] = full
        square = square + full * full
    scale = lax.rsqrt(jnp.sum(square, -1, keepdims=True) / WIDTH + EPS)
    scale = jnp.broadcast_to(scale, (count, LANES))
    for pair in range(PAIRS):
        span = lanes_of(pair)
        gain = table[ROW_MIXER : ROW_MIXER + 1, span]
        tail[:, span] = (gated[:, span] * scale * gain).astype(BF16)
    copies[0].wait()
    mixed = low_input[...].astype(F32) + branch[...] + dot(tail[...], mixer_here[...])
    mixed_sum[...] = mixed
    scale = lax.rsqrt(jnp.mean(mixed * mixed, -1, keepdims=True) + EPS)
    feed_low[...] = (mixed * scale * feed_gain[...].reshape(1, mixed.shape[1])).astype(BF16)
    copies[1].wait()
    copies[2].wait()
    for start in range(0, gate_raw.shape[1], 512):
        span = slice(start, start + 512)
        gate = dot(feed_low[...], gate_here[:, span])
        up = dot(feed_low[...], up_here[:, span])
        gate_raw[:, span] = gate
        up_raw[:, span] = up
        activated[:, span] = (gate * jax.nn.sigmoid(gate) * up).astype(BF16)


def tail_back_kernel(
    xs, position, branch, mixer_w, scanned, channels, gating, table, logs, marks, readout,
    scanned_slope, gating_slope, sums, *refs,
):
    states, (gated, hold, selector, wide, weighted, slope) = refs[:xs], refs[xs:]
    for start in range(0, WIDTH, 512):
        span = slice(start, start + 512)
        slope[:, span] = dot_lanes(branch[...], mixer_w[span])
    at_x = lax.rem(position[0], xs)
    count = logs.shape[0]
    enter = halves(jnp.exp(logs[...]) * marks[:, MARK_ENTER : MARK_ENTER + 1])
    head_lanes(selector)
    wide[...] = dot(enter, selector[...])
    square = jnp.zeros((count, LANES), F32)
    cross = jnp.zeros((count, LANES), F32)
    for pair in range(PAIRS):
        span = lanes_of(pair)
        gate = gating[:, span]
        full = scanned[:, span] + table[ROW_SKIP : ROW_SKIP + 1, span] * channels[:, span]
        full = full * (gate * jax.nn.sigmoid(gate))
        gated[:, span] = full
        gain = table[ROW_MIXER : ROW_MIXER + 1, span]
        square = square + full * full
        cross = cross + full * slope[:, span] * gain
    scale = lax.rsqrt(jnp.sum(square, -1, keepdims=True) / WIDTH + EPS)
    cross = jnp.sum(cross, -1, keepdims=True) / WIDTH * scale * scale * scale
    scale = jnp.broadcast_to(scale, (count, LANES))
    cross = jnp.broadcast_to(cross, (count, LANES))
    for pair in range(PAIRS):
        span = lanes_of(pair)
        gate = gating[:, span]
        sigmoid = jax.nn.sigmoid(gate)
        back = slope[:, span]
        value = gated[:, span]
        sums[0:1, span] = jnp.sum(back * value * scale, 0, keepdims=True)
        back = back * table[ROW_MIXER : ROW_MIXER + 1, span] * scale - value * cross
        held = channels[:, span]
        full = scanned[:, span] + table[ROW_SKIP : ROW_SKIP + 1, span] * held
        gating_slope[:, span] = (
            back * full * sigmoid * (1.0 + gate * (1.0 - sigmoid))
        ).astype(BF16)
        back = back * (gate * sigmoid)
        sums[1:2, span] = jnp.sum(back * held, 0, keepdims=True)
        scanned_slope[:, span] = back.astype(BF16)
        weighted[:, span] = (back * wide[:, span]).astype(BF16)
    hold_all(hold, slice(0, STATE), dot(readout[...].T, weighted[...]).astype(BF16))
    hand_out(hold, at_x, states)
    sums[2:8] = jnp.zeros((6, WIDTH), F32)


def leaving_kernel(
    xs, position, entering, scanned, scanned_slope, scaled, channels, scaled_slope,
    inflow, readout, inflow_part, readout_part, steps, raw, logs, marks, inner, factor, taps, table,
    *refs,
):
    pieces, outs = refs[:xs], refs[xs:]
    inner_low, edges, conv_sums, raw_slope, small, conv_slope, selector, *outs = outs
    low, outer, lengths, tails, enters, first, second, third, fourth, fifth = outs
    at_x = lax.rem(position[0], xs)
    rates = table[ROW_RATE : ROW_RATE + 1, :LANES]
    count = logs.shape[0]
    ending = logs[count - 1 : count]
    head_lanes(selector)
    stepped = steps[...]
    for pair in range(PAIRS):
        low[:, lanes_of(pair)] = picked(pieces, at_x, pair)
    outer[...] = dot(inflow[...], low[...])
    lengths[...] = dot(halves(stepped), selector[...])
    tail = jnp.exp(ending - logs[...]) * marks[:, MARK_TAIL : MARK_TAIL + 1]
    tails[...] = dot(halves(tail), selector[...])
    enter = jnp.exp(logs[...]) * marks[:, MARK_ENTER : MARK_ENTER + 1]
    enters[...] = dot(halves(enter), selector[...])
    through = jnp.zeros((8, LANES), F32)
    for pair in range(PAIRS):
        span = lanes_of(pair)
        wide = scanned_slope[:, span].astype(F32)
        held = channels[:, span]
        short = scaled[:, span].astype(F32)
        tail = tails[:, span]
        part = outer[:, span] * tail
        within = scaled_slope[:, span]
        both = within + part
        split_into(first, span, wide * scanned[:, span] - short * within)
        split_into(second, span, short * part)
        split_into(third, span, held * both)
        fourth[:, span] = (short * tail).astype(BF16)
        fifth[:, span] = (wide * enters[:, span]).astype(BF16)
        skip = table[ROW_SKIP : ROW_SKIP + 1, span]
        conv_slope[:, span] = both * lengths[:, span] + skip * wide
        kept = low[:, span].astype(F32) * entering[:, span].astype(F32)
        kept = jnp.sum(kept, 0, keepdims=True) * jnp.exp(spread_pair(ending, pair))
        kept = halves(jnp.broadcast_to(kept, (8, LANES)))
        chosen = selector[:LANES, span]
        through = through + dot_lanes(kept, jnp.concatenate([chosen, chosen], 1))
    inside, outward = head_sums(first, selector), head_sums(second, selector)
    direct = head_sums(third, selector)
    inflow_slope = inflow_part[...] + dot_lanes(fourth[...], low[...])
    readout_slope = readout_part[...] + dot_lanes(fifth[...], entering[...])
    conv_slope[:, lanes_of(PAIRS)] = inflow_slope
    conv_slope[:, lanes_of(PAIRS + 1)] = readout_slope
    enter_last = marks[count - 1 :, MARK_ENTER : MARK_ENTER + 1]
    along = (
        precise(triangle(count, upper=True), inside)
        + precise(triangle(count, strict=True), outward)
        + through[:1] * enter_last
    )
    step_slope = direct + rates * along
    step_slope = step_slope * jax.nn.sigmoid(raw[...] + table[ROW_STEP : ROW_STEP + 1, :LANES])
    raw_slope[...] = step_slope.astype(BF16)
    small[0:1] = jnp.sum(step_slope, 0, keepdims=True)
    small[1:2] = rates * jnp.sum(stepped * along, 0, keepdims=True)
    small[2:8] = jnp.zeros((6, LANES), F32)
    blank = jnp.zeros((HALO, LANES), F32)
    marked = wide_marks(marks)
    for chunk in range(PAIRS + 2):
        span = lanes_of(chunk)
        extended = inner[:, span].astype(F32)
        slope = conv_slope[:, span] * factor[:, span].astype(F32)
        spread = jnp.zeros((HALO + count, LANES), F32)
        for tap in range(KERNEL):
            part = slope * marked[tap] if tap < KERNEL - 1 else slope
            part = jnp.concatenate([blank, part], 0)
            if tap < KERNEL - 1:
                part = pltpu.roll(part, HALO + count - (KERNEL - 1 - tap), 0)
            conv_sums[tap : tap + 1, span] = jnp.sum(part * extended, 0, keepdims=True)
            spread = spread + part * taps[tap : tap + 1, span]
        conv_sums[KERNEL : KERNEL + 1, span] = jnp.sum(slope, 0, keepdims=True)
        conv_sums[KERNEL + 1 :, span] = jnp.zeros((8 - KERNEL - 1, LANES), F32)
        inner_low[:, span] = spread[HALO:].astype(BF16)
        edges[:HALO, span] = spread[:HALO]
        edges[HALO:, span] = spread[count:]


PACK_ROWS = 48


def unit_back_kernel(slope, down_w, gate_raw, up_raw, gate_low, up_low):
    for start in range(0, gate_raw.shape[1], 512):
        span = slice(start, start + 512)
        back = dot_lanes(slope[...], down_w[span])
        gate = gate_raw[:, span]
        sigmoid = jax.nn.sigmoid(gate)
        up_low[:, span] = (back * (gate * sigmoid)).astype(BF16)
        back = back * up_raw[:, span]
        gate_low[:, span] = (back * (sigmoid * (1.0 + gate * (1.0 - sigmoid)))).astype(BF16)


def feed_back_kernel(
    gate_low, up_low, gate_w, up_w, mixed_sum, slope, gain, mixed_slope, branch_low, sums
):
    values = mixed_sum[...]
    count, width = values.shape
    scale = lax.rsqrt(jnp.mean(values * values, -1, keepdims=True) + EPS)
    back = dot_lanes(gate_low[...], gate_w[...]) + dot_lanes(up_low[...], up_w[...])
    sums[...] = jnp.broadcast_to(jnp.sum(back * values * scale, 0, keepdims=True), sums.shape)
    back = back * gain[...].reshape(1, width)
    cross = jnp.mean(back * values, -1, keepdims=True) * scale * scale * scale
    whole = slope[...].astype(F32) + back * scale - values * cross
    mixed_slope[...] = whole
    branch_low[...] = whole.astype(BF16)


def finish_kernel(
    gating_low, query_low, inner_low, pair_low, gating_w, query_w, inner_w, key_w, value_w, step_w,
    low_input, table, mixed_slope, raw_slope, normed, tail_sums, conv_sums, small, feed,
    input_gradient, packed,
):
    normed_slope = (
        dot_lanes(gating_low[...], gating_w[...])
        + dot_lanes(query_low[...], query_w[...])
        + dot_lanes(inner_low[...], inner_w[...])
        + dot_lanes(pair_low[:, :LANES], key_w[...])
        + dot_lanes(pair_low[:, LANES:], value_w[...])
        + dot(raw_slope[:, :SSM_HEADS], step_w[...])
    )
    values = low_input[...].astype(F32)
    width = values.shape[1]
    scale = lax.rsqrt(jnp.mean(values * values, -1, keepdims=True) + EPS)
    slope = normed_slope
    packed[SSM_HEADS : SSM_HEADS + 1] = jnp.sum(slope * values * scale, 0, keepdims=True)
    slope = slope * table[ROW_GAIN : ROW_GAIN + 1, :width]
    cross = jnp.mean(slope * values, -1, keepdims=True) * scale * scale * scale
    input_gradient[...] = mixed_slope[...] + slope * scale - values * cross
    packed[:SSM_HEADS] = dot_rows(raw_slope[...], normed[...])[:SSM_HEADS]
    packed[SSM_HEADS + 1 : SSM_HEADS + 2] = feed[:1]
    packed[SSM_HEADS + 2 :] = jnp.zeros((PACK_ROWS - SSM_HEADS - 2, width), F32)
    row = SSM_HEADS + 2
    for source, rows in ((tail_sums, 2), (small, 2), (conv_sums, KERNEL + 1)):
        for index in range(rows):
            for start in range(0, source.shape[1], width):
                stop = min(start + width, source.shape[1])
                packed[row : row + 1, : stop - start] = source[index : index + 1, start:stop]
                row += 1


def unpack_kernel(packed, step, gain, feed, mixer_gain, skip, step_bias, decay, conv, conv_bias):
    width = packed.shape[1]
    step[...] = packed[:SSM_HEADS].T
    row = SSM_HEADS

    def taken(size):
        nonlocal row
        pieces = []
        for start in range(0, size, width):
            pieces.append(packed[row : row + 1, : min(width, size - start)])
            row += 1
        return pieces[0] if len(pieces) == 1 else jnp.concatenate(pieces, 1)

    gain[...] = taken(width).reshape(width)
    feed[...] = taken(width).reshape(width)
    mixer_gain[...] = taken(WIDTH).reshape(WIDTH)
    lanes = taken(WIDTH)
    head = lax.broadcasted_iota(jnp.int32, (1, LANES), 1)
    sums = jnp.zeros((1, LANES), F32)
    for index in range(SSM_HEADS):
        part = lanes[:, index * SSM_HEAD : (index + 1) * SSM_HEAD]
        sums = jnp.where(head == index, jnp.sum(part, 1, keepdims=True), sums)
    skip[...] = sums[:, :SSM_HEADS].reshape(SSM_HEADS)
    step_bias[...] = taken(LANES)[:, :SSM_HEADS].reshape(SSM_HEADS)
    decay[...] = taken(LANES)[:, :SSM_HEADS].reshape(SSM_HEADS)
    for tap in range(KERNEL):
        conv[tap : tap + 1] = taken(conv.shape[1])
    conv_bias[...] = taken(conv.shape[1]).reshape(conv.shape[1])


def all_sum(place, shard, axes):
    for name in axes:
        axis = name[0] if name[0] == "z" else name
        bit = 2 if name == "zh" else 1
        while bit < (2 if name == "zl" else place.sizes[axis]):
            low = shard.astype(BF16)
            shard = low.astype(F32) + place.swap(low, axis, bit).astype(F32)
            bit *= 2
    return shard


def joint_kernel(xs, ys, widths, left, left_sib, right, right_sib, *outs):
    rows = left.shape[0] // len(widths)
    part = rows // (xs * ys)
    start = offset = 0
    for section, width in enumerate(widths):
        span = slice(section * rows, (section + 1) * rows)
        half = width // 2
        tile = next(t for t in (512, 384, 256, 128) if half % t == 0)
        for first in range(2):
            targets = outs[xs:] if first else outs[:xs]
            for column in range(0, half, tile):
                source = slice(start + first * half + column, start + first * half + column + tile)
                total = dot(left[span], right[:, source]) + dot(left_sib[span], right_sib[:, source])
                total = total.astype(BF16)
                into = slice(offset + column, offset + column + tile)
                for x in range(xs):
                    for y in range(ys):
                        piece = total[(x * ys + y) * part : (x * ys + y + 1) * part]
                        if first:
                            targets[y][x * part : (x + 1) * part, into] = piece
                        else:
                            targets[x][y * part : (y + 1) * part, into] = piece
        start += width
        offset += half


def joint_gradient(place, left, right, left_sib, right_sib, widths):
    sections = len(widths)
    rows, tokens = left.shape[0] // sections, left.shape[1]
    width = sum(widths)
    xs, ys = place.sizes["x"], place.sizes["y"]
    half = width // 2
    shapes = [(rows // xs, half)] * xs + [(rows // ys, half)] * ys
    outs = local_call(
        functools.partial(joint_kernel, xs, ys, widths),
        [(shape, BF16) for shape in shapes],
        (left, left_sib, right, right_sib),
        "joint_gradient",
    )
    return outs[:xs], outs[xs:]


def arranged(order, left):
    return lax.dot_general(
        order, left, (((1,), (1,)), ((), ())), preferred_element_type=jnp.float32
    ).astype(jnp.bfloat16)


def own_half(ordered):
    return ordered[: ordered.shape[0] // CORES]


def other_half(ordered):
    return ordered[ordered.shape[0] // CORES :]


def together(*values):
    return lax.optimization_barrier(values)


def fold_kernel(counts, splits, merged, *refs):
    at = 0
    outs = refs[sum(counts) :]
    for block, count in enumerate(counts):
        total = refs[at][...].astype(F32)
        for ref in refs[at + 1 : at + count]:
            total = total + ref[...].astype(F32)
        at += count
        low = total.astype(BF16)
        rows = low.shape[-2] // splits[block]
        for k in range(splits[block]):
            piece = low[..., k * rows : (k + 1) * rows, :]
            if merged:
                outs[k][block] = piece
            else:
                outs[sum(splits[:block]) + k][...] = piece


def fold(blocks, splits, merged):
    flat = [a for block in blocks for a in block]
    shape = flat[0].shape
    columns = shape[-1]
    tile = max(t for t in range(LANES, 1025, LANES) if columns % t == 0 and t <= columns // 2)

    def spec(full):
        lead = (0,) * (len(full) - 1)
        return pl.BlockSpec(full[:-1] + (tile,), lambda j: lead + (j,))

    if merged:
        outs = [(len(blocks), shape[0] // splits[0], columns)] * splits[0]
    else:
        outs = []
        for block, cuts in zip(blocks, splits):
            full = block[0].shape
            outs += [full[:-2] + (full[-2] // cuts, columns)] * cuts
    return pl.pallas_call(
        functools.partial(fold_kernel, [len(b) for b in blocks], splits, merged),
        grid=(columns // tile,),
        in_specs=[spec(a.shape) for a in flat],
        out_specs=[spec(full) for full in outs],
        out_shape=[jax.ShapeDtypeStruct(full, BF16) for full in outs],
        compiler_params=pltpu.CompilerParams(vmem_limit_bytes=12 * 1024 * 1024),
        cost_estimate=pl.CostEstimate(flops=0, bytes_accessed=0, transcendentals=0),
        name="fold",
    )(*flat)


class Shares:
    ORDERS = (("x", "y"), ("y", "x"))

    def __init__(self, place, lefts, rights):
        self.place = place
        self.widths = [sum(r.shape[1] for r in section) for section in rights]
        self.columns = [[r.shape[1] for r in section] for section in rights]
        flat = [r for section in rights for r in section]
        self.right = jnp.concatenate(flat, 1) if len(flat) > 1 else flat[0]
        self.lefts = lefts

    def to_core(self):
        return self.right

    def go_core(self, sent):
        return self.place.turn(sent, "core", 1)

    def join(self, left_siblings, right_sibling):
        left, sibling = (
            (pieces[0] if len(pieces) == 1 else jnp.concatenate(pieces, 0))
            for pieces in ([own_half(left) for left in self.lefts], left_siblings)
        )
        self.pieces = joint_gradient(
            self.place, left, self.right, sibling, right_sibling, self.widths
        )
        return tuple(tuple(pieces[1:]) for pieces in self.pieces)

    def go(self, sent, stage):
        return tuple(
            tuple(self.place.turn(piece, order[stage], k + 1) for k, piece in enumerate(pieces))
            for pieces, order in zip(sent, self.ORDERS)
        )

    def to_second(self, arrived):
        splits = [self.place.sizes[order[1]] for order in self.ORDERS]
        blocks = [(self.pieces[half][0],) + arrived[half] for half in range(2)]
        outs = fold(blocks, splits, False)
        self.kept = (outs[0], outs[splits[0]])
        return tuple(outs[1 : splits[0]]), tuple(outs[splits[0] + 1 :])

    def to_third(self, arrived):
        blocks = [(self.kept[half],) + arrived[half] for half in range(2)]
        self.kept, sent = fold(blocks, (2, 2), True)
        return sent

    def go_third(self, sent):
        return self.place.swap(sent, "z", 1)

    def to_fourth(self, arrived):
        self.kept, sent = fold([(self.kept, arrived)], (2,), False)
        return sent

    def go_fourth(self, sent):
        return self.place.swap(sent, "z", 2)

    def to_owners(self, arrived):
        cuts = self.place.sizes["z"]
        blocks = [(self.kept[half],) + arrived[half] for half in range(2)]
        self.kept, *sent = fold(blocks, (cuts, cuts), True)
        return tuple(sent)

    def go_owners(self, sent):
        return tuple(
            self.place.swap(piece, "z", k // 2 + 2 * (k % 2))
            for k, piece in enumerate(sent, start=1)
        )

    def split(self, arrived, widths):
        rows = self.kept.shape[1]
        summands = (self.kept,) + tuple(arrived)
        return local_call(
            functools.partial(split_kernel, len(summands)),
            [((rows, w), F32) for w in widths],
            summands,
            "split",
        )

    def shares(self, *arrived):
        total = self.kept.astype(F32)
        for piece in arrived:
            total = total + piece.astype(F32)
        shares = []
        offset = 0
        for width, columns in zip(self.widths, self.columns):
            section = jnp.concatenate(
                [total[half, :, offset : offset + width // 2] for half in range(2)], 1
            )
            offset += width // 2
            start = 0
            for w in columns:
                shares.append(section[:, start : start + w])
                start += w
        return shares


def split_kernel(count, *refs):
    total = sum(ref[...].astype(F32) for ref in refs[:count])
    half = total.shape[2]
    start = 0
    for out in refs[count:]:
        stop = start + out.shape[1]
        for k in range(2):
            low, high = max(start, k * half), min(stop, (k + 1) * half)
            if low < high:
                out[:, low - start : high - start] = total[k, :, low - k * half : high - k * half]
        start = stop


class KeyOwners:
    def __init__(self, place, slopes):
        self.place = place
        self.paired = place.sizes["x"] == 2
        self.kept = slopes

    def to_first(self):
        if not self.paired:
            return self.kept
        half = self.kept.shape[0] // 2
        sent = self.kept[half:]
        self.kept = self.kept[:half]
        return sent

    def go(self, sent, stage):
        if not self.paired:
            if stage:
                return sent
            return lax.psum_scatter(sent, "seq", scatter_dimension=0, tiled=True)
        axis, bit = (("z", 1), ("z", 2), ("x", 1))[stage]
        return self.place.swap(sent, axis, bit)

    def to_next(self, arrived):
        if not self.paired:
            return arrived
        total = (self.kept.astype(F32) + arrived.astype(F32)).astype(BF16)
        half = total.shape[0] // 2
        self.kept = total[:half]
        return total[half:]

    def summands(self, arrived):
        return (self.kept, arrived) if self.paired else (arrived,)


def body(
    inputs,
    segments,
    cotangent,
    input_gain,
    query_weight,
    key_weight,
    value_weight,
    attention_weight,
    gating_weight,
    inner_weight,
    step_weight,
    step_bias,
    decay_log,
    skip_scale,
    conv_weight,
    conv_bias,
    mixer_gain,
    mixer_weight,
    feed_gain,
    gate_weight,
    up_weight,
    down_weight,
):
    place = Place()
    xs = place.sizes["x"]
    count, width = inputs.shape[1], inputs.shape[2]
    low_input = inputs[0]
    hidden = low_input.astype(F32)
    slope = cotangent[0]
    seg_row = segments[0]
    length = seg_row.shape[0]
    group, along = lax.axis_index("dp"), lax.axis_index("seq")
    position = along.reshape(1).astype(jnp.int32)
    inner_width = inner_weight.shape[1]
    part_width = WIDTH // xs

    halo, low_input = together(low_input[count - HALO :], low_input)
    halo = passed_along(halo, "seq", 1)
    cosine, sine = turn_tables(along * count, count)
    normed_low, pairs, table = local_call(
        front_kernel,
        [((count, width), BF16), ((count, 2 * LANES), BF16), ((8, inner_width), F32)],
        (
            low_input,
            key_weight,
            value_weight,
            cosine,
            sine,
            conv_bias,
            input_gain,
            mixer_gain,
            skip_scale,
            step_bias,
            decay_log,
        ),
        "front",
        alone=True,
    )
    near = jnp.concatenate([pairs] + [place.turn(pairs, "x", k) for k in range(1, xs)], 0)
    near, halo, normed_low = together(near, halo, normed_low)
    far = tuple(place.turn(near, "z", k) for k in range(1, place.sizes["z"]))
    step_turned = step_weight.T
    (
        inner,
        raw,
        channels,
        scaled,
        inflow,
        readout,
        steps,
        logs,
        logs_turned,
        marks,
        marks_turned,
        factor,
        *states,
    ) = local_call(
        functools.partial(prep_kernel, xs),
        [
            ((HALO + count, inner_width), BF16),
            ((count, LANES), F32),
            ((count, WIDTH), F32),
            ((count, WIDTH), BF16),
            ((count, STATE), BF16),
            ((count, STATE), BF16),
            ((count, LANES), F32),
            ((count, LANES), F32),
            ((LANES, count), F32),
            ((count, 8), F32),
            ((8, count), F32),
            ((count, inner_width), BF16),
        ]
        + [((STATE + EXTRA, part_width), BF16)] * xs,
        (position, halo, normed_low, table, inner_weight, step_turned, conv_weight, segments),
        "prepare",
        alone=True,
        scratch=[
            pltpu.VMEM((HALO + count, width), BF16),
            pltpu.VMEM((xs, STATE + EXTRA, part_width), BF16),
            pltpu.VMEM((2 * LANES, WIDTH), BF16),
            pltpu.VMEM((count, WIDTH), F32),
            pltpu.VMEM((count, WIDTH), F32),
            pltpu.VMEM((count, WIDTH), BF16),
        ],
        smem=(0,),
    )

    states, normed_low, group, along = together(tuple(states), normed_low, group, along)
    pieces = dealt(place, states)
    gating = product(normed_low, gating_weight)
    order = place.share_order(width, group, along)
    ordered = arranged(order, normed_low)
    pieces, gating, normed_low, order, ordered = together(
        pieces, gating, normed_low, order, ordered
    )
    total, walls = level(place, pieces, position, seg_row, count)

    total, normed_low, ordered, scaled = together(total, normed_low, ordered, scaled)
    totals = levels_met(place, total)
    fixed = (logs, logs_turned, marks, marks_turned, inflow, readout)
    (inner_part,) = inner_call(inner_kernel, fixed, (scaled,), (F32,), (), "inner", 2)

    ordered_sibling = place.turn(other_half(ordered), "core", 1)
    queries, attention_low, exact, spread, everything = local_call(
        functools.partial(attend_kernel, xs),
        [
            ((count, HEADS * HEAD), BF16),
            ((count, HEADS * HEAD), BF16),
            ((HEADS * HEAD, count), F32),
            ((HEADS, count), F32),
            ((length, 2 * LANES), BF16),
        ],
        (position, normed_low, query_weight, cosine, sine, segments, near, *far),
        "attend",
        slack=8,
        scratch=[
            pltpu.VMEM((HEADS, count), F32),
            pltpu.VMEM((HEADS, count), F32),
            pltpu.VMEM((HEADS * HEAD, count), F32),
        ],
        smem=(0,),
        far=tuple(range(6, 7 + len(far))),
        sems=(1 + len(far),),
    )
    totals, attention_low, ordered_sibling, inner_part, slope, order = together(
        totals, attention_low, ordered_sibling, inner_part, slope, order
    )
    results, level_walls = arrival(
        place, pieces, totals, walls, total, position, seg_row, count
    )

    results, attention_low, slope, order = together(results, attention_low, slope, order)
    pieces = dealt(place, results)
    attention_branch = product(attention_low, attention_weight)
    ordered_slope = arranged(order, slope)
    pieces, attention_branch, ordered_slope = together(pieces, attention_branch, ordered_slope)
    hidden_width = gate_weight.shape[1]
    (
        tail_low,
        scanned,
        entering,
        mixed_sum,
        feed_low,
        gate_raw,
        up_raw,
        activated_low,
    ) = local_call(
        functools.partial(entering_kernel, xs),
        [
            ((count, WIDTH), BF16),
            ((count, WIDTH), F32),
            ((STATE, WIDTH), BF16),
            ((count, width), F32),
            ((count, width), BF16),
            ((count, hidden_width), F32),
            ((count, hidden_width), F32),
            ((count, hidden_width), BF16),
        ],
        (
            position,
            inner_part,
            readout,
            logs,
            marks,
            channels,
            gating,
            table,
            low_input,
            attention_branch,
            feed_gain,
            mixer_weight,
            gate_weight,
            up_weight,
            *pieces,
        ),
        "entering",
        scratch=[
            pltpu.VMEM((count, WIDTH), F32),
            pltpu.VMEM((2 * LANES, WIDTH), BF16),
            pltpu.VMEM((count, WIDTH), F32),
            pltpu.VMEM(mixer_weight.shape, BF16),
            pltpu.VMEM(gate_weight.shape, BF16),
            pltpu.VMEM(up_weight.shape, BF16),
        ],
        sems=(3,),
        smem=(0,),
        far=(11, 12, 13),
    )

    down = Shares(place, (ordered_slope,), ((activated_low,),))
    sent, slope_half, gate_raw, up_raw, slope, feed_low, order = together(
        down.to_core(), other_half(ordered_slope), gate_raw, up_raw, slope, feed_low, order
    )
    arrived = down.go_core(sent)
    slope_sibling = place.turn(slope_half, "core", 1)
    gate_low, up_low = local_call(
        unit_back_kernel,
        [(gate_raw.shape, BF16), (up_raw.shape, BF16)],
        (slope, down_weight, gate_raw, up_raw),
        "unit_back",
    )
    ordered_feed = arranged(order, feed_low)
    arrived, slope_sibling, gate_low, up_low, ordered_feed = together(
        arrived, slope_sibling, gate_low, up_low, ordered_feed
    )
    sent = down.join([slope_sibling], arrived)

    gate = Shares(place, (ordered_feed,), ((gate_low,),))
    up = Shares(place, (ordered_feed,), ((up_low,),))
    sent, feed_half, gate_low, up_low = together(
        sent, other_half(ordered_feed), gate_low, up_low
    )
    arrived = down.go(sent, 0)
    gate_arrived, up_arrived = gate.go_core(gate_low), up.go_core(up_low)
    feed_sibling = place.turn(feed_half, "core", 1)
    mixed_slope, branch_low, feed_sums = local_call(
        feed_back_kernel,
        [((count, width), F32), ((count, width), BF16), ((8, width), F32)],
        (gate_low, up_low, gate_weight, up_weight, mixed_sum, slope, feed_gain),
        "feed_back",
    )
    scanned_slope, gating_low, tail_sums, *state_slopes = local_call(
        functools.partial(tail_back_kernel, xs),
        [((count, WIDTH), BF16), ((count, WIDTH), BF16), ((8, WIDTH), F32)]
        + [((STATE, part_width), BF16)] * xs,
        (
            position,
            branch_low,
            mixer_weight,
            scanned,
            channels,
            gating,
            table,
            logs,
            marks,
            readout,
        ),
        "tail_back",
        scratch=[
            pltpu.VMEM((count, WIDTH), F32),
            pltpu.VMEM((xs, STATE, part_width), BF16),
            pltpu.VMEM((2 * LANES, WIDTH), BF16),
            pltpu.VMEM((count, WIDTH), F32),
            pltpu.VMEM((count, WIDTH), BF16),
            pltpu.VMEM((count, WIDTH), F32),
        ],
        smem=(0,),
    )
    (
        arrived,
        gate_arrived,
        up_arrived,
        feed_sibling,
        state_slopes,
        branch_low,
        scanned_slope,
        gating_low,
        order,
    ) = together(
        arrived,
        gate_arrived,
        up_arrived,
        feed_sibling,
        tuple(state_slopes),
        branch_low,
        scanned_slope,
        gating_low,
        order,
    )

    gate_sent = gate.join([feed_sibling], gate_arrived)
    ordered_branch = arranged(order, branch_low)
    mixers = Shares(place, (ordered_branch, ordered), ((attention_low, tail_low), (gating_low,)))
    state_slopes, gate_sent, mixers_sent, branch_half, arrived, branch_low = together(
        state_slopes,
        gate_sent,
        mixers.to_core(),
        other_half(ordered_branch),
        arrived,
        branch_low,
    )
    state_pieces = dealt(place, state_slopes)
    gate_arrived = gate.go(gate_sent, 0)
    mixers_arrived = mixers.go_core(mixers_sent)
    branch_sibling = place.turn(branch_half, "core", 1)
    attention_slope = product_right(branch_low, attention_weight).astype(BF16)
    down_sent = down.to_second(arrived)
    mixers_sent = mixers.join([branch_sibling, ordered_sibling], mixers_arrived)
    state_pieces, gate_arrived, mixers_sent, down_sent, attention_slope = together(
        state_pieces, gate_arrived, mixers_sent, down_sent, attention_slope
    )
    total = level_back(place, state_pieces, walls, position, seg_row, count)

    total, mixers_sent, attention_slope, up_arrived, feed_sibling, gate_arrived = together(
        total, mixers_sent, attention_slope, up_arrived, feed_sibling, gate_arrived
    )
    totals = levels_met(place, total)
    mixers_arrived = mixers.go(mixers_sent, 0)
    query_low, pair_slope = local_call(
        functools.partial(attend_back_kernel, xs),
        [((count, HEADS * HEAD), BF16), ((length, 2 * LANES), BF16)],
        (
            position,
            queries,
            everything,
            attention_slope,
            exact,
            spread,
            segments,
            cosine,
            sine,
        ),
        "attend_back",
        scratch=[
            pltpu.VMEM((HEADS * HEAD, count), F32),
            pltpu.VMEM((HEADS, count), F32),
            pltpu.VMEM((HEADS * HEAD, count), F32),
        ],
        smem=(0,),
    )
    owners = KeyOwners(place, pair_slope)
    pair_sent = owners.to_first()
    up_sent = up.join([feed_sibling], up_arrived)
    totals, mixers_arrived, pair_sent, up_sent = together(
        totals, mixers_arrived, pair_sent, up_sent
    )
    results = arrival_back(
        place, state_pieces, totals, walls, level_walls, position, seg_row, count
    )

    (
        results,
        pair_sent,
        up_sent,
        mixers_arrived,
        gate_arrived,
        scanned_slope,
        activated_low,
    ) = together(
        results, pair_sent, up_sent, mixers_arrived, gate_arrived, scanned_slope, activated_low
    )
    pieces = dealt(place, results)
    pair_arrived = owners.go(pair_sent, 0)
    up_arrived = up.go(up_sent, 0)
    scaled_slope, inflow_part, readout_part = inner_call(
        inner_back_kernel,
        fixed,
        (scaled, scanned_slope),
        (F32,),
        (((count, STATE), F32), ((count, STATE), F32)),
        "inner_back",
        3,
    )
    mixers_sent = mixers.to_second(mixers_arrived)
    gate_sent = gate.to_second(gate_arrived)
    output = (mixed_sum + product(activated_low, down_weight)).astype(BF16)
    pieces, pair_arrived, up_arrived, mixers_sent, gate_sent, scaled_slope, output = together(
        pieces, pair_arrived, up_arrived, mixers_sent, gate_sent, scaled_slope, output
    )

    pieces, pair_sent, mixers_sent, gate_sent, up_arrived = together(
        pieces, owners.to_next(pair_arrived), mixers_sent, gate_sent, up_arrived
    )
    mixers_arrived = mixers.go(mixers_sent, 1)
    gate_arrived = gate.go(gate_sent, 1)
    pair_arrived = owners.go(pair_sent, 1)
    inner_low, edges, conv_sums, raw_slope, small = local_call(
        functools.partial(leaving_kernel, xs),
        [
            ((count, inner_width), BF16),
            ((2 * HALO, inner_width), F32),
            ((8, inner_width), F32),
            ((count, LANES), BF16),
            ((8, LANES), F32),
        ],
        (
            position,
            entering,
            scanned,
            scanned_slope,
            scaled,
            channels,
            scaled_slope,
            inflow,
            readout,
            inflow_part,
            readout_part,
            steps,
            raw,
            logs,
            marks,
            inner,
            factor,
            conv_weight,
            table,
            *pieces,
        ),
        "leaving",
        scratch=[
            pltpu.VMEM((count, inner_width), F32),
            pltpu.VMEM((2 * LANES, WIDTH), BF16),
            pltpu.VMEM((STATE, WIDTH), BF16),
        ]
        + [pltpu.VMEM((count, WIDTH), F32)] * 4
        + [pltpu.VMEM((2, count, WIDTH), BF16)] * 3
        + [pltpu.VMEM((count, WIDTH), BF16)] * 2,
        smem=(0,),
    )
    mixers_arrived, gate_arrived, pair_arrived, inner_low, edges = together(
        mixers_arrived, gate_arrived, pair_arrived, inner_low, edges
    )

    mixers_sent, pair_sent, down_sent, inner_low, edges, up_arrived, gate_arrived = together(
        mixers.to_third(mixers_arrived),
        owners.to_next(pair_arrived),
        down_sent,
        inner_low,
        edges,
        up_arrived,
        gate_arrived,
    )
    returned = passed_along(edges[:HALO], "seq", -1)
    pair_arrived = owners.go(pair_sent, 2)
    down_arrived = down.go(down_sent, 1)
    mixers_arrived = mixers.go_third(mixers_sent)
    up_sent = up.to_second(up_arrived)
    gate_sent = gate.to_third(gate_arrived)
    returned, pair_arrived, down_arrived, mixers_arrived, up_sent, gate_sent = together(
        returned, pair_arrived, down_arrived, mixers_arrived, up_sent, gate_sent
    )
    inner_low = lax.dynamic_update_slice(
        inner_low, (edges[HALO:] + returned).astype(BF16), (count - HALO, 0)
    )
    (pair_low,) = local_call(
        pairs_back_kernel,
        [((count, 2 * LANES), BF16)],
        (*owners.summands(pair_arrived), cosine, sine),
        "pairs_back",
    )

    rest = Shares(place, (ordered,), ((inner_low, query_low, pair_low),))
    (
        rest_sent,
        up_sent,
        mixers_arrived,
        gate_sent,
        down_arrived,
        gating_low,
        query_low,
        pair_low,
        inner_low,
    ) = together(
        rest.to_core(),
        up_sent,
        mixers_arrived,
        gate_sent,
        down_arrived,
        gating_low,
        query_low,
        pair_low,
        inner_low,
    )
    rest_arrived = rest.go_core(rest_sent)
    up_arrived = up.go(up_sent, 1)
    mixers_arrived = mixers.go_fourth(mixers.to_fourth(mixers_arrived))
    gate_arrived = gate.go_third(gate_sent)
    input_gradient, packed = local_call(
        finish_kernel,
        [((count, width), F32), ((PACK_ROWS, width), F32)],
        (
            gating_low,
            query_low,
            inner_low,
            pair_low,
            gating_weight,
            query_weight,
            inner_weight,
            key_weight,
            value_weight,
            step_turned,
            low_input,
            table,
            mixed_slope,
            raw_slope,
            normed_low,
            tail_sums,
            conv_sums,
            small,
            feed_sums,
        ),
        "finish",
    )
    rest_sent = rest.join([ordered_sibling], rest_arrived)
    rest_sent, up_arrived, mixers_arrived, gate_arrived, down_arrived, packed, input_gradient = (
        together(
            rest_sent, up_arrived, mixers_arrived, gate_arrived, down_arrived, packed, input_gradient
        )
    )

    rest_arrived = rest.go(rest_sent, 0)
    packed = all_sum(place, packed, ("core",))
    up_arrived, mixers_arrived, gate_arrived, down_arrived, packed = together(
        up_arrived, mixers_arrived, gate_arrived, down_arrived, packed
    )
    gate_arrived = gate.go_fourth(gate.to_fourth(gate_arrived))
    up_arrived = up.go_third(up.to_third(up_arrived))
    down_arrived = down.go_third(down.to_third(down_arrived))
    share_attention, share_mixer, share_gating = mixers.shares(mixers_arrived)
    share_attention, share_mixer = share_attention.T, share_mixer.T
    rest_arrived, gate_arrived, up_arrived, down_arrived, packed, share_attention, share_mixer = (
        together(
            rest_arrived,
            gate_arrived,
            up_arrived,
            down_arrived,
            packed,
            share_attention,
            share_mixer,
        )
    )

    rest_sent, up_sent, down_sent, gate_arrived, packed = together(
        rest.to_second(rest_arrived),
        up.to_fourth(up_arrived),
        down.to_fourth(down_arrived),
        gate_arrived,
        packed,
    )
    rest_arrived = rest.go(rest_sent, 1)
    up_arrived = up.go_fourth(up_sent)
    down_arrived = down.go_fourth(down_sent)
    packed = all_sum(place, packed, ("z",))
    (share_gate,) = gate.shares(gate_arrived)
    rest_arrived, up_arrived, down_arrived, packed, share_gate = together(
        rest_arrived, up_arrived, down_arrived, packed, share_gate
    )

    rest_sent, up_arrived, down_arrived, packed = together(
        rest.to_owners(rest_arrived), up_arrived, down_arrived, packed
    )
    rest_arrived = rest.go_owners(rest_sent)
    packed = all_sum(place, packed, ("x", "y"))
    (share_up,), (share_down,) = up.shares(up_arrived), down.shares(down_arrived)
    share_down = share_down.T
    sums = tuple(
        local_call(
            unpack_kernel,
            [
                ((width, SSM_HEADS), F32),
                ((width,), F32),
                ((width,), F32),
                ((WIDTH,), F32),
                ((SSM_HEADS,), F32),
                ((SSM_HEADS,), F32),
                ((SSM_HEADS,), F32),
                ((KERNEL, inner_width), F32),
                ((inner_width,), F32),
            ],
            (packed,),
            "unpack",
        )
    )
    rest_arrived, sums, share_up, share_down = together(rest_arrived, sums, share_up, share_down)
    (
        step_sum,
        gain_sum,
        feed_gain_sum,
        mixer_gain_sum,
        skip_sum,
        step_bias_sum,
        decay_sum,
        conv_sum,
        conv_bias_sum,
    ) = sums
    share_inner, share_query, share_key, share_value = rest.split(
        rest_arrived, (inner_width, HEADS * HEAD, LANES, LANES)
    )
    return (
        output[None],
        input_gradient[None],
        gain_sum,
        share_query,
        share_key,
        share_value,
        share_attention,
        share_gating,
        share_inner,
        step_sum,
        step_bias_sum,
        decay_sum,
        skip_sum,
        conv_sum,
        conv_bias_sum,
        mixer_gain_sum,
        share_mixer,
        feed_gain_sum,
        share_gate,
        share_up,
        share_down,
    )


def solution(mesh):
    in_specs = (
        P("dp", "seq", None),
        P("dp", None),
        P("dp", "seq", None),
        P(),
        P(),
        P(),
        P(),
        P(),
        P(),
        P(),
        P(),
        P(),
        P(),
        P(),
        P(),
        P(),
        P(),
        P(),
        P(),
        P(),
        P(),
        P(),
    )
    out_specs = (
        P("dp", "seq", None),
        P("dp", "seq", None),
        P(),
        P(("dp", "seq"), None),
        P(("dp", "seq"), None),
        P(("dp", "seq"), None),
        P(None, ("dp", "seq")),
        P(("dp", "seq"), None),
        P(("dp", "seq"), None),
        P(),
        P(),
        P(),
        P(),
        P(),
        P(),
        P(),
        P(None, ("dp", "seq")),
        P(),
        P(("dp", "seq"), None),
        P(("dp", "seq"), None),
        P(None, ("dp", "seq")),
    )
    return jax.shard_map(body, mesh=mesh, in_specs=in_specs, out_specs=out_specs, check_vma=False)
```

```python
import functools
import math

import jax
import jax.numpy as jnp
from jax import lax
from jax.experimental import pallas as pl
from jax.experimental.pallas import tpu as pltpu
from jax.sharding import PartitionSpec as P

HEADS = 8
KV_HEADS = 2
HEAD = 64
SSM_HEADS = 24
SSM_HEAD = 64
STATE = 128
KERNEL = 4


EPS = 1e-05
ROPE_BASE = 100000000000.0
NEG = -1e30
HIGH = lax.Precision.HIGHEST


def passed_along(shard, axis, by):
    peers = lax.axis_size(axis)
    pairs = [(i, i + by) for i in range(peers) if 0 <= i + by < peers]
    return lax.ppermute(shard, axis, pairs)


def product(left, right):
    return jnp.dot(left, right, preferred_element_type=jnp.float32)


def product_left(left, right):
    return lax.dot_general(
        left, right, (((0,), (0,)), ((), ())), preferred_element_type=jnp.float32
    )


def product_right(left, right):
    return lax.dot_general(
        left, right, (((1,), (1,)), ((), ())), preferred_element_type=jnp.float32
    )


def precise(left, right):
    return jnp.dot(left, right, preferred_element_type=jnp.float32, precision=HIGH)


def norm_rows(values, gain):
    return values * lax.rsqrt(jnp.mean(values * values, -1, keepdims=True) + EPS) * gain


def gated_unit(gate, upward):
    return jax.nn.silu(gate) * upward


CORES = 2
DEPTH = 4
LANES = 128


class Place:
    def __init__(self):
        self.dp = lax.axis_size("dp")
        self.seq = lax.axis_size("seq")
        self.sizes = {
            "y": self.dp // CORES,
            "core": CORES,
            "z": DEPTH,
            "x": self.seq // DEPTH,
        }

    def split(self, index):
        dp, seq = index // self.seq, index % self.seq
        return {
            "y": dp // CORES,
            "core": dp % CORES,
            "z": seq // self.sizes["x"],
            "x": seq % self.sizes["x"],
        }

    def join(self, at):
        return (at["y"] * CORES + at["core"]) * self.seq + at["z"] * self.sizes["x"] + at["x"]

    def turn(self, shard, axis, by):
        pairs = []
        for index in range(self.dp * self.seq):
            at = self.split(index)
            at[axis] = (at[axis] + by) % self.sizes[axis]
            pairs.append((index, self.join(at)))
        return lax.ppermute(shard, ("dp", "seq"), pairs)

    def swap(self, shard, axis, bit):
        pairs = []
        for index in range(self.dp * self.seq):
            at = self.split(index)
            at[axis] ^= bit
            pairs.append((index, self.join(at)))
        return lax.ppermute(shard, ("dp", "seq"), pairs)

    def share_order(self, width, group, along):
        sizes, at = self.sizes, self.split(group * self.seq + along)
        rows = width // (self.dp * self.seq)
        k = lax.broadcasted_iota(jnp.int32, (width, 1), 0)
        within = k % rows
        rest = k // rows
        dz = rest % sizes["z"]
        rest = rest // sizes["z"]
        dy = rest % sizes["y"]
        rest = rest // sizes["y"]
        dx = rest % sizes["x"]
        dc = rest // sizes["x"]
        owner = self.join(
            {
                "y": (at["y"] + dy) % sizes["y"],
                "core": (at["core"] + dc) % sizes["core"],
                "z": at["z"] ^ (dz // 2 + 2 * (dz % 2)),
                "x": (at["x"] + dx) % sizes["x"],
            }
        )
        source = owner * rows + within
        columns = lax.broadcasted_iota(jnp.int32, (1, width), 1)
        return (source == columns).astype(jnp.bfloat16)


F32 = jnp.float32
BF16 = jnp.bfloat16
PAIR = 2 * SSM_HEAD
WIDTH = SSM_HEADS * SSM_HEAD
PAIRS = WIDTH // PAIR
HALO = 16
EXTRA = 16
WALLS = 16
VMEM = pl.BlockSpec(memory_space=pltpu.VMEM)
SMEM = pl.BlockSpec(memory_space=pltpu.SMEM)
FAR = pl.BlockSpec(memory_space=pl.ANY)


def room(arrays):
    total = 0
    for a in arrays:
        *lead, last = a.shape if len(a.shape) > 1 else (8, *a.shape)
        total += math.prod(lead) * (-(-last // LANES) * LANES) * jnp.dtype(a.dtype).itemsize
    return total


def local_call(kernel, outs, args, name, scratch=(), smem=(), slack=4, alone=False, far=(), sems=()):
    shapes = [jax.ShapeDtypeStruct(shape, kind) for shape, kind in outs]
    held = [a for i, a in enumerate(args) if i not in smem and i not in far]
    needed = (56 if alone else slack) * 1024 * 1024
    if not alone:
        needed += room(held) + room(shapes) + room(scratch)
    return pl.pallas_call(
        kernel,
        in_specs=[
            SMEM if i in smem else (FAR if i in far else VMEM) for i in range(len(args))
        ],
        out_specs=[VMEM] * len(shapes),
        out_shape=shapes,
        scratch_shapes=list(scratch) + [pltpu.SemaphoreType.DMA((n,)) for n in sems],
        compiler_params=pltpu.CompilerParams(vmem_limit_bytes=needed),
        cost_estimate=pl.CostEstimate(flops=0, bytes_accessed=0, transcendentals=0),
        name=name,
    )(*args)


def dot(left, right):
    return jnp.dot(left, right, preferred_element_type=F32)


def dot_rows(left, right):
    return lax.dot_general(left, right, (((0,), (0,)), ((), ())), preferred_element_type=F32)


def dot_lanes(left, right):
    return lax.dot_general(left, right, (((1,), (1,)), ((), ())), preferred_element_type=F32)


def turned(values, cosine, sine):
    lane = lax.broadcasted_iota(jnp.int32, values.shape, 1)
    half = HEAD // 2
    swapped = jnp.where(
        lane % HEAD < half,
        pltpu.roll(values, LANES - half, 1),
        pltpu.roll(values, half, 1),
    )
    return values * cosine + swapped * sine


def turn_tables(first, count):
    lane = jnp.arange(LANES)
    place = (first + jnp.arange(count)).astype(F32)
    half = HEAD // 2
    freq = ROPE_BASE ** (-((lane % half).astype(F32) * 2.0 / HEAD))
    angle = place[:, None] * freq[None, :]
    sign = jnp.where(lane % HEAD < half, -1.0, 1.0)[None, :]
    return jnp.cos(angle), jnp.sin(angle) * sign


def lanes_of(index):
    return slice(index * LANES, (index + 1) * LANES)


def spread_pair(values, pair):
    rows = values.shape[0]
    lane = lax.broadcasted_iota(jnp.int32, (rows, LANES), 1)
    return jnp.where(
        lane < SSM_HEAD, values[:, 2 * pair : 2 * pair + 1], values[:, 2 * pair + 1 : 2 * pair + 2]
    )


def head_lanes(selector):
    head = lax.broadcasted_iota(jnp.int32, (LANES, LANES), 0)
    lane = lax.broadcasted_iota(jnp.int32, (LANES, LANES), 1)
    for pair in range(PAIRS):
        chosen = (lane // SSM_HEAD + 2 * pair == head).astype(F32).astype(BF16)
        selector[:LANES, lanes_of(pair)] = chosen
        selector[LANES:, lanes_of(pair)] = chosen


def halves(values):
    upper = values.astype(BF16)
    return jnp.concatenate([upper, (values - upper.astype(F32)).astype(BF16)], 1)


def split_into(target, span, values):
    upper = values.astype(BF16)
    target[0, :, span] = upper
    target[1, :, span] = (values - upper.astype(F32)).astype(BF16)


def head_sums(parts, selector):
    chosen = selector[:LANES]
    return dot_lanes(parts[0], chosen) + dot_lanes(parts[1], chosen)


def silu_slope(values):
    gate = jax.nn.sigmoid(values)
    return gate * (1.0 + values * (1.0 - gate))


def front_kernel(
    x, key_w, value_w, cosine, sine, conv_bias, input_gain, mixer_gain, skip, step_bias, decay_log,
    normed, pairs, table,
):
    table[...] = jnp.zeros(table.shape, F32)
    for row, source in (
        (ROW_CONV, conv_bias),
        (ROW_GAIN, input_gain),
        (ROW_MIXER, mixer_gain),
        (ROW_STEP, step_bias),
    ):
        table[row : row + 1, : source.shape[0]] = source[...].reshape(1, source.shape[0])
    rates = -jnp.exp(decay_log[...].reshape(1, SSM_HEADS))
    table[ROW_RATE : ROW_RATE + 1, :SSM_HEADS] = rates
    skips = skip[...].reshape(1, SSM_HEADS)
    for pair in range(PAIRS):
        table[ROW_SKIP : ROW_SKIP + 1, lanes_of(pair)] = spread_pair(skips, pair)
    values = x[...].astype(F32)
    scale = lax.rsqrt(jnp.mean(values * values, -1, keepdims=True) + EPS)
    gain = table[ROW_GAIN : ROW_GAIN + 1, : values.shape[1]]
    normed[...] = (values * scale * gain).astype(BF16)
    low = normed[...]
    pairs[:, :LANES] = turned(dot(low, key_w[...]), cosine[...], sine[...]).astype(BF16)
    pairs[:, LANES:] = dot(low, value_w[...]).astype(BF16)


def block_mask(first, start, segments, count):
    def row(at):
        return segments[:, pl.ds(pl.multiple_of(at, LANES), count)].astype(F32)

    place = lax.broadcasted_iota(jnp.int32, (count, count), 0) + start
    reach = lax.broadcasted_iota(jnp.int32, (count, count), 1) + first
    keys = jnp.broadcast_to(row(start), (8, count)).T[:, :1]
    return (keys == row(first)) & (place <= reach)


def key_rows(xs, position, index, count):
    far = position // xs - index // xs
    side = lax.rem(lax.rem(position, xs) - lax.rem(index, xs) + xs, xs)
    return pl.ds(pl.multiple_of((far * xs + side) * count, count), count)


def head_columns(pairs, rows):
    keys = [pairs[rows, kv * HEAD : (kv + 1) * HEAD] for kv in range(KV_HEADS)]
    values = [
        pairs[rows, LANES + kv * HEAD : LANES + (kv + 1) * HEAD] for kv in range(KV_HEADS)
    ]
    return keys, values


def attend_kernel(
    xs, position, normed, query_w, cosine, sine, segments, *refs
):
    *pieces, queries, low, exact, spread, pairs, top, total, gathered, arrived = refs
    count = queries.shape[0]
    block = pieces[0].shape[0]
    copies = [
        pltpu.make_async_copy(piece, pairs.at[k * block : (k + 1) * block], arrived.at[k])
        for k, piece in enumerate(pieces)
    ]
    for copy in copies:
        copy.start()
    raw = dot(normed[...], query_w[...])
    for chunk_at in range(HEADS * HEAD // LANES):
        part = turned(raw[:, lanes_of(chunk_at)], cosine[...], sine[...]) * HEAD**-0.5
        queries[:, lanes_of(chunk_at)] = part.astype(BF16)
    first = position[0] * count
    group = HEADS // KV_HEADS
    top[...] = jnp.full(top.shape, NEG, F32)
    total[...] = jnp.zeros(total.shape, F32)
    gathered[...] = jnp.zeros(gathered.shape, F32)

    def chunk(index, carry):
        start = pl.multiple_of(index * count, count)
        rows = key_rows(xs, position[0], index, count)
        mask = block_mask(first, start, segments, count)
        keys, values = head_columns(pairs, rows)
        values = [value.T for value in values]
        before = top[...]
        scores = []
        for head in range(HEADS):
            score = dot_lanes(keys[head // group], queries[:, head * HEAD : (head + 1) * HEAD])
            scores.append(jnp.where(mask, score, NEG))
        now = jnp.maximum(
            before, jnp.concatenate([jnp.max(score, 0, keepdims=True) for score in scores], 0)
        )
        fade = jnp.exp(before - now)
        weights = [jnp.exp(score - now[head : head + 1]) for head, score in enumerate(scores)]
        sums = jnp.concatenate([jnp.sum(weight, 0, keepdims=True) for weight in weights], 0)
        top[...] = now
        total[...] = total[...] * fade + sums
        for head in range(HEADS):
            span = slice(head * HEAD, (head + 1) * HEAD)
            gathered[span] = gathered[span] * fade[head : head + 1] + dot(
                values[head // group], weights[head].astype(BF16)
            )
        return carry

    for copy in copies:
        copy.wait()
    lax.fori_loop(0, first // count + 1, chunk, 0)
    spread[...] = top[...] + jnp.log(total[...])
    for head in range(HEADS):
        span = slice(head * HEAD, (head + 1) * HEAD)
        exact[span] = gathered[span] / total[head : head + 1]
    for chunk_at in range(HEADS * HEAD // LANES):
        low[:, lanes_of(chunk_at)] = exact[lanes_of(chunk_at)].T.astype(BF16)


def attend_back_kernel(
    xs, position, queries, pairs, slope, exact, spread, segments, cosine, sine,
    query_low, pair_slope, turned_slope, delta, query_slope,
):
    count = queries.shape[0]
    length = pairs.shape[0]
    first = position[0] * count
    group = HEADS // KV_HEADS
    for chunk_at in range(HEADS * HEAD // LANES):
        turned_slope[lanes_of(chunk_at)] = slope[:, lanes_of(chunk_at)].astype(F32).T
    for head in range(HEADS):
        span = slice(head * HEAD, (head + 1) * HEAD)
        delta[head : head + 1] = jnp.sum(turned_slope[span] * exact[span], 0, keepdims=True)
    query_slope[...] = jnp.zeros(query_slope.shape, F32)

    def target(index):
        if xs != 2:
            return pl.ds(pl.multiple_of(index * count, count), count)
        far = (index // xs) ^ (position[0] // xs)
        side = lax.rem(index, xs) ^ lax.rem(position[0], xs)
        turn = (far & 1) * 4 + (far >> 1) * 2 + side
        return pl.ds(pl.multiple_of(turn * count, count), count)

    def chunk(index, carry):
        start = pl.multiple_of(index * count, count)
        rows = key_rows(xs, position[0], index, count)
        mask = block_mask(first, start, segments, count)
        into = target(index)
        keys, values = head_columns(pairs, rows)
        asked = [queries[:, head * HEAD : (head + 1) * HEAD] for head in range(HEADS)]
        sloped = [slope[:, head * HEAD : (head + 1) * HEAD] for head in range(HEADS)]
        scores = [dot_lanes(keys[head // group], asked[head]) for head in range(HEADS)]
        dots = [dot_lanes(values[head // group], sloped[head]) for head in range(HEADS)]
        weights, score_slopes = [], []
        for head in range(HEADS):
            row = slice(head, head + 1)
            weight = jnp.exp(jnp.where(mask, scores[head] - spread[row], NEG))
            score_slopes.append((weight * (dots[head] - delta[row])).astype(BF16))
            weights.append(weight.astype(BF16))
        for kv in range(KV_HEADS):
            heads = range(kv * group, (kv + 1) * group)
            value_part = sum(dot(weights[head], sloped[head]) for head in heads)
            key_part = sum(dot(score_slopes[head], asked[head]) for head in heads)
            pair_slope[into, kv * HEAD : (kv + 1) * HEAD] = key_part.astype(BF16)
            pair_slope[into, LANES + kv * HEAD : LANES + (kv + 1) * HEAD] = value_part.astype(BF16)
        keys = [key.T for key in keys]
        for head in range(HEADS):
            span = slice(head * HEAD, (head + 1) * HEAD)
            query_slope[span] = query_slope[span] + dot(keys[head // group], score_slopes[head])
        return carry

    def blank(index, carry):
        pair_slope[target(index), :] = jnp.zeros((count, 2 * LANES), BF16)
        return carry

    live = first // count + 1
    lax.fori_loop(0, live, chunk, 0)
    lax.fori_loop(live, length // count, blank, 0)
    for chunk_at in range(HEADS * HEAD // LANES):
        part = query_slope[lanes_of(chunk_at)].T * HEAD**-0.5
        query_low[:, lanes_of(chunk_at)] = turned(part, cosine[...], -sine[...]).astype(BF16)


def pairs_back_kernel(*refs):
    *summands, cosine, sine, low = refs
    owned = sum(ref[...].astype(F32) for ref in summands)
    low[:, :LANES] = turned(owned[:, :LANES], cosine[...], -sine[...]).astype(BF16)
    low[:, LANES:] = owned[:, LANES:].astype(BF16)


def wide_marks(marks):
    return [
        jnp.broadcast_to(marks[:, tap : tap + 1], (marks.shape[0], LANES))
        for tap in range(KERNEL - 1)
    ]


def conv_total(inner, taps, table, wide, chunk):
    span = lanes_of(chunk)
    extended = inner[:, span].astype(F32)
    total = table[ROW_CONV : ROW_CONV + 1, span] + taps[KERNEL - 1 : KERNEL, span] * extended[HALO:]
    for tap in range(KERNEL - 1):
        moved = pltpu.roll(extended, KERNEL - 1 - tap, 0)[HALO:] * wide[tap]
        total = total + taps[tap : tap + 1, span] * moved
    return total


def triangle(count, strict=False, upper=False):
    row = lax.broadcasted_iota(jnp.int32, (count, count), 0)
    column = lax.broadcasted_iota(jnp.int32, (count, count), 1)
    if upper:
        row, column = column, row
    return (row > column if strict else row >= column).astype(F32)


def soft(values):
    return jnp.maximum(values, 0.0) + jnp.log1p(jnp.exp(-jnp.abs(values)))


def part_pieces(parts, pair):
    width = WIDTH // parts
    if width % LANES == 0:
        start = pair * LANES % width
        return [(pair * LANES // width, slice(start, start + LANES), slice(0, LANES))]
    pieces = []
    for half in range(2):
        column = pair * LANES + half * SSM_HEAD
        start = column % width
        pieces.append(
            (
                column // width,
                slice(start, start + SSM_HEAD),
                slice(half * SSM_HEAD, (half + 1) * SSM_HEAD),
            )
        )
    return pieces


ROW_CONV, ROW_GAIN, ROW_MIXER, ROW_SKIP, ROW_STEP, ROW_RATE, ROW_FEED = range(7)
MARK_ENTER, MARK_TAIL, MARK_SEGMENT = KERNEL - 1, KERNEL, KERNEL + 1


def mark_rows(position, segments, count):
    first = pl.multiple_of(position * count, LANES)
    here = segments[:, pl.ds(first, count)].astype(F32)
    before = segments[:, pl.ds(pl.multiple_of(jnp.maximum(first - count, 0), LANES), count)]
    before = jnp.where(position > 0, before.astype(F32), -1.0)
    both = jnp.concatenate([before, here], 1)
    rows = []
    for tap in range(KERNEL - 1):
        moved = pltpu.roll(jnp.broadcast_to(both, (8, 2 * count)), KERNEL - 1 - tap, 1)
        rows.append(flag(moved[:1, count:] == here))
    rows.append(flag(here == before[:, count - 1 :]))
    rows.append(flag(here == here[:, count - 1 :]))
    rows.append(here)
    rows += [jnp.zeros((1, count), F32)] * (8 - len(rows))
    return jnp.concatenate(rows, 0)


def hold_part(hold, pair, rows, value):
    for part, lanes, within in part_pieces(hold.shape[0], pair):
        hold[part, rows, lanes] = value[:, within]


def hold_all(hold, rows, values):
    width = hold.shape[2]
    for part in range(hold.shape[0]):
        hold[part, rows] = values[:, part * width : (part + 1) * width]


def hand_out(hold, at_x, targets):
    for k, target in enumerate(targets):
        target[...] = hold[lax.rem(at_x + k, len(targets))]


def picked(pieces, at_x, pair):
    xs = len(pieces)
    values = []
    for part, lanes, _ in part_pieces(xs, pair):
        value = pieces[0][:, lanes]
        for k in range(1, xs):
            value = jnp.where(lax.rem(at_x - k + xs, xs) == part, pieces[k][:, lanes], value)
        values.append(value)
    return values[0] if len(values) == 1 else jnp.concatenate(values, 1)


def flag(condition):
    return jnp.where(condition, 1.0, 0.0)


def wall_rows(high, middle, low):
    row = lax.broadcasted_iota(jnp.int32, (EXTRA, high.shape[1]), 0)
    return jnp.where(
        row == 0, high, jnp.where(row == 1, middle, jnp.where(row == 2, low, 0.0))
    ).astype(BF16)


def ahead(forward, one, other):
    return one < other if forward else one > other


def mixed(flags, rows, width):
    total = jnp.zeros((1, width), F32)
    for chosen, row in zip(flags, rows):
        total = total + row * chosen
    return jnp.exp(total)


class Endings:
    def __init__(self, segments, count):
        self.segments, self.count = segments, count

    def __getitem__(self, index):
        return self.segments[index * self.count + self.count - 1]


def level_kernel(forward, xs, count, position, segments, *refs):
    pieces = refs[:xs]
    if forward:
        total_out, walls = refs[xs:]
    else:
        walls, total_out = refs[xs:]
    at_z, at_x = position[0] // xs, lax.rem(position[0], xs)
    endings = Endings(segments, count)
    width = pieces[0].shape[1]
    places = [lax.rem(at_x - k + xs, xs) for k in range(xs)]
    if forward:
        rows = []
        for k in range(xs):
            rows.append(jnp.sum(pieces[k][STATE:].astype(F32), 0, keepdims=True))
            walls[k : k + 1] = rows[k]
        walls[xs:] = jnp.zeros((WALLS - xs, width), F32)
        border = endings[at_z * xs + xs - 1]
    else:
        rows = [walls[k : k + 1] for k in range(xs)]
        border = endings[jnp.maximum(at_z * xs - 1, 0)]
    total = jnp.zeros((STATE, width), F32)
    for k in range(xs):
        index = at_z * xs + places[k]
        reached = endings[index if forward else jnp.maximum(index - 1, 0)] == border
        flags = [flag(ahead(forward, places[k], places[m])) for m in range(xs)]
        total = total + pieces[k][:STATE].astype(F32) * (
            mixed(flags, rows, width) * flag(reached)
        )
    total_out[:STATE] = total.astype(BF16)
    if forward:
        whole = sum(rows)
        high = whole.astype(BF16).astype(F32)
        middle = (whole - high).astype(BF16).astype(F32)
        total_out[STATE:] = wall_rows(high, middle, whole - high - middle)


def arrival_kernel(forward, xs, zs, count, position, segments, *refs):
    pieces = refs[:xs]
    totals = refs[xs : xs + zs - 1]
    walls = refs[xs + zs - 1]
    if forward:
        own, *results, level_walls = refs[xs + zs :]
    else:
        level_walls, *results = refs[xs + zs :]
    at_z, at_x = position[0] // xs, lax.rem(position[0], xs)
    endings = Endings(segments, count)
    width = pieces[0].shape[1]
    x_at = [lax.rem(at_x - k + xs, xs) for k in range(xs)]
    z_at = [lax.rem(at_z - k + zs, zs) for k in range(zs)]
    rows = [walls[k : k + 1] for k in range(xs)]
    if forward:
        levels = [jnp.sum(own[STATE:].astype(F32), 0, keepdims=True)]
        for total in totals:
            levels.append(jnp.sum(total[STATE:].astype(F32), 0, keepdims=True))
        for k in range(zs):
            level_walls[k : k + 1] = levels[k]
        level_walls[zs:] = jnp.zeros((WALLS - zs, width), F32)
        border = endings[jnp.maximum(at_z * xs - 1, 0)]
    else:
        levels = [level_walls[k : k + 1] for k in range(zs)]
        border = endings[at_z * xs + xs - 1]
    outside = jnp.zeros((STATE, width), F32)
    for k in range(1, zs):
        far = endings[z_at[k] * xs + xs - 1 if forward else jnp.maximum(z_at[k] * xs - 1, 0)]
        reached = ahead(forward, z_at[k], at_z) & (far == border)
        flags = [
            flag(ahead(forward, z_at[k], z_at[m]) & ahead(forward, z_at[m], at_z))
            for m in range(zs)
        ]
        outside = outside + totals[k - 1][:STATE].astype(F32) * (
            mixed(flags, levels, width) * flag(reached)
        )
    for r in range(xs):
        target = lax.rem(at_x + r, xs)
        index = at_z * xs + target
        edge = endings[jnp.maximum(index - 1, 0) if forward else index]
        flags = [flag(ahead(forward, x_at[m], target)) for m in range(xs)]
        total = outside * (mixed(flags, rows, width) * flag(edge == border))
        for k in range(xs):
            source = at_z * xs + x_at[k]
            far = endings[source if forward else jnp.maximum(source - 1, 0)]
            reached = ahead(forward, x_at[k], target) & (far == edge)
            flags = [
                flag(ahead(forward, x_at[k], x_at[m]) & ahead(forward, x_at[m], target))
                for m in range(xs)
            ]
            total = total + pieces[k][:STATE].astype(F32) * (
                mixed(flags, rows, width) * flag(reached)
            )
        results[r][...] = total.astype(BF16)


def dealt(place, parts):
    return (parts[0],) + tuple(
        place.turn(part, "x", k) for k, part in enumerate(parts[1:], start=1)
    )


def levels_met(place, total):
    return tuple(place.turn(total, "z", k) for k in range(1, place.sizes["z"]))


def level(place, pieces, position, segments, count):
    xs, width = place.sizes["x"], pieces[0].shape[1]
    return local_call(
        functools.partial(level_kernel, True, xs, count),
        [((STATE + EXTRA, width), BF16), ((WALLS, width), F32)],
        (position, segments, *pieces),
        "level",
        smem=(0, 1),
    )


def level_back(place, pieces, walls, position, segments, count):
    xs, width = place.sizes["x"], pieces[0].shape[1]
    return local_call(
        functools.partial(level_kernel, False, xs, count),
        [((STATE, width), BF16)],
        (position, segments, *pieces, walls),
        "level_back",
        smem=(0, 1),
    )[0]


def arrival(place, pieces, totals, walls, total, position, segments, count):
    xs, zs, width = place.sizes["x"], place.sizes["z"], pieces[0].shape[1]
    *results, level_walls = local_call(
        functools.partial(arrival_kernel, True, xs, zs, count),
        [((STATE, width), BF16)] * xs + [((WALLS, width), F32)],
        (position, segments, *pieces, *totals, walls, total),
        "arrival",
        smem=(0, 1),
    )
    return tuple(results), level_walls


def arrival_back(place, pieces, totals, walls, level_walls, position, segments, count):
    xs, zs, width = place.sizes["x"], place.sizes["z"], pieces[0].shape[1]
    return tuple(
        local_call(
            functools.partial(arrival_kernel, False, xs, zs, count),
            [((STATE, width), BF16)] * xs,
            (position, segments, *pieces, *totals, walls, level_walls),
            "arrival_back",
            smem=(0, 1),
        )
    )


def prep_kernel(
    xs, position, halo, normed, table, inner_w, step_w, taps, segments,
    inner, raw, channels, scaled, inflow, readout, steps, logs, logs_turned, marks, marks_turned,
    factor, *refs,
):
    states, (extended, hold, selector, lengths, tails, weighted) = refs[:xs], refs[xs:]
    count, width = normed.shape
    at_x = lax.rem(position[0], xs)
    marks_turned[...] = mark_rows(position[0], segments, count)
    marks[...] = marks_turned[...].T
    values = halo[...].astype(F32)
    scale = lax.rsqrt(jnp.mean(values * values, -1, keepdims=True) + EPS)
    extended[:HALO] = (values * scale * table[ROW_GAIN : ROW_GAIN + 1, :width]).astype(BF16)
    extended[HALO:] = normed[...]
    raw[...] = jnp.zeros(raw.shape, F32)
    raw[:, :SSM_HEADS] = dot_lanes(normed[...], step_w[...])
    head_lanes(selector)
    chunks = range(PAIRS + 2)
    for chunk in reversed(chunks):
        span = lanes_of(chunk)
        inner[:, span] = dot(extended[...], inner_w[:, span]).astype(BF16)
    steps[...] = soft(raw[...] + table[ROW_STEP : ROW_STEP + 1, :LANES])
    logs[...] = precise(triangle(count), steps[...] * table[ROW_RATE : ROW_RATE + 1, :LANES])
    logs_turned[...] = logs[...].T
    ending = logs[count - 1 : count]
    tail = jnp.exp(ending - logs[...]) * marks[:, MARK_TAIL : MARK_TAIL + 1]
    lengths[...] = dot(halves(steps[...]), selector[...])
    tails[...] = dot(halves(tail), selector[...])
    wide = wide_marks(marks)
    for chunk in reversed(chunks):
        span = lanes_of(chunk)
        total = conv_total(inner, taps, table, wide, chunk)
        gate = jax.nn.sigmoid(total)
        factor[:, span] = (gate * (1.0 + total * (1.0 - gate))).astype(BF16)
        value = total * gate
        if chunk == PAIRS + 1:
            readout[...] = value.astype(BF16)
        elif chunk == PAIRS:
            inflow[...] = value.astype(BF16)
        else:
            channels[:, span] = value
            value = value * lengths[:, span]
            scaled[:, span] = value.astype(BF16)
            weighted[:, span] = (value * tails[:, span]).astype(BF16)
    hold_all(hold, slice(0, STATE), dot(inflow[...].T, weighted[...]).astype(BF16))
    for pair in range(PAIRS):
        whole = spread_pair(ending, pair)
        high = whole.astype(BF16).astype(F32)
        middle = (whole - high).astype(BF16).astype(F32)
        wall = wall_rows(high, middle, whole - high - middle)
        hold_part(hold, pair, slice(STATE, STATE + EXTRA), wall)
    hand_out(hold, at_x, states)


def decay_kernel_parts(marks, marks_turned, bias):
    count = marks.shape[0]
    row = lax.broadcasted_iota(jnp.int32, (count, count), 0)
    column = lax.broadcasted_iota(jnp.int32, (count, count), 1)
    span = slice(MARK_SEGMENT, MARK_SEGMENT + 1)
    inside = (marks[:, span] == marks_turned[span]) & (row >= column)
    bias[...] = jnp.where(inside, 0.0, NEG)


IN_STEP = 4


def inner_kernel(logs, logs_turned, marks, marks_turned, inflow, readout, scaled, result, bias, meet):
    count = logs.shape[0]
    step = pl.program_id(0)

    @pl.when(step == 0)
    def _():
        decay_kernel_parts(marks, marks_turned, bias)
        meet[...] = dot_lanes(readout[...], inflow[...])

    columns = pltpu.roll(logs[...], (LANES - IN_STEP * step) % LANES, 1)
    half = count // 2
    for k in range(IN_STEP):
        across = logs_turned[pl.ds(IN_STEP * step + k, 1), :]
        span = slice(k * SSM_HEAD, (k + 1) * SSM_HEAD)
        for top, width in ((0, half), (half, count)):
            rows = slice(top, top + half)
            gap = columns[rows, k : k + 1] - across[:, :width] + bias[rows, :width]
            mixing = (jnp.exp(gap) * meet[rows, :width]).astype(BF16)
            result[rows, span] = dot(mixing, scaled[:width, span])


def inner_back_kernel(
    logs,
    logs_turned,
    marks,
    marks_turned,
    inflow,
    readout,
    scaled,
    slope,
    scaled_slope,
    inflow_slope,
    readout_slope,
    bias,
    meet,
    meet_slope,
):
    count = logs.shape[0]
    step = pl.program_id(0)

    @pl.when(step == 0)
    def _():
        decay_kernel_parts(marks, marks_turned, bias)
        meet[...] = dot_lanes(readout[...], inflow[...])
        meet_slope[...] = jnp.zeros(meet_slope.shape, F32)

    columns = pltpu.roll(logs[...], (LANES - IN_STEP * step) % LANES, 1)
    half = count // 2
    for top, width in ((0, half), (half, count)):
        rows = slice(top, top + half)
        gathered = jnp.zeros((half, width), F32)
        for k in range(IN_STEP):
            across = logs_turned[pl.ds(IN_STEP * step + k, 1), :]
            span = slice(k * SSM_HEAD, (k + 1) * SSM_HEAD)
            gap = columns[rows, k : k + 1] - across[:, :width] + bias[rows, :width]
            decay = jnp.exp(gap)
            mixing = (decay * meet[rows, :width]).astype(BF16)
            gathered = gathered + decay * dot_lanes(slope[rows, span], scaled[:width, span])
            part = dot_rows(mixing, slope[rows, span])
            if top:
                scaled_slope[:half, span] = scaled_slope[:half, span] + part[:half]
                scaled_slope[half:, span] = part[half:]
            else:
                scaled_slope[:half, span] = part
        meet_slope[rows, :width] = meet_slope[rows, :width] + gathered

    @pl.when(step == SSM_HEADS // IN_STEP - 1)
    def _():
        low = meet_slope[...].astype(BF16)
        inflow_slope[...] = dot_rows(low, readout[...])
        readout_slope[...] = dot(low, inflow[...])


def inner_call(kernel, fixed, moving, outs, fixed_outs, name, scratch):
    count = fixed[0].shape[0]
    steps = SSM_HEADS // IN_STEP
    width = IN_STEP * SSM_HEAD
    held = [pl.BlockSpec(a.shape, lambda j: (0, 0)) for a in fixed]
    passing = pl.BlockSpec((count, width), lambda j: (0, j))
    return pl.pallas_call(
        kernel,
        grid=(steps,),
        in_specs=held + [passing] * len(moving),
        out_specs=[passing] * len(outs)
        + [pl.BlockSpec(shape, lambda j: (0, 0)) for shape, _ in fixed_outs],
        out_shape=[jax.ShapeDtypeStruct((count, WIDTH), kind) for kind in outs]
        + [jax.ShapeDtypeStruct(shape, kind) for shape, kind in fixed_outs],
        scratch_shapes=[pltpu.VMEM((count, count), F32)] * scratch,
        compiler_params=pltpu.CompilerParams(vmem_limit_bytes=8 * 1024 * 1024),
        cost_estimate=pl.CostEstimate(flops=0, bytes_accessed=0, transcendentals=0),
        name=name,
    )(*fixed, *moving)


def entering_kernel(
    xs, position, inner_part, readout, logs, marks, channels, gating, table, low_input, branch,
    feed_gain, mixer_w, gate_w, up_w, *refs,
):
    pieces, outs = refs[:xs], refs[xs:]
    tail, scanned, entering, mixed_sum, feed_low, gate_raw, up_raw, activated, *outs = outs
    gated, selector, wide, mixer_here, gate_here, up_here, arrived = outs
    copies = [
        pltpu.make_async_copy(source, target, arrived.at[k])
        for k, (source, target) in enumerate(
            ((mixer_w, mixer_here), (gate_w, gate_here), (up_w, up_here))
        )
    ]
    for copy in copies:
        copy.start()
    at_x = lax.rem(position[0], xs)
    count = logs.shape[0]
    enter = halves(jnp.exp(logs[...]) * marks[:, MARK_ENTER : MARK_ENTER + 1])
    head_lanes(selector)
    for pair in range(PAIRS):
        entering[:, lanes_of(pair)] = picked(pieces, at_x, pair)
    wide[...] = dot(enter, selector[...])
    gated[...] = dot(readout[...], entering[...])
    square = jnp.zeros((count, LANES), F32)
    for pair in range(PAIRS):
        span = lanes_of(pair)
        full = inner_part[:, span] + gated[:, span] * wide[:, span]
        scanned[:, span] = full
        gate = gating[:, span]
        skip = table[ROW_SKIP : ROW_SKIP + 1, span]
        full = (full + skip * channels[:, span]) * (gate * jax.nn.sigmoid(gate))
        gated[:, span] = full
        square = square + full * full
    scale = lax.rsqrt(jnp.sum(square, -1, keepdims=True) / WIDTH + EPS)
    scale = jnp.broadcast_to(scale, (count, LANES))
    for pair in range(PAIRS):
        span = lanes_of(pair)
        gain = table[ROW_MIXER : ROW_MIXER + 1, span]
        tail[:, span] = (gated[:, span] * scale * gain).astype(BF16)
    copies[0].wait()
    mixed = low_input[...].astype(F32) + branch[...] + dot(tail[...], mixer_here[...])
    mixed_sum[...] = mixed
    scale = lax.rsqrt(jnp.mean(mixed * mixed, -1, keepdims=True) + EPS)
    feed_low[...] = (mixed * scale * feed_gain[...].reshape(1, mixed.shape[1])).astype(BF16)
    copies[1].wait()
    copies[2].wait()
    for start in range(0, gate_raw.shape[1], 512):
        span = slice(start, start + 512)
        gate = dot(feed_low[...], gate_here[:, span])
        up = dot(feed_low[...], up_here[:, span])
        gate_raw[:, span] = gate
        up_raw[:, span] = up
        activated[:, span] = (gate * jax.nn.sigmoid(gate) * up).astype(BF16)


def tail_back_kernel(
    xs, position, branch, mixer_w, scanned, channels, gating, table, logs, marks, readout,
    scanned_slope, gating_slope, sums, *refs,
):
    states, (gated, hold, selector, wide, weighted, slope) = refs[:xs], refs[xs:]
    for start in range(0, WIDTH, 512):
        span = slice(start, start + 512)
        slope[:, span] = dot_lanes(branch[...], mixer_w[span])
    at_x = lax.rem(position[0], xs)
    count = logs.shape[0]
    enter = halves(jnp.exp(logs[...]) * marks[:, MARK_ENTER : MARK_ENTER + 1])
    head_lanes(selector)
    wide[...] = dot(enter, selector[...])
    square = jnp.zeros((count, LANES), F32)
    cross = jnp.zeros((count, LANES), F32)
    for pair in range(PAIRS):
        span = lanes_of(pair)
        gate = gating[:, span]
        full = scanned[:, span] + table[ROW_SKIP : ROW_SKIP + 1, span] * channels[:, span]
        full = full * (gate * jax.nn.sigmoid(gate))
        gated[:, span] = full
        gain = table[ROW_MIXER : ROW_MIXER + 1, span]
        square = square + full * full
        cross = cross + full * slope[:, span] * gain
    scale = lax.rsqrt(jnp.sum(square, -1, keepdims=True) / WIDTH + EPS)
    cross = jnp.sum(cross, -1, keepdims=True) / WIDTH * scale * scale * scale
    scale = jnp.broadcast_to(scale, (count, LANES))
    cross = jnp.broadcast_to(cross, (count, LANES))
    for pair in range(PAIRS):
        span = lanes_of(pair)
        gate = gating[:, span]
        sigmoid = jax.nn.sigmoid(gate)
        back = slope[:, span]
        value = gated[:, span]
        sums[0:1, span] = jnp.sum(back * value * scale, 0, keepdims=True)
        back = back * table[ROW_MIXER : ROW_MIXER + 1, span] * scale - value * cross
        held = channels[:, span]
        full = scanned[:, span] + table[ROW_SKIP : ROW_SKIP + 1, span] * held
        gating_slope[:, span] = (
            back * full * sigmoid * (1.0 + gate * (1.0 - sigmoid))
        ).astype(BF16)
        back = back * (gate * sigmoid)
        sums[1:2, span] = jnp.sum(back * held, 0, keepdims=True)
        scanned_slope[:, span] = back.astype(BF16)
        weighted[:, span] = (back * wide[:, span]).astype(BF16)
    hold_all(hold, slice(0, STATE), dot(readout[...].T, weighted[...]).astype(BF16))
    hand_out(hold, at_x, states)
    sums[2:8] = jnp.zeros((6, WIDTH), F32)


def leaving_kernel(
    xs, position, entering, scanned, scanned_slope, scaled, channels, scaled_slope,
    inflow, readout, inflow_part, readout_part, steps, raw, logs, marks, inner, factor, taps, table,
    *refs,
):
    pieces, outs = refs[:xs], refs[xs:]
    inner_low, edges, conv_sums, raw_slope, small, conv_slope, selector, *outs = outs
    low, outer, lengths, tails, enters, first, second, third, fourth, fifth = outs
    at_x = lax.rem(position[0], xs)
    rates = table[ROW_RATE : ROW_RATE + 1, :LANES]
    count = logs.shape[0]
    ending = logs[count - 1 : count]
    head_lanes(selector)
    stepped = steps[...]
    for pair in range(PAIRS):
        low[:, lanes_of(pair)] = picked(pieces, at_x, pair)
    outer[...] = dot(inflow[...], low[...])
    lengths[...] = dot(halves(stepped), selector[...])
    tail = jnp.exp(ending - logs[...]) * marks[:, MARK_TAIL : MARK_TAIL + 1]
    tails[...] = dot(halves(tail), selector[...])
    enter = jnp.exp(logs[...]) * marks[:, MARK_ENTER : MARK_ENTER + 1]
    enters[...] = dot(halves(enter), selector[...])
    through = jnp.zeros((8, LANES), F32)
    for pair in range(PAIRS):
        span = lanes_of(pair)
        wide = scanned_slope[:, span].astype(F32)
        held = channels[:, span]
        short = scaled[:, span].astype(F32)
        tail = tails[:, span]
        part = outer[:, span] * tail
        within = scaled_slope[:, span]
        both = within + part
        split_into(first, span, wide * scanned[:, span] - short * within)
        split_into(second, span, short * part)
        split_into(third, span, held * both)
        fourth[:, span] = (short * tail).astype(BF16)
        fifth[:, span] = (wide * enters[:, span]).astype(BF16)
        skip = table[ROW_SKIP : ROW_SKIP + 1, span]
        conv_slope[:, span] = both * lengths[:, span] + skip * wide
        kept = low[:, span].astype(F32) * entering[:, span].astype(F32)
        kept = jnp.sum(kept, 0, keepdims=True) * jnp.exp(spread_pair(ending, pair))
        kept = halves(jnp.broadcast_to(kept, (8, LANES)))
        chosen = selector[:LANES, span]
        through = through + dot_lanes(kept, jnp.concatenate([chosen, chosen], 1))
    inside, outward = head_sums(first, selector), head_sums(second, selector)
    direct = head_sums(third, selector)
    inflow_slope = inflow_part[...] + dot_lanes(fourth[...], low[...])
    readout_slope = readout_part[...] + dot_lanes(fifth[...], entering[...])
    conv_slope[:, lanes_of(PAIRS)] = inflow_slope
    conv_slope[:, lanes_of(PAIRS + 1)] = readout_slope
    enter_last = marks[count - 1 :, MARK_ENTER : MARK_ENTER + 1]
    along = (
        precise(triangle(count, upper=True), inside)
        + precise(triangle(count, strict=True), outward)
        + through[:1] * enter_last
    )
    step_slope = direct + rates * along
    step_slope = step_slope * jax.nn.sigmoid(raw[...] + table[ROW_STEP : ROW_STEP + 1, :LANES])
    raw_slope[...] = step_slope.astype(BF16)
    small[0:1] = jnp.sum(step_slope, 0, keepdims=True)
    small[1:2] = rates * jnp.sum(stepped * along, 0, keepdims=True)
    small[2:8] = jnp.zeros((6, LANES), F32)
    blank = jnp.zeros((HALO, LANES), F32)
    marked = wide_marks(marks)
    for chunk in range(PAIRS + 2):
        span = lanes_of(chunk)
        extended = inner[:, span].astype(F32)
        slope = conv_slope[:, span] * factor[:, span].astype(F32)
        spread = jnp.zeros((HALO + count, LANES), F32)
        for tap in range(KERNEL):
            part = slope * marked[tap] if tap < KERNEL - 1 else slope
            part = jnp.concatenate([blank, part], 0)
            if tap < KERNEL - 1:
                part = pltpu.roll(part, HALO + count - (KERNEL - 1 - tap), 0)
            conv_sums[tap : tap + 1, span] = jnp.sum(part * extended, 0, keepdims=True)
            spread = spread + part * taps[tap : tap + 1, span]
        conv_sums[KERNEL : KERNEL + 1, span] = jnp.sum(slope, 0, keepdims=True)
        conv_sums[KERNEL + 1 :, span] = jnp.zeros((8 - KERNEL - 1, LANES), F32)
        inner_low[:, span] = spread[HALO:].astype(BF16)
        edges[:HALO, span] = spread[:HALO]
        edges[HALO:, span] = spread[count:]


PACK_ROWS = 48


def unit_back_kernel(slope, down_w, gate_raw, up_raw, gate_low, up_low):
    for start in range(0, gate_raw.shape[1], 512):
        span = slice(start, start + 512)
        back = dot_lanes(slope[...], down_w[span])
        gate = gate_raw[:, span]
        sigmoid = jax.nn.sigmoid(gate)
        up_low[:, span] = (back * (gate * sigmoid)).astype(BF16)
        back = back * up_raw[:, span]
        gate_low[:, span] = (back * (sigmoid * (1.0 + gate * (1.0 - sigmoid)))).astype(BF16)


def feed_back_kernel(
    gate_low, up_low, gate_w, up_w, mixed_sum, slope, gain, mixed_slope, branch_low, sums
):
    values = mixed_sum[...]
    count, width = values.shape
    scale = lax.rsqrt(jnp.mean(values * values, -1, keepdims=True) + EPS)
    back = dot_lanes(gate_low[...], gate_w[...]) + dot_lanes(up_low[...], up_w[...])
    sums[...] = jnp.broadcast_to(jnp.sum(back * values * scale, 0, keepdims=True), sums.shape)
    back = back * gain[...].reshape(1, width)
    cross = jnp.mean(back * values, -1, keepdims=True) * scale * scale * scale
    whole = slope[...].astype(F32) + back * scale - values * cross
    mixed_slope[...] = whole
    branch_low[...] = whole.astype(BF16)


def finish_kernel(
    gating_low, query_low, inner_low, pair_low, gating_w, query_w, inner_w, key_w, value_w, step_w,
    low_input, table, mixed_slope, raw_slope, normed, tail_sums, conv_sums, small, feed,
    input_gradient, packed,
):
    normed_slope = (
        dot_lanes(gating_low[...], gating_w[...])
        + dot_lanes(query_low[...], query_w[...])
        + dot_lanes(inner_low[...], inner_w[...])
        + dot_lanes(pair_low[:, :LANES], key_w[...])
        + dot_lanes(pair_low[:, LANES:], value_w[...])
        + dot(raw_slope[:, :SSM_HEADS], step_w[...])
    )
    values = low_input[...].astype(F32)
    width = values.shape[1]
    scale = lax.rsqrt(jnp.mean(values * values, -1, keepdims=True) + EPS)
    slope = normed_slope
    packed[SSM_HEADS : SSM_HEADS + 1] = jnp.sum(slope * values * scale, 0, keepdims=True)
    slope = slope * table[ROW_GAIN : ROW_GAIN + 1, :width]
    cross = jnp.mean(slope * values, -1, keepdims=True) * scale * scale * scale
    input_gradient[...] = mixed_slope[...] + slope * scale - values * cross
    packed[:SSM_HEADS] = dot_rows(raw_slope[...], normed[...])[:SSM_HEADS]
    packed[SSM_HEADS + 1 : SSM_HEADS + 2] = feed[:1]
    packed[SSM_HEADS + 2 :] = jnp.zeros((PACK_ROWS - SSM_HEADS - 2, width), F32)
    row = SSM_HEADS + 2
    for source, rows in ((tail_sums, 2), (small, 2), (conv_sums, KERNEL + 1)):
        for index in range(rows):
            for start in range(0, source.shape[1], width):
                stop = min(start + width, source.shape[1])
                packed[row : row + 1, : stop - start] = source[index : index + 1, start:stop]
                row += 1


def unpack_kernel(packed, step, gain, feed, mixer_gain, skip, step_bias, decay, conv, conv_bias):
    width = packed.shape[1]
    step[...] = packed[:SSM_HEADS].T
    row = SSM_HEADS

    def taken(size):
        nonlocal row
        pieces = []
        for start in range(0, size, width):
            pieces.append(packed[row : row + 1, : min(width, size - start)])
            row += 1
        return pieces[0] if len(pieces) == 1 else jnp.concatenate(pieces, 1)

    gain[...] = taken(width).reshape(width)
    feed[...] = taken(width).reshape(width)
    mixer_gain[...] = taken(WIDTH).reshape(WIDTH)
    lanes = taken(WIDTH)
    head = lax.broadcasted_iota(jnp.int32, (1, LANES), 1)
    sums = jnp.zeros((1, LANES), F32)
    for index in range(SSM_HEADS):
        part = lanes[:, index * SSM_HEAD : (index + 1) * SSM_HEAD]
        sums = jnp.where(head == index, jnp.sum(part, 1, keepdims=True), sums)
    skip[...] = sums[:, :SSM_HEADS].reshape(SSM_HEADS)
    step_bias[...] = taken(LANES)[:, :SSM_HEADS].reshape(SSM_HEADS)
    decay[...] = taken(LANES)[:, :SSM_HEADS].reshape(SSM_HEADS)
    for tap in range(KERNEL):
        conv[tap : tap + 1] = taken(conv.shape[1])
    conv_bias[...] = taken(conv.shape[1]).reshape(conv.shape[1])


def all_sum(place, shard, axes):
    for name in axes:
        axis = name[0] if name[0] == "z" else name
        bit = 2 if name == "zh" else 1
        while bit < (2 if name == "zl" else place.sizes[axis]):
            low = shard.astype(BF16)
            shard = low.astype(F32) + place.swap(low, axis, bit).astype(F32)
            bit *= 2
    return shard


def joint_kernel(xs, ys, widths, left, left_sib, right, right_sib, *outs):
    rows = left.shape[0] // len(widths)
    part = rows // (xs * ys)
    start = offset = 0
    for section, width in enumerate(widths):
        span = slice(section * rows, (section + 1) * rows)
        half = width // 2
        tile = next(t for t in (512, 384, 256, 128) if half % t == 0)
        for first in range(2):
            targets = outs[xs:] if first else outs[:xs]
            for column in range(0, half, tile):
                source = slice(start + first * half + column, start + first * half + column + tile)
                total = dot(left[span], right[:, source]) + dot(left_sib[span], right_sib[:, source])
                total = total.astype(BF16)
                into = slice(offset + column, offset + column + tile)
                for x in range(xs):
                    for y in range(ys):
                        piece = total[(x * ys + y) * part : (x * ys + y + 1) * part]
                        if first:
                            targets[y][x * part : (x + 1) * part, into] = piece
                        else:
                            targets[x][y * part : (y + 1) * part, into] = piece
        start += width
        offset += half


def joint_gradient(place, left, right, left_sib, right_sib, widths):
    sections = len(widths)
    rows, tokens = left.shape[0] // sections, left.shape[1]
    width = sum(widths)
    xs, ys = place.sizes["x"], place.sizes["y"]
    half = width // 2
    shapes = [(rows // xs, half)] * xs + [(rows // ys, half)] * ys
    outs = local_call(
        functools.partial(joint_kernel, xs, ys, widths),
        [(shape, BF16) for shape in shapes],
        (left, left_sib, right, right_sib),
        "joint_gradient",
    )
    return outs[:xs], outs[xs:]


def arranged(order, left):
    return lax.dot_general(
        order, left, (((1,), (1,)), ((), ())), preferred_element_type=jnp.float32
    ).astype(jnp.bfloat16)


def own_half(ordered):
    return ordered[: ordered.shape[0] // CORES]


def other_half(ordered):
    return ordered[ordered.shape[0] // CORES :]


def together(*values):
    return lax.optimization_barrier(values)


def fold_kernel(counts, splits, merged, *refs):
    at = 0
    outs = refs[sum(counts) :]
    for block, count in enumerate(counts):
        total = refs[at][...].astype(F32)
        for ref in refs[at + 1 : at + count]:
            total = total + ref[...].astype(F32)
        at += count
        low = total.astype(BF16)
        rows = low.shape[-2] // splits[block]
        for k in range(splits[block]):
            piece = low[..., k * rows : (k + 1) * rows, :]
            if merged:
                outs[k][block] = piece
            else:
                outs[sum(splits[:block]) + k][...] = piece


def fold(blocks, splits, merged):
    flat = [a for block in blocks for a in block]
    shape = flat[0].shape
    columns = shape[-1]
    tile = max(t for t in range(LANES, 1025, LANES) if columns % t == 0 and t <= columns // 2)

    def spec(full):
        lead = (0,) * (len(full) - 1)
        return pl.BlockSpec(full[:-1] + (tile,), lambda j: lead + (j,))

    if merged:
        outs = [(len(blocks), shape[0] // splits[0], columns)] * splits[0]
    else:
        outs = []
        for block, cuts in zip(blocks, splits):
            full = block[0].shape
            outs += [full[:-2] + (full[-2] // cuts, columns)] * cuts
    return pl.pallas_call(
        functools.partial(fold_kernel, [len(b) for b in blocks], splits, merged),
        grid=(columns // tile,),
        in_specs=[spec(a.shape) for a in flat],
        out_specs=[spec(full) for full in outs],
        out_shape=[jax.ShapeDtypeStruct(full, BF16) for full in outs],
        compiler_params=pltpu.CompilerParams(vmem_limit_bytes=12 * 1024 * 1024),
        cost_estimate=pl.CostEstimate(flops=0, bytes_accessed=0, transcendentals=0),
        name="fold",
    )(*flat)


class Shares:
    ORDERS = (("x", "y"), ("y", "x"))

    def __init__(self, place, lefts, rights):
        self.place = place
        self.widths = [sum(r.shape[1] for r in section) for section in rights]
        self.columns = [[r.shape[1] for r in section] for section in rights]
        flat = [r for section in rights for r in section]
        self.right = jnp.concatenate(flat, 1) if len(flat) > 1 else flat[0]
        self.lefts = lefts

    def to_core(self):
        return self.right

    def go_core(self, sent):
        return self.place.turn(sent, "core", 1)

    def join(self, left_siblings, right_sibling):
        left, sibling = (
            (pieces[0] if len(pieces) == 1 else jnp.concatenate(pieces, 0))
            for pieces in ([own_half(left) for left in self.lefts], left_siblings)
        )
        self.pieces = joint_gradient(
            self.place, left, self.right, sibling, right_sibling, self.widths
        )
        return tuple(tuple(pieces[1:]) for pieces in self.pieces)

    def go(self, sent, stage):
        return tuple(
            tuple(self.place.turn(piece, order[stage], k + 1) for k, piece in enumerate(pieces))
            for pieces, order in zip(sent, self.ORDERS)
        )

    def to_second(self, arrived):
        splits = [self.place.sizes[order[1]] for order in self.ORDERS]
        blocks = [(self.pieces[half][0],) + arrived[half] for half in range(2)]
        outs = fold(blocks, splits, False)
        self.kept = (outs[0], outs[splits[0]])
        return tuple(outs[1 : splits[0]]), tuple(outs[splits[0] + 1 :])

    def to_third(self, arrived):
        blocks = [(self.kept[half],) + arrived[half] for half in range(2)]
        self.kept, sent = fold(blocks, (2, 2), True)
        return sent

    def go_third(self, sent):
        return self.place.swap(sent, "z", 1)

    def to_fourth(self, arrived):
        self.kept, sent = fold([(self.kept, arrived)], (2,), False)
        return sent

    def go_fourth(self, sent):
        return self.place.swap(sent, "z", 2)

    def to_owners(self, arrived):
        cuts = self.place.sizes["z"]
        blocks = [(self.kept[half],) + arrived[half] for half in range(2)]
        self.kept, *sent = fold(blocks, (cuts, cuts), True)
        return tuple(sent)

    def go_owners(self, sent):
        return tuple(
            self.place.swap(piece, "z", k // 2 + 2 * (k % 2))
            for k, piece in enumerate(sent, start=1)
        )

    def split(self, arrived, widths):
        rows = self.kept.shape[1]
        summands = (self.kept,) + tuple(arrived)
        return local_call(
            functools.partial(split_kernel, len(summands)),
            [((rows, w), F32) for w in widths],
            summands,
            "split",
        )

    def shares(self, *arrived):
        total = self.kept.astype(F32)
        for piece in arrived:
            total = total + piece.astype(F32)
        shares = []
        offset = 0
        for width, columns in zip(self.widths, self.columns):
            section = jnp.concatenate(
                [total[half, :, offset : offset + width // 2] for half in range(2)], 1
            )
            offset += width // 2
            start = 0
            for w in columns:
                shares.append(section[:, start : start + w])
                start += w
        return shares


def split_kernel(count, *refs):
    total = sum(ref[...].astype(F32) for ref in refs[:count])
    half = total.shape[2]
    start = 0
    for out in refs[count:]:
        stop = start + out.shape[1]
        for k in range(2):
            low, high = max(start, k * half), min(stop, (k + 1) * half)
            if low < high:
                out[:, low - start : high - start] = total[k, :, low - k * half : high - k * half]
        start = stop


class KeyOwners:
    def __init__(self, place, slopes):
        self.place = place
        self.paired = place.sizes["x"] == 2
        self.kept = slopes

    def to_first(self):
        if not self.paired:
            return self.kept
        half = self.kept.shape[0] // 2
        sent = self.kept[half:]
        self.kept = self.kept[:half]
        return sent

    def go(self, sent, stage):
        if not self.paired:
            if stage:
                return sent
            return lax.psum_scatter(sent, "seq", scatter_dimension=0, tiled=True)
        axis, bit = (("z", 1), ("z", 2), ("x", 1))[stage]
        return self.place.swap(sent, axis, bit)

    def to_next(self, arrived):
        if not self.paired:
            return arrived
        total = (self.kept.astype(F32) + arrived.astype(F32)).astype(BF16)
        half = total.shape[0] // 2
        self.kept = total[:half]
        return total[half:]

    def summands(self, arrived):
        return (self.kept, arrived) if self.paired else (arrived,)


def body(
    inputs,
    segments,
    cotangent,
    input_gain,
    query_weight,
    key_weight,
    value_weight,
    attention_weight,
    gating_weight,
    inner_weight,
    step_weight,
    step_bias,
    decay_log,
    skip_scale,
    conv_weight,
    conv_bias,
    mixer_gain,
    mixer_weight,
    feed_gain,
    gate_weight,
    up_weight,
    down_weight,
):
    place = Place()
    xs = place.sizes["x"]
    count, width = inputs.shape[1], inputs.shape[2]
    low_input = inputs[0]
    hidden = low_input.astype(F32)
    slope = cotangent[0]
    seg_row = segments[0]
    length = seg_row.shape[0]
    group, along = lax.axis_index("dp"), lax.axis_index("seq")
    position = along.reshape(1).astype(jnp.int32)
    inner_width = inner_weight.shape[1]
    part_width = WIDTH // xs

    halo, low_input = together(low_input[count - HALO :], low_input)
    halo = passed_along(halo, "seq", 1)
    cosine, sine = turn_tables(along * count, count)
    normed_low, pairs, table = local_call(
        front_kernel,
        [((count, width), BF16), ((count, 2 * LANES), BF16), ((8, inner_width), F32)],
        (
            low_input,
            key_weight,
            value_weight,
            cosine,
            sine,
            conv_bias,
            input_gain,
            mixer_gain,
            skip_scale,
            step_bias,
            decay_log,
        ),
        "front",
        alone=True,
    )
    near = jnp.concatenate([pairs] + [place.turn(pairs, "x", k) for k in range(1, xs)], 0)
    near, halo, normed_low = together(near, halo, normed_low)
    far = tuple(place.turn(near, "z", k) for k in range(1, place.sizes["z"]))
    step_turned = step_weight.T
    (
        inner,
        raw,
        channels,
        scaled,
        inflow,
        readout,
        steps,
        logs,
        logs_turned,
        marks,
        marks_turned,
        factor,
        *states,
    ) = local_call(
        functools.partial(prep_kernel, xs),
        [
            ((HALO + count, inner_width), BF16),
            ((count, LANES), F32),
            ((count, WIDTH), F32),
            ((count, WIDTH), BF16),
            ((count, STATE), BF16),
            ((count, STATE), BF16),
            ((count, LANES), F32),
            ((count, LANES), F32),
            ((LANES, count), F32),
            ((count, 8), F32),
            ((8, count), F32),
            ((count, inner_width), BF16),
        ]
        + [((STATE + EXTRA, part_width), BF16)] * xs,
        (position, halo, normed_low, table, inner_weight, step_turned, conv_weight, segments),
        "prepare",
        alone=True,
        scratch=[
            pltpu.VMEM((HALO + count, width), BF16),
            pltpu.VMEM((xs, STATE + EXTRA, part_width), BF16),
            pltpu.VMEM((2 * LANES, WIDTH), BF16),
            pltpu.VMEM((count, WIDTH), F32),
            pltpu.VMEM((count, WIDTH), F32),
            pltpu.VMEM((count, WIDTH), BF16),
        ],
        smem=(0,),
    )

    states, normed_low, group, along = together(tuple(states), normed_low, group, along)
    pieces = dealt(place, states)
    gating = product(normed_low, gating_weight)
    order = place.share_order(width, group, along)
    ordered = arranged(order, normed_low)
    pieces, gating, normed_low, order, ordered = together(
        pieces, gating, normed_low, order, ordered
    )
    total, walls = level(place, pieces, position, seg_row, count)

    total, normed_low, ordered, scaled = together(total, normed_low, ordered, scaled)
    totals = levels_met(place, total)
    fixed = (logs, logs_turned, marks, marks_turned, inflow, readout)
    (inner_part,) = inner_call(inner_kernel, fixed, (scaled,), (F32,), (), "inner", 2)

    ordered_sibling = place.turn(other_half(ordered), "core", 1)
    queries, attention_low, exact, spread, everything = local_call(
        functools.partial(attend_kernel, xs),
        [
            ((count, HEADS * HEAD), BF16),
            ((count, HEADS * HEAD), BF16),
            ((HEADS * HEAD, count), F32),
            ((HEADS, count), F32),
            ((length, 2 * LANES), BF16),
        ],
        (position, normed_low, query_weight, cosine, sine, segments, near, *far),
        "attend",
        slack=8,
        scratch=[
            pltpu.VMEM((HEADS, count), F32),
            pltpu.VMEM((HEADS, count), F32),
            pltpu.VMEM((HEADS * HEAD, count), F32),
        ],
        smem=(0,),
        far=tuple(range(6, 7 + len(far))),
        sems=(1 + len(far),),
    )
    totals, attention_low, ordered_sibling, inner_part, slope, order = together(
        totals, attention_low, ordered_sibling, inner_part, slope, order
    )
    results, level_walls = arrival(
        place, pieces, totals, walls, total, position, seg_row, count
    )

    results, attention_low, slope, order = together(results, attention_low, slope, order)
    pieces = dealt(place, results)
    attention_branch = product(attention_low, attention_weight)
    ordered_slope = arranged(order, slope)
    pieces, attention_branch, ordered_slope = together(pieces, attention_branch, ordered_slope)
    hidden_width = gate_weight.shape[1]
    (
        tail_low,
        scanned,
        entering,
        mixed_sum,
        feed_low,
        gate_raw,
        up_raw,
        activated_low,
    ) = local_call(
        functools.partial(entering_kernel, xs),
        [
            ((count, WIDTH), BF16),
            ((count, WIDTH), F32),
            ((STATE, WIDTH), BF16),
            ((count, width), F32),
            ((count, width), BF16),
            ((count, hidden_width), F32),
            ((count, hidden_width), F32),
            ((count, hidden_width), BF16),
        ],
        (
            position,
            inner_part,
            readout,
            logs,
            marks,
            channels,
            gating,
            table,
            low_input,
            attention_branch,
            feed_gain,
            mixer_weight,
            gate_weight,
            up_weight,
            *pieces,
        ),
        "entering",
        scratch=[
            pltpu.VMEM((count, WIDTH), F32),
            pltpu.VMEM((2 * LANES, WIDTH), BF16),
            pltpu.VMEM((count, WIDTH), F32),
            pltpu.VMEM(mixer_weight.shape, BF16),
            pltpu.VMEM(gate_weight.shape, BF16),
            pltpu.VMEM(up_weight.shape, BF16),
        ],
        sems=(3,),
        smem=(0,),
        far=(11, 12, 13),
    )

    down = Shares(place, (ordered_slope,), ((activated_low,),))
    sent, slope_half, gate_raw, up_raw, slope, feed_low, order = together(
        down.to_core(), other_half(ordered_slope), gate_raw, up_raw, slope, feed_low, order
    )
    arrived = down.go_core(sent)
    slope_sibling = place.turn(slope_half, "core", 1)
    gate_low, up_low = local_call(
        unit_back_kernel,
        [(gate_raw.shape, BF16), (up_raw.shape, BF16)],
        (slope, down_weight, gate_raw, up_raw),
        "unit_back",
    )
    ordered_feed = arranged(order, feed_low)
    arrived, slope_sibling, gate_low, up_low, ordered_feed = together(
        arrived, slope_sibling, gate_low, up_low, ordered_feed
    )
    sent = down.join([slope_sibling], arrived)

    gate = Shares(place, (ordered_feed,), ((gate_low,),))
    up = Shares(place, (ordered_feed,), ((up_low,),))
    sent, feed_half, gate_low, up_low = together(
        sent, other_half(ordered_feed), gate_low, up_low
    )
    arrived = down.go(sent, 0)
    gate_arrived, up_arrived = gate.go_core(gate_low), up.go_core(up_low)
    feed_sibling = place.turn(feed_half, "core", 1)
    mixed_slope, branch_low, feed_sums = local_call(
        feed_back_kernel,
        [((count, width), F32), ((count, width), BF16), ((8, width), F32)],
        (gate_low, up_low, gate_weight, up_weight, mixed_sum, slope, feed_gain),
        "feed_back",
    )
    scanned_slope, gating_low, tail_sums, *state_slopes = local_call(
        functools.partial(tail_back_kernel, xs),
        [((count, WIDTH), BF16), ((count, WIDTH), BF16), ((8, WIDTH), F32)]
        + [((STATE, part_width), BF16)] * xs,
        (
            position,
            branch_low,
            mixer_weight,
            scanned,
            channels,
            gating,
            table,
            logs,
            marks,
            readout,
        ),
        "tail_back",
        scratch=[
            pltpu.VMEM((count, WIDTH), F32),
            pltpu.VMEM((xs, STATE, part_width), BF16),
            pltpu.VMEM((2 * LANES, WIDTH), BF16),
            pltpu.VMEM((count, WIDTH), F32),
            pltpu.VMEM((count, WIDTH), BF16),
            pltpu.VMEM((count, WIDTH), F32),
        ],
        smem=(0,),
    )
    (
        arrived,
        gate_arrived,
        up_arrived,
        feed_sibling,
        state_slopes,
        branch_low,
        scanned_slope,
        gating_low,
        order,
    ) = together(
        arrived,
        gate_arrived,
        up_arrived,
        feed_sibling,
        tuple(state_slopes),
        branch_low,
        scanned_slope,
        gating_low,
        order,
    )

    gate_sent = gate.join([feed_sibling], gate_arrived)
    ordered_branch = arranged(order, branch_low)
    mixers = Shares(place, (ordered_branch, ordered), ((attention_low, tail_low), (gating_low,)))
    state_slopes, gate_sent, mixers_sent, branch_half, arrived, branch_low = together(
        state_slopes,
        gate_sent,
        mixers.to_core(),
        other_half(ordered_branch),
        arrived,
        branch_low,
    )
    state_pieces = dealt(place, state_slopes)
    gate_arrived = gate.go(gate_sent, 0)
    mixers_arrived = mixers.go_core(mixers_sent)
    branch_sibling = place.turn(branch_half, "core", 1)
    attention_slope = product_right(branch_low, attention_weight).astype(BF16)
    down_sent = down.to_second(arrived)
    mixers_sent = mixers.join([branch_sibling, ordered_sibling], mixers_arrived)
    state_pieces, gate_arrived, mixers_sent, down_sent, attention_slope = together(
        state_pieces, gate_arrived, mixers_sent, down_sent, attention_slope
    )
    total = level_back(place, state_pieces, walls, position, seg_row, count)

    total, mixers_sent, attention_slope, up_arrived, feed_sibling, gate_arrived = together(
        total, mixers_sent, attention_slope, up_arrived, feed_sibling, gate_arrived
    )
    totals = levels_met(place, total)
    mixers_arrived = mixers.go(mixers_sent, 0)
    query_low, pair_slope = local_call(
        functools.partial(attend_back_kernel, xs),
        [((count, HEADS * HEAD), BF16), ((length, 2 * LANES), BF16)],
        (
            position,
            queries,
            everything,
            attention_slope,
            exact,
            spread,
            segments,
            cosine,
            sine,
        ),
        "attend_back",
        scratch=[
            pltpu.VMEM((HEADS * HEAD, count), F32),
            pltpu.VMEM((HEADS, count), F32),
            pltpu.VMEM((HEADS * HEAD, count), F32),
        ],
        smem=(0,),
    )
    owners = KeyOwners(place, pair_slope)
    pair_sent = owners.to_first()
    up_sent = up.join([feed_sibling], up_arrived)
    totals, mixers_arrived, pair_sent, up_sent = together(
        totals, mixers_arrived, pair_sent, up_sent
    )
    results = arrival_back(
        place, state_pieces, totals, walls, level_walls, position, seg_row, count
    )

    (
        results,
        pair_sent,
        up_sent,
        mixers_arrived,
        gate_arrived,
        scanned_slope,
        activated_low,
    ) = together(
        results, pair_sent, up_sent, mixers_arrived, gate_arrived, scanned_slope, activated_low
    )
    pieces = dealt(place, results)
    pair_arrived = owners.go(pair_sent, 0)
    up_arrived = up.go(up_sent, 0)
    scaled_slope, inflow_part, readout_part = inner_call(
        inner_back_kernel,
        fixed,
        (scaled, scanned_slope),
        (F32,),
        (((count, STATE), F32), ((count, STATE), F32)),
        "inner_back",
        3,
    )
    mixers_sent = mixers.to_second(mixers_arrived)
    gate_sent = gate.to_second(gate_arrived)
    output = (mixed_sum + product(activated_low, down_weight)).astype(BF16)
    pieces, pair_arrived, up_arrived, mixers_sent, gate_sent, scaled_slope, output = together(
        pieces, pair_arrived, up_arrived, mixers_sent, gate_sent, scaled_slope, output
    )

    pieces, pair_sent, mixers_sent, gate_sent, up_arrived = together(
        pieces, owners.to_next(pair_arrived), mixers_sent, gate_sent, up_arrived
    )
    mixers_arrived = mixers.go(mixers_sent, 1)
    gate_arrived = gate.go(gate_sent, 1)
    pair_arrived = owners.go(pair_sent, 1)
    inner_low, edges, conv_sums, raw_slope, small = local_call(
        functools.partial(leaving_kernel, xs),
        [
            ((count, inner_width), BF16),
            ((2 * HALO, inner_width), F32),
            ((8, inner_width), F32),
            ((count, LANES), BF16),
            ((8, LANES), F32),
        ],
        (
            position,
            entering,
            scanned,
            scanned_slope,
            scaled,
            channels,
            scaled_slope,
            inflow,
            readout,
            inflow_part,
            readout_part,
            steps,
            raw,
            logs,
            marks,
            inner,
            factor,
            conv_weight,
            table,
            *pieces,
        ),
        "leaving",
        scratch=[
            pltpu.VMEM((count, inner_width), F32),
            pltpu.VMEM((2 * LANES, WIDTH), BF16),
            pltpu.VMEM((STATE, WIDTH), BF16),
        ]
        + [pltpu.VMEM((count, WIDTH), F32)] * 4
        + [pltpu.VMEM((2, count, WIDTH), BF16)] * 3
        + [pltpu.VMEM((count, WIDTH), BF16)] * 2,
        smem=(0,),
    )
    mixers_arrived, gate_arrived, pair_arrived, inner_low, edges = together(
        mixers_arrived, gate_arrived, pair_arrived, inner_low, edges
    )

    mixers_sent, pair_sent, down_sent, inner_low, edges, up_arrived, gate_arrived = together(
        mixers.to_third(mixers_arrived),
        owners.to_next(pair_arrived),
        down_sent,
        inner_low,
        edges,
        up_arrived,
        gate_arrived,
    )
    returned = passed_along(edges[HALO - 8 : HALO], "seq", -1)
    pair_arrived = owners.go(pair_sent, 2)
    down_arrived = down.go(down_sent, 1)
    mixers_arrived = mixers.go_third(mixers_sent)
    up_sent = up.to_second(up_arrived)
    gate_sent = gate.to_third(gate_arrived)
    returned, pair_arrived, down_arrived, mixers_arrived, up_sent, gate_sent = together(
        returned, pair_arrived, down_arrived, mixers_arrived, up_sent, gate_sent
    )
    inner_low = lax.dynamic_update_slice(
        inner_low,
        (edges[HALO:] + jnp.pad(returned, ((HALO - 8, 0), (0, 0)))).astype(BF16),
        (count - HALO, 0),
    )
    (pair_low,) = local_call(
        pairs_back_kernel,
        [((count, 2 * LANES), BF16)],
        (*owners.summands(pair_arrived), cosine, sine),
        "pairs_back",
    )

    rest = Shares(place, (ordered,), ((inner_low, query_low, pair_low),))
    (
        rest_sent,
        up_sent,
        mixers_arrived,
        gate_sent,
        down_arrived,
        gating_low,
        query_low,
        pair_low,
        inner_low,
    ) = together(
        rest.to_core(),
        up_sent,
        mixers_arrived,
        gate_sent,
        down_arrived,
        gating_low,
        query_low,
        pair_low,
        inner_low,
    )
    rest_arrived = rest.go_core(rest_sent)
    up_arrived = up.go(up_sent, 1)
    mixers_arrived = mixers.go_fourth(mixers.to_fourth(mixers_arrived))
    gate_arrived = gate.go_third(gate_sent)
    input_gradient, packed = local_call(
        finish_kernel,
        [((count, width), F32), ((PACK_ROWS, width), F32)],
        (
            gating_low,
            query_low,
            inner_low,
            pair_low,
            gating_weight,
            query_weight,
            inner_weight,
            key_weight,
            value_weight,
            step_turned,
            low_input,
            table,
            mixed_slope,
            raw_slope,
            normed_low,
            tail_sums,
            conv_sums,
            small,
            feed_sums,
        ),
        "finish",
    )
    rest_sent = rest.join([ordered_sibling], rest_arrived)
    rest_sent, up_arrived, mixers_arrived, gate_arrived, down_arrived, packed, input_gradient = (
        together(
            rest_sent, up_arrived, mixers_arrived, gate_arrived, down_arrived, packed, input_gradient
        )
    )

    rest_arrived = rest.go(rest_sent, 0)
    packed = all_sum(place, packed, ("core",))
    up_arrived, mixers_arrived, gate_arrived, down_arrived, packed = together(
        up_arrived, mixers_arrived, gate_arrived, down_arrived, packed
    )
    gate_arrived = gate.go_fourth(gate.to_fourth(gate_arrived))
    up_arrived = up.go_third(up.to_third(up_arrived))
    down_arrived = down.go_third(down.to_third(down_arrived))
    share_attention, share_mixer, share_gating = mixers.shares(mixers_arrived)
    share_attention, share_mixer = share_attention.T, share_mixer.T
    rest_arrived, gate_arrived, up_arrived, down_arrived, packed, share_attention, share_mixer = (
        together(
            rest_arrived,
            gate_arrived,
            up_arrived,
            down_arrived,
            packed,
            share_attention,
            share_mixer,
        )
    )

    rest_sent, up_sent, down_sent, gate_arrived, packed = together(
        rest.to_second(rest_arrived),
        up.to_fourth(up_arrived),
        down.to_fourth(down_arrived),
        gate_arrived,
        packed,
    )
    rest_arrived = rest.go(rest_sent, 1)
    up_arrived = up.go_fourth(up_sent)
    down_arrived = down.go_fourth(down_sent)
    packed = all_sum(place, packed, ("z",))
    (share_gate,) = gate.shares(gate_arrived)
    rest_arrived, up_arrived, down_arrived, packed, share_gate = together(
        rest_arrived, up_arrived, down_arrived, packed, share_gate
    )

    rest_sent, up_arrived, down_arrived, packed = together(
        rest.to_owners(rest_arrived), up_arrived, down_arrived, packed
    )
    rest_arrived = rest.go_owners(rest_sent)
    packed = all_sum(place, packed, ("x", "y"))
    (share_up,), (share_down,) = up.shares(up_arrived), down.shares(down_arrived)
    share_down = share_down.T
    sums = tuple(
        local_call(
            unpack_kernel,
            [
                ((width, SSM_HEADS), F32),
                ((width,), F32),
                ((width,), F32),
                ((WIDTH,), F32),
                ((SSM_HEADS,), F32),
                ((SSM_HEADS,), F32),
                ((SSM_HEADS,), F32),
                ((KERNEL, inner_width), F32),
                ((inner_width,), F32),
            ],
            (packed,),
            "unpack",
        )
    )
    rest_arrived, sums, share_up, share_down = together(rest_arrived, sums, share_up, share_down)
    (
        step_sum,
        gain_sum,
        feed_gain_sum,
        mixer_gain_sum,
        skip_sum,
        step_bias_sum,
        decay_sum,
        conv_sum,
        conv_bias_sum,
    ) = sums
    share_inner, share_query, share_key, share_value = rest.split(
        rest_arrived, (inner_width, HEADS * HEAD, LANES, LANES)
    )
    return (
        output[None],
        input_gradient[None],
        gain_sum,
        share_query,
        share_key,
        share_value,
        share_attention,
        share_gating,
        share_inner,
        step_sum,
        step_bias_sum,
        decay_sum,
        skip_sum,
        conv_sum,
        conv_bias_sum,
        mixer_gain_sum,
        share_mixer,
        feed_gain_sum,
        share_gate,
        share_up,
        share_down,
    )


def solution(mesh):
    in_specs = (
        P("dp", "seq", None),
        P("dp", None),
        P("dp", "seq", None),
        P(),
        P(),
        P(),
        P(),
        P(),
        P(),
        P(),
        P(),
        P(),
        P(),
        P(),
        P(),
        P(),
        P(),
        P(),
        P(),
        P(),
        P(),
        P(),
    )
    out_specs = (
        P("dp", "seq", None),
        P("dp", "seq", None),
        P(),
        P(("dp", "seq"), None),
        P(("dp", "seq"), None),
        P(("dp", "seq"), None),
        P(None, ("dp", "seq")),
        P(("dp", "seq"), None),
        P(("dp", "seq"), None),
        P(),
        P(),
        P(),
        P(),
        P(),
        P(),
        P(),
        P(None, ("dp", "seq")),
        P(),
        P(("dp", "seq"), None),
        P(("dp", "seq"), None),
        P(None, ("dp", "seq")),
    )
    return jax.shard_map(body, mesh=mesh, in_specs=in_specs, out_specs=out_specs, check_vma=False)
```

```python
import functools
import math

import jax
import jax.numpy as jnp
from jax import lax
from jax.experimental import pallas as pl
from jax.experimental.pallas import tpu as pltpu
from jax.sharding import PartitionSpec as P

HEADS = 8
KV_HEADS = 2
HEAD = 64
SSM_HEADS = 24
SSM_HEAD = 64
STATE = 128
KERNEL = 4


EPS = 1e-05
ROPE_BASE = 100000000000.0
NEG = -1e30
HIGH = lax.Precision.HIGHEST


def passed_along(shard, axis, by):
    peers = lax.axis_size(axis)
    pairs = [(i, i + by) for i in range(peers) if 0 <= i + by < peers]
    return lax.ppermute(shard, axis, pairs)


def product(left, right):
    return jnp.dot(left, right, preferred_element_type=jnp.float32)


def product_left(left, right):
    return lax.dot_general(
        left, right, (((0,), (0,)), ((), ())), preferred_element_type=jnp.float32
    )


def product_right(left, right):
    return lax.dot_general(
        left, right, (((1,), (1,)), ((), ())), preferred_element_type=jnp.float32
    )


def precise(left, right):
    return jnp.dot(left, right, preferred_element_type=jnp.float32, precision=HIGH)


def norm_rows(values, gain):
    return values * lax.rsqrt(jnp.mean(values * values, -1, keepdims=True) + EPS) * gain


def gated_unit(gate, upward):
    return jax.nn.silu(gate) * upward


CORES = 2
DEPTH = 4
LANES = 128


class Place:
    def __init__(self):
        self.dp = lax.axis_size("dp")
        self.seq = lax.axis_size("seq")
        self.sizes = {
            "y": self.dp // CORES,
            "core": CORES,
            "z": DEPTH,
            "x": self.seq // DEPTH,
        }

    def split(self, index):
        dp, seq = index // self.seq, index % self.seq
        return {
            "y": dp // CORES,
            "core": dp % CORES,
            "z": seq // self.sizes["x"],
            "x": seq % self.sizes["x"],
        }

    def join(self, at):
        return (at["y"] * CORES + at["core"]) * self.seq + at["z"] * self.sizes["x"] + at["x"]

    def turn(self, shard, axis, by):
        pairs = []
        for index in range(self.dp * self.seq):
            at = self.split(index)
            at[axis] = (at[axis] + by) % self.sizes[axis]
            pairs.append((index, self.join(at)))
        return lax.ppermute(shard, ("dp", "seq"), pairs)

    def swap(self, shard, axis, bit):
        pairs = []
        for index in range(self.dp * self.seq):
            at = self.split(index)
            at[axis] ^= bit
            pairs.append((index, self.join(at)))
        return lax.ppermute(shard, ("dp", "seq"), pairs)

    def share_order(self, width, group, along):
        sizes, at = self.sizes, self.split(group * self.seq + along)
        rows = width // (self.dp * self.seq)
        k = lax.broadcasted_iota(jnp.int32, (width, 1), 0)
        within = k % rows
        rest = k // rows
        dz = rest % sizes["z"]
        rest = rest // sizes["z"]
        dy = rest % sizes["y"]
        rest = rest // sizes["y"]
        dx = rest % sizes["x"]
        dc = rest // sizes["x"]
        owner = self.join(
            {
                "y": (at["y"] + dy) % sizes["y"],
                "core": (at["core"] + dc) % sizes["core"],
                "z": at["z"] ^ (dz // 2 + 2 * (dz % 2)),
                "x": (at["x"] + dx) % sizes["x"],
            }
        )
        source = owner * rows + within
        columns = lax.broadcasted_iota(jnp.int32, (1, width), 1)
        return (source == columns).astype(jnp.bfloat16)


F32 = jnp.float32
BF16 = jnp.bfloat16
PAIR = 2 * SSM_HEAD
WIDTH = SSM_HEADS * SSM_HEAD
PAIRS = WIDTH // PAIR
HALO = 16
EXTRA = 16
WALLS = 16
VMEM = pl.BlockSpec(memory_space=pltpu.VMEM)
SMEM = pl.BlockSpec(memory_space=pltpu.SMEM)
FAR = pl.BlockSpec(memory_space=pl.ANY)


def room(arrays):
    total = 0
    for a in arrays:
        *lead, last = a.shape if len(a.shape) > 1 else (8, *a.shape)
        total += math.prod(lead) * (-(-last // LANES) * LANES) * jnp.dtype(a.dtype).itemsize
    return total


def local_call(kernel, outs, args, name, scratch=(), smem=(), slack=4, alone=False, far=(), sems=()):
    shapes = [jax.ShapeDtypeStruct(shape, kind) for shape, kind in outs]
    held = [a for i, a in enumerate(args) if i not in smem and i not in far]
    needed = (56 if alone else slack) * 1024 * 1024
    if not alone:
        needed += room(held) + room(shapes) + room(scratch)
    return pl.pallas_call(
        kernel,
        in_specs=[
            SMEM if i in smem else (FAR if i in far else VMEM) for i in range(len(args))
        ],
        out_specs=[VMEM] * len(shapes),
        out_shape=shapes,
        scratch_shapes=list(scratch) + [pltpu.SemaphoreType.DMA((n,)) for n in sems],
        compiler_params=pltpu.CompilerParams(vmem_limit_bytes=needed),
        cost_estimate=pl.CostEstimate(flops=0, bytes_accessed=0, transcendentals=0),
        name=name,
    )(*args)


def dot(left, right):
    return jnp.dot(left, right, preferred_element_type=F32)


def dot_rows(left, right):
    return lax.dot_general(left, right, (((0,), (0,)), ((), ())), preferred_element_type=F32)


def dot_lanes(left, right):
    return lax.dot_general(left, right, (((1,), (1,)), ((), ())), preferred_element_type=F32)


def turned(values, cosine, sine):
    lane = lax.broadcasted_iota(jnp.int32, values.shape, 1)
    half = HEAD // 2
    swapped = jnp.where(
        lane % HEAD < half,
        pltpu.roll(values, LANES - half, 1),
        pltpu.roll(values, half, 1),
    )
    return values * cosine + swapped * sine


def turn_tables(first, count):
    lane = jnp.arange(LANES)
    place = (first + jnp.arange(count)).astype(F32)
    half = HEAD // 2
    freq = ROPE_BASE ** (-((lane % half).astype(F32) * 2.0 / HEAD))
    angle = place[:, None] * freq[None, :]
    sign = jnp.where(lane % HEAD < half, -1.0, 1.0)[None, :]
    return jnp.cos(angle), jnp.sin(angle) * sign


def lanes_of(index):
    return slice(index * LANES, (index + 1) * LANES)


def spread_pair(values, pair):
    rows = values.shape[0]
    lane = lax.broadcasted_iota(jnp.int32, (rows, LANES), 1)
    return jnp.where(
        lane < SSM_HEAD, values[:, 2 * pair : 2 * pair + 1], values[:, 2 * pair + 1 : 2 * pair + 2]
    )


def head_lanes(selector):
    head = lax.broadcasted_iota(jnp.int32, (LANES, LANES), 0)
    lane = lax.broadcasted_iota(jnp.int32, (LANES, LANES), 1)
    for pair in range(PAIRS):
        chosen = (lane // SSM_HEAD + 2 * pair == head).astype(F32).astype(BF16)
        selector[:LANES, lanes_of(pair)] = chosen
        selector[LANES:, lanes_of(pair)] = chosen


def halves(values):
    upper = values.astype(BF16)
    return jnp.concatenate([upper, (values - upper.astype(F32)).astype(BF16)], 1)


def split_into(target, span, values):
    upper = values.astype(BF16)
    target[0, :, span] = upper
    target[1, :, span] = (values - upper.astype(F32)).astype(BF16)


def head_sums(parts, selector):
    chosen = selector[:LANES]
    return dot_lanes(parts[0], chosen) + dot_lanes(parts[1], chosen)


def silu_slope(values):
    gate = jax.nn.sigmoid(values)
    return gate * (1.0 + values * (1.0 - gate))


def front_kernel(
    x, key_w, value_w, cosine, sine, conv_bias, input_gain, mixer_gain, skip, step_bias, decay_log,
    normed, pairs, table,
):
    table[...] = jnp.zeros(table.shape, F32)
    for row, source in (
        (ROW_CONV, conv_bias),
        (ROW_GAIN, input_gain),
        (ROW_MIXER, mixer_gain),
        (ROW_STEP, step_bias),
    ):
        table[row : row + 1, : source.shape[0]] = source[...].reshape(1, source.shape[0])
    rates = -jnp.exp(decay_log[...].reshape(1, SSM_HEADS))
    table[ROW_RATE : ROW_RATE + 1, :SSM_HEADS] = rates
    skips = skip[...].reshape(1, SSM_HEADS)
    for pair in range(PAIRS):
        table[ROW_SKIP : ROW_SKIP + 1, lanes_of(pair)] = spread_pair(skips, pair)
    values = x[...].astype(F32)
    scale = lax.rsqrt(jnp.mean(values * values, -1, keepdims=True) + EPS)
    gain = table[ROW_GAIN : ROW_GAIN + 1, : values.shape[1]]
    normed[...] = (values * scale * gain).astype(BF16)
    low = normed[...]
    pairs[:, :LANES] = turned(dot(low, key_w[...]), cosine[...], sine[...]).astype(BF16)
    pairs[:, LANES:] = dot(low, value_w[...]).astype(BF16)


def block_mask(first, start, segments, count):
    def row(at):
        return segments[:, pl.ds(pl.multiple_of(at, LANES), count)].astype(F32)

    place = lax.broadcasted_iota(jnp.int32, (count, count), 0) + start
    reach = lax.broadcasted_iota(jnp.int32, (count, count), 1) + first
    keys = jnp.broadcast_to(row(start), (8, count)).T[:, :1]
    return (keys == row(first)) & (place <= reach)


def key_rows(xs, position, index, count):
    far = position // xs - index // xs
    side = lax.rem(lax.rem(position, xs) - lax.rem(index, xs) + xs, xs)
    return pl.ds(pl.multiple_of((far * xs + side) * count, count), count)


def head_columns(pairs, rows):
    keys = [pairs[rows, kv * HEAD : (kv + 1) * HEAD] for kv in range(KV_HEADS)]
    values = [
        pairs[rows, LANES + kv * HEAD : LANES + (kv + 1) * HEAD] for kv in range(KV_HEADS)
    ]
    return keys, values


def attend_kernel(
    xs, position, normed, query_w, cosine, sine, segments, *refs
):
    *pieces, queries, low, exact, spread, pairs, top, total, gathered, arrived = refs
    count = queries.shape[0]
    block = pieces[0].shape[0]
    copies = [
        pltpu.make_async_copy(piece, pairs.at[k * block : (k + 1) * block], arrived.at[k])
        for k, piece in enumerate(pieces)
    ]
    for copy in copies:
        copy.start()
    raw = dot(normed[...], query_w[...])
    for chunk_at in range(HEADS * HEAD // LANES):
        part = turned(raw[:, lanes_of(chunk_at)], cosine[...], sine[...]) * HEAD**-0.5
        queries[:, lanes_of(chunk_at)] = part.astype(BF16)
    first = position[0] * count
    group = HEADS // KV_HEADS
    top[...] = jnp.full(top.shape, NEG, F32)
    total[...] = jnp.zeros(total.shape, F32)
    gathered[...] = jnp.zeros(gathered.shape, F32)

    def chunk(index, carry):
        start = pl.multiple_of(index * count, count)
        rows = key_rows(xs, position[0], index, count)
        mask = block_mask(first, start, segments, count)
        keys, values = head_columns(pairs, rows)
        values = [value.T for value in values]
        before = top[...]
        scores = []
        for head in range(HEADS):
            score = dot_lanes(keys[head // group], queries[:, head * HEAD : (head + 1) * HEAD])
            scores.append(jnp.where(mask, score, NEG))
        now = jnp.maximum(
            before, jnp.concatenate([jnp.max(score, 0, keepdims=True) for score in scores], 0)
        )
        fade = jnp.exp(before - now)
        weights = [jnp.exp(score - now[head : head + 1]) for head, score in enumerate(scores)]
        sums = jnp.concatenate([jnp.sum(weight, 0, keepdims=True) for weight in weights], 0)
        top[...] = now
        total[...] = total[...] * fade + sums
        for head in range(HEADS):
            span = slice(head * HEAD, (head + 1) * HEAD)
            gathered[span] = gathered[span] * fade[head : head + 1] + dot(
                values[head // group], weights[head].astype(BF16)
            )
        return carry

    for copy in copies:
        copy.wait()
    lax.fori_loop(0, first // count + 1, chunk, 0)
    spread[...] = top[...] + jnp.log(total[...])
    for head in range(HEADS):
        span = slice(head * HEAD, (head + 1) * HEAD)
        exact[span] = gathered[span] / total[head : head + 1]
    for chunk_at in range(HEADS * HEAD // LANES):
        low[:, lanes_of(chunk_at)] = exact[lanes_of(chunk_at)].T.astype(BF16)


def attend_back_kernel(
    xs, position, queries, pairs, slope, exact, spread, segments, cosine, sine,
    query_low, pair_slope, turned_slope, delta, query_slope,
):
    count = queries.shape[0]
    length = pairs.shape[0]
    first = position[0] * count
    group = HEADS // KV_HEADS
    for chunk_at in range(HEADS * HEAD // LANES):
        turned_slope[lanes_of(chunk_at)] = slope[:, lanes_of(chunk_at)].astype(F32).T
    for head in range(HEADS):
        span = slice(head * HEAD, (head + 1) * HEAD)
        delta[head : head + 1] = jnp.sum(turned_slope[span] * exact[span], 0, keepdims=True)
    query_slope[...] = jnp.zeros(query_slope.shape, F32)

    def target(index):
        if xs != 2:
            return pl.ds(pl.multiple_of(index * count, count), count)
        far = (index // xs) ^ (position[0] // xs)
        side = lax.rem(index, xs) ^ lax.rem(position[0], xs)
        turn = (far & 1) * 4 + (far >> 1) * 2 + side
        return pl.ds(pl.multiple_of(turn * count, count), count)

    def chunk(index, carry):
        start = pl.multiple_of(index * count, count)
        rows = key_rows(xs, position[0], index, count)
        mask = block_mask(first, start, segments, count)
        into = target(index)
        keys, values = head_columns(pairs, rows)
        asked = [queries[:, head * HEAD : (head + 1) * HEAD] for head in range(HEADS)]
        sloped = [slope[:, head * HEAD : (head + 1) * HEAD] for head in range(HEADS)]
        scores = [dot_lanes(keys[head // group], asked[head]) for head in range(HEADS)]
        dots = [dot_lanes(values[head // group], sloped[head]) for head in range(HEADS)]
        weights, score_slopes = [], []
        for head in range(HEADS):
            row = slice(head, head + 1)
            weight = jnp.exp(jnp.where(mask, scores[head] - spread[row], NEG))
            score_slopes.append((weight * (dots[head] - delta[row])).astype(BF16))
            weights.append(weight.astype(BF16))
        for kv in range(KV_HEADS):
            heads = range(kv * group, (kv + 1) * group)
            value_part = sum(dot(weights[head], sloped[head]) for head in heads)
            key_part = sum(dot(score_slopes[head], asked[head]) for head in heads)
            pair_slope[into, kv * HEAD : (kv + 1) * HEAD] = key_part.astype(BF16)
            pair_slope[into, LANES + kv * HEAD : LANES + (kv + 1) * HEAD] = value_part.astype(BF16)
        keys = [key.T for key in keys]
        for head in range(HEADS):
            span = slice(head * HEAD, (head + 1) * HEAD)
            query_slope[span] = query_slope[span] + dot(keys[head // group], score_slopes[head])
        return carry

    def blank(index, carry):
        pair_slope[target(index), :] = jnp.zeros((count, 2 * LANES), BF16)
        return carry

    live = first // count + 1
    lax.fori_loop(0, live, chunk, 0)
    lax.fori_loop(live, length // count, blank, 0)
    for chunk_at in range(HEADS * HEAD // LANES):
        part = query_slope[lanes_of(chunk_at)].T * HEAD**-0.5
        query_low[:, lanes_of(chunk_at)] = turned(part, cosine[...], -sine[...]).astype(BF16)


def pairs_back_kernel(*refs):
    *summands, cosine, sine, low = refs
    owned = sum(ref[...].astype(F32) for ref in summands)
    low[:, :LANES] = turned(owned[:, :LANES], cosine[...], -sine[...]).astype(BF16)
    low[:, LANES:] = owned[:, LANES:].astype(BF16)


def wide_marks(marks):
    return [
        jnp.broadcast_to(marks[:, tap : tap + 1], (marks.shape[0], LANES))
        for tap in range(KERNEL - 1)
    ]


def conv_total(inner, taps, table, wide, chunk):
    span = lanes_of(chunk)
    extended = inner[:, span].astype(F32)
    total = table[ROW_CONV : ROW_CONV + 1, span] + taps[KERNEL - 1 : KERNEL, span] * extended[HALO:]
    for tap in range(KERNEL - 1):
        moved = pltpu.roll(extended, KERNEL - 1 - tap, 0)[HALO:] * wide[tap]
        total = total + taps[tap : tap + 1, span] * moved
    return total


def triangle(count, strict=False, upper=False):
    row = lax.broadcasted_iota(jnp.int32, (count, count), 0)
    column = lax.broadcasted_iota(jnp.int32, (count, count), 1)
    if upper:
        row, column = column, row
    return (row > column if strict else row >= column).astype(F32)


def soft(values):
    return jnp.maximum(values, 0.0) + jnp.log1p(jnp.exp(-jnp.abs(values)))


def part_pieces(parts, pair):
    width = WIDTH // parts
    if width % LANES == 0:
        start = pair * LANES % width
        return [(pair * LANES // width, slice(start, start + LANES), slice(0, LANES))]
    pieces = []
    for half in range(2):
        column = pair * LANES + half * SSM_HEAD
        start = column % width
        pieces.append(
            (
                column // width,
                slice(start, start + SSM_HEAD),
                slice(half * SSM_HEAD, (half + 1) * SSM_HEAD),
            )
        )
    return pieces


ROW_CONV, ROW_GAIN, ROW_MIXER, ROW_SKIP, ROW_STEP, ROW_RATE, ROW_FEED = range(7)
MARK_ENTER, MARK_TAIL, MARK_SEGMENT = KERNEL - 1, KERNEL, KERNEL + 1


def mark_rows(position, segments, count):
    first = pl.multiple_of(position * count, LANES)
    here = segments[:, pl.ds(first, count)].astype(F32)
    before = segments[:, pl.ds(pl.multiple_of(jnp.maximum(first - count, 0), LANES), count)]
    before = jnp.where(position > 0, before.astype(F32), -1.0)
    both = jnp.concatenate([before, here], 1)
    rows = []
    for tap in range(KERNEL - 1):
        moved = pltpu.roll(jnp.broadcast_to(both, (8, 2 * count)), KERNEL - 1 - tap, 1)
        rows.append(flag(moved[:1, count:] == here))
    rows.append(flag(here == before[:, count - 1 :]))
    rows.append(flag(here == here[:, count - 1 :]))
    rows.append(here)
    rows += [jnp.zeros((1, count), F32)] * (8 - len(rows))
    return jnp.concatenate(rows, 0)


def hold_part(hold, pair, rows, value):
    for part, lanes, within in part_pieces(hold.shape[0], pair):
        hold[part, rows, lanes] = value[:, within]


def hold_all(hold, rows, values):
    width = hold.shape[2]
    for part in range(hold.shape[0]):
        hold[part, rows] = values[:, part * width : (part + 1) * width]


def hand_out(hold, at_x, targets):
    for k, target in enumerate(targets):
        target[...] = hold[lax.rem(at_x + k, len(targets))]


def picked(pieces, at_x, pair):
    xs = len(pieces)
    values = []
    for part, lanes, _ in part_pieces(xs, pair):
        value = pieces[0][:, lanes]
        for k in range(1, xs):
            value = jnp.where(lax.rem(at_x - k + xs, xs) == part, pieces[k][:, lanes], value)
        values.append(value)
    return values[0] if len(values) == 1 else jnp.concatenate(values, 1)


def flag(condition):
    return jnp.where(condition, 1.0, 0.0)


def wall_rows(high, middle, low):
    row = lax.broadcasted_iota(jnp.int32, (EXTRA, high.shape[1]), 0)
    return jnp.where(
        row == 0, high, jnp.where(row == 1, middle, jnp.where(row == 2, low, 0.0))
    ).astype(BF16)


def ahead(forward, one, other):
    return one < other if forward else one > other


def mixed(flags, rows, width):
    total = jnp.zeros((1, width), F32)
    for chosen, row in zip(flags, rows):
        total = total + row * chosen
    return jnp.exp(total)


class Endings:
    def __init__(self, segments, count):
        self.segments, self.count = segments, count

    def __getitem__(self, index):
        return self.segments[index * self.count + self.count - 1]


def level_kernel(forward, xs, count, position, segments, *refs):
    pieces = refs[:xs]
    if forward:
        total_out, walls = refs[xs:]
    else:
        walls, total_out = refs[xs:]
    at_z, at_x = position[0] // xs, lax.rem(position[0], xs)
    endings = Endings(segments, count)
    width = pieces[0].shape[1]
    places = [lax.rem(at_x - k + xs, xs) for k in range(xs)]
    if forward:
        rows = []
        for k in range(xs):
            rows.append(jnp.sum(pieces[k][STATE:].astype(F32), 0, keepdims=True))
            walls[k : k + 1] = rows[k]
        walls[xs:] = jnp.zeros((WALLS - xs, width), F32)
        border = endings[at_z * xs + xs - 1]
    else:
        rows = [walls[k : k + 1] for k in range(xs)]
        border = endings[jnp.maximum(at_z * xs - 1, 0)]
    total = jnp.zeros((STATE, width), F32)
    for k in range(xs):
        index = at_z * xs + places[k]
        reached = endings[index if forward else jnp.maximum(index - 1, 0)] == border
        flags = [flag(ahead(forward, places[k], places[m])) for m in range(xs)]
        total = total + pieces[k][:STATE].astype(F32) * (
            mixed(flags, rows, width) * flag(reached)
        )
    total_out[:STATE] = total.astype(BF16)
    if forward:
        whole = sum(rows)
        high = whole.astype(BF16).astype(F32)
        middle = (whole - high).astype(BF16).astype(F32)
        total_out[STATE:] = wall_rows(high, middle, whole - high - middle)


def arrival_kernel(forward, xs, zs, count, position, segments, *refs):
    pieces = refs[:xs]
    totals = refs[xs : xs + zs - 1]
    walls = refs[xs + zs - 1]
    if forward:
        own, *results, level_walls = refs[xs + zs :]
    else:
        level_walls, *results = refs[xs + zs :]
    at_z, at_x = position[0] // xs, lax.rem(position[0], xs)
    endings = Endings(segments, count)
    width = pieces[0].shape[1]
    x_at = [lax.rem(at_x - k + xs, xs) for k in range(xs)]
    z_at = [lax.rem(at_z - k + zs, zs) for k in range(zs)]
    rows = [walls[k : k + 1] for k in range(xs)]
    if forward:
        levels = [jnp.sum(own[STATE:].astype(F32), 0, keepdims=True)]
        for total in totals:
            levels.append(jnp.sum(total[STATE:].astype(F32), 0, keepdims=True))
        for k in range(zs):
            level_walls[k : k + 1] = levels[k]
        level_walls[zs:] = jnp.zeros((WALLS - zs, width), F32)
        border = endings[jnp.maximum(at_z * xs - 1, 0)]
    else:
        levels = [level_walls[k : k + 1] for k in range(zs)]
        border = endings[at_z * xs + xs - 1]
    outside = jnp.zeros((STATE, width), F32)
    for k in range(1, zs):
        far = endings[z_at[k] * xs + xs - 1 if forward else jnp.maximum(z_at[k] * xs - 1, 0)]
        reached = ahead(forward, z_at[k], at_z) & (far == border)
        flags = [
            flag(ahead(forward, z_at[k], z_at[m]) & ahead(forward, z_at[m], at_z))
            for m in range(zs)
        ]
        outside = outside + totals[k - 1][:STATE].astype(F32) * (
            mixed(flags, levels, width) * flag(reached)
        )
    for r in range(xs):
        target = lax.rem(at_x + r, xs)
        index = at_z * xs + target
        edge = endings[jnp.maximum(index - 1, 0) if forward else index]
        flags = [flag(ahead(forward, x_at[m], target)) for m in range(xs)]
        total = outside * (mixed(flags, rows, width) * flag(edge == border))
        for k in range(xs):
            source = at_z * xs + x_at[k]
            far = endings[source if forward else jnp.maximum(source - 1, 0)]
            reached = ahead(forward, x_at[k], target) & (far == edge)
            flags = [
                flag(ahead(forward, x_at[k], x_at[m]) & ahead(forward, x_at[m], target))
                for m in range(xs)
            ]
            total = total + pieces[k][:STATE].astype(F32) * (
                mixed(flags, rows, width) * flag(reached)
            )
        results[r][...] = total.astype(BF16)


def dealt(place, parts):
    return (parts[0],) + tuple(
        place.turn(part, "x", k) for k, part in enumerate(parts[1:], start=1)
    )


def levels_met(place, total):
    return tuple(place.turn(total, "z", k) for k in range(1, place.sizes["z"]))


def level(place, pieces, position, segments, count):
    xs, width = place.sizes["x"], pieces[0].shape[1]
    return local_call(
        functools.partial(level_kernel, True, xs, count),
        [((STATE + EXTRA, width), BF16), ((WALLS, width), F32)],
        (position, segments, *pieces),
        "level",
        smem=(0, 1),
    )


def level_back(place, pieces, walls, position, segments, count):
    xs, width = place.sizes["x"], pieces[0].shape[1]
    return local_call(
        functools.partial(level_kernel, False, xs, count),
        [((STATE, width), BF16)],
        (position, segments, *pieces, walls),
        "level_back",
        smem=(0, 1),
    )[0]


def arrival(place, pieces, totals, walls, total, position, segments, count):
    xs, zs, width = place.sizes["x"], place.sizes["z"], pieces[0].shape[1]
    *results, level_walls = local_call(
        functools.partial(arrival_kernel, True, xs, zs, count),
        [((STATE, width), BF16)] * xs + [((WALLS, width), F32)],
        (position, segments, *pieces, *totals, walls, total),
        "arrival",
        smem=(0, 1),
    )
    return tuple(results), level_walls


def arrival_back(place, pieces, totals, walls, level_walls, position, segments, count):
    xs, zs, width = place.sizes["x"], place.sizes["z"], pieces[0].shape[1]
    return tuple(
        local_call(
            functools.partial(arrival_kernel, False, xs, zs, count),
            [((STATE, width), BF16)] * xs,
            (position, segments, *pieces, *totals, walls, level_walls),
            "arrival_back",
            smem=(0, 1),
        )
    )


def prep_kernel(
    xs, position, halo, normed, table, inner_w, step_w, taps, segments,
    inner, raw, channels, scaled, inflow, readout, steps, logs, logs_turned, marks, marks_turned,
    factor, *refs,
):
    states, (extended, hold, selector, lengths, tails, weighted) = refs[:xs], refs[xs:]
    count, width = normed.shape
    at_x = lax.rem(position[0], xs)
    marks_turned[...] = mark_rows(position[0], segments, count)
    marks[...] = marks_turned[...].T
    values = halo[...].astype(F32)
    scale = lax.rsqrt(jnp.mean(values * values, -1, keepdims=True) + EPS)
    extended[:HALO] = (values * scale * table[ROW_GAIN : ROW_GAIN + 1, :width]).astype(BF16)
    extended[HALO:] = normed[...]
    raw[...] = jnp.zeros(raw.shape, F32)
    raw[:, :SSM_HEADS] = dot_lanes(normed[...], step_w[...])
    head_lanes(selector)
    chunks = range(PAIRS + 2)
    for chunk in reversed(chunks):
        span = lanes_of(chunk)
        inner[:, span] = dot(extended[...], inner_w[:, span]).astype(BF16)
    steps[...] = soft(raw[...] + table[ROW_STEP : ROW_STEP + 1, :LANES])
    logs[...] = precise(triangle(count), steps[...] * table[ROW_RATE : ROW_RATE + 1, :LANES])
    logs_turned[...] = logs[...].T
    ending = logs[count - 1 : count]
    tail = jnp.exp(ending - logs[...]) * marks[:, MARK_TAIL : MARK_TAIL + 1]
    lengths[...] = dot(halves(steps[...]), selector[...])
    tails[...] = dot(halves(tail), selector[...])
    wide = wide_marks(marks)
    for chunk in reversed(chunks):
        span = lanes_of(chunk)
        total = conv_total(inner, taps, table, wide, chunk)
        gate = jax.nn.sigmoid(total)
        factor[:, span] = (gate * (1.0 + total * (1.0 - gate))).astype(BF16)
        value = total * gate
        if chunk == PAIRS + 1:
            readout[...] = value.astype(BF16)
        elif chunk == PAIRS:
            inflow[...] = value.astype(BF16)
        else:
            channels[:, span] = value
            value = value * lengths[:, span]
            scaled[:, span] = value.astype(BF16)
            weighted[:, span] = (value * tails[:, span]).astype(BF16)
    hold_all(hold, slice(0, STATE), dot(inflow[...].T, weighted[...]).astype(BF16))
    for pair in range(PAIRS):
        whole = spread_pair(ending, pair)
        high = whole.astype(BF16).astype(F32)
        middle = (whole - high).astype(BF16).astype(F32)
        wall = wall_rows(high, middle, whole - high - middle)
        hold_part(hold, pair, slice(STATE, STATE + EXTRA), wall)
    hand_out(hold, at_x, states)


def decay_kernel_parts(marks, marks_turned, bias):
    count = marks.shape[0]
    row = lax.broadcasted_iota(jnp.int32, (count, count), 0)
    column = lax.broadcasted_iota(jnp.int32, (count, count), 1)
    span = slice(MARK_SEGMENT, MARK_SEGMENT + 1)
    inside = (marks[:, span] == marks_turned[span]) & (row >= column)
    bias[...] = jnp.where(inside, 0.0, NEG)


IN_STEP = 4


def inner_kernel(logs, logs_turned, marks, marks_turned, inflow, readout, scaled, result, bias, meet):
    count = logs.shape[0]
    step = pl.program_id(0)

    @pl.when(step == 0)
    def _():
        decay_kernel_parts(marks, marks_turned, bias)
        meet[...] = dot_lanes(readout[...], inflow[...])

    columns = pltpu.roll(logs[...], (LANES - IN_STEP * step) % LANES, 1)
    half = count // 2
    for k in range(IN_STEP):
        across = logs_turned[pl.ds(IN_STEP * step + k, 1), :]
        span = slice(k * SSM_HEAD, (k + 1) * SSM_HEAD)
        for top, width in ((0, half), (half, count)):
            rows = slice(top, top + half)
            gap = columns[rows, k : k + 1] - across[:, :width] + bias[rows, :width]
            mixing = (jnp.exp(gap) * meet[rows, :width]).astype(BF16)
            result[rows, span] = dot(mixing, scaled[:width, span])


def inner_back_kernel(
    logs,
    logs_turned,
    marks,
    marks_turned,
    inflow,
    readout,
    scaled,
    slope,
    scaled_slope,
    inflow_slope,
    readout_slope,
    bias,
    meet,
    meet_slope,
):
    count = logs.shape[0]
    step = pl.program_id(0)

    @pl.when(step == 0)
    def _():
        decay_kernel_parts(marks, marks_turned, bias)
        meet[...] = dot_lanes(readout[...], inflow[...])
        meet_slope[...] = jnp.zeros(meet_slope.shape, F32)

    columns = pltpu.roll(logs[...], (LANES - IN_STEP * step) % LANES, 1)
    half = count // 2
    for top, width in ((0, half), (half, count)):
        rows = slice(top, top + half)
        gathered = jnp.zeros((half, width), F32)
        for k in range(IN_STEP):
            across = logs_turned[pl.ds(IN_STEP * step + k, 1), :]
            span = slice(k * SSM_HEAD, (k + 1) * SSM_HEAD)
            gap = columns[rows, k : k + 1] - across[:, :width] + bias[rows, :width]
            decay = jnp.exp(gap)
            mixing = (decay * meet[rows, :width]).astype(BF16)
            gathered = gathered + decay * dot_lanes(slope[rows, span], scaled[:width, span])
            part = dot_rows(mixing, slope[rows, span])
            if top:
                scaled_slope[:half, span] = scaled_slope[:half, span] + part[:half]
                scaled_slope[half:, span] = part[half:]
            else:
                scaled_slope[:half, span] = part
        meet_slope[rows, :width] = meet_slope[rows, :width] + gathered

    @pl.when(step == SSM_HEADS // IN_STEP - 1)
    def _():
        low = meet_slope[...].astype(BF16)
        inflow_slope[...] = dot_rows(low, readout[...])
        readout_slope[...] = dot(low, inflow[...])


def inner_call(kernel, fixed, moving, outs, fixed_outs, name, scratch):
    count = fixed[0].shape[0]
    steps = SSM_HEADS // IN_STEP
    width = IN_STEP * SSM_HEAD
    held = [pl.BlockSpec(a.shape, lambda j: (0, 0)) for a in fixed]
    passing = pl.BlockSpec((count, width), lambda j: (0, j))
    return pl.pallas_call(
        kernel,
        grid=(steps,),
        in_specs=held + [passing] * len(moving),
        out_specs=[passing] * len(outs)
        + [pl.BlockSpec(shape, lambda j: (0, 0)) for shape, _ in fixed_outs],
        out_shape=[jax.ShapeDtypeStruct((count, WIDTH), kind) for kind in outs]
        + [jax.ShapeDtypeStruct(shape, kind) for shape, kind in fixed_outs],
        scratch_shapes=[pltpu.VMEM((count, count), F32)] * scratch,
        compiler_params=pltpu.CompilerParams(vmem_limit_bytes=8 * 1024 * 1024),
        cost_estimate=pl.CostEstimate(flops=0, bytes_accessed=0, transcendentals=0),
        name=name,
    )(*fixed, *moving)


def entering_kernel(
    xs, position, inner_part, readout, logs, marks, channels, gating, table, low_input, branch,
    feed_gain, mixer_w, gate_w, up_w, *refs,
):
    pieces, outs = refs[:xs], refs[xs:]
    tail, scanned, entering, mixed_sum, feed_low, gate_raw, up_raw, activated, *outs = outs
    gated, selector, wide, mixer_here, gate_here, up_here, arrived = outs
    copies = [
        pltpu.make_async_copy(source, target, arrived.at[k])
        for k, (source, target) in enumerate(
            ((mixer_w, mixer_here), (gate_w, gate_here), (up_w, up_here))
        )
    ]
    for copy in copies:
        copy.start()
    at_x = lax.rem(position[0], xs)
    count = logs.shape[0]
    enter = halves(jnp.exp(logs[...]) * marks[:, MARK_ENTER : MARK_ENTER + 1])
    head_lanes(selector)
    for pair in range(PAIRS):
        entering[:, lanes_of(pair)] = picked(pieces, at_x, pair)
    wide[...] = dot(enter, selector[...])
    gated[...] = dot(readout[...], entering[...])
    square = jnp.zeros((count, LANES), F32)
    for pair in range(PAIRS):
        span = lanes_of(pair)
        full = inner_part[:, span] + gated[:, span] * wide[:, span]
        scanned[:, span] = full
        gate = gating[:, span]
        skip = table[ROW_SKIP : ROW_SKIP + 1, span]
        full = (full + skip * channels[:, span]) * (gate * jax.nn.sigmoid(gate))
        gated[:, span] = full
        square = square + full * full
    scale = lax.rsqrt(jnp.sum(square, -1, keepdims=True) / WIDTH + EPS)
    scale = jnp.broadcast_to(scale, (count, LANES))
    for pair in range(PAIRS):
        span = lanes_of(pair)
        gain = table[ROW_MIXER : ROW_MIXER + 1, span]
        tail[:, span] = (gated[:, span] * scale * gain).astype(BF16)
    copies[0].wait()
    mixed = low_input[...].astype(F32) + branch[...] + dot(tail[...], mixer_here[...])
    mixed_sum[...] = mixed
    scale = lax.rsqrt(jnp.mean(mixed * mixed, -1, keepdims=True) + EPS)
    feed_low[...] = (mixed * scale * feed_gain[...].reshape(1, mixed.shape[1])).astype(BF16)
    copies[1].wait()
    copies[2].wait()
    for start in range(0, gate_raw.shape[1], 512):
        span = slice(start, start + 512)
        gate = dot(feed_low[...], gate_here[:, span])
        up = dot(feed_low[...], up_here[:, span])
        gate_raw[:, span] = gate
        up_raw[:, span] = up
        activated[:, span] = (gate * jax.nn.sigmoid(gate) * up).astype(BF16)


def tail_back_kernel(
    xs, position, branch, mixer_w, scanned, channels, gating, table, logs, marks, readout,
    scanned_slope, gating_slope, sums, *refs,
):
    states, (gated, hold, selector, wide, weighted, slope) = refs[:xs], refs[xs:]
    for start in range(0, WIDTH, 512):
        span = slice(start, start + 512)
        slope[:, span] = dot_lanes(branch[...], mixer_w[span])
    at_x = lax.rem(position[0], xs)
    count = logs.shape[0]
    enter = halves(jnp.exp(logs[...]) * marks[:, MARK_ENTER : MARK_ENTER + 1])
    head_lanes(selector)
    wide[...] = dot(enter, selector[...])
    square = jnp.zeros((count, LANES), F32)
    cross = jnp.zeros((count, LANES), F32)
    for pair in range(PAIRS):
        span = lanes_of(pair)
        gate = gating[:, span]
        full = scanned[:, span] + table[ROW_SKIP : ROW_SKIP + 1, span] * channels[:, span]
        full = full * (gate * jax.nn.sigmoid(gate))
        gated[:, span] = full
        gain = table[ROW_MIXER : ROW_MIXER + 1, span]
        square = square + full * full
        cross = cross + full * slope[:, span] * gain
    scale = lax.rsqrt(jnp.sum(square, -1, keepdims=True) / WIDTH + EPS)
    cross = jnp.sum(cross, -1, keepdims=True) / WIDTH * scale * scale * scale
    scale = jnp.broadcast_to(scale, (count, LANES))
    cross = jnp.broadcast_to(cross, (count, LANES))
    for pair in range(PAIRS):
        span = lanes_of(pair)
        gate = gating[:, span]
        sigmoid = jax.nn.sigmoid(gate)
        back = slope[:, span]
        value = gated[:, span]
        sums[0:1, span] = jnp.sum(back * value * scale, 0, keepdims=True)
        back = back * table[ROW_MIXER : ROW_MIXER + 1, span] * scale - value * cross
        held = channels[:, span]
        full = scanned[:, span] + table[ROW_SKIP : ROW_SKIP + 1, span] * held
        gating_slope[:, span] = (
            back * full * sigmoid * (1.0 + gate * (1.0 - sigmoid))
        ).astype(BF16)
        back = back * (gate * sigmoid)
        sums[1:2, span] = jnp.sum(back * held, 0, keepdims=True)
        scanned_slope[:, span] = back.astype(BF16)
        weighted[:, span] = (back * wide[:, span]).astype(BF16)
    hold_all(hold, slice(0, STATE), dot(readout[...].T, weighted[...]).astype(BF16))
    hand_out(hold, at_x, states)
    sums[2:8] = jnp.zeros((6, WIDTH), F32)


def leaving_kernel(
    xs, position, entering, scanned, scanned_slope, scaled, channels, scaled_slope,
    inflow, readout, inflow_part, readout_part, steps, raw, logs, marks, inner, factor, taps, table,
    *refs,
):
    pieces, outs = refs[:xs], refs[xs:]
    inner_low, edges, conv_sums, raw_slope, small, conv_slope, selector, *outs = outs
    low, outer, lengths, tails, enters, first, second, third, fourth, fifth = outs
    at_x = lax.rem(position[0], xs)
    rates = table[ROW_RATE : ROW_RATE + 1, :LANES]
    count = logs.shape[0]
    ending = logs[count - 1 : count]
    head_lanes(selector)
    stepped = steps[...]
    for pair in range(PAIRS):
        low[:, lanes_of(pair)] = picked(pieces, at_x, pair)
    outer[...] = dot(inflow[...], low[...])
    lengths[...] = dot(halves(stepped), selector[...])
    tail = jnp.exp(ending - logs[...]) * marks[:, MARK_TAIL : MARK_TAIL + 1]
    tails[...] = dot(halves(tail), selector[...])
    enter = jnp.exp(logs[...]) * marks[:, MARK_ENTER : MARK_ENTER + 1]
    enters[...] = dot(halves(enter), selector[...])
    through = jnp.zeros((8, LANES), F32)
    for pair in range(PAIRS):
        span = lanes_of(pair)
        wide = scanned_slope[:, span].astype(F32)
        held = channels[:, span]
        short = scaled[:, span].astype(F32)
        tail = tails[:, span]
        part = outer[:, span] * tail
        within = scaled_slope[:, span]
        both = within + part
        split_into(first, span, wide * scanned[:, span] - short * within)
        split_into(second, span, short * part)
        split_into(third, span, held * both)
        fourth[:, span] = (short * tail).astype(BF16)
        fifth[:, span] = (wide * enters[:, span]).astype(BF16)
        skip = table[ROW_SKIP : ROW_SKIP + 1, span]
        conv_slope[:, span] = both * lengths[:, span] + skip * wide
        kept = low[:, span].astype(F32) * entering[:, span].astype(F32)
        kept = jnp.sum(kept, 0, keepdims=True) * jnp.exp(spread_pair(ending, pair))
        kept = halves(jnp.broadcast_to(kept, (8, LANES)))
        chosen = selector[:LANES, span]
        through = through + dot_lanes(kept, jnp.concatenate([chosen, chosen], 1))
    inside, outward = head_sums(first, selector), head_sums(second, selector)
    direct = head_sums(third, selector)
    inflow_slope = inflow_part[...] + dot_lanes(fourth[...], low[...])
    readout_slope = readout_part[...] + dot_lanes(fifth[...], entering[...])
    conv_slope[:, lanes_of(PAIRS)] = inflow_slope
    conv_slope[:, lanes_of(PAIRS + 1)] = readout_slope
    enter_last = marks[count - 1 :, MARK_ENTER : MARK_ENTER + 1]
    along = (
        precise(triangle(count, upper=True), inside)
        + precise(triangle(count, strict=True), outward)
        + through[:1] * enter_last
    )
    step_slope = direct + rates * along
    step_slope = step_slope * jax.nn.sigmoid(raw[...] + table[ROW_STEP : ROW_STEP + 1, :LANES])
    raw_slope[...] = step_slope.astype(BF16)
    small[0:1] = jnp.sum(step_slope, 0, keepdims=True)
    small[1:2] = rates * jnp.sum(stepped * along, 0, keepdims=True)
    small[2:8] = jnp.zeros((6, LANES), F32)
    blank = jnp.zeros((HALO, LANES), F32)
    marked = wide_marks(marks)
    for chunk in range(PAIRS + 2):
        span = lanes_of(chunk)
        extended = inner[:, span].astype(F32)
        slope = conv_slope[:, span] * factor[:, span].astype(F32)
        spread = jnp.zeros((HALO + count, LANES), F32)
        for tap in range(KERNEL):
            part = slope * marked[tap] if tap < KERNEL - 1 else slope
            part = jnp.concatenate([blank, part], 0)
            if tap < KERNEL - 1:
                part = pltpu.roll(part, HALO + count - (KERNEL - 1 - tap), 0)
            conv_sums[tap : tap + 1, span] = jnp.sum(part * extended, 0, keepdims=True)
            spread = spread + part * taps[tap : tap + 1, span]
        conv_sums[KERNEL : KERNEL + 1, span] = jnp.sum(slope, 0, keepdims=True)
        conv_sums[KERNEL + 1 :, span] = jnp.zeros((8 - KERNEL - 1, LANES), F32)
        inner_low[:, span] = spread[HALO:].astype(BF16)
        edges[:HALO, span] = spread[:HALO]
        edges[HALO:, span] = spread[count:]


PACK_ROWS = 48


def unit_back_kernel(slope, down_w, gate_raw, up_raw, gate_low, up_low):
    for start in range(0, gate_raw.shape[1], 512):
        span = slice(start, start + 512)
        back = dot_lanes(slope[...], down_w[span])
        gate = gate_raw[:, span]
        sigmoid = jax.nn.sigmoid(gate)
        up_low[:, span] = (back * (gate * sigmoid)).astype(BF16)
        back = back * up_raw[:, span]
        gate_low[:, span] = (back * (sigmoid * (1.0 + gate * (1.0 - sigmoid)))).astype(BF16)


def feed_back_kernel(
    gate_low, up_low, gate_w, up_w, mixed_sum, slope, gain, mixed_slope, branch_low, sums
):
    values = mixed_sum[...]
    count, width = values.shape
    scale = lax.rsqrt(jnp.mean(values * values, -1, keepdims=True) + EPS)
    back = dot_lanes(gate_low[...], gate_w[...]) + dot_lanes(up_low[...], up_w[...])
    sums[...] = jnp.broadcast_to(jnp.sum(back * values * scale, 0, keepdims=True), sums.shape)
    back = back * gain[...].reshape(1, width)
    cross = jnp.mean(back * values, -1, keepdims=True) * scale * scale * scale
    whole = slope[...].astype(F32) + back * scale - values * cross
    mixed_slope[...] = whole
    branch_low[...] = whole.astype(BF16)


def finish_kernel(
    gating_low, query_low, inner_low, pair_low, gating_w, query_w, inner_w, key_w, value_w, step_w,
    low_input, table, mixed_slope, raw_slope, normed, tail_sums, conv_sums, small, feed,
    input_gradient, packed, gating_here, query_here, inner_here, key_here, value_here, arrived,
):
    copies = [
        pltpu.make_async_copy(source, target, arrived.at[k])
        for k, (source, target) in enumerate(
            (
                (query_w, query_here),
                (gating_w, gating_here),
                (key_w, key_here),
                (value_w, value_here),
                (inner_w, inner_here),
            )
        )
    ]
    for copy in copies:
        copy.start()
    normed_slope = dot(raw_slope[:, :SSM_HEADS], step_w[...])
    for copy, left, right in (
        (copies[0], query_low[...], query_here),
        (copies[1], gating_low[...], gating_here),
        (copies[2], pair_low[:, :LANES], key_here),
        (copies[3], pair_low[:, LANES:], value_here),
        (copies[4], inner_low[...], inner_here),
    ):
        copy.wait()
        normed_slope = normed_slope + dot_lanes(left, right[...])
    values = low_input[...].astype(F32)
    width = values.shape[1]
    scale = lax.rsqrt(jnp.mean(values * values, -1, keepdims=True) + EPS)
    slope = normed_slope
    packed[SSM_HEADS : SSM_HEADS + 1] = jnp.sum(slope * values * scale, 0, keepdims=True)
    slope = slope * table[ROW_GAIN : ROW_GAIN + 1, :width]
    cross = jnp.mean(slope * values, -1, keepdims=True) * scale * scale * scale
    input_gradient[...] = mixed_slope[...] + slope * scale - values * cross
    packed[:SSM_HEADS] = dot_rows(raw_slope[...], normed[...])[:SSM_HEADS]
    packed[SSM_HEADS + 1 : SSM_HEADS + 2] = feed[:1]
    packed[SSM_HEADS + 2 :] = jnp.zeros((PACK_ROWS - SSM_HEADS - 2, width), F32)
    row = SSM_HEADS + 2
    for source, rows in ((tail_sums, 2), (small, 2), (conv_sums, KERNEL + 1)):
        for index in range(rows):
            for start in range(0, source.shape[1], width):
                stop = min(start + width, source.shape[1])
                packed[row : row + 1, : stop - start] = source[index : index + 1, start:stop]
                row += 1


def unpack_kernel(packed, step, gain, feed, mixer_gain, skip, step_bias, decay, conv, conv_bias):
    width = packed.shape[1]
    step[...] = packed[:SSM_HEADS].T
    row = SSM_HEADS

    def taken(size):
        nonlocal row
        pieces = []
        for start in range(0, size, width):
            pieces.append(packed[row : row + 1, : min(width, size - start)])
            row += 1
        return pieces[0] if len(pieces) == 1 else jnp.concatenate(pieces, 1)

    gain[...] = taken(width).reshape(width)
    feed[...] = taken(width).reshape(width)
    mixer_gain[...] = taken(WIDTH).reshape(WIDTH)
    lanes = taken(WIDTH)
    head = lax.broadcasted_iota(jnp.int32, (1, LANES), 1)
    sums = jnp.zeros((1, LANES), F32)
    for index in range(SSM_HEADS):
        part = lanes[:, index * SSM_HEAD : (index + 1) * SSM_HEAD]
        sums = jnp.where(head == index, jnp.sum(part, 1, keepdims=True), sums)
    skip[...] = sums[:, :SSM_HEADS].reshape(SSM_HEADS)
    step_bias[...] = taken(LANES)[:, :SSM_HEADS].reshape(SSM_HEADS)
    decay[...] = taken(LANES)[:, :SSM_HEADS].reshape(SSM_HEADS)
    for tap in range(KERNEL):
        conv[tap : tap + 1] = taken(conv.shape[1])
    conv_bias[...] = taken(conv.shape[1]).reshape(conv.shape[1])


def all_sum(place, shard, axes):
    for name in axes:
        axis = name[0] if name[0] == "z" else name
        bit = 2 if name == "zh" else 1
        while bit < (2 if name == "zl" else place.sizes[axis]):
            low = shard.astype(BF16)
            shard = low.astype(F32) + place.swap(low, axis, bit).astype(F32)
            bit *= 2
    return shard


def joint_kernel(xs, ys, widths, left, left_sib, right, right_sib, *outs):
    rows = left.shape[0] // len(widths)
    part = rows // (xs * ys)
    start = offset = 0
    for section, width in enumerate(widths):
        span = slice(section * rows, (section + 1) * rows)
        half = width // 2
        tile = next(t for t in (512, 384, 256, 128) if half % t == 0)
        for first in range(2):
            targets = outs[xs:] if first else outs[:xs]
            for column in range(0, half, tile):
                source = slice(start + first * half + column, start + first * half + column + tile)
                total = dot(left[span], right[:, source]) + dot(left_sib[span], right_sib[:, source])
                total = total.astype(BF16)
                into = slice(offset + column, offset + column + tile)
                for x in range(xs):
                    for y in range(ys):
                        piece = total[(x * ys + y) * part : (x * ys + y + 1) * part]
                        if first:
                            targets[y][x * part : (x + 1) * part, into] = piece
                        else:
                            targets[x][y * part : (y + 1) * part, into] = piece
        start += width
        offset += half


def joint_gradient(place, left, right, left_sib, right_sib, widths):
    sections = len(widths)
    rows, tokens = left.shape[0] // sections, left.shape[1]
    width = sum(widths)
    xs, ys = place.sizes["x"], place.sizes["y"]
    half = width // 2
    shapes = [(rows // xs, half)] * xs + [(rows // ys, half)] * ys
    outs = local_call(
        functools.partial(joint_kernel, xs, ys, widths),
        [(shape, BF16) for shape in shapes],
        (left, left_sib, right, right_sib),
        "joint_gradient",
    )
    return outs[:xs], outs[xs:]


def arranged(order, left):
    return lax.dot_general(
        order, left, (((1,), (1,)), ((), ())), preferred_element_type=jnp.float32
    ).astype(jnp.bfloat16)


def own_half(ordered):
    return ordered[: ordered.shape[0] // CORES]


def other_half(ordered):
    return ordered[ordered.shape[0] // CORES :]


def together(*values):
    return lax.optimization_barrier(values)


def fold_kernel(counts, splits, merged, *refs):
    at = 0
    outs = refs[sum(counts) :]
    for block, count in enumerate(counts):
        total = refs[at][...].astype(F32)
        for ref in refs[at + 1 : at + count]:
            total = total + ref[...].astype(F32)
        at += count
        low = total.astype(BF16)
        rows = low.shape[-2] // splits[block]
        for k in range(splits[block]):
            piece = low[..., k * rows : (k + 1) * rows, :]
            if merged:
                outs[k][block] = piece
            else:
                outs[sum(splits[:block]) + k][...] = piece


def fold(blocks, splits, merged):
    flat = [a for block in blocks for a in block]
    shape = flat[0].shape
    columns = shape[-1]
    tile = max(t for t in range(LANES, 1025, LANES) if columns % t == 0 and t <= columns // 2)

    def spec(full):
        lead = (0,) * (len(full) - 1)
        return pl.BlockSpec(full[:-1] + (tile,), lambda j: lead + (j,))

    if merged:
        outs = [(len(blocks), shape[0] // splits[0], columns)] * splits[0]
    else:
        outs = []
        for block, cuts in zip(blocks, splits):
            full = block[0].shape
            outs += [full[:-2] + (full[-2] // cuts, columns)] * cuts
    return pl.pallas_call(
        functools.partial(fold_kernel, [len(b) for b in blocks], splits, merged),
        grid=(columns // tile,),
        in_specs=[spec(a.shape) for a in flat],
        out_specs=[spec(full) for full in outs],
        out_shape=[jax.ShapeDtypeStruct(full, BF16) for full in outs],
        compiler_params=pltpu.CompilerParams(vmem_limit_bytes=12 * 1024 * 1024),
        cost_estimate=pl.CostEstimate(flops=0, bytes_accessed=0, transcendentals=0),
        name="fold",
    )(*flat)


class Shares:
    ORDERS = (("x", "y"), ("y", "x"))

    def __init__(self, place, lefts, rights):
        self.place = place
        self.widths = [sum(r.shape[1] for r in section) for section in rights]
        self.columns = [[r.shape[1] for r in section] for section in rights]
        flat = [r for section in rights for r in section]
        self.right = jnp.concatenate(flat, 1) if len(flat) > 1 else flat[0]
        self.lefts = lefts

    def to_core(self):
        return self.right

    def go_core(self, sent):
        return self.place.turn(sent, "core", 1)

    def join(self, left_siblings, right_sibling):
        left, sibling = (
            (pieces[0] if len(pieces) == 1 else jnp.concatenate(pieces, 0))
            for pieces in ([own_half(left) for left in self.lefts], left_siblings)
        )
        self.pieces = joint_gradient(
            self.place, left, self.right, sibling, right_sibling, self.widths
        )
        return tuple(tuple(pieces[1:]) for pieces in self.pieces)

    def go(self, sent, stage):
        return tuple(
            tuple(self.place.turn(piece, order[stage], k + 1) for k, piece in enumerate(pieces))
            for pieces, order in zip(sent, self.ORDERS)
        )

    def to_second(self, arrived):
        splits = [self.place.sizes[order[1]] for order in self.ORDERS]
        blocks = [(self.pieces[half][0],) + arrived[half] for half in range(2)]
        outs = fold(blocks, splits, False)
        self.kept = (outs[0], outs[splits[0]])
        return tuple(outs[1 : splits[0]]), tuple(outs[splits[0] + 1 :])

    def to_third(self, arrived):
        blocks = [(self.kept[half],) + arrived[half] for half in range(2)]
        self.kept, sent = fold(blocks, (2, 2), True)
        return sent

    def go_third(self, sent):
        return self.place.swap(sent, "z", 1)

    def to_fourth(self, arrived):
        self.kept, sent = fold([(self.kept, arrived)], (2,), False)
        return sent

    def go_fourth(self, sent):
        return self.place.swap(sent, "z", 2)

    def to_owners(self, arrived):
        cuts = self.place.sizes["z"]
        blocks = [(self.kept[half],) + arrived[half] for half in range(2)]
        self.kept, *sent = fold(blocks, (cuts, cuts), True)
        return tuple(sent)

    def go_owners(self, sent):
        return tuple(
            self.place.swap(piece, "z", k // 2 + 2 * (k % 2))
            for k, piece in enumerate(sent, start=1)
        )

    def split(self, arrived, widths):
        rows = self.kept.shape[1]
        summands = (self.kept,) + tuple(arrived)
        return local_call(
            functools.partial(split_kernel, len(summands)),
            [((rows, w), F32) for w in widths],
            summands,
            "split",
        )

    def shares(self, *arrived):
        total = self.kept.astype(F32)
        for piece in arrived:
            total = total + piece.astype(F32)
        shares = []
        offset = 0
        for width, columns in zip(self.widths, self.columns):
            section = jnp.concatenate(
                [total[half, :, offset : offset + width // 2] for half in range(2)], 1
            )
            offset += width // 2
            start = 0
            for w in columns:
                shares.append(section[:, start : start + w])
                start += w
        return shares


def split_kernel(count, *refs):
    total = sum(ref[...].astype(F32) for ref in refs[:count])
    half = total.shape[2]
    start = 0
    for out in refs[count:]:
        stop = start + out.shape[1]
        for k in range(2):
            low, high = max(start, k * half), min(stop, (k + 1) * half)
            if low < high:
                out[:, low - start : high - start] = total[k, :, low - k * half : high - k * half]
        start = stop


class KeyOwners:
    def __init__(self, place, slopes):
        self.place = place
        self.paired = place.sizes["x"] == 2
        self.kept = slopes

    def to_first(self):
        if not self.paired:
            return self.kept
        half = self.kept.shape[0] // 2
        sent = self.kept[half:]
        self.kept = self.kept[:half]
        return sent

    def go(self, sent, stage):
        if not self.paired:
            if stage:
                return sent
            return lax.psum_scatter(sent, "seq", scatter_dimension=0, tiled=True)
        axis, bit = (("z", 1), ("z", 2), ("x", 1))[stage]
        return self.place.swap(sent, axis, bit)

    def to_next(self, arrived):
        if not self.paired:
            return arrived
        total = (self.kept.astype(F32) + arrived.astype(F32)).astype(BF16)
        half = total.shape[0] // 2
        self.kept = total[:half]
        return total[half:]

    def summands(self, arrived):
        return (self.kept, arrived) if self.paired else (arrived,)


def body(
    inputs,
    segments,
    cotangent,
    input_gain,
    query_weight,
    key_weight,
    value_weight,
    attention_weight,
    gating_weight,
    inner_weight,
    step_weight,
    step_bias,
    decay_log,
    skip_scale,
    conv_weight,
    conv_bias,
    mixer_gain,
    mixer_weight,
    feed_gain,
    gate_weight,
    up_weight,
    down_weight,
):
    place = Place()
    xs = place.sizes["x"]
    count, width = inputs.shape[1], inputs.shape[2]
    low_input = inputs[0]
    hidden = low_input.astype(F32)
    slope = cotangent[0]
    seg_row = segments[0]
    length = seg_row.shape[0]
    group, along = lax.axis_index("dp"), lax.axis_index("seq")
    position = along.reshape(1).astype(jnp.int32)
    inner_width = inner_weight.shape[1]
    part_width = WIDTH // xs

    halo, low_input = together(low_input[count - HALO :], low_input)
    halo = passed_along(halo, "seq", 1)
    cosine, sine = turn_tables(along * count, count)
    normed_low, pairs, table = local_call(
        front_kernel,
        [((count, width), BF16), ((count, 2 * LANES), BF16), ((8, inner_width), F32)],
        (
            low_input,
            key_weight,
            value_weight,
            cosine,
            sine,
            conv_bias,
            input_gain,
            mixer_gain,
            skip_scale,
            step_bias,
            decay_log,
        ),
        "front",
        alone=True,
    )
    near = jnp.concatenate([pairs] + [place.turn(pairs, "x", k) for k in range(1, xs)], 0)
    near, halo, normed_low = together(near, halo, normed_low)
    far = tuple(place.turn(near, "z", k) for k in range(1, place.sizes["z"]))
    step_turned = step_weight.T
    (
        inner,
        raw,
        channels,
        scaled,
        inflow,
        readout,
        steps,
        logs,
        logs_turned,
        marks,
        marks_turned,
        factor,
        *states,
    ) = local_call(
        functools.partial(prep_kernel, xs),
        [
            ((HALO + count, inner_width), BF16),
            ((count, LANES), F32),
            ((count, WIDTH), F32),
            ((count, WIDTH), BF16),
            ((count, STATE), BF16),
            ((count, STATE), BF16),
            ((count, LANES), F32),
            ((count, LANES), F32),
            ((LANES, count), F32),
            ((count, 8), F32),
            ((8, count), F32),
            ((count, inner_width), BF16),
        ]
        + [((STATE + EXTRA, part_width), BF16)] * xs,
        (position, halo, normed_low, table, inner_weight, step_turned, conv_weight, segments),
        "prepare",
        alone=True,
        scratch=[
            pltpu.VMEM((HALO + count, width), BF16),
            pltpu.VMEM((xs, STATE + EXTRA, part_width), BF16),
            pltpu.VMEM((2 * LANES, WIDTH), BF16),
            pltpu.VMEM((count, WIDTH), F32),
            pltpu.VMEM((count, WIDTH), F32),
            pltpu.VMEM((count, WIDTH), BF16),
        ],
        smem=(0,),
    )

    states, normed_low, group, along = together(tuple(states), normed_low, group, along)
    pieces = dealt(place, states)
    gating = product(normed_low, gating_weight)
    order = place.share_order(width, group, along)
    ordered = arranged(order, normed_low)
    pieces, gating, normed_low, order, ordered = together(
        pieces, gating, normed_low, order, ordered
    )
    total, walls = level(place, pieces, position, seg_row, count)

    total, normed_low, ordered, scaled = together(total, normed_low, ordered, scaled)
    totals = levels_met(place, total)
    fixed = (logs, logs_turned, marks, marks_turned, inflow, readout)
    (inner_part,) = inner_call(inner_kernel, fixed, (scaled,), (F32,), (), "inner", 2)

    ordered_sibling = place.turn(other_half(ordered), "core", 1)
    queries, attention_low, exact, spread, everything = local_call(
        functools.partial(attend_kernel, xs),
        [
            ((count, HEADS * HEAD), BF16),
            ((count, HEADS * HEAD), BF16),
            ((HEADS * HEAD, count), F32),
            ((HEADS, count), F32),
            ((length, 2 * LANES), BF16),
        ],
        (position, normed_low, query_weight, cosine, sine, segments, near, *far),
        "attend",
        slack=8,
        scratch=[
            pltpu.VMEM((HEADS, count), F32),
            pltpu.VMEM((HEADS, count), F32),
            pltpu.VMEM((HEADS * HEAD, count), F32),
        ],
        smem=(0,),
        far=tuple(range(6, 7 + len(far))),
        sems=(1 + len(far),),
    )
    totals, attention_low, ordered_sibling, inner_part, slope, order = together(
        totals, attention_low, ordered_sibling, inner_part, slope, order
    )
    results, level_walls = arrival(
        place, pieces, totals, walls, total, position, seg_row, count
    )

    results, attention_low, slope, order = together(results, attention_low, slope, order)
    pieces = dealt(place, results)
    attention_branch = product(attention_low, attention_weight)
    ordered_slope = arranged(order, slope)
    pieces, attention_branch, ordered_slope = together(pieces, attention_branch, ordered_slope)
    hidden_width = gate_weight.shape[1]
    (
        tail_low,
        scanned,
        entering,
        mixed_sum,
        feed_low,
        gate_raw,
        up_raw,
        activated_low,
    ) = local_call(
        functools.partial(entering_kernel, xs),
        [
            ((count, WIDTH), BF16),
            ((count, WIDTH), F32),
            ((STATE, WIDTH), BF16),
            ((count, width), F32),
            ((count, width), BF16),
            ((count, hidden_width), F32),
            ((count, hidden_width), F32),
            ((count, hidden_width), BF16),
        ],
        (
            position,
            inner_part,
            readout,
            logs,
            marks,
            channels,
            gating,
            table,
            low_input,
            attention_branch,
            feed_gain,
            mixer_weight,
            gate_weight,
            up_weight,
            *pieces,
        ),
        "entering",
        scratch=[
            pltpu.VMEM((count, WIDTH), F32),
            pltpu.VMEM((2 * LANES, WIDTH), BF16),
            pltpu.VMEM((count, WIDTH), F32),
            pltpu.VMEM(mixer_weight.shape, BF16),
            pltpu.VMEM(gate_weight.shape, BF16),
            pltpu.VMEM(up_weight.shape, BF16),
        ],
        sems=(3,),
        smem=(0,),
        far=(11, 12, 13),
    )

    down = Shares(place, (ordered_slope,), ((activated_low,),))
    sent, slope_half, gate_raw, up_raw, slope, feed_low, order = together(
        down.to_core(), other_half(ordered_slope), gate_raw, up_raw, slope, feed_low, order
    )
    arrived = down.go_core(sent)
    slope_sibling = place.turn(slope_half, "core", 1)
    gate_low, up_low = local_call(
        unit_back_kernel,
        [(gate_raw.shape, BF16), (up_raw.shape, BF16)],
        (slope, down_weight, gate_raw, up_raw),
        "unit_back",
    )
    ordered_feed = arranged(order, feed_low)
    arrived, slope_sibling, gate_low, up_low, ordered_feed = together(
        arrived, slope_sibling, gate_low, up_low, ordered_feed
    )
    sent = down.join([slope_sibling], arrived)

    gate = Shares(place, (ordered_feed,), ((gate_low,),))
    up = Shares(place, (ordered_feed,), ((up_low,),))
    sent, feed_half, gate_low, up_low = together(
        sent, other_half(ordered_feed), gate_low, up_low
    )
    arrived = down.go(sent, 0)
    gate_arrived, up_arrived = gate.go_core(gate_low), up.go_core(up_low)
    feed_sibling = place.turn(feed_half, "core", 1)
    mixed_slope, branch_low, feed_sums = local_call(
        feed_back_kernel,
        [((count, width), F32), ((count, width), BF16), ((8, width), F32)],
        (gate_low, up_low, gate_weight, up_weight, mixed_sum, slope, feed_gain),
        "feed_back",
    )
    scanned_slope, gating_low, tail_sums, *state_slopes = local_call(
        functools.partial(tail_back_kernel, xs),
        [((count, WIDTH), BF16), ((count, WIDTH), BF16), ((8, WIDTH), F32)]
        + [((STATE, part_width), BF16)] * xs,
        (
            position,
            branch_low,
            mixer_weight,
            scanned,
            channels,
            gating,
            table,
            logs,
            marks,
            readout,
        ),
        "tail_back",
        scratch=[
            pltpu.VMEM((count, WIDTH), F32),
            pltpu.VMEM((xs, STATE, part_width), BF16),
            pltpu.VMEM((2 * LANES, WIDTH), BF16),
            pltpu.VMEM((count, WIDTH), F32),
            pltpu.VMEM((count, WIDTH), BF16),
            pltpu.VMEM((count, WIDTH), F32),
        ],
        smem=(0,),
    )
    (
        arrived,
        gate_arrived,
        up_arrived,
        feed_sibling,
        state_slopes,
        branch_low,
        scanned_slope,
        gating_low,
        order,
    ) = together(
        arrived,
        gate_arrived,
        up_arrived,
        feed_sibling,
        tuple(state_slopes),
        branch_low,
        scanned_slope,
        gating_low,
        order,
    )

    gate_sent = gate.join([feed_sibling], gate_arrived)
    ordered_branch = arranged(order, branch_low)
    mixers = Shares(place, (ordered_branch, ordered), ((attention_low, tail_low), (gating_low,)))
    state_slopes, gate_sent, mixers_sent, branch_half, arrived, branch_low = together(
        state_slopes,
        gate_sent,
        mixers.to_core(),
        other_half(ordered_branch),
        arrived,
        branch_low,
    )
    state_pieces = dealt(place, state_slopes)
    gate_arrived = gate.go(gate_sent, 0)
    mixers_arrived = mixers.go_core(mixers_sent)
    branch_sibling = place.turn(branch_half, "core", 1)
    attention_slope = product_right(branch_low, attention_weight).astype(BF16)
    down_sent = down.to_second(arrived)
    mixers_sent = mixers.join([branch_sibling, ordered_sibling], mixers_arrived)
    state_pieces, gate_arrived, mixers_sent, down_sent, attention_slope = together(
        state_pieces, gate_arrived, mixers_sent, down_sent, attention_slope
    )
    total = level_back(place, state_pieces, walls, position, seg_row, count)

    total, mixers_sent, attention_slope, up_arrived, feed_sibling, gate_arrived = together(
        total, mixers_sent, attention_slope, up_arrived, feed_sibling, gate_arrived
    )
    totals = levels_met(place, total)
    mixers_arrived = mixers.go(mixers_sent, 0)
    query_low, pair_slope = local_call(
        functools.partial(attend_back_kernel, xs),
        [((count, HEADS * HEAD), BF16), ((length, 2 * LANES), BF16)],
        (
            position,
            queries,
            everything,
            attention_slope,
            exact,
            spread,
            segments,
            cosine,
            sine,
        ),
        "attend_back",
        scratch=[
            pltpu.VMEM((HEADS * HEAD, count), F32),
            pltpu.VMEM((HEADS, count), F32),
            pltpu.VMEM((HEADS * HEAD, count), F32),
        ],
        smem=(0,),
    )
    owners = KeyOwners(place, pair_slope)
    pair_sent = owners.to_first()
    up_sent = up.join([feed_sibling], up_arrived)
    totals, mixers_arrived, pair_sent, up_sent = together(
        totals, mixers_arrived, pair_sent, up_sent
    )
    results = arrival_back(
        place, state_pieces, totals, walls, level_walls, position, seg_row, count
    )

    (
        results,
        pair_sent,
        up_sent,
        mixers_arrived,
        gate_arrived,
        scanned_slope,
        activated_low,
    ) = together(
        results, pair_sent, up_sent, mixers_arrived, gate_arrived, scanned_slope, activated_low
    )
    pieces = dealt(place, results)
    pair_arrived = owners.go(pair_sent, 0)
    up_arrived = up.go(up_sent, 0)
    scaled_slope, inflow_part, readout_part = inner_call(
        inner_back_kernel,
        fixed,
        (scaled, scanned_slope),
        (F32,),
        (((count, STATE), F32), ((count, STATE), F32)),
        "inner_back",
        3,
    )
    mixers_sent = mixers.to_second(mixers_arrived)
    gate_sent = gate.to_second(gate_arrived)
    output = (mixed_sum + product(activated_low, down_weight)).astype(BF16)
    pieces, pair_arrived, up_arrived, mixers_sent, gate_sent, scaled_slope, output = together(
        pieces, pair_arrived, up_arrived, mixers_sent, gate_sent, scaled_slope, output
    )

    pieces, pair_sent, mixers_sent, gate_sent, up_arrived = together(
        pieces, owners.to_next(pair_arrived), mixers_sent, gate_sent, up_arrived
    )
    mixers_arrived = mixers.go(mixers_sent, 1)
    gate_arrived = gate.go(gate_sent, 1)
    pair_arrived = owners.go(pair_sent, 1)
    inner_low, edges, conv_sums, raw_slope, small = local_call(
        functools.partial(leaving_kernel, xs),
        [
            ((count, inner_width), BF16),
            ((2 * HALO, inner_width), F32),
            ((8, inner_width), F32),
            ((count, LANES), BF16),
            ((8, LANES), F32),
        ],
        (
            position,
            entering,
            scanned,
            scanned_slope,
            scaled,
            channels,
            scaled_slope,
            inflow,
            readout,
            inflow_part,
            readout_part,
            steps,
            raw,
            logs,
            marks,
            inner,
            factor,
            conv_weight,
            table,
            *pieces,
        ),
        "leaving",
        scratch=[
            pltpu.VMEM((count, inner_width), F32),
            pltpu.VMEM((2 * LANES, WIDTH), BF16),
            pltpu.VMEM((STATE, WIDTH), BF16),
        ]
        + [pltpu.VMEM((count, WIDTH), F32)] * 4
        + [pltpu.VMEM((2, count, WIDTH), BF16)] * 3
        + [pltpu.VMEM((count, WIDTH), BF16)] * 2,
        smem=(0,),
    )
    mixers_arrived, gate_arrived, pair_arrived, inner_low, edges = together(
        mixers_arrived, gate_arrived, pair_arrived, inner_low, edges
    )

    mixers_sent, pair_sent, down_sent, inner_low, edges, up_arrived, gate_arrived = together(
        mixers.to_third(mixers_arrived),
        owners.to_next(pair_arrived),
        down_sent,
        inner_low,
        edges,
        up_arrived,
        gate_arrived,
    )
    returned = passed_along(edges[HALO - 8 : HALO], "seq", -1)
    pair_arrived = owners.go(pair_sent, 2)
    down_arrived = down.go(down_sent, 1)
    mixers_arrived = mixers.go_third(mixers_sent)
    up_sent = up.to_second(up_arrived)
    gate_sent = gate.to_third(gate_arrived)
    returned, pair_arrived, down_arrived, mixers_arrived, up_sent, gate_sent = together(
        returned, pair_arrived, down_arrived, mixers_arrived, up_sent, gate_sent
    )
    inner_low = lax.dynamic_update_slice(
        inner_low,
        (edges[HALO:] + jnp.pad(returned, ((HALO - 8, 0), (0, 0)))).astype(BF16),
        (count - HALO, 0),
    )
    (pair_low,) = local_call(
        pairs_back_kernel,
        [((count, 2 * LANES), BF16)],
        (*owners.summands(pair_arrived), cosine, sine),
        "pairs_back",
    )

    rest = Shares(place, (ordered,), ((inner_low, query_low, pair_low),))
    (
        rest_sent,
        up_sent,
        mixers_arrived,
        gate_sent,
        down_arrived,
        gating_low,
        query_low,
        pair_low,
        inner_low,
    ) = together(
        rest.to_core(),
        up_sent,
        mixers_arrived,
        gate_sent,
        down_arrived,
        gating_low,
        query_low,
        pair_low,
        inner_low,
    )
    rest_arrived = rest.go_core(rest_sent)
    up_arrived = up.go(up_sent, 1)
    mixers_arrived = mixers.go_fourth(mixers.to_fourth(mixers_arrived))
    gate_arrived = gate.go_third(gate_sent)
    input_gradient, packed = local_call(
        finish_kernel,
        [((count, width), F32), ((PACK_ROWS, width), F32)],
        (
            gating_low,
            query_low,
            inner_low,
            pair_low,
            gating_weight,
            query_weight,
            inner_weight,
            key_weight,
            value_weight,
            step_turned,
            low_input,
            table,
            mixed_slope,
            raw_slope,
            normed_low,
            tail_sums,
            conv_sums,
            small,
            feed_sums,
        ),
        "finish",
        scratch=[
            pltpu.VMEM(weight.shape, BF16)
            for weight in (gating_weight, query_weight, inner_weight, key_weight, value_weight)
        ],
        far=(4, 5, 6, 7, 8),
        sems=(5,),
    )
    rest_sent = rest.join([ordered_sibling], rest_arrived)
    rest_sent, up_arrived, mixers_arrived, gate_arrived, down_arrived, packed, input_gradient = (
        together(
            rest_sent, up_arrived, mixers_arrived, gate_arrived, down_arrived, packed, input_gradient
        )
    )

    rest_arrived = rest.go(rest_sent, 0)
    packed = all_sum(place, packed, ("core",))
    up_arrived, mixers_arrived, gate_arrived, down_arrived, packed = together(
        up_arrived, mixers_arrived, gate_arrived, down_arrived, packed
    )
    gate_arrived = gate.go_fourth(gate.to_fourth(gate_arrived))
    up_arrived = up.go_third(up.to_third(up_arrived))
    down_arrived = down.go_third(down.to_third(down_arrived))
    share_attention, share_mixer, share_gating = mixers.shares(mixers_arrived)
    share_attention, share_mixer = share_attention.T, share_mixer.T
    rest_arrived, gate_arrived, up_arrived, down_arrived, packed, share_attention, share_mixer = (
        together(
            rest_arrived,
            gate_arrived,
            up_arrived,
            down_arrived,
            packed,
            share_attention,
            share_mixer,
        )
    )

    rest_sent, up_sent, down_sent, gate_arrived, packed = together(
        rest.to_second(rest_arrived),
        up.to_fourth(up_arrived),
        down.to_fourth(down_arrived),
        gate_arrived,
        packed,
    )
    rest_arrived = rest.go(rest_sent, 1)
    up_arrived = up.go_fourth(up_sent)
    down_arrived = down.go_fourth(down_sent)
    packed = all_sum(place, packed, ("z",))
    (share_gate,) = gate.shares(gate_arrived)
    rest_arrived, up_arrived, down_arrived, packed, share_gate = together(
        rest_arrived, up_arrived, down_arrived, packed, share_gate
    )

    rest_sent, up_arrived, down_arrived, packed = together(
        rest.to_owners(rest_arrived), up_arrived, down_arrived, packed
    )
    rest_arrived = rest.go_owners(rest_sent)
    packed = all_sum(place, packed, ("x", "y"))
    (share_up,), (share_down,) = up.shares(up_arrived), down.shares(down_arrived)
    share_down = share_down.T
    sums = tuple(
        local_call(
            unpack_kernel,
            [
                ((width, SSM_HEADS), F32),
                ((width,), F32),
                ((width,), F32),
                ((WIDTH,), F32),
                ((SSM_HEADS,), F32),
                ((SSM_HEADS,), F32),
                ((SSM_HEADS,), F32),
                ((KERNEL, inner_width), F32),
                ((inner_width,), F32),
            ],
            (packed,),
            "unpack",
        )
    )
    rest_arrived, sums, share_up, share_down = together(rest_arrived, sums, share_up, share_down)
    (
        step_sum,
        gain_sum,
        feed_gain_sum,
        mixer_gain_sum,
        skip_sum,
        step_bias_sum,
        decay_sum,
        conv_sum,
        conv_bias_sum,
    ) = sums
    share_inner, share_query, share_key, share_value = rest.split(
        rest_arrived, (inner_width, HEADS * HEAD, LANES, LANES)
    )
    return (
        output[None],
        input_gradient[None],
        gain_sum,
        share_query,
        share_key,
        share_value,
        share_attention,
        share_gating,
        share_inner,
        step_sum,
        step_bias_sum,
        decay_sum,
        skip_sum,
        conv_sum,
        conv_bias_sum,
        mixer_gain_sum,
        share_mixer,
        feed_gain_sum,
        share_gate,
        share_up,
        share_down,
    )


def solution(mesh):
    in_specs = (
        P("dp", "seq", None),
        P("dp", None),
        P("dp", "seq", None),
        P(),
        P(),
        P(),
        P(),
        P(),
        P(),
        P(),
        P(),
        P(),
        P(),
        P(),
        P(),
        P(),
        P(),
        P(),
        P(),
        P(),
        P(),
        P(),
    )
    out_specs = (
        P("dp", "seq", None),
        P("dp", "seq", None),
        P(),
        P(("dp", "seq"), None),
        P(("dp", "seq"), None),
        P(("dp", "seq"), None),
        P(None, ("dp", "seq")),
        P(("dp", "seq"), None),
        P(("dp", "seq"), None),
        P(),
        P(),
        P(),
        P(),
        P(),
        P(),
        P(),
        P(None, ("dp", "seq")),
        P(),
        P(("dp", "seq"), None),
        P(("dp", "seq"), None),
        P(None, ("dp", "seq")),
    )
    return jax.shard_map(body, mesh=mesh, in_specs=in_specs, out_specs=out_specs, check_vma=False)
```
